32 devices in a mesh: gx: 2 (over y), gy: 4 (over z), gz: 4 (over x, core).
Axes of the slice: x: 2, y: 2, z: 4, core: 2. Of those that a mesh axis runs over, the one named last changes fastest.
Arguments:
- right_side: float32 [3, 16, 32, 512], P(None, 'gx', 'gy', 'gz'), may hold values from -17 to 17
- phase_labels: int32 [8, 16, 256], P('gx', 'gy', 'gz'), may hold values from 0 to 7
- phase_moduli: float32 [8], replicated, may hold values from 0.03 to 0.3
- coarse_nodes: int32 [16, 32, 512], P('gx', 'gy', 'gz'), may hold values from 0 to 5
- coarse_inverse: float32 [1152, 1152], P(('gx', 'gy', 'gz')), as said below
Outputs:
- solution_field: float32 [3, 16, 32, 512], P(None, 'gx', 'gy', 'gz')
- residual: float32 [3, 16, 32, 512], P(None, 'gx', 'gy', 'gz')
The draws below stay inside these ranges and needn't reach their ends.
Inputs may be any that keep to these rules, and one draw needn't show every extreme that they name: `coarse_inverse`: symmetric.
All inputs are finite; a program needn't handle non-finite values.
Results may differ from the reference program's by a relative error of at most 0.0003.
Values sent between devices are 32-bit elements; how exact they have to be, the bound alone decides.
No kernel may reach another device: no remote copies, remote signals or barrier semaphores. Data moves between devices by JAX's collectives and lax.ppermute only.
A program may use at most 64 MiB of HBM per device.

```python
import math
import jax
import jax.numpy as jnp
from jax import lax

CX = 8
CY = 8
CZ = 128
NPHASE = 8
NAGG = 6
SWEEPS = 4
ITERS = 2
NC = 1152
NX = 16
NY = 32
NZ = 512
N_GX = 2
N_GY = 4
N_GZ = 4


def draw_right_side(key, part):
    across_x = (jnp.arange(NX, dtype=jnp.float32) + 0.5) / NX
    ramp = (1.0 + 2.0 * across_x)[None, :, None, None]
    return jax.random.truncated_normal(key, -4.0, 4.0, (3, NX, NY, NZ), jnp.float32) * ramp


def draw_coarse_inverse(key, part):
    order = NC
    base = 0.3 * math.sqrt(NAGG / (CX * CY * CZ))
    spread = base / (4.0 * math.sqrt(order / 6.0))
    first_key, second_key = jax.random.split(key)
    noise = jax.random.uniform(first_key, (order, order), jnp.float32, -1.0, 1.0)
    symmetric = 0.5 * (noise + noise.T) * spread
    lifted = base * jax.random.uniform(second_key, (order,), jnp.float32, 1.0, 1.5)
    rows = jnp.arange(order)[:, None]
    cols = jnp.arange(order)[None, :]
    return jnp.where(rows == cols, lifted[:, None], symmetric)


def place_ends(result, stream_key, smallest, largest):
    longest = result.shape.index(max(result.shape))
    spots = []
    for shift in (0, 1):
        where = [jax.random.randint(jax.random.fold_in(stream_key, axis), (), 0, length) for axis, length in enumerate(result.shape)]
        where[longest] = (where[longest] + shift) % result.shape[longest]
        spots.append(tuple(where))
    return result.at[spots[0]].set(smallest).at[spots[1]].set(largest)


def setup_inputs(seed: int = 0) -> dict:
    splits = jax.random.split(jax.random.key(seed), 6)
    return {
        "right_side": draw_right_side(jax.random.fold_in(splits[5], 71), 0),
        "phase_labels": place_ends(jax.random.randint(splits[1], (NX // 2, NY // 2, NZ // 2), 0, NPHASE), jax.random.fold_in(splits[1], 1), 0, NPHASE - 1).astype(jnp.int32),
        "phase_moduli": jnp.clip(jnp.exp(jax.random.uniform(splits[2], (NPHASE,), jnp.float32, math.log(0.03), math.log(0.3))), 0.03, 0.3),
        "coarse_nodes": place_ends(jax.random.randint(splits[3], (NX, NY, NZ), 0, NAGG), jax.random.fold_in(splits[3], 1), 0, NAGG - 1).astype(jnp.int32),
        "coarse_inverse": draw_coarse_inverse(jax.random.fold_in(splits[5], 71), 0),
    }


bond_ratio = 0.5
relax = 0.6
highest = lax.Precision.HIGHEST
neighbour_offsets = tuple((shift_x, shift_y, shift_z) for shift_x in (-1, 0, 1) for shift_y in (-1, 0, 1) for shift_z in (-1, 0, 1) if shift_x * shift_x + shift_y * shift_y + shift_z * shift_z > 0)


def inner_view(array, shift_x, shift_y, shift_z):
    size_x, size_y, size_z = array.shape[-3:]
    return array[..., 1 + shift_x:size_x - 1 + shift_x, 1 + shift_y:size_y - 1 + shift_y, 1 + shift_z:size_z - 1 + shift_z]


def spring_force(field_pad, stiff_pad):
    centre = inner_view(field_pad, 0, 0, 0)
    stiff_centre = inner_view(stiff_pad, 0, 0, 0)
    parts = [jnp.zeros_like(centre[0]) for component in range(3)]
    for offset in neighbour_offsets:
        length = offset[0] * offset[0] + offset[1] * offset[1] + offset[2] * offset[2]
        spring = 0.5 * (stiff_centre + inner_view(stiff_pad, offset[0], offset[1], offset[2])) / length
        partner = inner_view(field_pad, offset[0], offset[1], offset[2])
        stretch = [centre[component] - partner[component] for component in range(3)]
        projected = jnp.zeros_like(stretch[0])
        for component in range(3):
            if offset[component] != 0:
                projected = projected + offset[component] * stretch[component]
        for component in range(3):
            summand = stretch[component]
            if offset[component] != 0:
                summand = summand + (bond_ratio * offset[component] / length) * projected
            parts[component] = parts[component] + spring * summand
    return jnp.stack(parts)


def diagonal(stiff_pad):
    stiff_centre = inner_view(stiff_pad, 0, 0, 0)
    parts = [jnp.zeros_like(stiff_centre) for component in range(3)]
    for offset in neighbour_offsets:
        length = offset[0] * offset[0] + offset[1] * offset[1] + offset[2] * offset[2]
        spring = 0.5 * (stiff_centre + inner_view(stiff_pad, offset[0], offset[1], offset[2])) / length
        for component in range(3):
            parts[component] = parts[component] + spring * (1.0 + bond_ratio * offset[component] * offset[component] / length)
    return jnp.stack(parts)


def local_solve(residual_ext, stiff_rim, diag_ext):
    widths = [(0, 0)] * (residual_ext.ndim - 3) + [(1, 1)] * 3
    solution = relax * residual_ext / diag_ext
    for sweep in range(SWEEPS - 1):
        solution = solution + relax * (residual_ext - spring_force(jnp.pad(solution, widths), stiff_rim)) / diag_ext
    return solution


def solve_members(members):
    return local_solve(members[0], members[1], members[2])


def cross(first, second):
    return jnp.stack([first[1] * second[2] - first[2] * second[1], first[2] * second[0] - first[0] * second[2], first[0] * second[1] - first[1] * second[0]])


def local_coords(size_x, size_y, size_z):
    along_x = ((2.0 * jnp.arange(size_x, dtype=jnp.float32) + 1.0) / size_x - 1.0).reshape(size_x, 1, 1)
    along_y = ((2.0 * jnp.arange(size_y, dtype=jnp.float32) + 1.0) / size_y - 1.0).reshape(1, size_y, 1)
    along_z = ((2.0 * jnp.arange(size_z, dtype=jnp.float32) + 1.0) / size_z - 1.0).reshape(1, 1, size_z)
    return (along_x, along_y, along_z)


def fold_blocks(extended, block_axis, local_axis):
    size = extended.shape[local_axis]
    count = size - 2
    blocks = extended.shape[block_axis]
    inner = lax.slice_in_dim(extended, 1, size - 1, axis=local_axis)
    lower = lax.slice_in_dim(extended, 0, 1, axis=local_axis)
    upper = lax.slice_in_dim(extended, size - 1, size, axis=local_axis)
    empty = jnp.zeros_like(lax.slice_in_dim(upper, 0, 1, axis=block_axis))
    from_below = jnp.concatenate([empty, lax.slice_in_dim(upper, 0, blocks - 1, axis=block_axis)], axis=block_axis)
    from_above = jnp.concatenate([lax.slice_in_dim(lower, 1, blocks, axis=block_axis), empty], axis=block_axis)
    head = lax.slice_in_dim(inner, 0, 1, axis=local_axis) + from_below
    tail = lax.slice_in_dim(inner, count - 1, count, axis=local_axis) + from_above
    middle = lax.slice_in_dim(inner, 1, count - 1, axis=local_axis)
    return jnp.concatenate([head, middle, tail], axis=local_axis)


def reference(right_side, phase_labels, phase_moduli, coarse_nodes, coarse_inverse):
    coarse_stiff = jnp.take(phase_moduli, phase_labels, axis=0)
    stiffness = jnp.repeat(jnp.repeat(jnp.repeat(coarse_stiff, 2, axis=0), 2, axis=1), 2, axis=2)

    def blocks(padded, width):
        lead = padded.ndim - 3
        index_x = jnp.arange(N_GX, dtype=jnp.int32)[:, None] * CX + jnp.arange(CX + 2 * width, dtype=jnp.int32)[None, :]
        index_y = jnp.arange(N_GY, dtype=jnp.int32)[:, None] * CY + jnp.arange(CY + 2 * width, dtype=jnp.int32)[None, :]
        index_z = jnp.arange(N_GZ, dtype=jnp.int32)[:, None] * CZ + jnp.arange(CZ + 2 * width, dtype=jnp.int32)[None, :]
        moved = jnp.take(padded, index_x, axis=lead)
        moved = jnp.take(moved, index_y, axis=lead + 2)
        moved = jnp.take(moved, index_z, axis=lead + 4)
        order = list(range(lead)) + [lead, lead + 2, lead + 4, lead + 1, lead + 3, lead + 5]
        return jnp.transpose(moved, order)

    block_count = N_GX * N_GY * N_GZ
    stiff_rim = blocks(jnp.pad(stiffness, 2), 2)
    stiff_flat = stiff_rim.reshape((block_count,) + stiff_rim.shape[3:])
    diag_flat = lax.map(diagonal, stiff_flat)
    stiff_pad = jnp.pad(stiffness, 1)
    node_blocks = coarse_nodes.reshape(N_GX, CX, N_GY, CY, N_GZ, CZ).transpose(0, 2, 4, 1, 3, 5)
    coords = local_coords(CX, CY, CZ)
    widths = ((0, 0), (1, 1), (1, 1), (1, 1))

    def precondition(residual):
        extended = blocks(jnp.pad(residual, widths), 1)
        ext_flat = jnp.moveaxis(extended.reshape((3, block_count) + extended.shape[4:]), 1, 0)
        solved_flat = lax.map(solve_members, (ext_flat, stiff_flat, diag_flat))
        solution = jnp.moveaxis(solved_flat, 0, 1).reshape(extended.shape)
        folded = fold_blocks(fold_blocks(fold_blocks(solution, 1, 4), 2, 5), 3, 6)
        pieces = residual.reshape(3, N_GX, CX, N_GY, CY, N_GZ, CZ).transpose(0, 1, 3, 5, 2, 4, 6)
        moments = jnp.concatenate([pieces, cross(coords, pieces)], axis=0)
        sums = jnp.stack([jnp.sum(jnp.where(node_blocks == node, moments, 0.0), axis=(4, 5, 6)) for node in range(NAGG)], axis=-1)
        coarse = jnp.transpose(sums, (1, 2, 3, 4, 0)).reshape(-1)
        solved = jnp.dot(coarse_inverse, coarse, precision=highest).reshape(N_GX, N_GY, N_GZ, NAGG, 6)
        solved_modes = jnp.transpose(solved, (4, 0, 1, 2, 3))
        per_cell = jnp.zeros_like(moments)
        for node in range(NAGG):
            per_cell = per_cell + jnp.where(node_blocks == node, solved_modes[..., node][..., None, None, None], 0.0)
        total = folded + per_cell[:3] + cross(per_cell[3:], coords)
        return total.transpose(0, 1, 4, 2, 5, 3, 6).reshape(3, N_GX * CX, N_GY * CY, N_GZ * CZ)

    def operate(vector):
        return spring_force(jnp.pad(vector, widths), stiff_pad)

    solution_field = jnp.zeros_like(right_side)
    residual = right_side
    search = precondition(residual)
    direction = search
    norm_now = jnp.sum(residual * search)
    for step in range(ITERS):
        image = operate(direction)
        step_size = norm_now / jnp.sum(direction * image)
        solution_field = solution_field + step_size * direction
        residual = residual - step_size * image
        if step + 1 < ITERS:
            search = precondition(residual)
            norm_next = jnp.sum(residual * search)
            direction = search + (norm_next / norm_now) * direction
            norm_now = norm_next
    return (solution_field, residual)
```

```python
import jax
import jax.numpy as jnp
from jax import lax
from jax.experimental import pallas as pl
from jax.experimental.pallas import tpu as pltpu
from jax.sharding import PartitionSpec as P

AXES = ("gx", "gy", "gz")
SWEEPS = 4
relax = 0.6
highest = lax.Precision.HIGHEST
f32 = jnp.float32
LANES = 128
EDGE = 8
BLOCK = 16

ALONG1, ACROSS1 = 0.75, 0.5
ALONG2, ACROSS2, MIXED2 = 0.3125, 0.25, 0.0625
SAME3, MIXED3 = 7.0 / 36.0, 1.0 / 36.0
TOTAL = 2 * ALONG1 + 4 * ACROSS1 + 8 * ALONG2 + 4 * ACROSS2 + 8 * SAME3


class Exchange:
    def __init__(self, fields, layers, up, down):
        self.fields, self.layers, self.up, self.down = fields, layers, up, down


SPREAD = Exchange(4, 2, -2, 0)
DEEP = Exchange(3, 3, -2, -1)
NEAR = Exchange(3, 2, -1, -1)


class Shape:
    def __init__(self, size_x, size_y, size_z, phases, mesh_sizes):
        self.x, self.y, self.z = size_x, size_y, size_z
        self.pitch = size_y + 4
        self.used = (size_x + 2) * self.pitch
        assert self.used <= LANES and size_z % BLOCK == 0
        self.rows = size_z + 2 * EDGE
        self.tall = self.rows + 2 * EDGE
        self.phases = phases
        self.sizes = mesh_sizes
        self.devices = mesh_sizes[0] * mesh_sizes[1] * mesh_sizes[2]
        self.cells = size_x * size_y
        self.links = [1 if n <= 2 else 2 for n in mesh_sizes]
        self.x_links, self.y_links, self.z_links = self.links

    def lane_grid(self, rows):
        lane = lax.broadcasted_iota(jnp.int32, (rows, LANES), 1)
        column = jnp.zeros_like(lane)
        for j in range(1, self.x + 2):
            column = column + (lane >= j * self.pitch).astype(jnp.int32)
        offset = lane - column * self.pitch
        return lane, column - 1, offset - 2

    def here(self, axis):
        return lax.axis_index(AXES[axis])


def shift(value, amount):
    amount = amount % LANES
    return value if amount == 0 else pltpu.roll(value, amount, 1)


def pick(mask, value):
    return jnp.where(mask, value, 0.0)


def scale(flag, value):
    return value * flag.astype(f32)


def pair(links, even, upward, downward):
    first = jnp.where(even, upward, downward)
    return (first,) if links == 1 else (first, jnp.where(even, downward, upward))


def sides(sh, axis, received):
    index, size = sh.here(axis), sh.sizes[axis]
    even = index % 2 == 0
    first = received[0]
    second = received[1] if len(received) > 1 else jnp.zeros_like(first)
    below = jnp.where(even, second, first)
    above = jnp.where(even, first, second)
    return scale(index > 0, below), scale(index < size - 1, above)


def lane_range(lane, start, count):
    return (lane >= start) & (lane < start + count)


def pack_z(sh, ex, source, out_refs):
    even = sh.here(2) % 2 == 0
    zero = jnp.zeros((8 - ex.layers, LANES), f32)
    for f in range(ex.fields):
        upward = source(f, EDGE + sh.z + ex.up, ex.layers)
        downward = source(f, EDGE + ex.down, ex.layers)
        for ref, message in zip(out_refs, pair(sh.z_links, even, upward, downward)):
            ref[8 * f : 8 * f + ex.layers, :] = message
            ref[8 * f + ex.layers : 8 * f + 8, :] = zero


def merge_z(sh, ex, field_ref, received_refs, scratch, guard):
    below, above = sides(sh, 2, [ref[...] for ref in received_refs])
    for f in range(ex.fields):
        scratch[f, guard : guard + sh.rows, :] = field_ref[f]
        low = guard + EDGE + ex.up
        high = guard + EDGE + sh.z + ex.down
        scratch[f, low : low + ex.layers, :] += below[8 * f : 8 * f + ex.layers]
        scratch[f, high : high + ex.layers, :] += above[8 * f : 8 * f + ex.layers]


def pack_xy(sh, ex, scratch, x_refs, y_refs):
    rows = sh.rows
    lane, _, across = sh.lane_grid(1)
    even_x, even_y = sh.here(0) % 2 == 0, sh.here(1) % 2 == 0
    span = ex.layers * sh.pitch
    x_up = x_down = y_up = y_down = jnp.zeros((rows, LANES), f32)
    for f in range(ex.fields):
        value = scratch[f]
        start = (sh.x + ex.up + 1) * sh.pitch
        x_up = x_up + shift(pick(lane_range(lane, start, span), value), f * span - start)
        start = (ex.down + 1) * sh.pitch
        x_down = x_down + shift(pick(lane_range(lane, start, span), value), f * span - start)
        inside = lane < sh.used
        start = sh.y + ex.up
        y_up = y_up + shift(
            pick(inside & lane_range(across, start, ex.layers), value), f * ex.layers - start - 2
        )
        start = ex.down
        y_down = y_down + shift(
            pick(inside & lane_range(across, start, ex.layers), value), f * ex.layers - start - 2
        )
    for ref, message in zip(x_refs, pair(sh.x_links, even_x, x_up, x_down)):
        ref[...] = message
    for ref, message in zip(y_refs, pair(sh.y_links, even_y, y_up, y_down)):
        ref[...] = message


def merge_xy(sh, ex, scratch, rim, guard, y_refs, x_refs):
    lane, _, across = sh.lane_grid(1)
    inside = lane < sh.used
    low_mask = inside & lane_range(across, ex.up, ex.layers)
    high_mask = inside & lane_range(across, sh.y + ex.down, ex.layers)
    span = ex.layers * sh.pitch
    below_y, above_y = sides(sh, 1, [ref[...] for ref in y_refs])
    per_link = 1 + sh.y_links
    sums = []
    for link in range(sh.x_links):
        straight, diagonal = x_refs[link * per_link], x_refs[link * per_link + 1 : (link + 1) * per_link]
        below, above = sides(sh, 1, [ref[...] for ref in diagonal])
        sums.append(
            straight[...]
            + pick(low_mask, shift(below, -sh.y))
            + pick(high_mask, shift(above, sh.y))
        )
    below_x, above_x = sides(sh, 0, sums)
    first = 1 if ex.up == -2 else 0
    last = ex.layers - 1 if ex.down + ex.layers == 2 else ex.layers
    for f in range(ex.fields):
        addend = pick(low_mask, shift(below_y, ex.up + 2 - ex.layers * f))
        addend = addend + pick(high_mask, shift(above_y, sh.y + ex.down + 2 - ex.layers * f))
        start = (ex.up + first + 1) * sh.pitch
        count = (ex.layers - first) * sh.pitch
        moved = shift(below_x, start - f * span - first * sh.pitch)
        addend = addend + pick(lane_range(lane, start, count), moved)
        start = (sh.x + ex.down + 1) * sh.pitch
        moved = shift(above_x, start - f * span)
        addend = addend + pick(lane_range(lane, start, last * sh.pitch), moved)
        scratch[f, guard : guard + sh.rows, :] += addend
        if rim is not None:
            low = pick(lane_range(lane, 0, sh.pitch), shift(below_x, -f * span))
            start = (sh.x + 1) * sh.pitch
            moved = shift(above_x, start - f * span - last * sh.pitch)
            high = pick(lane_range(lane, start, sh.pitch), moved)
            rim[f, guard : guard + sh.rows, :] = low + high


def clear_guards(sh, refs):
    for ref in refs:
        for f in range(ref.shape[0]):
            ref[f, :EDGE, :] = jnp.zeros((EDGE, LANES), f32)
            ref[f, sh.tall - EDGE :, :] = jnp.zeros((EDGE, LANES), f32)


def z_stage(ref, f, base):
    centre = ref[f, pl.ds(base, BLOCK), :]
    after = ref[f, pl.ds(base + 1, BLOCK), :]
    before = ref[f, pl.ds(base - 1, BLOCK), :]
    return centre, before + after, after - before


def y_stage(value):
    after, before = shift(value, -1), shift(value, 1)
    return before + after, after - before


def yz_parts(ref, base):
    a, a_sum, a_dif = z_stage(ref, 0, base)
    b, b_sum, b_dif = z_stage(ref, 1, base)
    c, c_sum, c_dif = z_stage(ref, 2, base)
    pa, ma = y_stage(a)
    pas, mas = y_stage(a_sum)
    pad, _ = y_stage(a_dif)
    pb, mb = y_stage(b)
    pbs, mbs = y_stage(b_sum)
    _, mbd = y_stage(b_dif)
    pc, _ = y_stage(c)
    pcs, _ = y_stage(c_sum)
    pcd, mcd = y_stage(c_dif)
    own_x = ACROSS1 * (pa + a_sum) + ACROSS2 * pas
    even_x = ALONG1 * a + ALONG2 * (pa + a_sum) + SAME3 * pas
    odd_x = MIXED2 * (mb + c_dif) + MIXED3 * (mbs + pcd)
    own_y = ALONG1 * pb + ACROSS1 * b_sum + ALONG2 * pbs + MIXED2 * mcd
    even_y = ACROSS1 * b + ALONG2 * pb + ACROSS2 * b_sum + SAME3 * pbs + MIXED3 * mcd
    odd_y = MIXED2 * ma + MIXED3 * mas
    own_z = ALONG1 * c_sum + ACROSS1 * pc + ALONG2 * pcs + MIXED2 * mbd
    even_z = ACROSS1 * c + ACROSS2 * pc + ALONG2 * c_sum + SAME3 * pcs + MIXED3 * mbd
    odd_z = MIXED2 * a_dif + MIXED3 * pad
    return (own_x, even_x, odd_x), (own_y, even_y, odd_y), (own_z, even_z, odd_z)


def x_stage(sh, lane, own, plus, minus, rim_plus, rim_minus):
    after, before = shift(plus, -sh.pitch), shift(minus, sh.pitch)
    last = (sh.x + 1) * sh.pitch
    if rim_plus is None:
        return own + pick(lane < last, after) + pick(lane >= sh.pitch, before)
    return own + jnp.where(lane < last, after, rim_plus) + jnp.where(lane >= sh.pitch, before, rim_minus)


def stencil(sh, lane, ref, rim, base):
    parts = yz_parts(ref, base)
    rims = yz_parts(rim, base) if rim is not None else [None] * 3
    out = []
    for (own, even, odd), rim_part in zip(parts, rims):
        if rim_part is None:
            out.append(x_stage(sh, lane, own, even + odd, even - odd, None, None))
        else:
            _, rim_even, rim_odd = rim_part
            out.append(
                x_stage(sh, lane, own, even + odd, even - odd, rim_even + rim_odd, rim_even - rim_odd)
            )
    return out


def spring_parts(ref, base):
    k, k_sum, k_dif = z_stage(ref, 0, base)
    pk, mk = y_stage(k)
    pks, mks = y_stage(k_sum)
    pkd, mkd = y_stage(k_dif)
    zero = jnp.zeros_like(k)
    xx = (ACROSS1 * (pk + k_sum) + ACROSS2 * pks, ALONG1 * k + ALONG2 * (pk + k_sum) + SAME3 * pks, zero)
    yy = (
        ALONG1 * pk + ACROSS1 * k_sum + ALONG2 * pks,
        ACROSS1 * k + ALONG2 * pk + ACROSS2 * k_sum + SAME3 * pks,
        zero,
    )
    zz = (
        ALONG1 * k_sum + ACROSS1 * pk + ALONG2 * pks,
        ACROSS1 * k + ACROSS2 * pk + ALONG2 * k_sum + SAME3 * pks,
        zero,
    )
    xy = (zero, zero, MIXED2 * mk + MIXED3 * mks)
    xz = (zero, zero, MIXED2 * k_dif + MIXED3 * pkd)
    yz = (MIXED2 * mkd, MIXED3 * mkd, zero)
    return xx, yy, zz, xy, xz, yz


def own_block(sh, lane, springs, base):
    main, rim = springs
    k = main[0, pl.ds(base, BLOCK), :]
    out = []
    for index, ((own, even, odd), (_, rim_even, rim_odd)) in enumerate(
        zip(spring_parts(main, base), spring_parts(rim, base))
    ):
        total = x_stage(sh, lane, own, even + odd, even - odd, rim_even + rim_odd, rim_even - rim_odd)
        out.append(total + TOTAL * k if index < 3 else total)
    return out


def apply_block(d, v):
    return (
        d[0] * v[0] + d[3] * v[1] + d[4] * v[2],
        d[3] * v[0] + d[1] * v[1] + d[5] * v[2],
        d[4] * v[0] + d[5] * v[1] + d[2] * v[2],
    )


def image_at(sh, lane, v, kv, rims, k, d, base):
    outer = stencil(sh, lane, v, rims and rims[0], base)
    inner = stencil(sh, lane, kv, rims and rims[1], base)
    own = apply_block(d, [v[m, pl.ds(base, BLOCK), :] for m in range(3)])
    return [own[m] - (k * outer[m] + inner[m]) for m in range(3)]


def blocks(sh, step):
    def body(i, carry):
        step(pl.multiple_of(i * BLOCK, BLOCK))
        return carry

    lax.fori_loop(0, sh.rows // BLOCK, body, 0)


def extended_mask(sh, base):
    lane, _, across = sh.lane_grid(BLOCK)
    z = base - EDGE + lax.broadcasted_iota(jnp.int32, (BLOCK, LANES), 0)
    return (lane < sh.used) & (across >= -1) & (across <= sh.y) & (z >= -1) & (z <= sh.z)


def grid_mask(sh, rows, first):
    lane, along, across = sh.lane_grid(rows)
    z = first - EDGE + lax.broadcasted_iota(jnp.int32, (rows, LANES), 0)
    mask = lane < sh.used
    for axis, place, size in ((0, along, sh.x), (1, across, sh.y), (2, z, sh.z)):
        index = sh.here(axis)
        low = jnp.where(index > 0, -EDGE, 0)
        high = jnp.where(index < sh.sizes[axis] - 1, size + EDGE, size)
        mask = mask & (place >= low) & (place < high)
    return mask


def rim_mask(sh, rows, first):
    lane, _, across = sh.lane_grid(rows)
    z = first - EDGE + lax.broadcasted_iota(jnp.int32, (rows, LANES), 0)
    mask = lane < sh.used
    for axis, place, size in ((1, across, sh.y), (2, z, sh.z)):
        index = sh.here(axis)
        low = jnp.where(index > 0, -EDGE, 0)
        high = jnp.where(index < sh.sizes[axis] - 1, size + EDGE, size)
        mask = mask & (place >= low) & (place < high)
    return mask


def local_solve(sh, residual, k_ref, d_ref, v, kv):
    lane, _, _ = sh.lane_grid(1)
    at = lambda ref, f, base: ref[f, pl.ds(base, BLOCK), :]

    def inverse(base, mask):
        return [jnp.where(mask, relax / jnp.where(mask, at(d_ref, m, base), 1.0), 0.0) for m in range(3)]

    def start(base):
        inv = inverse(base, extended_mask(sh, base))
        k = k_ref[pl.ds(base, BLOCK), :]
        for m in range(3):
            z = residual(m, base) * inv[m]
            v[0][m, pl.ds(base + EDGE, BLOCK), :] = z
            kv[0][m, pl.ds(base + EDGE, BLOCK), :] = k * z

    blocks(sh, start)
    for sweep in range(SWEEPS - 1):
        old, new = sweep % 2, (sweep + 1) % 2

        def step(base, old=old, new=new):
            k = k_ref[pl.ds(base, BLOCK), :]
            d = [at(d_ref, f, base) for f in range(6)]
            inv = inverse(base, extended_mask(sh, base))
            image = image_at(sh, lane, v[old], kv[old], None, k, d, base + EDGE)
            for m in range(3):
                z = v[old][m, pl.ds(base + EDGE, BLOCK), :] + inv[m] * (residual(m, base) - image[m])
                v[new][m, pl.ds(base + EDGE, BLOCK), :] = z
                kv[new][m, pl.ds(base + EDGE, BLOCK), :] = k * z

        blocks(sh, step)
    return (SWEEPS - 1) % 2


def coords(sh):
    lane, along, across = sh.lane_grid(sh.z)
    z = lax.broadcasted_iota(jnp.int32, (sh.z, LANES), 0)
    place = lambda index, size: (2 * index + 1).astype(f32) / size - 1.0
    return place(along, sh.x), place(across, sh.y), place(z, sh.z)


def cross(a, b):
    return (a[1] * b[2] - a[2] * b[1], a[2] * b[0] - a[0] * b[2], a[0] * b[1] - a[1] * b[0])


def fold_rows(value):
    total = value[0:8]
    for i in range(8, value.shape[0], 8):
        total = total + value[i : i + 8]
    return jnp.sum(total, axis=0, keepdims=True)


def lane_sums(rows_ref):
    ones = jnp.ones((8, LANES), f32)
    return lax.dot_general(
        ones, rows_ref[...], (((1,), (1,)), ((), ())), precision=highest, preferred_element_type=f32
    )


def coarse_sums(sh, nodes, field, count, sums, slots_ref):
    moments = tuple(field) + cross(coords(sh), field)
    for node in range(count):
        mask = nodes == float(node)
        for m in range(6):
            sums[node * 6 + m : node * 6 + m + 1, :] = fold_rows(pick(mask, moments[m]))
    line = lane_sums(sums)[0:1]
    slots_ref[...] = jnp.broadcast_to(line, slots_ref.shape)


def coarse_values(sh, nodes, received, inverse_ref, values):
    unknowns, total = inverse_ref.shape
    column = lax.broadcasted_iota(jnp.int32, (1, total), 1)
    owner = column // unknowns
    place = column - owner * unknowns
    spread = (lax.broadcasted_iota(jnp.int32, (LANES, total), 0) == place).astype(f32)
    lines = jnp.dot(received, spread, precision=highest, preferred_element_type=f32)
    mine = lax.broadcasted_iota(jnp.int32, lines.shape, 0) == owner
    vector = jnp.sum(pick(mine, lines), axis=0, keepdims=True)
    product = inverse_ref[...] * vector
    part = product[:, 0:LANES]
    for i in range(LANES, total, LANES):
        part = part + product[:, i : i + LANES]
    values[0:unknowns, :] = jnp.dot(
        part, jnp.ones((LANES, LANES), f32), precision=highest, preferred_element_type=f32
    )
    cells = []
    for m in range(6):
        cell = jnp.zeros((sh.z, LANES), f32)
        for node in range(unknowns // 6):
            cell = jnp.where(nodes == float(node), values[node * 6 + m : node * 6 + m + 1, :], cell)
        cells.append(cell)
    turned = cross(cells[3:], coords(sh))
    return [cells[m] + turned[m] for m in range(3)]


def selection(sh):
    lane, along, across = sh.lane_grid(sh.cells)
    inside = (along >= 0) & (along < sh.x) & (across >= 0) & (across < sh.y)
    row = lax.broadcasted_iota(jnp.int32, (sh.cells, LANES), 0)
    return (inside & (row == along * sh.y + across)).astype(f32)


def to_lanes(value, select):
    return lax.dot_general(
        value, select, (((0,), (0,)), ((), ())), precision=highest, preferred_element_type=f32
    )


def to_cells(value, select):
    return lax.dot_general(
        select, value, (((1,), (1,)), ((), ())), precision=highest, preferred_element_type=f32
    )


def call(kernel, name, outs, ins, scratch=(), smem=()):
    return pl.pallas_call(
        kernel,
        out_shape=[jax.ShapeDtypeStruct(shape, f32) for shape in outs],
        in_specs=[
            pl.BlockSpec(memory_space=pltpu.SMEM if i in smem else pltpu.VMEM) for i in range(len(ins))
        ],
        out_specs=[pl.BlockSpec(memory_space=pltpu.VMEM) for _ in outs],
        scratch_shapes=[pltpu.VMEM(shape, f32) for shape in scratch],
        compiler_params=pltpu.CompilerParams(vmem_limit_bytes=48 * 1024 * 1024),
        name=name,
    )(*ins)


def permutation(sizes, moves):
    def partner(axis, link, index):
        size = sizes[axis]
        other = index ^ 1 if link == 0 else index + (1 if index % 2 else -1)
        if 0 <= other < size:
            return other
        return size - 1 - index if axis == 2 and size % 2 == 0 else index

    pairs = []
    for x in range(sizes[0]):
        for y in range(sizes[1]):
            for z in range(sizes[2]):
                place = [x, y, z]
                goal = [partner(a, moves[a], place[a]) if a in moves else place[a] for a in range(3)]
                if goal == place and 0 not in moves and sizes[0] % 2 == 0:
                    goal[0] = partner(0, 0, x)
                flat = [(p[0] * sizes[1] + p[1]) * sizes[2] + p[2] for p in (place, goal)]
                pairs.append(tuple(flat))
    return pairs


def send(sh, value, moves):
    return lax.ppermute(value, AXES, permutation(sh.sizes, moves))


def send_z(sh, messages):
    return [send(sh, message, {2: link}) for link, message in enumerate(messages)]


def send_xy(sh, x_messages, y_messages):
    from_y = [send(sh, message, {1: link}) for link, message in enumerate(y_messages)]
    from_x = []
    for link, message in enumerate(x_messages):
        from_x.append(send(sh, message, {0: link}))
        from_x.extend(send(sh, message, {0: link, 1: other}) for other in range(sh.y_links))
    return from_y, from_x


def to_all(slots):
    return lax.all_to_all(slots, AXES, 0, 0, tiled=True)


def exchange(sh, ex, name, field, z_messages):
    from_z = send_z(sh, z_messages)

    def packer(*refs):
        field_ref, z_refs = refs[0], refs[1 : 1 + sh.z_links]
        x_refs = refs[1 + sh.z_links : 1 + sh.z_links + sh.x_links]
        y_refs = refs[1 + sh.z_links + sh.x_links : -1]
        scratch = refs[-1]
        merge_z(sh, ex, field_ref, z_refs, scratch, 0)
        pack_xy(sh, ex, scratch, x_refs, y_refs)

    plane = (sh.rows, LANES)
    messages = call(
        packer,
        name,
        [plane] * (sh.x_links + sh.y_links),
        [field] + from_z,
        [(ex.fields,) + plane],
    )
    from_y, from_x = send_xy(sh, messages[: sh.x_links], messages[sh.x_links :])
    return from_z, from_y, from_x


class Taker:
    def __init__(self, refs):
        self.refs, self.at = refs, 0

    def __call__(self, count):
        self.at += count
        return self.refs[self.at - count : self.at]

    def one(self):
        return self(1)[0]


def merge_all(sh, ex, take, scratch, rim, guard):
    field = take.one()
    from_z, from_y = take(sh.z_links), take(sh.y_links)
    from_x = take(sh.x_links * (1 + sh.y_links))
    merge_z(sh, ex, field, from_z, scratch, guard)
    merge_xy(sh, ex, scratch, rim, guard, from_y, from_x)


def body(right_side, phase_labels, phase_moduli, coarse_nodes, coarse_inverse):
    sizes = tuple(lax.axis_size(axis) for axis in AXES)
    _, size_x, size_y, size_z = right_side.shape
    sh = Shape(size_x, size_y, size_z, phase_moduli.shape[0], sizes)
    unknowns = coarse_inverse.shape[0]
    node_count = unknowns // 6
    sum_rows = -(-unknowns // 8) * 8
    own = slice(EDGE, EDGE + sh.z)
    plane = (sh.rows, LANES)
    fields = (3,) + plane
    tall = (3, sh.tall, LANES)
    slots = (sh.devices, LANES)
    z_shape = lambda ex: [(8 * ex.fields, LANES)] * sh.z_links
    natural = right_side.reshape(3, sh.cells, sh.z)
    nodes_natural = coarse_nodes.reshape(sh.cells, sh.z)
    label_x, label_y, label_z = phase_labels.shape

    def begin(natural_ref, labels_ref, moduli_ref, nodes_ref, field_ref, lanes_ref, slots_ref, *rest):
        z_refs, (sums, stiff) = rest[: sh.z_links], rest[sh.z_links :]
        select = selection(sh)
        field_ref[...] = jnp.zeros(field_ref.shape, f32)
        residual = []
        for m in range(3):
            residual.append(to_lanes(natural_ref[m], select))
            field_ref[m, own, :] = residual[m]
        for i in range(label_x):
            labels = labels_ref[i]
            moduli = jnp.zeros(labels.shape, f32)
            for phase in range(sh.phases):
                moduli = jnp.where(labels == phase, moduli_ref[phase], moduli)
            stiff[i * label_y : (i + 1) * label_y, :] = moduli
        row = lax.broadcasted_iota(jnp.int32, (sh.z, label_z), 0)
        column = lax.broadcasted_iota(jnp.int32, (sh.z, label_z), 1)
        wide = ((row >= 2 * column) & (row < 2 * column + 2)).astype(f32)
        by_z = lax.dot_general(
            wide, stiff[...], (((1,), (1,)), ((), ())), precision=highest, preferred_element_type=f32
        )
        lane, along, across = sh.lane_grid(label_x * label_y)
        inside = (along >= 0) & (along < sh.x) & (across >= 0) & (across < sh.y)
        block = lax.broadcasted_iota(jnp.int32, along.shape, 0)
        to_block = (inside & (block == (along >> 1) * label_y + (across >> 1))).astype(f32)
        field_ref[3, own, :] = jnp.dot(by_z, to_block, precision=highest, preferred_element_type=f32)
        nodes = to_lanes(nodes_ref[...].astype(f32) + 1.0, select) - 1.0
        lanes_ref[...] = nodes
        sums[...] = jnp.zeros(sums.shape, f32)
        coarse_sums(sh, nodes, residual, node_count, sums, slots_ref)
        pack_z(sh, SPREAD, lambda f, start, count: field_ref[f, start : start + count, :], z_refs)

    start_field, nodes, sums, *z_messages = call(
        begin,
        "begin",
        [(4,) + plane, (sh.z, LANES), slots] + z_shape(SPREAD),
        [natural, phase_labels, phase_moduli, nodes_natural],
        [(LANES, LANES), (label_x * label_y, label_z)],
        smem=(2,),
    )
    from_z, from_y, from_x = exchange(sh, SPREAD, "spread", start_field, z_messages)
    coarse = to_all(sums)

    def finish_solve(index, v, nodes_ref, coarse_ref, inverse_ref, values, solution_ref, z_refs, ex):
        for m in range(3):
            solution_ref[m] = v[index][m, EDGE : EDGE + sh.rows, :]
        added = coarse_values(sh, nodes_ref[...], coarse_ref[...], inverse_ref, values)
        valid = nodes_ref[...] >= 0.0
        for m in range(3):
            solution_ref[m, own, :] += pick(valid, added[m])
        pack_z(sh, ex, lambda f, start, count: solution_ref[f, start : start + count, :], z_refs)

    def first_solve(*refs):
        take = Taker(refs)
        merging = take(1 + sh.z_links + sh.y_links + sh.x_links * (1 + sh.y_links))
        nodes_ref, coarse_ref, inverse_ref = take(3)
        solution_ref, springs_ref = take(2)
        z_refs = take(sh.z_links)
        all_fields, rims, stiff, stiff_rim, v0, v1, kv0, kv1, values = take(9)
        clear_guards(sh, (stiff, stiff_rim, v0, v1, kv0, kv1))
        merge_all(sh, SPREAD, Taker(merging), all_fields, rims, 0)
        stiff[0, EDGE : EDGE + sh.rows, :] = all_fields[3]
        stiff_rim[0, EDGE : EDGE + sh.rows, :] = rims[3]
        springs_ref[6] = all_fields[3]
        springs_ref[7] = rims[3]
        lane, _, _ = sh.lane_grid(1)

        def springs(base):
            for f, entry in enumerate(own_block(sh, lane, (stiff, stiff_rim), base + EDGE)):
                springs_ref[f, pl.ds(base, BLOCK), :] = entry

        blocks(sh, springs)
        residual = lambda m, base: all_fields[m, pl.ds(base, BLOCK), :]
        index = local_solve(sh, residual, springs_ref.at[6], springs_ref, (v0, v1), (kv0, kv1))
        finish_solve(index, (v0, v1), nodes_ref, coarse_ref, inverse_ref, values, solution_ref, z_refs, DEEP)

    solved, springs, *z_messages = call(
        first_solve,
        "first_solve",
        [fields, (8,) + plane] + z_shape(DEEP),
        [start_field, *from_z, *from_y, *from_x, nodes, coarse, coarse_inverse],
        [(4,) + plane, (4,) + plane, (1, sh.tall, LANES), (1, sh.tall, LANES)] + [tall] * 4 + [(LANES, LANES)],
    )
    from_z, from_y, from_x = exchange(sh, DEEP, "deep", solved, z_messages)

    def first_image(*refs):
        take = Taker(refs)
        merging = take(1 + sh.z_links + sh.y_links + sh.x_links * (1 + sh.y_links))
        nodes_ref, springs_ref = take(2)
        search_ref, image_ref, slots_ref = take(3)
        v, rim, kv, k_rim, sums = take(5)
        clear_guards(sh, (v, rim, kv, k_rim))
        merge_all(sh, DEEP, Taker(merging), v, rim, EDGE)
        lane, _, _ = sh.lane_grid(1)

        def mask(base):
            rows, tall_rows = pl.ds(base, BLOCK), pl.ds(base + EDGE, BLOCK)
            in_grid, in_rim = grid_mask(sh, BLOCK, base), rim_mask(sh, BLOCK, base)
            k, k_edge = springs_ref[6, rows, :], springs_ref[7, rows, :]
            for m in range(3):
                value = pick(in_grid, v[m, tall_rows, :])
                v[m, tall_rows, :] = value
                search_ref[m, rows, :] = value
                kv[m, tall_rows, :] = k * value
                value = pick(in_rim, rim[m, tall_rows, :])
                rim[m, tall_rows, :] = value
                k_rim[m, tall_rows, :] = k_edge * value

        blocks(sh, mask)

        def step(base):
            rows = pl.ds(base, BLOCK)
            d = [springs_ref[f, rows, :] for f in range(6)]
            image = image_at(sh, lane, v, kv, (rim, k_rim), springs_ref[6, rows, :], d, base + EDGE)
            keep = grid_mask(sh, BLOCK, base) & extended_mask(sh, base)
            for m in range(3):
                image_ref[m, rows, :] = pick(keep, image[m])

        blocks(sh, step)
        sums[...] = jnp.zeros(sums.shape, f32)
        coarse_sums(sh, nodes_ref[...], [image_ref[m, own, :] for m in range(3)], node_count, sums, slots_ref)

    search, image, sums = call(
        first_image,
        "first_image",
        [fields, fields, slots],
        [solved, *from_z, *from_y, *from_x, nodes, springs],
        [tall] * 4 + [(LANES, LANES)],
    )
    coarse = to_all(sums)

    def second_solve(*refs):
        take = Taker(refs)
        image_ref, springs_ref, nodes_ref, coarse_ref, inverse_ref = take(5)
        solution_ref = take.one()
        z_refs = take(sh.z_links)
        v0, v1, kv0, kv1, values = take(5)
        clear_guards(sh, (v0, v1, kv0, kv1))
        residual = lambda m, base: image_ref[m, pl.ds(base, BLOCK), :]
        index = local_solve(sh, residual, springs_ref.at[6], springs_ref, (v0, v1), (kv0, kv1))
        finish_solve(index, (v0, v1), nodes_ref, coarse_ref, inverse_ref, values, solution_ref, z_refs, NEAR)

    solved, *z_messages = call(
        second_solve,
        "second_solve",
        [fields] + z_shape(NEAR),
        [image, springs, nodes, coarse, coarse_inverse],
        [tall] * 4 + [(LANES, LANES)],
    )
    from_z, from_y, from_x = exchange(sh, NEAR, "near", solved, z_messages)

    def second_image(*refs):
        take = Taker(refs)
        merging = take(1 + sh.z_links + sh.y_links + sh.x_links * (1 + sh.y_links))
        nodes_ref, springs_ref, start_ref, search_ref, first_ref = take(5)
        second_ref, image_ref, slots_ref = take(3)
        v, kv, sums = take(3)
        clear_guards(sh, (v, kv))
        merge_all(sh, NEAR, Taker(merging), v, None, EDGE)
        lane, _, _ = sh.lane_grid(1)

        def mask(base):
            rows, tall_rows = pl.ds(base, BLOCK), pl.ds(base + EDGE, BLOCK)
            in_grid = grid_mask(sh, BLOCK, base)
            k = springs_ref[6, rows, :]
            for m in range(3):
                value = pick(in_grid, v[m, tall_rows, :])
                v[m, tall_rows, :] = value
                kv[m, tall_rows, :] = k * value

        blocks(sh, mask)

        def step(base):
            rows = pl.ds(base, BLOCK)
            d = [springs_ref[f, rows, :] for f in range(6)]
            image = image_at(sh, lane, v, kv, None, springs_ref[6, rows, :], d, base + EDGE)
            for m in range(3):
                image_ref[m, rows, :] = image[m]
                second_ref[m, rows, :] = v[m, pl.ds(base + EDGE, BLOCK), :]

        blocks(sh, step)
        valid = nodes_ref[...] >= 0.0
        names = ("r", "z", "w", "q", "v")
        sources = (start_ref, search_ref, first_ref, second_ref, image_ref)
        get = {name: [source[m, own, :] for m in range(3)] for name, source in zip(names, sources)}
        sums[...] = jnp.zeros(sums.shape, f32)
        for i, (a, b) in enumerate(("rz", "zw", "rq", "wq", "zv", "qv")):
            product = sum(get[a][m] * get[b][m] for m in range(3))
            sums[i : i + 1, :] = fold_rows(pick(valid, product))
        slots_ref[...] = jnp.broadcast_to(lane_sums(sums)[0:1], slots_ref.shape)

    second, second_image_field, sums = call(
        second_image,
        "second_image",
        [fields, fields, slots],
        [solved, *from_z, *from_y, *from_x, nodes, springs, start_field, search, image],
        [tall] * 2 + [(LANES, LANES)],
    )
    totals = to_all(sums)

    def finish(totals_ref, natural_ref, search_ref, first_ref, second_ref, image_ref, field_ref, residual_ref):
        total = jnp.sum(totals_ref[...], axis=0, keepdims=True)
        rz, zw, rq, wq, zv, qv = [total[:, i : i + 1] for i in range(6)]
        step0 = rz / zw
        rho = rz - step0 * zw - step0 * rq + step0 * step0 * wq
        grow = 1.0 + rho / rz
        curvature = grow * grow * zw - grow * step0 * (zv + wq) + step0 * step0 * qv
        step1 = rho / curvature
        first = step0 + step1 * grow
        second = step0 * step1
        select = selection(sh)
        for m in range(3):
            update = first * search_ref[m, own, :] - second * second_ref[m, own, :]
            field_ref[m] = to_cells(update, select)
            update = first * first_ref[m, own, :] - second * image_ref[m, own, :]
            residual_ref[m] = natural_ref[m] - to_cells(update, select)

    solution_field, residual = call(
        finish,
        "finish",
        [natural.shape, natural.shape],
        [totals, natural, search, image, second, second_image_field],
    )
    return solution_field.reshape(right_side.shape), residual.reshape(right_side.shape)


def solution(mesh):
    in_specs = (
        P(None, "gx", "gy", "gz"),
        P("gx", "gy", "gz"),
        P(),
        P("gx", "gy", "gz"),
        P(("gx", "gy", "gz"), None),
    )
    out_specs = (P(None, "gx", "gy", "gz"), P(None, "gx", "gy", "gz"))
    return jax.shard_map(body, mesh=mesh, in_specs=in_specs, out_specs=out_specs, check_vma=False)
```

```python
import jax
import jax.numpy as jnp
from jax import lax
from jax.experimental import pallas as pl
from jax.experimental.pallas import tpu as pltpu
from jax.sharding import PartitionSpec as P

AXES = ("gx", "gy", "gz")
SWEEPS = 4
relax = 0.6
highest = lax.Precision.HIGHEST
f32 = jnp.float32
LANES = 128
EDGE = 8

ALONG1, ACROSS1 = 0.75, 0.5
ALONG2, ACROSS2, MIXED2 = 0.3125, 0.25, 0.0625
SAME3, MIXED3 = 7.0 / 36.0, 1.0 / 36.0
TOTAL = 2 * ALONG1 + 4 * ACROSS1 + 8 * ALONG2 + 4 * ACROSS2 + 8 * SAME3


class Exchange:
    def __init__(self, fields, layers, up, down):
        self.fields, self.layers, self.up, self.down = fields, layers, up, down


SPREAD = Exchange(4, 2, -2, 0)
DEEP = Exchange(3, 3, -2, -1)
NEAR = Exchange(3, 2, -1, -1)


class Shape:
    def __init__(self, size_x, size_y, size_z, phases, mesh_sizes):
        self.x, self.y, self.z = size_x, size_y, size_z
        self.pitch = size_y + 4
        self.used = (size_x + 2) * self.pitch
        assert self.used <= LANES
        self.rows = size_z + 2 * EDGE
        self.tall = self.rows + 2 * EDGE
        self.phases = phases
        self.sizes = mesh_sizes
        self.devices = mesh_sizes[0] * mesh_sizes[1] * mesh_sizes[2]
        self.cells = size_x * size_y
        self.links = [1 if n <= 2 else 2 for n in mesh_sizes]
        self.x_links, self.y_links, self.z_links = self.links

    def lane_grid(self, rows):
        lane = lax.broadcasted_iota(jnp.int32, (rows, LANES), 1)
        column = jnp.zeros_like(lane)
        for j in range(1, self.x + 2):
            column = column + (lane >= j * self.pitch).astype(jnp.int32)
        offset = lane - column * self.pitch
        return lane, column - 1, offset - 2

    def here(self, axis):
        return lax.axis_index(AXES[axis])


def shift(value, amount):
    amount = amount % LANES
    return value if amount == 0 else pltpu.roll(value, amount, 1)


def pick(mask, value):
    return jnp.where(mask, value, 0.0)


def scale(flag, value):
    return value * flag.astype(f32)


def pair(links, even, upward, downward):
    first = jnp.where(even, upward, downward)
    return (first,) if links == 1 else (first, jnp.where(even, downward, upward))


def sides(sh, axis, received):
    index, size = sh.here(axis), sh.sizes[axis]
    even = index % 2 == 0
    first = received[0]
    second = received[1] if len(received) > 1 else jnp.zeros_like(first)
    below = jnp.where(even, second, first)
    above = jnp.where(even, first, second)
    return scale(index > 0, below), scale(index < size - 1, above)


def lane_range(lane, start, count):
    return (lane >= start) & (lane < start + count)


def pack_z(sh, ex, source, out_refs):
    even = sh.here(2) % 2 == 0
    zero = jnp.zeros((8 - ex.layers, LANES), f32)
    for f in range(ex.fields):
        upward = source(f, EDGE + sh.z + ex.up, ex.layers)
        downward = source(f, EDGE + ex.down, ex.layers)
        for ref, message in zip(out_refs, pair(sh.z_links, even, upward, downward)):
            ref[8 * f : 8 * f + ex.layers, :] = message
            ref[8 * f + ex.layers : 8 * f + 8, :] = zero


def merge_z(sh, ex, field_ref, received_refs, scratch, guard):
    below, above = sides(sh, 2, [ref[...] for ref in received_refs])
    for f in range(ex.fields):
        scratch[f, guard : guard + sh.rows, :] = field_ref[f]
        low = guard + EDGE + ex.up
        high = guard + EDGE + sh.z + ex.down
        scratch[f, low : low + ex.layers, :] += below[8 * f : 8 * f + ex.layers]
        scratch[f, high : high + ex.layers, :] += above[8 * f : 8 * f + ex.layers]


def pack_xy(sh, ex, scratch, x_refs, y_refs):
    rows = sh.rows
    lane, _, across = sh.lane_grid(1)
    even_x, even_y = sh.here(0) % 2 == 0, sh.here(1) % 2 == 0
    span = ex.layers * sh.pitch
    x_up = x_down = y_up = y_down = jnp.zeros((rows, LANES), f32)
    for f in range(ex.fields):
        value = scratch[f]
        start = (sh.x + ex.up + 1) * sh.pitch
        x_up = x_up + shift(pick(lane_range(lane, start, span), value), f * span - start)
        start = (ex.down + 1) * sh.pitch
        x_down = x_down + shift(pick(lane_range(lane, start, span), value), f * span - start)
        inside = lane < sh.used
        start = sh.y + ex.up
        y_up = y_up + shift(
            pick(inside & lane_range(across, start, ex.layers), value), f * ex.layers - start - 2
        )
        start = ex.down
        y_down = y_down + shift(
            pick(inside & lane_range(across, start, ex.layers), value), f * ex.layers - start - 2
        )
    for ref, message in zip(x_refs, pair(sh.x_links, even_x, x_up, x_down)):
        ref[...] = message
    for ref, message in zip(y_refs, pair(sh.y_links, even_y, y_up, y_down)):
        ref[...] = message


def merge_xy(sh, ex, scratch, rim, guard, y_refs, x_refs):
    lane, _, across = sh.lane_grid(1)
    inside = lane < sh.used
    low_mask = inside & lane_range(across, ex.up, ex.layers)
    high_mask = inside & lane_range(across, sh.y + ex.down, ex.layers)
    span = ex.layers * sh.pitch
    below_y, above_y = sides(sh, 1, [ref[...] for ref in y_refs])
    per_link = 1 + sh.y_links
    sums = []
    for link in range(sh.x_links):
        straight, diagonal = x_refs[link * per_link], x_refs[link * per_link + 1 : (link + 1) * per_link]
        below, above = sides(sh, 1, [ref[...] for ref in diagonal])
        sums.append(
            straight[...]
            + pick(low_mask, shift(below, -sh.y))
            + pick(high_mask, shift(above, sh.y))
        )
    below_x, above_x = sides(sh, 0, sums)
    first = 1 if ex.up == -2 else 0
    last = ex.layers - 1 if ex.down + ex.layers == 2 else ex.layers
    for f in range(ex.fields):
        addend = pick(low_mask, shift(below_y, ex.up + 2 - ex.layers * f))
        addend = addend + pick(high_mask, shift(above_y, sh.y + ex.down + 2 - ex.layers * f))
        start = (ex.up + first + 1) * sh.pitch
        count = (ex.layers - first) * sh.pitch
        moved = shift(below_x, start - f * span - first * sh.pitch)
        addend = addend + pick(lane_range(lane, start, count), moved)
        start = (sh.x + ex.down + 1) * sh.pitch
        moved = shift(above_x, start - f * span)
        addend = addend + pick(lane_range(lane, start, last * sh.pitch), moved)
        scratch[f, guard : guard + sh.rows, :] += addend
        if rim is not None:
            low = pick(lane_range(lane, 0, sh.pitch), shift(below_x, -f * span))
            start = (sh.x + 1) * sh.pitch
            moved = shift(above_x, start - f * span - last * sh.pitch)
            high = pick(lane_range(lane, start, sh.pitch), moved)
            rim[f, guard : guard + sh.rows, :] = low + high


def clear_guards(sh, refs):
    for ref in refs:
        for f in range(ref.shape[0]):
            ref[f, :EDGE, :] = jnp.zeros((EDGE, LANES), f32)
            ref[f, sh.tall - EDGE :, :] = jnp.zeros((EDGE, LANES), f32)


def inner(ref, f):
    return ref[f, EDGE : ref.shape[1] - EDGE, :]


def z_stage(ref, f):
    end = ref.shape[1] - EDGE
    after = ref[f, EDGE + 1 : end + 1, :]
    before = ref[f, EDGE - 1 : end - 1, :]
    return inner(ref, f), before + after, after - before


def y_stage(value):
    after, before = shift(value, -1), shift(value, 1)
    return before + after, after - before


def yz_parts(ref):
    a, a_sum, a_dif = z_stage(ref, 0)
    b, b_sum, b_dif = z_stage(ref, 1)
    c, c_sum, c_dif = z_stage(ref, 2)
    pa, ma = y_stage(a)
    pas, mas = y_stage(a_sum)
    pad, _ = y_stage(a_dif)
    pb, mb = y_stage(b)
    pbs, mbs = y_stage(b_sum)
    _, mbd = y_stage(b_dif)
    pc, _ = y_stage(c)
    pcs, _ = y_stage(c_sum)
    pcd, mcd = y_stage(c_dif)
    own_x = ACROSS1 * (pa + a_sum) + ACROSS2 * pas
    even_x = ALONG1 * a + ALONG2 * (pa + a_sum) + SAME3 * pas
    odd_x = MIXED2 * (mb + c_dif) + MIXED3 * (mbs + pcd)
    own_y = ALONG1 * pb + ACROSS1 * b_sum + ALONG2 * pbs + MIXED2 * mcd
    even_y = ACROSS1 * b + ALONG2 * pb + ACROSS2 * b_sum + SAME3 * pbs + MIXED3 * mcd
    odd_y = MIXED2 * ma + MIXED3 * mas
    own_z = ALONG1 * c_sum + ACROSS1 * pc + ALONG2 * pcs + MIXED2 * mbd
    even_z = ACROSS1 * c + ACROSS2 * pc + ALONG2 * c_sum + SAME3 * pcs + MIXED3 * mbd
    odd_z = MIXED2 * a_dif + MIXED3 * pad
    return (own_x, even_x, odd_x), (own_y, even_y, odd_y), (own_z, even_z, odd_z)


def x_stage(sh, lane, own, plus, minus, rim_plus, rim_minus):
    after, before = shift(plus, -sh.pitch), shift(minus, sh.pitch)
    last = (sh.x + 1) * sh.pitch
    if rim_plus is None:
        return own + pick(lane < last, after) + pick(lane >= sh.pitch, before)
    return own + jnp.where(lane < last, after, rim_plus) + jnp.where(lane >= sh.pitch, before, rim_minus)


def stencil(sh, lane, ref, rim):
    parts = yz_parts(ref)
    rims = yz_parts(rim) if rim is not None else [None] * 3
    out = []
    for (own, even, odd), rim_part in zip(parts, rims):
        if rim_part is None:
            out.append(x_stage(sh, lane, own, even + odd, even - odd, None, None))
        else:
            _, rim_even, rim_odd = rim_part
            out.append(
                x_stage(sh, lane, own, even + odd, even - odd, rim_even + rim_odd, rim_even - rim_odd)
            )
    return out


def spring_parts(ref):
    k, k_sum, k_dif = z_stage(ref, 0)
    pk, mk = y_stage(k)
    pks, mks = y_stage(k_sum)
    pkd, mkd = y_stage(k_dif)
    zero = jnp.zeros_like(k)
    xx = (ACROSS1 * (pk + k_sum) + ACROSS2 * pks, ALONG1 * k + ALONG2 * (pk + k_sum) + SAME3 * pks, zero)
    yy = (
        ALONG1 * pk + ACROSS1 * k_sum + ALONG2 * pks,
        ACROSS1 * k + ALONG2 * pk + ACROSS2 * k_sum + SAME3 * pks,
        zero,
    )
    zz = (
        ALONG1 * k_sum + ACROSS1 * pk + ALONG2 * pks,
        ACROSS1 * k + ACROSS2 * pk + ALONG2 * k_sum + SAME3 * pks,
        zero,
    )
    xy = (zero, zero, MIXED2 * mk + MIXED3 * mks)
    xz = (zero, zero, MIXED2 * k_dif + MIXED3 * pkd)
    yz = (MIXED2 * mkd, MIXED3 * mkd, zero)
    return xx, yy, zz, xy, xz, yz


def own_block(sh, lane, springs):
    main, rim = springs
    k = inner(main, 0)
    out = []
    for index, ((own, even, odd), (_, rim_even, rim_odd)) in enumerate(
        zip(spring_parts(main), spring_parts(rim))
    ):
        total = x_stage(sh, lane, own, even + odd, even - odd, rim_even + rim_odd, rim_even - rim_odd)
        out.append(total + TOTAL * k if index < 3 else total)
    return out


def apply_block(d, v):
    return (
        d[0] * v[0] + d[3] * v[1] + d[4] * v[2],
        d[3] * v[0] + d[1] * v[1] + d[5] * v[2],
        d[4] * v[0] + d[5] * v[1] + d[2] * v[2],
    )


def image_of(sh, lane, v, kv, rims, springs_ref):
    outer = stencil(sh, lane, v, rims and rims[0])
    scaled = stencil(sh, lane, kv, rims and rims[1])
    own = apply_block([springs_ref[f] for f in range(6)], [inner(v, m) for m in range(3)])
    return [own[m] - (springs_ref[6] * outer[m] + scaled[m]) for m in range(3)]


def level(sh):
    return lax.broadcasted_iota(jnp.int32, (sh.rows, LANES), 0) - EDGE


def extended_mask(sh):
    lane, _, across = sh.lane_grid(1)
    z = level(sh)
    return ((lane < sh.used) & (across >= -1) & (across <= sh.y)) & ((z >= -1) & (z <= sh.z))


def within(sh, axis, place, size):
    index = sh.here(axis)
    low = jnp.where(index > 0, -EDGE, 0)
    high = jnp.where(index < sh.sizes[axis] - 1, size + EDGE, size)
    return (place >= low) & (place < high)


def grid_masks(sh):
    lane, along, across = sh.lane_grid(1)
    lanes = (lane < sh.used) & within(sh, 1, across, sh.y)
    rows = within(sh, 2, level(sh), sh.z)
    return (lanes & within(sh, 0, along, sh.x)) & rows, lanes & rows


def put(ref, f, value):
    ref[f, EDGE : ref.shape[1] - EDGE, :] = value


def local_solve(sh, residual_ref, springs_ref, v, kv, factor):
    lane, _, _ = sh.lane_grid(1)
    mask = extended_mask(sh)
    for m in range(3):
        factor[m] = pick(mask, relax / jnp.where(mask, springs_ref[m], 1.0))
        z = residual_ref[m] * factor[m]
        put(v[0], m, z)
        put(kv[0], m, springs_ref[6] * z)
    for sweep in range(SWEEPS - 1):
        old, new = sweep % 2, (sweep + 1) % 2
        image = image_of(sh, lane, v[old], kv[old], None, springs_ref)
        for m in range(3):
            z = inner(v[old], m) + factor[m] * (residual_ref[m] - image[m])
            put(v[new], m, z)
            put(kv[new], m, springs_ref[6] * z)
    return (SWEEPS - 1) % 2


def coords(sh):
    lane, along, across = sh.lane_grid(sh.z)
    z = lax.broadcasted_iota(jnp.int32, (sh.z, LANES), 0)
    place = lambda index, size: (2 * index + 1).astype(f32) / size - 1.0
    return place(along, sh.x), place(across, sh.y), place(z, sh.z)


def cross(a, b):
    return (a[1] * b[2] - a[2] * b[1], a[2] * b[0] - a[0] * b[2], a[0] * b[1] - a[1] * b[0])


def fold_rows(value):
    total = value[0:8]
    for i in range(8, value.shape[0], 8):
        total = total + value[i : i + 8]
    return jnp.sum(total, axis=0, keepdims=True)


def lane_sums(rows_ref):
    ones = jnp.ones((8, LANES), f32)
    return lax.dot_general(
        ones, rows_ref[...], (((1,), (1,)), ((), ())), precision=highest, preferred_element_type=f32
    )


def coarse_sums(sh, nodes, field, count, sums, slots_ref):
    moments = tuple(field) + cross(coords(sh), field)
    for node in range(count):
        mask = nodes == float(node)
        for m in range(6):
            sums[node * 6 + m : node * 6 + m + 1, :] = fold_rows(pick(mask, moments[m]))
    line = lane_sums(sums)[0:1]
    slots_ref[...] = jnp.broadcast_to(line, slots_ref.shape)


def coarse_values(sh, nodes, received, inverse_ref, values):
    unknowns, total = inverse_ref.shape
    column = lax.broadcasted_iota(jnp.int32, (1, total), 1)
    owner = column // unknowns
    place = column - owner * unknowns
    spread = (lax.broadcasted_iota(jnp.int32, (LANES, total), 0) == place).astype(f32)
    lines = jnp.dot(received, spread, precision=highest, preferred_element_type=f32)
    mine = lax.broadcasted_iota(jnp.int32, lines.shape, 0) == owner
    vector = jnp.sum(pick(mine, lines), axis=0, keepdims=True)
    product = inverse_ref[...] * vector
    part = product[:, 0:LANES]
    for i in range(LANES, total, LANES):
        part = part + product[:, i : i + LANES]
    values[0:unknowns, :] = jnp.dot(
        part, jnp.ones((LANES, LANES), f32), precision=highest, preferred_element_type=f32
    )
    cells = []
    for m in range(6):
        cell = jnp.zeros((sh.z, LANES), f32)
        for node in range(unknowns // 6):
            cell = jnp.where(nodes == float(node), values[node * 6 + m : node * 6 + m + 1, :], cell)
        cells.append(cell)
    turned = cross(cells[3:], coords(sh))
    return [cells[m] + turned[m] for m in range(3)]


def selection(sh):
    lane, along, across = sh.lane_grid(sh.cells)
    inside = (along >= 0) & (along < sh.x) & (across >= 0) & (across < sh.y)
    row = lax.broadcasted_iota(jnp.int32, (sh.cells, LANES), 0)
    return (inside & (row == along * sh.y + across)).astype(f32)


def to_lanes(value, select):
    return lax.dot_general(
        value, select, (((0,), (0,)), ((), ())), precision=highest, preferred_element_type=f32
    )


def to_cells(value, select):
    return lax.dot_general(
        select, value, (((1,), (1,)), ((), ())), precision=highest, preferred_element_type=f32
    )


def call(kernel, name, outs, ins, scratch=(), smem=()):
    return pl.pallas_call(
        kernel,
        out_shape=[jax.ShapeDtypeStruct(shape, f32) for shape in outs],
        in_specs=[
            pl.BlockSpec(memory_space=pltpu.SMEM if i in smem else pltpu.VMEM) for i in range(len(ins))
        ],
        out_specs=[pl.BlockSpec(memory_space=pltpu.VMEM) for _ in outs],
        scratch_shapes=[pltpu.VMEM(shape, f32) for shape in scratch],
        compiler_params=pltpu.CompilerParams(vmem_limit_bytes=48 * 1024 * 1024),
        name=name,
    )(*ins)


def permutation(sizes, moves):
    def partner(axis, link, index):
        size = sizes[axis]
        other = index ^ 1 if link == 0 else index + (1 if index % 2 else -1)
        if 0 <= other < size:
            return other
        return size - 1 - index if axis == 2 and size % 2 == 0 else index

    pairs = []
    for x in range(sizes[0]):
        for y in range(sizes[1]):
            for z in range(sizes[2]):
                place = [x, y, z]
                goal = [partner(a, moves[a], place[a]) if a in moves else place[a] for a in range(3)]
                if goal == place and 0 not in moves and sizes[0] % 2 == 0:
                    goal[0] = partner(0, 0, x)
                flat = [(p[0] * sizes[1] + p[1]) * sizes[2] + p[2] for p in (place, goal)]
                pairs.append(tuple(flat))
    return pairs


def send(sh, value, moves):
    return lax.ppermute(value, AXES, permutation(sh.sizes, moves))


def send_z(sh, messages):
    return [send(sh, message, {2: link}) for link, message in enumerate(messages)]


def send_xy(sh, x_messages, y_messages):
    from_y = [send(sh, message, {1: link}) for link, message in enumerate(y_messages)]
    from_x = []
    for link, message in enumerate(x_messages):
        from_x.append(send(sh, message, {0: link}))
        from_x.extend(send(sh, message, {0: link, 1: other}) for other in range(sh.y_links))
    return from_y, from_x


def to_all(slots):
    return lax.all_to_all(slots, AXES, 0, 0, tiled=True)


def exchange(sh, ex, name, field, z_messages):
    from_z = send_z(sh, z_messages)

    def packer(*refs):
        field_ref, z_refs = refs[0], refs[1 : 1 + sh.z_links]
        x_refs = refs[1 + sh.z_links : 1 + sh.z_links + sh.x_links]
        y_refs = refs[1 + sh.z_links + sh.x_links : -1]
        scratch = refs[-1]
        merge_z(sh, ex, field_ref, z_refs, scratch, 0)
        pack_xy(sh, ex, scratch, x_refs, y_refs)

    plane = (sh.rows, LANES)
    messages = call(
        packer,
        name,
        [plane] * (sh.x_links + sh.y_links),
        [field] + from_z,
        [(ex.fields,) + plane],
    )
    from_y, from_x = send_xy(sh, messages[: sh.x_links], messages[sh.x_links :])
    return from_z, from_y, from_x


class Taker:
    def __init__(self, refs):
        self.refs, self.at = refs, 0

    def __call__(self, count):
        self.at += count
        return self.refs[self.at - count : self.at]

    def one(self):
        return self(1)[0]


def merge_all(sh, ex, take, scratch, rim, guard):
    field = take.one()
    from_z, from_y = take(sh.z_links), take(sh.y_links)
    from_x = take(sh.x_links * (1 + sh.y_links))
    merge_z(sh, ex, field, from_z, scratch, guard)
    merge_xy(sh, ex, scratch, rim, guard, from_y, from_x)


def body(right_side, phase_labels, phase_moduli, coarse_nodes, coarse_inverse):
    sizes = tuple(lax.axis_size(axis) for axis in AXES)
    _, size_x, size_y, size_z = right_side.shape
    sh = Shape(size_x, size_y, size_z, phase_moduli.shape[0], sizes)
    unknowns = coarse_inverse.shape[0]
    node_count = unknowns // 6
    sum_rows = -(-unknowns // 8) * 8
    own = slice(EDGE, EDGE + sh.z)
    plane = (sh.rows, LANES)
    fields = (3,) + plane
    tall = (3, sh.tall, LANES)
    slots = (sh.devices, LANES)
    z_shape = lambda ex: [(8 * ex.fields, LANES)] * sh.z_links
    natural = right_side.reshape(3, sh.cells, sh.z)
    nodes_natural = coarse_nodes.reshape(sh.cells, sh.z)
    label_x, label_y, label_z = phase_labels.shape

    def begin(natural_ref, labels_ref, moduli_ref, nodes_ref, field_ref, lanes_ref, slots_ref, *rest):
        z_refs, (sums, stiff) = rest[: sh.z_links], rest[sh.z_links :]
        select = selection(sh)
        field_ref[...] = jnp.zeros(field_ref.shape, f32)
        residual = []
        for m in range(3):
            residual.append(to_lanes(natural_ref[m], select))
            field_ref[m, own, :] = residual[m]
        for i in range(label_x):
            labels = labels_ref[i]
            moduli = jnp.zeros(labels.shape, f32)
            for phase in range(sh.phases):
                moduli = jnp.where(labels == phase, moduli_ref[phase], moduli)
            stiff[i * label_y : (i + 1) * label_y, :] = moduli
        row = lax.broadcasted_iota(jnp.int32, (sh.z, label_z), 0)
        column = lax.broadcasted_iota(jnp.int32, (sh.z, label_z), 1)
        wide = ((row >= 2 * column) & (row < 2 * column + 2)).astype(f32)
        by_z = lax.dot_general(
            wide, stiff[...], (((1,), (1,)), ((), ())), precision=highest, preferred_element_type=f32
        )
        lane, along, across = sh.lane_grid(label_x * label_y)
        inside = (along >= 0) & (along < sh.x) & (across >= 0) & (across < sh.y)
        block = lax.broadcasted_iota(jnp.int32, along.shape, 0)
        to_block = (inside & (block == (along >> 1) * label_y + (across >> 1))).astype(f32)
        field_ref[3, own, :] = jnp.dot(by_z, to_block, precision=highest, preferred_element_type=f32)
        nodes = to_lanes(nodes_ref[...].astype(f32) + 1.0, select) - 1.0
        lanes_ref[...] = nodes
        sums[...] = jnp.zeros(sums.shape, f32)
        coarse_sums(sh, nodes, residual, node_count, sums, slots_ref)
        pack_z(sh, SPREAD, lambda f, start, count: field_ref[f, start : start + count, :], z_refs)

    start_field, nodes, sums, *z_messages = call(
        begin,
        "begin",
        [(4,) + plane, (sh.z, LANES), slots] + z_shape(SPREAD),
        [natural, phase_labels, phase_moduli, nodes_natural],
        [(LANES, LANES), (label_x * label_y, label_z)],
        smem=(2,),
    )
    from_z, from_y, from_x = exchange(sh, SPREAD, "spread", start_field, z_messages)
    coarse = to_all(sums)

    def finish_solve(index, v, nodes_ref, coarse_ref, inverse_ref, values, solution_ref, z_refs, ex):
        for m in range(3):
            solution_ref[m] = v[index][m, EDGE : EDGE + sh.rows, :]
        added = coarse_values(sh, nodes_ref[...], coarse_ref[...], inverse_ref, values)
        valid = nodes_ref[...] >= 0.0
        for m in range(3):
            solution_ref[m, own, :] += pick(valid, added[m])
        pack_z(sh, ex, lambda f, start, count: solution_ref[f, start : start + count, :], z_refs)

    def first_solve(*refs):
        take = Taker(refs)
        merging = take(1 + sh.z_links + sh.y_links + sh.x_links * (1 + sh.y_links))
        nodes_ref, coarse_ref, inverse_ref = take(3)
        solution_ref, springs_ref = take(2)
        z_refs = take(sh.z_links)
        all_fields, rims, stiff, stiff_rim, v0, v1, kv0, kv1, factor, values = take(10)
        clear_guards(sh, (stiff, stiff_rim, v0, v1, kv0, kv1))
        merge_all(sh, SPREAD, Taker(merging), all_fields, rims, 0)
        put(stiff, 0, all_fields[3])
        put(stiff_rim, 0, rims[3])
        springs_ref[6] = all_fields[3]
        springs_ref[7] = rims[3]
        lane, _, _ = sh.lane_grid(1)

        for f, entry in enumerate(own_block(sh, lane, (stiff, stiff_rim))):
            springs_ref[f] = entry
        index = local_solve(sh, all_fields, springs_ref, (v0, v1), (kv0, kv1), factor)
        finish_solve(index, (v0, v1), nodes_ref, coarse_ref, inverse_ref, values, solution_ref, z_refs, DEEP)

    solved, springs, *z_messages = call(
        first_solve,
        "first_solve",
        [fields, (8,) + plane] + z_shape(DEEP),
        [start_field, *from_z, *from_y, *from_x, nodes, coarse, coarse_inverse],
        [(4,) + plane, (4,) + plane, (1, sh.tall, LANES), (1, sh.tall, LANES)] + [tall] * 4 + [fields, (LANES, LANES)],
    )
    from_z, from_y, from_x = exchange(sh, DEEP, "deep", solved, z_messages)

    def first_image(*refs):
        take = Taker(refs)
        merging = take(1 + sh.z_links + sh.y_links + sh.x_links * (1 + sh.y_links))
        nodes_ref, springs_ref = take(2)
        search_ref, image_ref, slots_ref = take(3)
        v, rim, kv, k_rim, sums = take(5)
        clear_guards(sh, (v, rim, kv, k_rim))
        merge_all(sh, DEEP, Taker(merging), v, rim, EDGE)
        lane, _, _ = sh.lane_grid(1)

        in_grid, in_rim = grid_masks(sh)
        for m in range(3):
            value = pick(in_grid, inner(v, m))
            put(v, m, value)
            search_ref[m] = value
            put(kv, m, springs_ref[6] * value)
            value = pick(in_rim, inner(rim, m))
            put(rim, m, value)
            put(k_rim, m, springs_ref[7] * value)
        image = image_of(sh, lane, v, kv, (rim, k_rim), springs_ref)
        keep = in_grid & extended_mask(sh)
        for m in range(3):
            image_ref[m] = pick(keep, image[m])
        sums[...] = jnp.zeros(sums.shape, f32)
        coarse_sums(sh, nodes_ref[...], [image_ref[m, own, :] for m in range(3)], node_count, sums, slots_ref)

    search, image, sums = call(
        first_image,
        "first_image",
        [fields, fields, slots],
        [solved, *from_z, *from_y, *from_x, nodes, springs],
        [tall] * 4 + [(LANES, LANES)],
    )
    coarse = to_all(sums)

    def second_solve(*refs):
        take = Taker(refs)
        image_ref, springs_ref, nodes_ref, coarse_ref, inverse_ref = take(5)
        solution_ref = take.one()
        z_refs = take(sh.z_links)
        v0, v1, kv0, kv1, factor, values = take(6)
        clear_guards(sh, (v0, v1, kv0, kv1))
        index = local_solve(sh, image_ref, springs_ref, (v0, v1), (kv0, kv1), factor)
        finish_solve(index, (v0, v1), nodes_ref, coarse_ref, inverse_ref, values, solution_ref, z_refs, NEAR)

    solved, *z_messages = call(
        second_solve,
        "second_solve",
        [fields] + z_shape(NEAR),
        [image, springs, nodes, coarse, coarse_inverse],
        [tall] * 4 + [fields, (LANES, LANES)],
    )
    from_z, from_y, from_x = exchange(sh, NEAR, "near", solved, z_messages)

    def second_image(*refs):
        take = Taker(refs)
        merging = take(1 + sh.z_links + sh.y_links + sh.x_links * (1 + sh.y_links))
        nodes_ref, springs_ref, start_ref, search_ref, first_ref = take(5)
        second_ref, image_ref, slots_ref = take(3)
        v, kv, sums = take(3)
        clear_guards(sh, (v, kv))
        merge_all(sh, NEAR, Taker(merging), v, None, EDGE)
        lane, _, _ = sh.lane_grid(1)

        in_grid, _ = grid_masks(sh)
        for m in range(3):
            value = pick(in_grid, inner(v, m))
            put(v, m, value)
            second_ref[m] = value
            put(kv, m, springs_ref[6] * value)
        image = image_of(sh, lane, v, kv, None, springs_ref)
        for m in range(3):
            image_ref[m] = image[m]
        valid = nodes_ref[...] >= 0.0
        names = ("r", "z", "w", "q", "v")
        sources = (start_ref, search_ref, first_ref, second_ref, image_ref)
        get = {name: [source[m, own, :] for m in range(3)] for name, source in zip(names, sources)}
        sums[...] = jnp.zeros(sums.shape, f32)
        for i, (a, b) in enumerate(("rz", "zw", "rq", "wq", "zv", "qv")):
            product = sum(get[a][m] * get[b][m] for m in range(3))
            sums[i : i + 1, :] = fold_rows(pick(valid, product))
        slots_ref[...] = jnp.broadcast_to(lane_sums(sums)[0:1], slots_ref.shape)

    second, second_image_field, sums = call(
        second_image,
        "second_image",
        [fields, fields, slots],
        [solved, *from_z, *from_y, *from_x, nodes, springs, start_field, search, image],
        [tall] * 2 + [(LANES, LANES)],
    )
    totals = to_all(sums)

    def finish(totals_ref, natural_ref, search_ref, first_ref, second_ref, image_ref, field_ref, residual_ref):
        total = jnp.sum(totals_ref[...], axis=0, keepdims=True)
        rz, zw, rq, wq, zv, qv = [total[:, i : i + 1] for i in range(6)]
        step0 = rz / zw
        rho = rz - step0 * zw - step0 * rq + step0 * step0 * wq
        grow = 1.0 + rho / rz
        curvature = grow * grow * zw - grow * step0 * (zv + wq) + step0 * step0 * qv
        step1 = rho / curvature
        first = step0 + step1 * grow
        second = step0 * step1
        select = selection(sh)
        for m in range(3):
            update = first * search_ref[m, own, :] - second * second_ref[m, own, :]
            field_ref[m] = to_cells(update, select)
            update = first * first_ref[m, own, :] - second * image_ref[m, own, :]
            residual_ref[m] = natural_ref[m] - to_cells(update, select)

    solution_field, residual = call(
        finish,
        "finish",
        [natural.shape, natural.shape],
        [totals, natural, search, image, second, second_image_field],
    )
    return solution_field.reshape(right_side.shape), residual.reshape(right_side.shape)


def solution(mesh):
    in_specs = (
        P(None, "gx", "gy", "gz"),
        P("gx", "gy", "gz"),
        P(),
        P("gx", "gy", "gz"),
        P(("gx", "gy", "gz"), None),
    )
    out_specs = (P(None, "gx", "gy", "gz"), P(None, "gx", "gy", "gz"))
    return jax.shard_map(body, mesh=mesh, in_specs=in_specs, out_specs=out_specs, check_vma=False)
```

```python
import jax
import jax.numpy as jnp
from jax import lax
from jax.experimental import pallas as pl
from jax.experimental.pallas import tpu as pltpu
from jax.sharding import PartitionSpec as P

AXES = ("gx", "gy", "gz")
SWEEPS = 4
relax = 0.6
highest = lax.Precision.HIGHEST
f32 = jnp.float32
LANES = 128
EDGE = 8

ALONG1, ACROSS1 = 0.75, 0.5
ALONG2, ACROSS2, MIXED2 = 0.3125, 0.25, 0.0625
SAME3, MIXED3 = 7.0 / 36.0, 1.0 / 36.0
TOTAL = 2 * ALONG1 + 4 * ACROSS1 + 8 * ALONG2 + 4 * ACROSS2 + 8 * SAME3


class Exchange:
    def __init__(self, fields, layers, up, down):
        self.fields, self.layers, self.up, self.down = fields, layers, up, down


SPREAD = Exchange(4, 2, -2, 0)
DEEP = Exchange(3, 3, -2, -1)
NEAR = Exchange(3, 2, -1, -1)


class Shape:
    def __init__(self, size_x, size_y, size_z, phases, mesh_sizes):
        self.x, self.y, self.z = size_x, size_y, size_z
        self.pitch = size_y + 4
        self.used = (size_x + 2) * self.pitch
        assert self.used <= LANES
        self.rows = size_z + 2 * EDGE
        self.tall = self.rows + 2 * EDGE
        self.phases = phases
        self.sizes = mesh_sizes
        self.devices = mesh_sizes[0] * mesh_sizes[1] * mesh_sizes[2]
        self.cells = size_x * size_y
        self.links = [1 if n <= 2 else 2 for n in mesh_sizes]
        self.x_links, self.y_links, self.z_links = self.links

    def lane_grid(self, rows):
        lane = lax.broadcasted_iota(jnp.int32, (rows, LANES), 1)
        column = jnp.zeros_like(lane)
        for j in range(1, self.x + 2):
            column = column + (lane >= j * self.pitch).astype(jnp.int32)
        offset = lane - column * self.pitch
        return lane, column - 1, offset - 2

    def here(self, axis):
        return lax.axis_index(AXES[axis])


def shift(value, amount):
    amount = amount % LANES
    return value if amount == 0 else pltpu.roll(value, amount, 1)


def pick(mask, value):
    return jnp.where(mask, value, 0.0)


def scale(flag, value):
    return value * flag.astype(f32)


def pair(links, even, upward, downward):
    first = jnp.where(even, upward, downward)
    return (first,) if links == 1 else (first, jnp.where(even, downward, upward))


def sides(sh, axis, received):
    index, size = sh.here(axis), sh.sizes[axis]
    even = index % 2 == 0
    first = received[0]
    second = received[1] if len(received) > 1 else jnp.zeros_like(first)
    below = jnp.where(even, second, first)
    above = jnp.where(even, first, second)
    return scale(index > 0, below), scale(index < size - 1, above)


def lane_range(lane, start, count):
    return (lane >= start) & (lane < start + count)


def pack_z(sh, ex, source, out_refs):
    even = sh.here(2) % 2 == 0
    zero = jnp.zeros((8 - ex.layers, LANES), f32)
    for f in range(ex.fields):
        upward = source(f, EDGE + sh.z + ex.up, ex.layers)
        downward = source(f, EDGE + ex.down, ex.layers)
        for ref, message in zip(out_refs, pair(sh.z_links, even, upward, downward)):
            ref[8 * f : 8 * f + ex.layers, :] = message
            ref[8 * f + ex.layers : 8 * f + 8, :] = zero


def merge_z(sh, ex, field_ref, received_refs, scratch, guard):
    below, above = sides(sh, 2, [ref[...] for ref in received_refs])
    for f in range(ex.fields):
        scratch[f, guard : guard + sh.rows, :] = field_ref[f]
        low = guard + EDGE + ex.up
        high = guard + EDGE + sh.z + ex.down
        scratch[f, low : low + ex.layers, :] += below[8 * f : 8 * f + ex.layers]
        scratch[f, high : high + ex.layers, :] += above[8 * f : 8 * f + ex.layers]


def pack_xy(sh, ex, scratch, x_refs, y_refs):
    rows = sh.rows
    lane, _, across = sh.lane_grid(1)
    even_x, even_y = sh.here(0) % 2 == 0, sh.here(1) % 2 == 0
    span = ex.layers * sh.pitch
    x_up = x_down = y_up = y_down = jnp.zeros((rows, LANES), f32)
    for f in range(ex.fields):
        value = scratch[f]
        start = (sh.x + ex.up + 1) * sh.pitch
        x_up = x_up + shift(pick(lane_range(lane, start, span), value), f * span - start)
        start = (ex.down + 1) * sh.pitch
        x_down = x_down + shift(pick(lane_range(lane, start, span), value), f * span - start)
        inside = lane < sh.used
        start = sh.y + ex.up
        y_up = y_up + shift(
            pick(inside & lane_range(across, start, ex.layers), value), f * ex.layers - start - 2
        )
        start = ex.down
        y_down = y_down + shift(
            pick(inside & lane_range(across, start, ex.layers), value), f * ex.layers - start - 2
        )
    for ref, message in zip(x_refs, pair(sh.x_links, even_x, x_up, x_down)):
        ref[...] = message
    for ref, message in zip(y_refs, pair(sh.y_links, even_y, y_up, y_down)):
        ref[...] = message


def merge_xy(sh, ex, scratch, rim, guard, y_refs, x_refs):
    lane, _, across = sh.lane_grid(1)
    inside = lane < sh.used
    low_mask = inside & lane_range(across, ex.up, ex.layers)
    high_mask = inside & lane_range(across, sh.y + ex.down, ex.layers)
    span = ex.layers * sh.pitch
    below_y, above_y = sides(sh, 1, [ref[...] for ref in y_refs])
    per_link = len(x_refs) // sh.x_links
    sums = []
    for link in range(sh.x_links):
        straight, diagonal = x_refs[link * per_link], x_refs[link * per_link + 1 : (link + 1) * per_link]
        total = straight[...]
        if diagonal:
            below, above = sides(sh, 1, [ref[...] for ref in diagonal])
            total = total + pick(low_mask, shift(below, -sh.y)) + pick(high_mask, shift(above, sh.y))
        sums.append(total)
    below_x, above_x = sides(sh, 0, sums)
    first = 1 if ex.up == -2 else 0
    last = ex.layers - 1 if ex.down + ex.layers == 2 else ex.layers
    for f in range(ex.fields):
        addend = pick(low_mask, shift(below_y, ex.up + 2 - ex.layers * f))
        addend = addend + pick(high_mask, shift(above_y, sh.y + ex.down + 2 - ex.layers * f))
        start = (ex.up + first + 1) * sh.pitch
        count = (ex.layers - first) * sh.pitch
        moved = shift(below_x, start - f * span - first * sh.pitch)
        addend = addend + pick(lane_range(lane, start, count), moved)
        start = (sh.x + ex.down + 1) * sh.pitch
        moved = shift(above_x, start - f * span)
        addend = addend + pick(lane_range(lane, start, last * sh.pitch), moved)
        scratch[f, guard : guard + sh.rows, :] += addend
        if rim is not None:
            low = pick(lane_range(lane, 0, sh.pitch), shift(below_x, -f * span))
            start = (sh.x + 1) * sh.pitch
            moved = shift(above_x, start - f * span - last * sh.pitch)
            high = pick(lane_range(lane, start, sh.pitch), moved)
            rim[f, guard : guard + sh.rows, :] = low + high


def clear_guards(sh, refs):
    for ref in refs:
        for f in range(ref.shape[0]):
            ref[f, :EDGE, :] = jnp.zeros((EDGE, LANES), f32)
            ref[f, sh.tall - EDGE :, :] = jnp.zeros((EDGE, LANES), f32)


def inner(ref, f):
    return ref[f, EDGE : ref.shape[1] - EDGE, :]


def z_stage(ref, f):
    end = ref.shape[1] - EDGE
    after = ref[f, EDGE + 1 : end + 1, :]
    before = ref[f, EDGE - 1 : end - 1, :]
    return inner(ref, f), before + after, after - before


def y_stage(value):
    after, before = shift(value, -1), shift(value, 1)
    return before + after, after - before


def yz_parts(ref):
    a, a_sum, a_dif = z_stage(ref, 0)
    b, b_sum, b_dif = z_stage(ref, 1)
    c, c_sum, c_dif = z_stage(ref, 2)
    pa, ma = y_stage(a)
    pas, mas = y_stage(a_sum)
    pad, _ = y_stage(a_dif)
    pb, mb = y_stage(b)
    pbs, mbs = y_stage(b_sum)
    _, mbd = y_stage(b_dif)
    pc, _ = y_stage(c)
    pcs, _ = y_stage(c_sum)
    pcd, mcd = y_stage(c_dif)
    own_x = ACROSS1 * (pa + a_sum) + ACROSS2 * pas
    even_x = ALONG1 * a + ALONG2 * (pa + a_sum) + SAME3 * pas
    odd_x = MIXED2 * (mb + c_dif) + MIXED3 * (mbs + pcd)
    own_y = ALONG1 * pb + ACROSS1 * b_sum + ALONG2 * pbs + MIXED2 * mcd
    even_y = ACROSS1 * b + ALONG2 * pb + ACROSS2 * b_sum + SAME3 * pbs + MIXED3 * mcd
    odd_y = MIXED2 * ma + MIXED3 * mas
    own_z = ALONG1 * c_sum + ACROSS1 * pc + ALONG2 * pcs + MIXED2 * mbd
    even_z = ACROSS1 * c + ACROSS2 * pc + ALONG2 * c_sum + SAME3 * pcs + MIXED3 * mbd
    odd_z = MIXED2 * a_dif + MIXED3 * pad
    return (own_x, even_x, odd_x), (own_y, even_y, odd_y), (own_z, even_z, odd_z)


def x_stage(sh, lane, own, plus, minus, rim_plus, rim_minus):
    after, before = shift(plus, -sh.pitch), shift(minus, sh.pitch)
    last = (sh.x + 1) * sh.pitch
    if rim_plus is None:
        return own + pick(lane < last, after) + pick(lane >= sh.pitch, before)
    return own + jnp.where(lane < last, after, rim_plus) + jnp.where(lane >= sh.pitch, before, rim_minus)


def stencil(sh, lane, ref, rim):
    parts = yz_parts(ref)
    rims = yz_parts(rim) if rim is not None else [None] * 3
    out = []
    for (own, even, odd), rim_part in zip(parts, rims):
        if rim_part is None:
            out.append(x_stage(sh, lane, own, even + odd, even - odd, None, None))
        else:
            _, rim_even, rim_odd = rim_part
            out.append(
                x_stage(sh, lane, own, even + odd, even - odd, rim_even + rim_odd, rim_even - rim_odd)
            )
    return out


def spring_parts(ref):
    k, k_sum, k_dif = z_stage(ref, 0)
    pk, mk = y_stage(k)
    pks, mks = y_stage(k_sum)
    pkd, mkd = y_stage(k_dif)
    zero = jnp.zeros_like(k)
    xx = (ACROSS1 * (pk + k_sum) + ACROSS2 * pks, ALONG1 * k + ALONG2 * (pk + k_sum) + SAME3 * pks, zero)
    yy = (
        ALONG1 * pk + ACROSS1 * k_sum + ALONG2 * pks,
        ACROSS1 * k + ALONG2 * pk + ACROSS2 * k_sum + SAME3 * pks,
        zero,
    )
    zz = (
        ALONG1 * k_sum + ACROSS1 * pk + ALONG2 * pks,
        ACROSS1 * k + ACROSS2 * pk + ALONG2 * k_sum + SAME3 * pks,
        zero,
    )
    xy = (zero, zero, MIXED2 * mk + MIXED3 * mks)
    xz = (zero, zero, MIXED2 * k_dif + MIXED3 * pkd)
    yz = (MIXED2 * mkd, MIXED3 * mkd, zero)
    return xx, yy, zz, xy, xz, yz


def own_block(sh, lane, springs):
    main, rim = springs
    k = inner(main, 0)
    out = []
    for index, ((own, even, odd), (_, rim_even, rim_odd)) in enumerate(
        zip(spring_parts(main), spring_parts(rim))
    ):
        total = x_stage(sh, lane, own, even + odd, even - odd, rim_even + rim_odd, rim_even - rim_odd)
        out.append(total + TOTAL * k if index < 3 else total)
    return out


def apply_block(d, v):
    return (
        d[0] * v[0] + d[3] * v[1] + d[4] * v[2],
        d[3] * v[0] + d[1] * v[1] + d[5] * v[2],
        d[4] * v[0] + d[5] * v[1] + d[2] * v[2],
    )


def image_of(sh, lane, v, kv, rims, springs_ref):
    outer = stencil(sh, lane, v, rims and rims[0])
    scaled = stencil(sh, lane, kv, rims and rims[1])
    own = apply_block([springs_ref[f] for f in range(6)], [inner(v, m) for m in range(3)])
    return [own[m] - (springs_ref[6] * outer[m] + scaled[m]) for m in range(3)]


def level(sh):
    return lax.broadcasted_iota(jnp.int32, (sh.rows, LANES), 0) - EDGE


def extended_mask(sh):
    lane, _, across = sh.lane_grid(1)
    z = level(sh)
    return ((lane < sh.used) & (across >= -1) & (across <= sh.y)) & ((z >= -1) & (z <= sh.z))


def within(sh, axis, place, size):
    index = sh.here(axis)
    low = jnp.where(index > 0, -EDGE, 0)
    high = jnp.where(index < sh.sizes[axis] - 1, size + EDGE, size)
    return (place >= low) & (place < high)


def grid_masks(sh):
    lane, along, across = sh.lane_grid(1)
    lanes = (lane < sh.used) & within(sh, 1, across, sh.y)
    rows = within(sh, 2, level(sh), sh.z)
    return (lanes & within(sh, 0, along, sh.x)) & rows, lanes & rows


def put(ref, f, value):
    ref[f, EDGE : ref.shape[1] - EDGE, :] = value


def local_solve(sh, residual_ref, springs_ref, v, kv, factor):
    lane, _, _ = sh.lane_grid(1)
    mask = extended_mask(sh)
    for m in range(3):
        factor[m] = pick(mask, relax / jnp.where(mask, springs_ref[m], 1.0))
        z = residual_ref[m] * factor[m]
        put(v[0], m, z)
        put(kv[0], m, springs_ref[6] * z)
    for sweep in range(SWEEPS - 1):
        old, new = sweep % 2, (sweep + 1) % 2
        image = image_of(sh, lane, v[old], kv[old], None, springs_ref)
        for m in range(3):
            z = inner(v[old], m) + factor[m] * (residual_ref[m] - image[m])
            put(v[new], m, z)
            put(kv[new], m, springs_ref[6] * z)
    return (SWEEPS - 1) % 2


def coords(sh):
    lane, along, across = sh.lane_grid(sh.z)
    z = lax.broadcasted_iota(jnp.int32, (sh.z, LANES), 0)
    place = lambda index, size: (2 * index + 1).astype(f32) / size - 1.0
    return place(along, sh.x), place(across, sh.y), place(z, sh.z)


def cross(a, b):
    return (a[1] * b[2] - a[2] * b[1], a[2] * b[0] - a[0] * b[2], a[0] * b[1] - a[1] * b[0])


def fold_rows(value):
    total = value[0:8]
    for i in range(8, value.shape[0], 8):
        total = total + value[i : i + 8]
    return jnp.sum(total, axis=0, keepdims=True)


def lane_sums(rows_ref):
    ones = jnp.ones((8, LANES), f32)
    return lax.dot_general(
        ones, rows_ref[...], (((1,), (1,)), ((), ())), precision=highest, preferred_element_type=f32
    )


def coarse_sums(sh, nodes, field, count, sums):
    moments = tuple(field) + cross(coords(sh), field)
    for node in range(count):
        mask = nodes == float(node)
        for m in range(6):
            sums[node * 6 + m : node * 6 + m + 1, :] = fold_rows(pick(mask, moments[m]))
    flat = (sh.here(0) * sh.sizes[1] + sh.here(1)) * sh.sizes[2] + sh.here(2)
    return pltpu.roll(lane_sums(sums), lax.rem(flat * (6 * count), LANES), 1)[0:1]


def coarse_values(sh, nodes, received, inverse_ref, values):
    unknowns, total = inverse_ref.shape
    row = lax.broadcasted_iota(jnp.int32, received.shape, 0)
    part = jnp.zeros((unknowns, LANES), f32)
    for i in range(0, total, LANES):
        owner = (i + lax.broadcasted_iota(jnp.int32, (1, LANES), 1)) // unknowns
        vector = jnp.sum(pick(row == owner, received), axis=0, keepdims=True)
        part = part + inverse_ref[:, i : i + LANES] * vector
    values[0:unknowns, :] = jnp.dot(
        part, jnp.ones((LANES, LANES), f32), precision=highest, preferred_element_type=f32
    )
    cells = []
    for m in range(6):
        cell = jnp.zeros((sh.z, LANES), f32)
        for node in range(unknowns // 6):
            cell = jnp.where(nodes == float(node), values[node * 6 + m : node * 6 + m + 1, :], cell)
        cells.append(cell)
    turned = cross(cells[3:], coords(sh))
    return [cells[m] + turned[m] for m in range(3)]


def selection(sh):
    lane, along, across = sh.lane_grid(sh.cells)
    inside = (along >= 0) & (along < sh.x) & (across >= 0) & (across < sh.y)
    row = lax.broadcasted_iota(jnp.int32, (sh.cells, LANES), 0)
    return (inside & (row == along * sh.y + across)).astype(f32)


def to_lanes(value, select):
    return lax.dot_general(
        value, select, (((0,), (0,)), ((), ())), precision=highest, preferred_element_type=f32
    )


def to_cells(value, select):
    return lax.dot_general(
        select, value, (((1,), (1,)), ((), ())), precision=highest, preferred_element_type=f32
    )


def send_lines(sh, lines, slots_ref):
    here = [sh.here(axis) for axis in range(3)]
    corner = [lines[8 * i : 8 * i + 8, :] for i in range(4)]
    top, bottom = lines[32:40, :], lines[40:48, :]
    for x in range(sh.sizes[0]):
        low_high = [jnp.where(x > here[0], corner[2 + high], corner[high]) for high in range(2)]
        for y in range(sh.sizes[1]):
            column = jnp.where(y > here[1], low_high[1], low_high[0])
            for z in range(sh.sizes[2]):
                slot = jnp.where(z == here[2] + 1, top, jnp.where(z == here[2] - 1, bottom, column))
                place = 8 * ((x * sh.sizes[1] + y) * sh.sizes[2] + z)
                slots_ref[place : place + 8, :] = slot


def slot_from(sh, received_ref, step):
    place, exists = 0, None
    for axis in range(3):
        index = sh.here(axis) + step[axis]
        inside = (index >= 0) & (index < sh.sizes[axis])
        exists = inside if exists is None else exists & inside
        place = place * sh.sizes[axis] + jnp.clip(index, 0, sh.sizes[axis] - 1)
    return scale(exists, received_ref[pl.ds(pl.multiple_of(place * 8, 8), 8), :])


def repeat_twice(count):
    row = lax.broadcasted_iota(jnp.int32, (2 * count, count), 0)
    column = lax.broadcasted_iota(jnp.int32, (2 * count, count), 1)
    return ((row >= 2 * column) & (row < 2 * column + 2)).astype(f32)


def merge_lines(sh, received_ref, all_fields, rims, corners, label_z):
    lane, along, across = sh.lane_grid(1)
    inside = lane < sh.used
    last = (sh.x + 1) * sh.pitch
    x_mask = {-1: lane < sh.pitch, 0: (lane >= sh.pitch) & (lane < last), 1: (lane >= last) & inside}
    y_mask = {-1: across < 0, 0: (across >= 0) & (across < sh.y), 1: across >= sh.y}
    for dz in (-1, 1):
        main = edge = jnp.zeros((8, LANES), f32)
        for dx in (-1, 0, 1):
            for dy in (-1, 0, 1):
                slot = slot_from(sh, received_ref, (dx, dy, dz))
                mask = x_mask[dx] & y_mask[dy]
                main = main + pick(mask, shift(slot, dx * sh.x * sh.pitch + dy * sh.y))
                if dx:
                    edge = edge + pick(mask, shift(slot, dx * (sh.x - 1) * sh.pitch + dy * sh.y))
        near = EDGE + sh.z if dz > 0 else EDGE - 1
        for f in range(4):
            all_fields[f, near : near + 1, :] += main[f : f + 1]
        rims[3, near : near + 1, :] += edge[3:4]
        all_fields[3, near + dz : near + dz + 1, :] += main[3:4]
        rims[3, near + dz : near + dz + 1, :] += edge[3:4]
    corners[...] = jnp.zeros(corners.shape, f32)
    number = lax.broadcasted_iota(jnp.int32, (8, LANES), 0)
    lanes, lanes_along, lanes_across = sh.lane_grid(8)
    same = thick = lanes < 0
    for i, (dx, dy) in enumerate(((-1, -1), (-1, 1), (1, -1), (1, 1))):
        slot = slot_from(sh, received_ref, (dx, dy, 0))
        for f in range(4):
            corners[8 * f + i : 8 * f + i + 1, :] = slot[f : f + 1]
        here = (number == i) & (lanes < sh.used)
        at_x = lanes_along == (sh.x if dx > 0 else -1)
        beyond = lanes_across >= sh.y if dy > 0 else lanes_across < 0
        same = same | (here & at_x & (lanes_across == (sh.y if dy > 0 else -1)))
        thick = thick | (here & at_x & beyond)
    own = slice(EDGE, EDGE + sh.z)
    for m in range(3):
        all_fields[m, own, :] += to_lanes(corners[8 * m : 8 * m + 8, :], same.astype(f32))
    by_z = lax.dot_general(
        repeat_twice(label_z),
        corners[24:32, 0:label_z],
        (((1,), (1,)), ((), ())),
        precision=highest,
        preferred_element_type=f32,
    )
    columns = jnp.dot(by_z, thick.astype(f32), precision=highest, preferred_element_type=f32)
    all_fields[3, own, :] += columns
    rims[3, own, :] += columns


def call(kernel, name, outs, ins, scratch=(), remote_ins=False):
    space = pltpu.HBM if remote_ins else pltpu.VMEM
    return pl.pallas_call(
        kernel,
        out_shape=[jax.ShapeDtypeStruct(shape, f32) for shape in outs],
        in_specs=[pl.BlockSpec(memory_space=space) for _ in ins],
        out_specs=[pl.BlockSpec(memory_space=pltpu.VMEM) for _ in outs],
        scratch_shapes=[pltpu.VMEM(shape, f32) if isinstance(shape, tuple) else shape for shape in scratch],
        compiler_params=pltpu.CompilerParams(vmem_limit_bytes=48 * 1024 * 1024),
        name=name,
    )(*ins)


def permutation(sizes, moves):
    def partner(axis, link, index):
        size = sizes[axis]
        other = index ^ 1 if link == 0 else index + (1 if index % 2 else -1)
        if 0 <= other < size:
            return other
        return size - 1 - index if axis == 2 and size % 2 == 0 else index

    pairs = []
    for x in range(sizes[0]):
        for y in range(sizes[1]):
            for z in range(sizes[2]):
                place = [x, y, z]
                goal = [partner(a, moves[a], place[a]) if a in moves else place[a] for a in range(3)]
                if goal == place and 0 not in moves and sizes[0] % 2 == 0:
                    goal[0] = partner(0, 0, x)
                flat = [(p[0] * sizes[1] + p[1]) * sizes[2] + p[2] for p in (place, goal)]
                pairs.append(tuple(flat))
    return pairs


def send(sh, value, moves):
    return lax.ppermute(value, AXES, permutation(sh.sizes, moves))


def send_z(sh, messages):
    return [send(sh, message, {2: link}) for link, message in enumerate(messages)]


def send_xy(sh, x_messages, y_messages, diagonal=True):
    from_y = [send(sh, message, {1: link}) for link, message in enumerate(y_messages)]
    from_x = []
    for link, message in enumerate(x_messages):
        from_x.append(send(sh, message, {0: link}))
        if diagonal:
            from_x.extend(send(sh, message, {0: link, 1: other}) for other in range(sh.y_links))
    return from_y, from_x


def to_all(slots):
    return lax.all_to_all(slots, AXES, 0, 0, tiled=True)


def exchange(sh, ex, name, field, z_messages):
    from_z = send_z(sh, z_messages)

    def packer(*refs):
        field_ref, z_refs = refs[0], refs[1 : 1 + sh.z_links]
        x_refs = refs[1 + sh.z_links : 1 + sh.z_links + sh.x_links]
        y_refs = refs[1 + sh.z_links + sh.x_links : -1]
        scratch = refs[-1]
        merge_z(sh, ex, field_ref, z_refs, scratch, 0)
        pack_xy(sh, ex, scratch, x_refs, y_refs)

    plane = (sh.rows, LANES)
    messages = call(
        packer,
        name,
        [plane] * (sh.x_links + sh.y_links),
        [field] + from_z,
        [(ex.fields,) + plane],
    )
    from_y, from_x = send_xy(sh, messages[: sh.x_links], messages[sh.x_links :])
    return from_z, from_y, from_x


class Taker:
    def __init__(self, refs):
        self.refs, self.at = refs, 0

    def __call__(self, count):
        self.at += count
        return self.refs[self.at - count : self.at]

    def one(self):
        return self(1)[0]


def merge_all(sh, ex, take, scratch, rim, guard):
    field = take.one()
    from_z, from_y = take(sh.z_links), take(sh.y_links)
    from_x = take(sh.x_links * (1 + sh.y_links))
    merge_z(sh, ex, field, from_z, scratch, guard)
    merge_xy(sh, ex, scratch, rim, guard, from_y, from_x)


def body(right_side, phase_labels, phase_moduli, coarse_nodes, coarse_inverse):
    sizes = tuple(lax.axis_size(axis) for axis in AXES)
    _, size_x, size_y, size_z = right_side.shape
    sh = Shape(size_x, size_y, size_z, phase_moduli.shape[0], sizes)
    unknowns = coarse_inverse.shape[0]
    node_count = unknowns // 6
    sum_rows = -(-unknowns // 8) * 8
    own = slice(EDGE, EDGE + sh.z)
    plane = (sh.rows, LANES)
    fields = (3,) + plane
    tall = (3, sh.tall, LANES)
    slots = (sh.devices, LANES)
    z_shape = lambda ex: [(8 * ex.fields, LANES)] * sh.z_links
    natural = right_side.reshape(3, sh.cells, sh.z)
    nodes_natural = coarse_nodes.reshape(sh.cells, sh.z)
    label_x, label_y, label_z = phase_labels.shape

    def begin(natural_in, labels_in, moduli_in, nodes_in, field_ref, lanes_ref, slots_ref, *rest):
        x_refs, y_refs = rest[: sh.x_links], rest[sh.x_links : sh.x_links + sh.y_links]
        natural_ref, labels_ref, moduli_ref, nodes_ref, sems, sums, stiff, lines = rest[sh.x_links + sh.y_links :]
        pairs = ((natural_in, natural_ref), (labels_in, labels_ref), (moduli_in, moduli_ref), (nodes_in, nodes_ref))
        copies = [pltpu.make_async_copy(a, b, sems.at[i]) for i, (a, b) in enumerate(pairs)]
        for copy in copies:
            copy.start()
        select = selection(sh)
        field_ref[...] = jnp.zeros(field_ref.shape, f32)
        sums[...] = jnp.zeros(sums.shape, f32)
        lines[...] = jnp.zeros(lines.shape, f32)
        for copy in copies:
            copy.wait()
        residual = []
        for m in range(3):
            residual.append(to_lanes(natural_ref[m], select))
            field_ref[m, own, :] = residual[m]
        for i in range(label_x):
            labels = labels_ref[i]
            moduli = jnp.zeros(labels.shape, f32)
            for phase in range(sh.phases):
                moduli = jnp.where(labels == phase, moduli_ref[phase], moduli)
            stiff[i * label_y : (i + 1) * label_y, :] = moduli
        by_z = lax.dot_general(
            repeat_twice(label_z), stiff[...], (((1,), (1,)), ((), ())), precision=highest, preferred_element_type=f32
        )
        lane, along, across = sh.lane_grid(label_x * label_y)
        inside = (along >= 0) & (along < sh.x) & (across >= 0) & (across < sh.y)
        block = lax.broadcasted_iota(jnp.int32, along.shape, 0)
        to_block = (inside & (block == (along >> 1) * label_y + (across >> 1))).astype(f32)
        field_ref[3, own, :] = jnp.dot(by_z, to_block, precision=highest, preferred_element_type=f32)
        nodes = to_lanes(nodes_ref[...].astype(f32) + 1.0, select) - 1.0
        lanes_ref[...] = nodes
        line = coarse_sums(sh, nodes, residual, node_count, sums)
        for i, (cell, block) in enumerate(
            (
                (0, 0),
                (sh.y - 1, label_y - 1),
                ((sh.x - 1) * sh.y, (label_x - 1) * label_y),
                (sh.cells - 1, label_x * label_y - 1),
            )
        ):
            for m in range(3):
                lines[8 * i + m : 8 * i + m + 1, :] = natural_ref[m, cell : cell + 1, :]
            lines[8 * i + 3 : 8 * i + 4, 0:label_z] = stiff[block : block + 1, :]
        for i, layer in ((4, EDGE + sh.z - 1), (5, EDGE)):
            for f in range(4):
                lines[8 * i + f : 8 * i + f + 1, :] = field_ref[f, layer : layer + 1, :]
        for i in range(6):
            lines[8 * i + 4 : 8 * i + 5, :] = line
        send_lines(sh, lines, slots_ref)
        pack_xy(sh, SPREAD, field_ref, x_refs, y_refs)

    start_field, nodes, lines, *messages = call(
        begin,
        "begin",
        [(4,) + plane, (sh.z, LANES), (8 * sh.devices, LANES)] + [plane] * (sh.x_links + sh.y_links),
        [natural, phase_labels, phase_moduli, nodes_natural],
        [
            natural.shape,
            pltpu.VMEM(phase_labels.shape, jnp.int32),
            pltpu.SMEM(phase_moduli.shape, f32),
            pltpu.VMEM(nodes_natural.shape, jnp.int32),
            pltpu.SemaphoreType.DMA((4,)),
            (LANES, LANES),
            (label_x * label_y, label_z),
            (48, LANES),
        ],
        remote_ins=True,
    )
    from_y, from_x = send_xy(sh, messages[: sh.x_links], messages[sh.x_links :], diagonal=False)
    lines = to_all(lines)

    def finish_solve(index, v, nodes_ref, coarse, inverse_ref, values, solution_ref, z_refs, ex):
        for m in range(3):
            solution_ref[m] = v[index][m, EDGE : EDGE + sh.rows, :]
        added = coarse_values(sh, nodes_ref[...], coarse, inverse_ref, values)
        valid = nodes_ref[...] >= 0.0
        for m in range(3):
            solution_ref[m, own, :] += pick(valid, added[m])
        pack_z(sh, ex, lambda f, start, count: solution_ref[f, start : start + count, :], z_refs)

    def first_solve(*refs):
        take = Taker(refs)
        field_ref = take.one()
        y_refs, x_refs = take(sh.y_links), take(sh.x_links)
        nodes_ref, lines_ref, inverse_ref = take(3)
        solution_ref, springs_ref = take(2)
        z_refs = take(sh.z_links)
        all_fields, rims, stiff, stiff_rim, v0, v1, kv0, kv1, factor, values, corners = take(11)
        clear_guards(sh, (stiff, stiff_rim, v0, v1, kv0, kv1))
        all_fields[...] = field_ref[...]
        merge_xy(sh, SPREAD, all_fields, rims, 0, y_refs, x_refs)
        merge_lines(sh, lines_ref, all_fields, rims, corners, label_z)
        put(stiff, 0, all_fields[3])
        put(stiff_rim, 0, rims[3])
        springs_ref[6] = all_fields[3]
        springs_ref[7] = rims[3]
        lane, _, _ = sh.lane_grid(1)

        for f, entry in enumerate(own_block(sh, lane, (stiff, stiff_rim))):
            springs_ref[f] = entry
        index = local_solve(sh, all_fields, springs_ref, (v0, v1), (kv0, kv1), factor)
        coarse = lines_ref[pl.ds(4, sh.devices, stride=8), :]
        finish_solve(index, (v0, v1), nodes_ref, coarse, inverse_ref, values, solution_ref, z_refs, DEEP)

    solved, springs, *z_messages = call(
        first_solve,
        "first_solve",
        [fields, (8,) + plane] + z_shape(DEEP),
        [start_field, *from_y, *from_x, nodes, lines, coarse_inverse],
        [(4,) + plane, (4,) + plane, (1, sh.tall, LANES), (1, sh.tall, LANES)]
        + [tall] * 4
        + [fields, (LANES, LANES), (32, LANES)],
    )
    from_z, from_y, from_x = exchange(sh, DEEP, "deep", solved, z_messages)

    def first_image(*refs):
        take = Taker(refs)
        merging = take(1 + sh.z_links + sh.y_links + sh.x_links * (1 + sh.y_links))
        nodes_ref, springs_ref = take(2)
        search_ref, image_ref, slots_ref = take(3)
        v, rim, kv, k_rim, sums = take(5)
        clear_guards(sh, (v, rim, kv, k_rim))
        merge_all(sh, DEEP, Taker(merging), v, rim, EDGE)
        lane, _, _ = sh.lane_grid(1)

        in_grid, in_rim = grid_masks(sh)
        for m in range(3):
            value = pick(in_grid, inner(v, m))
            put(v, m, value)
            search_ref[m] = value
            put(kv, m, springs_ref[6] * value)
            value = pick(in_rim, inner(rim, m))
            put(rim, m, value)
            put(k_rim, m, springs_ref[7] * value)
        image = image_of(sh, lane, v, kv, (rim, k_rim), springs_ref)
        keep = in_grid & extended_mask(sh)
        for m in range(3):
            image_ref[m] = pick(keep, image[m])
        sums[...] = jnp.zeros(sums.shape, f32)
        line = coarse_sums(sh, nodes_ref[...], [image_ref[m, own, :] for m in range(3)], node_count, sums)
        slots_ref[...] = jnp.broadcast_to(line, slots_ref.shape)

    search, image, sums = call(
        first_image,
        "first_image",
        [fields, fields, slots],
        [solved, *from_z, *from_y, *from_x, nodes, springs],
        [tall] * 4 + [(LANES, LANES)],
    )
    coarse = to_all(sums)

    def second_solve(*refs):
        take = Taker(refs)
        image_ref, springs_ref, nodes_ref, coarse_ref, inverse_ref = take(5)
        solution_ref = take.one()
        z_refs = take(sh.z_links)
        v0, v1, kv0, kv1, factor, values = take(6)
        clear_guards(sh, (v0, v1, kv0, kv1))
        index = local_solve(sh, image_ref, springs_ref, (v0, v1), (kv0, kv1), factor)
        finish_solve(index, (v0, v1), nodes_ref, coarse_ref[...], inverse_ref, values, solution_ref, z_refs, NEAR)

    solved, *z_messages = call(
        second_solve,
        "second_solve",
        [fields] + z_shape(NEAR),
        [image, springs, nodes, coarse, coarse_inverse],
        [tall] * 4 + [fields, (LANES, LANES)],
    )
    from_z, from_y, from_x = exchange(sh, NEAR, "near", solved, z_messages)

    def second_image(*refs):
        take = Taker(refs)
        merging = take(1 + sh.z_links + sh.y_links + sh.x_links * (1 + sh.y_links))
        nodes_ref, springs_ref, start_ref, search_ref, first_ref = take(5)
        second_ref, image_ref, slots_ref = take(3)
        v, kv, sums = take(3)
        clear_guards(sh, (v, kv))
        merge_all(sh, NEAR, Taker(merging), v, None, EDGE)
        lane, _, _ = sh.lane_grid(1)

        in_grid, _ = grid_masks(sh)
        for m in range(3):
            value = pick(in_grid, inner(v, m))
            put(v, m, value)
            second_ref[m] = value
            put(kv, m, springs_ref[6] * value)
        image = image_of(sh, lane, v, kv, None, springs_ref)
        for m in range(3):
            image_ref[m] = image[m]
        valid = nodes_ref[...] >= 0.0
        names = ("r", "z", "w", "q", "v")
        sources = (start_ref, search_ref, first_ref, second_ref, image_ref)
        get = {name: [source[m, own, :] for m in range(3)] for name, source in zip(names, sources)}
        sums[...] = jnp.zeros(sums.shape, f32)
        for i, (a, b) in enumerate(("rz", "zw", "rq", "wq", "zv", "qv")):
            product = sum(get[a][m] * get[b][m] for m in range(3))
            sums[i : i + 1, :] = fold_rows(pick(valid, product))
        slots_ref[...] = jnp.broadcast_to(lane_sums(sums)[0:1], slots_ref.shape)

    second, second_image_field, sums = call(
        second_image,
        "second_image",
        [fields, fields, slots],
        [solved, *from_z, *from_y, *from_x, nodes, springs, start_field, search, image],
        [tall] * 2 + [(LANES, LANES)],
    )
    totals = to_all(sums)

    def finish(totals_ref, natural_ref, search_ref, first_ref, second_ref, image_ref, field_ref, residual_ref):
        total = jnp.sum(totals_ref[...], axis=0, keepdims=True)
        rz, zw, rq, wq, zv, qv = [total[:, i : i + 1] for i in range(6)]
        step0 = rz / zw
        rho = rz - step0 * zw - step0 * rq + step0 * step0 * wq
        grow = 1.0 + rho / rz
        curvature = grow * grow * zw - grow * step0 * (zv + wq) + step0 * step0 * qv
        step1 = rho / curvature
        first = step0 + step1 * grow
        second = step0 * step1
        select = selection(sh)
        for m in range(3):
            update = first * search_ref[m, own, :] - second * second_ref[m, own, :]
            field_ref[m] = to_cells(update, select)
            update = first * first_ref[m, own, :] - second * image_ref[m, own, :]
            residual_ref[m] = natural_ref[m] - to_cells(update, select)

    solution_field, residual = call(
        finish,
        "finish",
        [natural.shape, natural.shape],
        [totals, natural, search, image, second, second_image_field],
    )
    return solution_field.reshape(right_side.shape), residual.reshape(right_side.shape)


def solution(mesh):
    in_specs = (
        P(None, "gx", "gy", "gz"),
        P("gx", "gy", "gz"),
        P(),
        P("gx", "gy", "gz"),
        P(("gx", "gy", "gz"), None),
    )
    out_specs = (P(None, "gx", "gy", "gz"), P(None, "gx", "gy", "gz"))
    return jax.shard_map(body, mesh=mesh, in_specs=in_specs, out_specs=out_specs, check_vma=False)
```

```python
import jax
import jax.numpy as jnp
from jax import lax
from jax.experimental import pallas as pl
from jax.experimental.pallas import tpu as pltpu
from jax.sharding import PartitionSpec as P

AXES = ("gx", "gy", "gz")
SWEEPS = 4
relax = 0.6
highest = lax.Precision.HIGHEST
f32 = jnp.float32
LANES = 128
EDGE = 8

ALONG1, ACROSS1 = 0.75, 0.5
ALONG2, ACROSS2, MIXED2 = 0.3125, 0.25, 0.0625
SAME3, MIXED3 = 7.0 / 36.0, 1.0 / 36.0
TOTAL = 2 * ALONG1 + 4 * ACROSS1 + 8 * ALONG2 + 4 * ACROSS2 + 8 * SAME3


class Exchange:
    def __init__(self, fields, layers, up, down):
        self.fields, self.layers, self.up, self.down = fields, layers, up, down


DEEP = Exchange(3, 3, -2, -1)
NEAR = Exchange(3, 2, -1, -1)


class Shape:
    def __init__(self, size_x, size_y, size_z, phases, mesh_sizes):
        self.x, self.y, self.z = size_x, size_y, size_z
        self.pitch = size_y + 4
        self.used = (size_x + 2) * self.pitch
        assert self.used <= LANES
        self.rows = size_z + 2 * EDGE
        self.tall = self.rows + 2 * EDGE
        self.phases = phases
        self.sizes = mesh_sizes
        self.devices = mesh_sizes[0] * mesh_sizes[1] * mesh_sizes[2]
        self.cells = size_x * size_y
        self.links = [1 if n <= 2 else 2 for n in mesh_sizes]
        self.x_links, self.y_links, self.z_links = self.links

    def lane_grid(self, rows):
        lane = lax.broadcasted_iota(jnp.int32, (rows, LANES), 1)
        column = jnp.zeros_like(lane)
        for j in range(1, self.x + 2):
            column = column + (lane >= j * self.pitch).astype(jnp.int32)
        offset = lane - column * self.pitch
        return lane, column - 1, offset - 2

    def here(self, axis):
        return lax.axis_index(AXES[axis])


def shift(value, amount):
    amount = amount % LANES
    return value if amount == 0 else pltpu.roll(value, amount, 1)


def pick(mask, value):
    return jnp.where(mask, value, 0.0)


def scale(flag, value):
    return value * flag.astype(f32)


def pair(links, even, upward, downward):
    first = jnp.where(even, upward, downward)
    return (first,) if links == 1 else (first, jnp.where(even, downward, upward))


def sides(sh, axis, received):
    index, size = sh.here(axis), sh.sizes[axis]
    even = index % 2 == 0
    first = received[0]
    second = received[1] if len(received) > 1 else jnp.zeros_like(first)
    below = jnp.where(even, second, first)
    above = jnp.where(even, first, second)
    return scale(index > 0, below), scale(index < size - 1, above)


def lane_range(lane, start, count):
    return (lane >= start) & (lane < start + count)


def pack_z(sh, ex, source, out_refs):
    even = sh.here(2) % 2 == 0
    zero = jnp.zeros((8 - ex.layers, LANES), f32)
    for f in range(ex.fields):
        upward = source(f, EDGE + sh.z + ex.up, ex.layers)
        downward = source(f, EDGE + ex.down, ex.layers)
        for ref, message in zip(out_refs, pair(sh.z_links, even, upward, downward)):
            ref[8 * f : 8 * f + ex.layers, :] = message
            ref[8 * f + ex.layers : 8 * f + 8, :] = zero


def merge_z(sh, ex, field_ref, received_refs, scratch, guard):
    below, above = sides(sh, 2, [ref[...] for ref in received_refs])
    for f in range(ex.fields):
        scratch[f, guard : guard + sh.rows, :] = field_ref[f]
        low = guard + EDGE + ex.up
        high = guard + EDGE + sh.z + ex.down
        scratch[f, low : low + ex.layers, :] += below[8 * f : 8 * f + ex.layers]
        scratch[f, high : high + ex.layers, :] += above[8 * f : 8 * f + ex.layers]


def fold(sh, value, layers, start=None):
    folds = sh.pitch // layers
    height = -(-sh.rows // (8 * folds)) * 8
    lane, _, across = sh.lane_grid(1)
    total = jnp.zeros((height, LANES), f32)
    for i, first in enumerate(range(0, sh.rows, height)):
        part = value[first : first + height]
        if start is not None:
            part = pick((lane < sh.used) & lane_range(across, start, layers), part)
        part = shift(part, i * layers - (0 if start is None else start + 2))
        if part.shape[0] < height:
            part = jnp.concatenate([part, jnp.zeros((height - part.shape[0], LANES), f32)], axis=0)
        total = total + part
    return total


def folded_shape(sh, layers):
    return (-(-sh.rows // (8 * (sh.pitch // layers))) * 8, LANES)


def unfold(sh, message, layers, start):
    height = message.shape[0]
    lane, _, across = sh.lane_grid(1)
    mask = (lane < sh.used) & lane_range(across, start, layers)
    parts = []
    for i, first in enumerate(range(0, sh.rows, height)):
        part = message[0 : min(height, sh.rows - first)]
        parts.append(pick(mask, shift(part, start + 2 - i * layers)))
    return jnp.concatenate(parts, axis=0) if len(parts) > 1 else parts[0]


def pack_xy(sh, ex, scratch, x_refs, y_refs, corner_refs):
    rows = sh.rows
    lane, _, across = sh.lane_grid(1)
    even_x, even_y = sh.here(0) % 2 == 0, sh.here(1) % 2 == 0
    span = ex.layers * sh.pitch
    x_up = x_down = y_up = y_down = jnp.zeros((rows, LANES), f32)
    inside = lane < sh.used
    y_above, y_below = sh.y + ex.up, ex.down
    for f in range(ex.fields):
        value = scratch[f]
        start = (sh.x + ex.up + 1) * sh.pitch
        x_up = x_up + shift(pick(lane_range(lane, start, span), value), f * span - start)
        start = (ex.down + 1) * sh.pitch
        x_down = x_down + shift(pick(lane_range(lane, start, span), value), f * span - start)
        mask = inside & lane_range(across, y_above, ex.layers)
        y_up = y_up + shift(pick(mask, value), f * ex.layers - y_above - 2)
        mask = inside & lane_range(across, y_below, ex.layers)
        y_down = y_down + shift(pick(mask, value), f * ex.layers - y_below - 2)
    packed = ex.fields * ex.layers
    y_up, y_down = fold(sh, y_up, packed), fold(sh, y_down, packed)
    for ref, message in zip(y_refs, pair(sh.y_links, even_y, y_up, y_down)):
        ref[...] = message
    for i, message in enumerate(pair(sh.x_links, even_x, x_up, x_down)):
        x_refs[i][...] = message
        upward, downward = fold(sh, message, ex.layers, y_above), fold(sh, message, ex.layers, y_below)
        for j, corner in enumerate(pair(sh.y_links, even_y, upward, downward)):
            corner_refs[i * sh.y_links + j][...] = corner


def merge_xy(sh, ex, scratch, rim, guard, y_refs, x_refs):
    lane, _, across = sh.lane_grid(1)
    inside = lane < sh.used
    low_mask = inside & lane_range(across, ex.up, ex.layers)
    high_mask = inside & lane_range(across, sh.y + ex.down, ex.layers)
    span = ex.layers * sh.pitch
    packed = ex.fields * ex.layers
    below_y, above_y = [unfold(sh, value, packed, -2) for value in sides(sh, 1, [ref[...] for ref in y_refs])]
    per_link = 1 + sh.y_links
    sums = []
    for link in range(sh.x_links):
        straight, diagonal = x_refs[link * per_link], x_refs[link * per_link + 1 : (link + 1) * per_link]
        total = straight[...]
        below, above = sides(sh, 1, [ref[...] for ref in diagonal])
        total = total + unfold(sh, below, ex.layers, ex.up)
        sums.append(total + unfold(sh, above, ex.layers, sh.y + ex.down))
    below_x, above_x = sides(sh, 0, sums)
    first = 1 if ex.up == -2 else 0
    last = ex.layers - 1 if ex.down + ex.layers == 2 else ex.layers
    for f in range(ex.fields):
        addend = pick(low_mask, shift(below_y, ex.up + 2 - ex.layers * f))
        addend = addend + pick(high_mask, shift(above_y, sh.y + ex.down + 2 - ex.layers * f))
        start = (ex.up + first + 1) * sh.pitch
        count = (ex.layers - first) * sh.pitch
        moved = shift(below_x, start - f * span - first * sh.pitch)
        addend = addend + pick(lane_range(lane, start, count), moved)
        start = (sh.x + ex.down + 1) * sh.pitch
        moved = shift(above_x, start - f * span)
        addend = addend + pick(lane_range(lane, start, last * sh.pitch), moved)
        scratch[f, guard : guard + sh.rows, :] += addend
        if rim is not None:
            low = pick(lane_range(lane, 0, sh.pitch), shift(below_x, -f * span))
            start = (sh.x + 1) * sh.pitch
            moved = shift(above_x, start - f * span - last * sh.pitch)
            high = pick(lane_range(lane, start, sh.pitch), moved)
            rim[f, guard : guard + sh.rows, :] = low + high


def clear_guards(sh, refs):
    for ref in refs:
        for f in range(ref.shape[0]):
            ref[f, :EDGE, :] = jnp.zeros((EDGE, LANES), f32)
            ref[f, sh.tall - EDGE :, :] = jnp.zeros((EDGE, LANES), f32)


def inner(ref, f):
    return ref[f, EDGE : ref.shape[1] - EDGE, :]


def z_stage(ref, f):
    end = ref.shape[1] - EDGE
    after = ref[f, EDGE + 1 : end + 1, :]
    before = ref[f, EDGE - 1 : end - 1, :]
    return inner(ref, f), before + after, after - before


def y_stage(value):
    after, before = shift(value, -1), shift(value, 1)
    return before + after, after - before


def yz_parts(ref):
    a, a_sum, a_dif = z_stage(ref, 0)
    b, b_sum, b_dif = z_stage(ref, 1)
    c, c_sum, c_dif = z_stage(ref, 2)
    pa, ma = y_stage(a)
    pas, mas = y_stage(a_sum)
    pad, _ = y_stage(a_dif)
    pb, mb = y_stage(b)
    pbs, mbs = y_stage(b_sum)
    _, mbd = y_stage(b_dif)
    pc, _ = y_stage(c)
    pcs, _ = y_stage(c_sum)
    pcd, mcd = y_stage(c_dif)
    own_x = ACROSS1 * (pa + a_sum) + ACROSS2 * pas
    even_x = ALONG1 * a + ALONG2 * (pa + a_sum) + SAME3 * pas
    odd_x = MIXED2 * (mb + c_dif) + MIXED3 * (mbs + pcd)
    own_y = ALONG1 * pb + ACROSS1 * b_sum + ALONG2 * pbs + MIXED2 * mcd
    even_y = ACROSS1 * b + ALONG2 * pb + ACROSS2 * b_sum + SAME3 * pbs + MIXED3 * mcd
    odd_y = MIXED2 * ma + MIXED3 * mas
    own_z = ALONG1 * c_sum + ACROSS1 * pc + ALONG2 * pcs + MIXED2 * mbd
    even_z = ACROSS1 * c + ACROSS2 * pc + ALONG2 * c_sum + SAME3 * pcs + MIXED3 * mbd
    odd_z = MIXED2 * a_dif + MIXED3 * pad
    return (own_x, even_x, odd_x), (own_y, even_y, odd_y), (own_z, even_z, odd_z)


def x_stage(sh, lane, own, plus, minus, rim_plus, rim_minus):
    after, before = shift(plus, -sh.pitch), shift(minus, sh.pitch)
    last = (sh.x + 1) * sh.pitch
    if rim_plus is None:
        return own + pick(lane < last, after) + pick(lane >= sh.pitch, before)
    return own + jnp.where(lane < last, after, rim_plus) + jnp.where(lane >= sh.pitch, before, rim_minus)


def stencil(sh, lane, ref, rim):
    parts = yz_parts(ref)
    rims = yz_parts(rim) if rim is not None else [None] * 3
    out = []
    for (own, even, odd), rim_part in zip(parts, rims):
        if rim_part is None:
            out.append(x_stage(sh, lane, own, even + odd, even - odd, None, None))
        else:
            _, rim_even, rim_odd = rim_part
            out.append(
                x_stage(sh, lane, own, even + odd, even - odd, rim_even + rim_odd, rim_even - rim_odd)
            )
    return out


def spring_parts(ref):
    k, k_sum, k_dif = z_stage(ref, 0)
    pk, mk = y_stage(k)
    pks, mks = y_stage(k_sum)
    pkd, mkd = y_stage(k_dif)
    zero = jnp.zeros_like(k)
    xx = (ACROSS1 * (pk + k_sum) + ACROSS2 * pks, ALONG1 * k + ALONG2 * (pk + k_sum) + SAME3 * pks, zero)
    yy = (
        ALONG1 * pk + ACROSS1 * k_sum + ALONG2 * pks,
        ACROSS1 * k + ALONG2 * pk + ACROSS2 * k_sum + SAME3 * pks,
        zero,
    )
    zz = (
        ALONG1 * k_sum + ACROSS1 * pk + ALONG2 * pks,
        ACROSS1 * k + ACROSS2 * pk + ALONG2 * k_sum + SAME3 * pks,
        zero,
    )
    xy = (zero, zero, MIXED2 * mk + MIXED3 * mks)
    xz = (zero, zero, MIXED2 * k_dif + MIXED3 * pkd)
    yz = (MIXED2 * mkd, MIXED3 * mkd, zero)
    return xx, yy, zz, xy, xz, yz


def own_block(sh, lane, springs):
    main, rim = springs
    k = inner(main, 0)
    out = []
    for index, ((own, even, odd), (_, rim_even, rim_odd)) in enumerate(
        zip(spring_parts(main), spring_parts(rim))
    ):
        total = x_stage(sh, lane, own, even + odd, even - odd, rim_even + rim_odd, rim_even - rim_odd)
        out.append(total + TOTAL * k if index < 3 else total)
    return out


def apply_block(d, v):
    return (
        d[0] * v[0] + d[3] * v[1] + d[4] * v[2],
        d[3] * v[0] + d[1] * v[1] + d[5] * v[2],
        d[4] * v[0] + d[5] * v[1] + d[2] * v[2],
    )


def image_of(sh, lane, v, kv, rims, springs_ref):
    outer = stencil(sh, lane, v, rims and rims[0])
    scaled = stencil(sh, lane, kv, rims and rims[1])
    own = apply_block([springs_ref[f] for f in range(6)], [inner(v, m) for m in range(3)])
    return [own[m] - (springs_ref[6] * outer[m] + scaled[m]) for m in range(3)]


def level(sh):
    return lax.broadcasted_iota(jnp.int32, (sh.rows, LANES), 0) - EDGE


def extended_mask(sh):
    lane, _, across = sh.lane_grid(1)
    z = level(sh)
    return ((lane < sh.used) & (across >= -1) & (across <= sh.y)) & ((z >= -1) & (z <= sh.z))


def within(sh, axis, place, size):
    index = sh.here(axis)
    low = jnp.where(index > 0, -EDGE, 0)
    high = jnp.where(index < sh.sizes[axis] - 1, size + EDGE, size)
    return (place >= low) & (place < high)


def grid_masks(sh):
    lane, along, across = sh.lane_grid(1)
    lanes = (lane < sh.used) & within(sh, 1, across, sh.y)
    rows = within(sh, 2, level(sh), sh.z)
    return (lanes & within(sh, 0, along, sh.x)) & rows, lanes & rows


def put(ref, f, value):
    ref[f, EDGE : ref.shape[1] - EDGE, :] = value


def local_solve(sh, residual_ref, springs_ref, v, kv, factor):
    lane, _, _ = sh.lane_grid(1)
    mask = extended_mask(sh)
    for m in range(3):
        factor[m] = pick(mask, relax / jnp.where(mask, springs_ref[m], 1.0))
        z = residual_ref[m] * factor[m]
        put(v[0], m, z)
        put(kv[0], m, springs_ref[6] * z)
    for sweep in range(SWEEPS - 1):
        old, new = sweep % 2, (sweep + 1) % 2
        image = image_of(sh, lane, v[old], kv[old], None, springs_ref)
        for m in range(3):
            z = inner(v[old], m) + factor[m] * (residual_ref[m] - image[m])
            put(v[new], m, z)
            put(kv[new], m, springs_ref[6] * z)
    return (SWEEPS - 1) % 2


def coords(sh):
    lane, along, across = sh.lane_grid(sh.z)
    z = lax.broadcasted_iota(jnp.int32, (sh.z, LANES), 0)
    place = lambda index, size: (2 * index + 1).astype(f32) / size - 1.0
    return place(along, sh.x), place(across, sh.y), place(z, sh.z)


def cross(a, b):
    return (a[1] * b[2] - a[2] * b[1], a[2] * b[0] - a[0] * b[2], a[0] * b[1] - a[1] * b[0])


def fold_rows(value):
    total = value[0:8]
    for i in range(8, value.shape[0], 8):
        total = total + value[i : i + 8]
    return jnp.sum(total, axis=0, keepdims=True)


def lane_sums(rows_ref):
    ones = jnp.ones((8, LANES), f32)
    return lax.dot_general(
        ones, rows_ref[...], (((1,), (1,)), ((), ())), precision=highest, preferred_element_type=f32
    )


def coarse_sums(sh, nodes, field, count, sums):
    moments = tuple(field) + cross(coords(sh), field)
    for node in range(count):
        mask = nodes == float(node)
        for m in range(6):
            sums[node * 6 + m : node * 6 + m + 1, :] = fold_rows(pick(mask, moments[m]))
    flat = (sh.here(0) * sh.sizes[1] + sh.here(1)) * sh.sizes[2] + sh.here(2)
    return pltpu.roll(lane_sums(sums), lax.rem(flat * (6 * count), LANES), 1)[0:1]


def coarse_values(sh, nodes, received, inverse_ref, values):
    unknowns, total = inverse_ref.shape
    row = lax.broadcasted_iota(jnp.int32, received.shape, 0)
    part = jnp.zeros((unknowns, LANES), f32)
    for i in range(0, total, LANES):
        owner = (i + lax.broadcasted_iota(jnp.int32, (1, LANES), 1)) // unknowns
        vector = jnp.sum(pick(row == owner, received), axis=0, keepdims=True)
        part = part + inverse_ref[:, i : i + LANES] * vector
    values[0:unknowns, :] = jnp.dot(
        part, jnp.ones((LANES, LANES), f32), precision=highest, preferred_element_type=f32
    )
    cells = []
    for m in range(6):
        cell = jnp.zeros((sh.z, LANES), f32)
        for node in range(unknowns // 6):
            cell = jnp.where(nodes == float(node), values[node * 6 + m : node * 6 + m + 1, :], cell)
        cells.append(cell)
    turned = cross(cells[3:], coords(sh))
    return [cells[m] + turned[m] for m in range(3)]


def selection(sh):
    lane, along, across = sh.lane_grid(sh.cells)
    inside = (along >= 0) & (along < sh.x) & (across >= 0) & (across < sh.y)
    row = lax.broadcasted_iota(jnp.int32, (sh.cells, LANES), 0)
    return (inside & (row == along * sh.y + across)).astype(f32)


def to_lanes(value, select):
    return lax.dot_general(
        value, select, (((0,), (0,)), ((), ())), precision=highest, preferred_element_type=f32
    )


def to_cells(value, select):
    return lax.dot_general(
        select, value, (((1,), (1,)), ((), ())), precision=highest, preferred_element_type=f32
    )


def send_lines(sh, lines, slots_ref):
    here = [sh.here(axis) for axis in range(3)]
    corner = [lines[8 * i : 8 * i + 8, :] for i in range(4)]
    top, bottom = lines[32:40, :], lines[40:48, :]
    for x in range(sh.sizes[0]):
        low_high = [jnp.where(x > here[0], corner[2 + high], corner[high]) for high in range(2)]
        for y in range(sh.sizes[1]):
            column = jnp.where(y > here[1], low_high[1], low_high[0])
            for z in range(sh.sizes[2]):
                slot = jnp.where(z == here[2] + 1, top, jnp.where(z == here[2] - 1, bottom, column))
                place = 8 * ((x * sh.sizes[1] + y) * sh.sizes[2] + z)
                slots_ref[place : place + 8, :] = slot


def slot_from(sh, received_ref, step):
    place, exists = 0, None
    for axis in range(3):
        index = sh.here(axis) + step[axis]
        inside = (index >= 0) & (index < sh.sizes[axis])
        exists = inside if exists is None else exists & inside
        place = place * sh.sizes[axis] + jnp.clip(index, 0, sh.sizes[axis] - 1)
    return scale(exists, received_ref[pl.ds(pl.multiple_of(place * 8, 8), 8), :])


def repeat_twice(count):
    row = lax.broadcasted_iota(jnp.int32, (2 * count, count), 0)
    column = lax.broadcasted_iota(jnp.int32, (2 * count, count), 1)
    return ((row >= 2 * column) & (row < 2 * column + 2)).astype(f32)


def ring(size_x, size_y, rows):
    row = lax.broadcasted_iota(jnp.int32, (rows, LANES), 0)
    sides_x, both = 2 * size_y, 2 * size_y + 2 * size_x
    corner = row - both
    x = jnp.where(row < size_y, -1, size_x)
    x = jnp.where(row < sides_x, x, jnp.where(row < sides_x + size_x, row - sides_x, row - sides_x - size_x))
    x = jnp.where(row < both, x, jnp.where(corner < 2, -1, size_x))
    y = jnp.where(row < size_y, row, row - size_y)
    y = jnp.where(row < sides_x, y, jnp.where(row < sides_x + size_x, -1, size_y))
    y = jnp.where(row < both, y, jnp.where((corner == 0) | (corner == 2), -1, size_y))
    return x, y, (row < sides_x) | (row >= both), row < both + 4


def face_shape(sh, label_x, label_y):
    rows = max(3 * sh.x + label_x, 3 * sh.y + label_y)
    return (-(-rows // 8) * 8, LANES)


def pack_faces(sh, natural_ref, stiff, label_x, label_y, x_refs, y_refs):
    even_x, even_y = sh.here(0) % 2 == 0, sh.here(1) % 2 == 0

    def face(at, count, stride, label_at, label_count, label_stride):
        rows = [natural_ref[m, pl.ds(at, count, stride=stride), :] for m in range(3)]
        return rows, stiff[pl.ds(label_at, label_count, stride=label_stride), :]

    above = face(sh.cells - sh.y, sh.y, 1, (label_x - 1) * label_y, label_y, 1)
    below = face(0, sh.y, 1, 0, label_y, 1)
    for refs, links, even, above, below in (
        (x_refs, sh.x_links, even_x, above, below),
        (
            y_refs,
            sh.y_links,
            even_y,
            face(sh.y - 1, sh.x, sh.y, label_y - 1, label_x, label_y),
            face(0, sh.x, sh.y, 0, label_x, label_y),
        ),
    ):
        for i, ref in enumerate(refs):
            ref[...] = jnp.zeros(ref.shape, f32)
            count = above[0][0].shape[0]
            for m in range(3):
                ref[m * count : (m + 1) * count, :] = pair(links, even, above[0][m], below[0][m])[i]
            labels, length = above[1].shape
            ref[3 * count : 3 * count + labels, 0:length] = pair(links, even, above[1], below[1])[i]


def merge_start(sh, refs, x_refs, y_refs, received_ref, sizes, cells, labels):
    residual, stiff, stiff_rim = refs
    label_x, label_y, label_z = sizes
    lane, along, across = sh.lane_grid(1)
    inside = lane < sh.used
    last = (sh.x + 1) * sh.pitch
    x_mask = {-1: lane < sh.pitch, 0: (lane >= sh.pitch) & (lane < last), 1: (lane >= last) & inside}
    y_mask = {-1: across < 0, 0: (across >= 0) & (across < sh.y), 1: across >= sh.y}
    cells[...] = jnp.zeros(cells.shape, f32)
    labels[...] = jnp.zeros(labels.shape, f32)
    count, label_count = cells.shape[1], labels.shape[0]
    at = label_at = 0
    for axis, face_refs, size, label_size in ((0, x_refs, sh.y, label_y), (1, y_refs, sh.x, label_x)):
        for message in sides(sh, axis, [ref[...] for ref in face_refs]):
            for m in range(3):
                cells[m, at : at + size, :] = message[m * size : (m + 1) * size]
            labels[label_at : label_at + label_size, :] = message[3 * size : 3 * size + label_size, 0:label_z]
            at, label_at = at + size, label_at + label_size
    for dx, dy in ((-1, -1), (-1, 1), (1, -1), (1, 1)):
        slot = slot_from(sh, received_ref, (dx, dy, 0))
        for m in range(3):
            cells[m, at : at + 1, :] = slot[m : m + 1]
        labels[label_at : label_at + 1, :] = slot[3:4, 0:label_z]
        at, label_at = at + 1, label_at + 1
    x, y, _, valid = ring(sh.x, sh.y, count)
    place = (valid & inside & (along == x) & (across == y)).astype(f32)
    own = slice(EDGE, EDGE + sh.z)
    tall_own = slice(2 * EDGE, 2 * EDGE + sh.z)
    for m in range(3):
        residual[m, own, :] += to_lanes(cells[m], place)
    by_z = lax.dot_general(
        repeat_twice(label_z), labels[...], (((1,), (1,)), ((), ())), precision=highest, preferred_element_type=f32
    )
    x, y, at_x, valid = ring(label_x, label_y, label_count)
    match = valid & inside & ((along >> 1) == x) & ((across >> 1) == y)
    columns = jnp.dot(by_z, (match & at_x).astype(f32), precision=highest, preferred_element_type=f32)
    stiff_rim[0, tall_own, :] = columns
    columns = columns + jnp.dot(by_z, (match & ~at_x).astype(f32), precision=highest, preferred_element_type=f32)
    stiff[0, tall_own, :] += columns
    for dz in (-1, 1):
        main = edge = jnp.zeros((8, LANES), f32)
        for dx in (-1, 0, 1):
            for dy in (-1, 0, 1):
                slot = slot_from(sh, received_ref, (dx, dy, dz))
                mask = x_mask[dx] & y_mask[dy]
                main = main + pick(mask, shift(slot, dx * sh.x * sh.pitch + dy * sh.y))
                if dx:
                    edge = edge + pick(mask, shift(slot, dx * (sh.x - 1) * sh.pitch + dy * sh.y))
        near = EDGE + sh.z if dz > 0 else EDGE - 1
        for m in range(3):
            residual[m, near : near + 1, :] = main[m : m + 1]
        for row in (EDGE + near, EDGE + near + dz):
            stiff[0, row : row + 1, :] = main[3:4]
            stiff_rim[0, row : row + 1, :] = edge[3:4]


def call(kernel, name, outs, ins, scratch=(), remote_ins=False):
    space = pltpu.HBM if remote_ins else pltpu.VMEM
    return pl.pallas_call(
        kernel,
        out_shape=[jax.ShapeDtypeStruct(shape, f32) for shape in outs],
        in_specs=[pl.BlockSpec(memory_space=space) for _ in ins],
        out_specs=[pl.BlockSpec(memory_space=pltpu.VMEM) for _ in outs],
        scratch_shapes=[pltpu.VMEM(shape, f32) if isinstance(shape, tuple) else shape for shape in scratch],
        compiler_params=pltpu.CompilerParams(vmem_limit_bytes=48 * 1024 * 1024),
        name=name,
    )(*ins)


def permutation(sizes, moves):
    def partner(axis, link, index):
        size = sizes[axis]
        other = index ^ 1 if link == 0 else index + (1 if index % 2 else -1)
        if 0 <= other < size:
            return other
        return size - 1 - index if axis == 2 and size % 2 == 0 else index

    pairs = []
    for x in range(sizes[0]):
        for y in range(sizes[1]):
            for z in range(sizes[2]):
                place = [x, y, z]
                goal = [partner(a, moves[a], place[a]) if a in moves else place[a] for a in range(3)]
                if goal == place and 0 not in moves and sizes[0] % 2 == 0:
                    goal[0] = partner(0, 0, x)
                flat = [(p[0] * sizes[1] + p[1]) * sizes[2] + p[2] for p in (place, goal)]
                pairs.append(tuple(flat))
    return pairs


def send(sh, value, moves):
    return lax.ppermute(value, AXES, permutation(sh.sizes, moves))


def send_z(sh, messages):
    return [send(sh, message, {2: link}) for link, message in enumerate(messages)]


def send_faces(sh, x_messages, y_messages):
    from_y = [send(sh, message, {1: link}) for link, message in enumerate(y_messages)]
    from_x = [send(sh, message, {0: link}) for link, message in enumerate(x_messages)]
    return from_y, from_x


def to_all(slots):
    return lax.all_to_all(slots, AXES, 0, 0, tiled=True)


def exchange(sh, ex, name, field, z_messages):
    from_z = send_z(sh, z_messages)

    corners = sh.x_links * sh.y_links

    def packer(*refs):
        take = Taker(refs)
        field_ref, z_refs = take.one(), take(sh.z_links)
        x_refs, y_refs, corner_refs, scratch = take(sh.x_links), take(sh.y_links), take(corners), take.one()
        merge_z(sh, ex, field_ref, z_refs, scratch, 0)
        pack_xy(sh, ex, scratch, x_refs, y_refs, corner_refs)

    plane = (sh.rows, LANES)
    messages = call(
        packer,
        name,
        [plane] * sh.x_links
        + [folded_shape(sh, ex.fields * ex.layers)] * sh.y_links
        + [folded_shape(sh, ex.layers)] * corners,
        [field] + from_z,
        [(ex.fields,) + plane],
    )
    take = Taker(messages)
    x_messages, y_messages = take(sh.x_links), take(sh.y_links)
    from_y, straight = send_faces(sh, x_messages, y_messages)
    from_x = []
    for link in range(sh.x_links):
        from_x.append(straight[link])
        from_x.extend(send(sh, take.one(), {0: link, 1: other}) for other in range(sh.y_links))
    return from_z, from_y, from_x


class Taker:
    def __init__(self, refs):
        self.refs, self.at = refs, 0

    def __call__(self, count):
        self.at += count
        return self.refs[self.at - count : self.at]

    def one(self):
        return self(1)[0]


def merge_all(sh, ex, take, scratch, rim, guard):
    field = take.one()
    from_z, from_y = take(sh.z_links), take(sh.y_links)
    from_x = take(sh.x_links * (1 + sh.y_links))
    merge_z(sh, ex, field, from_z, scratch, guard)
    merge_xy(sh, ex, scratch, rim, guard, from_y, from_x)


def body(right_side, phase_labels, phase_moduli, coarse_nodes, coarse_inverse):
    sizes = tuple(lax.axis_size(axis) for axis in AXES)
    _, size_x, size_y, size_z = right_side.shape
    sh = Shape(size_x, size_y, size_z, phase_moduli.shape[0], sizes)
    unknowns = coarse_inverse.shape[0]
    node_count = unknowns // 6
    sum_rows = -(-unknowns // 8) * 8
    own = slice(EDGE, EDGE + sh.z)
    plane = (sh.rows, LANES)
    fields = (3,) + plane
    tall = (3, sh.tall, LANES)
    slots = (sh.devices, LANES)
    z_shape = lambda ex: [(8 * ex.fields, LANES)] * sh.z_links
    natural = right_side.reshape(3, sh.cells, sh.z)
    nodes_natural = coarse_nodes.reshape(sh.cells, sh.z)
    label_x, label_y, label_z = phase_labels.shape

    def begin(natural_in, labels_in, moduli_in, nodes_in, field_ref, lanes_ref, slots_ref, *rest):
        x_refs, y_refs = rest[: sh.x_links], rest[sh.x_links : sh.x_links + sh.y_links]
        natural_ref, labels_ref, moduli_ref, nodes_ref, sems, sums, stiff, lines = rest[sh.x_links + sh.y_links :]
        pairs = ((natural_in, natural_ref), (labels_in, labels_ref), (moduli_in, moduli_ref), (nodes_in, nodes_ref))
        copies = [pltpu.make_async_copy(a, b, sems.at[i]) for i, (a, b) in enumerate(pairs)]
        for copy in copies:
            copy.start()
        select = selection(sh)
        field_ref[...] = jnp.zeros(field_ref.shape, f32)
        sums[...] = jnp.zeros(sums.shape, f32)
        lines[...] = jnp.zeros(lines.shape, f32)
        for copy in copies:
            copy.wait()
        residual = []
        for m in range(3):
            residual.append(to_lanes(natural_ref[m], select))
            field_ref[m, own, :] = residual[m]
        for i in range(label_x):
            labels = labels_ref[i]
            moduli = jnp.zeros(labels.shape, f32)
            for phase in range(sh.phases):
                moduli = jnp.where(labels == phase, moduli_ref[phase], moduli)
            stiff[i * label_y : (i + 1) * label_y, :] = moduli
        by_z = lax.dot_general(
            repeat_twice(label_z), stiff[...], (((1,), (1,)), ((), ())), precision=highest, preferred_element_type=f32
        )
        lane, along, across = sh.lane_grid(label_x * label_y)
        inside = (along >= 0) & (along < sh.x) & (across >= 0) & (across < sh.y)
        block = lax.broadcasted_iota(jnp.int32, along.shape, 0)
        to_block = (inside & (block == (along >> 1) * label_y + (across >> 1))).astype(f32)
        field_ref[3, own, :] = jnp.dot(by_z, to_block, precision=highest, preferred_element_type=f32)
        nodes = to_lanes(nodes_ref[...].astype(f32) + 1.0, select) - 1.0
        lanes_ref[...] = nodes
        line = coarse_sums(sh, nodes, residual, node_count, sums)
        for i, (cell, block) in enumerate(
            (
                (0, 0),
                (sh.y - 1, label_y - 1),
                ((sh.x - 1) * sh.y, (label_x - 1) * label_y),
                (sh.cells - 1, label_x * label_y - 1),
            )
        ):
            for m in range(3):
                lines[8 * i + m : 8 * i + m + 1, :] = natural_ref[m, cell : cell + 1, :]
            lines[8 * i + 3 : 8 * i + 4, 0:label_z] = stiff[block : block + 1, :]
        for i, layer in ((4, EDGE + sh.z - 1), (5, EDGE)):
            for f in range(4):
                lines[8 * i + f : 8 * i + f + 1, :] = field_ref[f, layer : layer + 1, :]
        for i in range(6):
            lines[8 * i + 4 : 8 * i + 5, :] = line
        send_lines(sh, lines, slots_ref)
        pack_faces(sh, natural_ref, stiff, label_x, label_y, x_refs, y_refs)

    start_field, nodes, lines, *messages = call(
        begin,
        "begin",
        [(4,) + plane, (sh.z, LANES), (8 * sh.devices, LANES)]
        + [face_shape(sh, label_x, label_y)] * (sh.x_links + sh.y_links),
        [natural, phase_labels, phase_moduli, nodes_natural],
        [
            natural.shape,
            pltpu.VMEM(phase_labels.shape, jnp.int32),
            pltpu.SMEM(phase_moduli.shape, f32),
            pltpu.VMEM(nodes_natural.shape, jnp.int32),
            pltpu.SemaphoreType.DMA((4,)),
            (LANES, LANES),
            (label_x * label_y, label_z),
            (48, LANES),
        ],
        remote_ins=True,
    )
    from_y, from_x = send_faces(sh, messages[: sh.x_links], messages[sh.x_links :])
    lines = to_all(lines)

    def add_coarse(nodes_ref, coarse, inverse_ref, values, solution_ref, z_refs, ex):
        added = coarse_values(sh, nodes_ref[...], coarse, inverse_ref, values)
        valid = nodes_ref[...] >= 0.0
        for m in range(3):
            solution_ref[m, own, :] += pick(valid, added[m])
        pack_z(sh, ex, lambda f, start, count: solution_ref[f, start : start + count, :], z_refs)

    def first_solve(*refs):
        take = Taker(refs)
        field_ref = take.one()
        y_refs, x_refs = take(sh.y_links), take(sh.x_links)
        nodes_ref, lines_ref, inverse_ref = take(3)
        solution_ref, springs_ref = take(2)
        z_refs = take(sh.z_links)
        residual, stiff, stiff_rim, v0, v1, kv0, kv1, factor, values, cells, labels = take(11)
        clear_guards(sh, (stiff, stiff_rim, v0, v1, kv0, kv1))
        residual[...] = field_ref[0:3]
        put(stiff, 0, field_ref[3])
        put(stiff_rim, 0, jnp.zeros(plane, f32))
        sizes = phase_labels.shape
        merge_start(sh, (residual, stiff, stiff_rim), x_refs, y_refs, lines_ref, sizes, cells, labels)
        springs_ref[6] = inner(stiff, 0)
        springs_ref[7] = inner(stiff_rim, 0)
        lane, _, _ = sh.lane_grid(1)
        for f, entry in enumerate(own_block(sh, lane, (stiff, stiff_rim))):
            springs_ref[f] = entry
        index = local_solve(sh, residual, springs_ref, (v0, v1), (kv0, kv1), factor)
        coarse = lines_ref[pl.ds(4, sh.devices, stride=8), :]
        for m in range(3):
            solution_ref[m] = inner((v0, v1)[index], m)
        add_coarse(nodes_ref, coarse, inverse_ref, values, solution_ref, z_refs, DEEP)

    solved, springs, *z_messages = call(
        first_solve,
        "first_solve",
        [fields, (8,) + plane] + z_shape(DEEP),
        [start_field, *from_y, *from_x, nodes, lines, coarse_inverse],
        [fields, (1, sh.tall, LANES), (1, sh.tall, LANES)]
        + [tall] * 4
        + [fields, (LANES, LANES)]
        + [
            (3, 8 * -(-(2 * sh.x + 2 * sh.y + 4) // 8), LANES),
            (8 * -(-(2 * label_x + 2 * label_y + 4) // 8), label_z),
        ],
    )
    from_z, from_y, from_x = exchange(sh, DEEP, "deep", solved, z_messages)

    def first_image(*refs):
        take = Taker(refs)
        merging = take(1 + sh.z_links + sh.y_links + sh.x_links * (1 + sh.y_links))
        nodes_ref, springs_ref = take(2)
        search_ref, image_ref, slots_ref = take(3)
        v, rim, kv, k_rim, sums = take(5)
        clear_guards(sh, (v, rim, kv, k_rim))
        merge_all(sh, DEEP, Taker(merging), v, rim, EDGE)
        lane, _, _ = sh.lane_grid(1)

        in_grid, in_rim = grid_masks(sh)
        for m in range(3):
            value = pick(in_grid, inner(v, m))
            put(v, m, value)
            search_ref[m] = value
            put(kv, m, springs_ref[6] * value)
            value = pick(in_rim, inner(rim, m))
            put(rim, m, value)
            put(k_rim, m, springs_ref[7] * value)
        image = image_of(sh, lane, v, kv, (rim, k_rim), springs_ref)
        keep = in_grid & extended_mask(sh)
        for m in range(3):
            image_ref[m] = pick(keep, image[m])
        sums[...] = jnp.zeros(sums.shape, f32)
        line = coarse_sums(sh, nodes_ref[...], [image_ref[m, own, :] for m in range(3)], node_count, sums)
        slots_ref[...] = jnp.broadcast_to(line, slots_ref.shape)

    search, image, sums = call(
        first_image,
        "first_image",
        [fields, fields, slots],
        [solved, *from_z, *from_y, *from_x, nodes, springs],
        [tall] * 4 + [(LANES, LANES)],
    )
    coarse = to_all(sums)

    def second_solve(image_ref, springs_ref, local_ref, v0, v1, kv0, kv1, factor):
        clear_guards(sh, (v0, v1, kv0, kv1))
        index = local_solve(sh, image_ref, springs_ref, (v0, v1), (kv0, kv1), factor)
        for m in range(3):
            local_ref[m] = inner((v0, v1)[index], m)

    (local,) = call(second_solve, "second_solve", [fields], [image, springs], [tall] * 4 + [fields])

    def second_add(local_ref, nodes_ref, coarse_ref, inverse_ref, *rest):
        solution_ref, z_refs, values = rest[0], rest[1:-1], rest[-1]
        solution_ref[...] = local_ref[...]
        add_coarse(nodes_ref, coarse_ref[...], inverse_ref, values, solution_ref, z_refs, NEAR)

    solved, *z_messages = call(
        second_add,
        "second_add",
        [fields] + z_shape(NEAR),
        [local, nodes, coarse, coarse_inverse],
        [(LANES, LANES)],
    )
    from_z, from_y, from_x = exchange(sh, NEAR, "near", solved, z_messages)

    def second_image(*refs):
        take = Taker(refs)
        merging = take(1 + sh.z_links + sh.y_links + sh.x_links * (1 + sh.y_links))
        nodes_ref, springs_ref, start_ref, search_ref, first_ref = take(5)
        second_ref, image_ref, slots_ref = take(3)
        v, kv, sums = take(3)
        clear_guards(sh, (v, kv))
        merge_all(sh, NEAR, Taker(merging), v, None, EDGE)
        lane, _, _ = sh.lane_grid(1)

        in_grid, _ = grid_masks(sh)
        for m in range(3):
            value = pick(in_grid, inner(v, m))
            put(v, m, value)
            second_ref[m] = value
            put(kv, m, springs_ref[6] * value)
        image = image_of(sh, lane, v, kv, None, springs_ref)
        for m in range(3):
            image_ref[m] = image[m]
        valid = nodes_ref[...] >= 0.0
        names = ("r", "z", "w", "q", "v")
        sources = (start_ref, search_ref, first_ref, second_ref, image_ref)
        get = {name: [source[m, own, :] for m in range(3)] for name, source in zip(names, sources)}
        sums[...] = jnp.zeros(sums.shape, f32)
        for i, (a, b) in enumerate(("rz", "zw", "rq", "wq", "zv", "qv")):
            product = sum(get[a][m] * get[b][m] for m in range(3))
            sums[i : i + 1, :] = fold_rows(pick(valid, product))
        slots_ref[...] = jnp.broadcast_to(lane_sums(sums)[0:1], slots_ref.shape)

    second, second_image_field, sums = call(
        second_image,
        "second_image",
        [fields, fields, slots],
        [solved, *from_z, *from_y, *from_x, nodes, springs, start_field, search, image],
        [tall] * 2 + [(LANES, LANES)],
    )
    totals = to_all(sums)

    def turn(search_ref, first_ref, second_ref, image_ref, out_ref):
        select = selection(sh)
        for i, ref in enumerate((search_ref, first_ref, second_ref, image_ref)):
            for m in range(3):
                out_ref[i, m] = to_cells(ref[m, own, :], select)

    (turned,) = call(turn, "turn", [(4,) + natural.shape], [search, image, second, second_image_field])

    def finish(totals_ref, natural_ref, turned_ref, field_ref, residual_ref):
        total = jnp.sum(totals_ref[...], axis=0, keepdims=True)
        rz, zw, rq, wq, zv, qv = [total[:, i : i + 1] for i in range(6)]
        step0 = rz / zw
        rho = rz - step0 * zw - step0 * rq + step0 * step0 * wq
        grow = 1.0 + rho / rz
        curvature = grow * grow * zw - grow * step0 * (zv + wq) + step0 * step0 * qv
        step1 = rho / curvature
        first = step0 + step1 * grow
        second = step0 * step1
        for m in range(3):
            field_ref[m] = first * turned_ref[0, m] - second * turned_ref[2, m]
            residual_ref[m] = natural_ref[m] - (first * turned_ref[1, m] - second * turned_ref[3, m])

    solution_field, residual = call(
        finish, "finish", [natural.shape, natural.shape], [totals, natural, turned]
    )
    return solution_field.reshape(right_side.shape), residual.reshape(right_side.shape)


def solution(mesh):
    in_specs = (
        P(None, "gx", "gy", "gz"),
        P("gx", "gy", "gz"),
        P(),
        P("gx", "gy", "gz"),
        P(("gx", "gy", "gz"), None),
    )
    out_specs = (P(None, "gx", "gy", "gz"), P(None, "gx", "gy", "gz"))
    return jax.shard_map(body, mesh=mesh, in_specs=in_specs, out_specs=out_specs, check_vma=False)
```

```python
import jax
import jax.numpy as jnp
from jax import lax
from jax.experimental import pallas as pl
from jax.experimental.pallas import tpu as pltpu
from jax.sharding import PartitionSpec as P

AXES = ("gx", "gy", "gz")
SWEEPS = 4
relax = 0.6
highest = lax.Precision.HIGHEST
f32 = jnp.float32
LANES = 128
EDGE = 8

ALONG1, ACROSS1 = 0.75, 0.5
ALONG2, ACROSS2, MIXED2 = 0.3125, 0.25, 0.0625
SAME3, MIXED3 = 7.0 / 36.0, 1.0 / 36.0
TOTAL = 2 * ALONG1 + 4 * ACROSS1 + 8 * ALONG2 + 4 * ACROSS2 + 8 * SAME3


class Exchange:
    def __init__(self, fields, layers, up, down):
        self.fields, self.layers, self.up, self.down = fields, layers, up, down


DEEP = Exchange(3, 3, -2, -1)
NEAR = Exchange(3, 2, -1, -1)


class Shape:
    def __init__(self, size_x, size_y, size_z, phases, mesh_sizes):
        self.x, self.y, self.z = size_x, size_y, size_z
        self.pitch = size_y + 4
        self.used = (size_x + 2) * self.pitch
        assert self.used <= LANES
        self.rows = size_z + 2 * EDGE
        self.tall = self.rows + 2 * EDGE
        self.phases = phases
        self.sizes = mesh_sizes
        self.devices = mesh_sizes[0] * mesh_sizes[1] * mesh_sizes[2]
        self.cells = size_x * size_y
        self.links = [1 if n <= 2 else 2 for n in mesh_sizes]
        self.x_links, self.y_links, self.z_links = self.links

    def lane_grid(self, rows):
        lane = lax.broadcasted_iota(jnp.int32, (rows, LANES), 1)
        column = jnp.zeros_like(lane)
        for j in range(1, self.x + 2):
            column = column + (lane >= j * self.pitch).astype(jnp.int32)
        offset = lane - column * self.pitch
        return lane, column - 1, offset - 2

    def here(self, axis):
        return lax.axis_index(AXES[axis])


def shift(value, amount):
    amount = amount % LANES
    return value if amount == 0 else pltpu.roll(value, amount, 1)


def pick(mask, value):
    return jnp.where(mask, value, 0.0)


def scale(flag, value):
    return value * flag.astype(f32)


def pair(links, even, upward, downward):
    first = jnp.where(even, upward, downward)
    return (first,) if links == 1 else (first, jnp.where(even, downward, upward))


def sides(sh, axis, received):
    index, size = sh.here(axis), sh.sizes[axis]
    even = index % 2 == 0
    first = received[0]
    second = received[1] if len(received) > 1 else jnp.zeros_like(first)
    below = jnp.where(even, second, first)
    above = jnp.where(even, first, second)
    return scale(index > 0, below), scale(index < size - 1, above)


def lane_range(lane, start, count):
    return (lane >= start) & (lane < start + count)


def pack_z(sh, ex, source, out_refs):
    even = sh.here(2) % 2 == 0
    zero = jnp.zeros((8 - ex.layers, LANES), f32)
    for f in range(ex.fields):
        upward = source(f, EDGE + sh.z + ex.up, ex.layers)
        downward = source(f, EDGE + ex.down, ex.layers)
        for ref, message in zip(out_refs, pair(sh.z_links, even, upward, downward)):
            ref[8 * f : 8 * f + ex.layers, :] = message
            ref[8 * f + ex.layers : 8 * f + 8, :] = zero


def merge_z(sh, ex, field_ref, received_refs, scratch, guard):
    below, above = sides(sh, 2, [ref[...] for ref in received_refs])
    for f in range(ex.fields):
        scratch[f, guard : guard + sh.rows, :] = field_ref[f]
        low = guard + EDGE + ex.up
        high = guard + EDGE + sh.z + ex.down
        scratch[f, low : low + ex.layers, :] += below[8 * f : 8 * f + ex.layers]
        scratch[f, high : high + ex.layers, :] += above[8 * f : 8 * f + ex.layers]


def fold(sh, value, layers, start=None):
    folds = sh.pitch // layers
    height = -(-sh.rows // (8 * folds)) * 8
    lane, _, across = sh.lane_grid(1)
    total = jnp.zeros((height, LANES), f32)
    for i, first in enumerate(range(0, sh.rows, height)):
        part = value[first : first + height]
        if start is not None:
            part = pick((lane < sh.used) & lane_range(across, start, layers), part)
        part = shift(part, i * layers - (0 if start is None else start + 2))
        if part.shape[0] < height:
            part = jnp.concatenate([part, jnp.zeros((height - part.shape[0], LANES), f32)], axis=0)
        total = total + part
    return total


def folded_shape(sh, layers):
    return (-(-sh.rows // (8 * (sh.pitch // layers))) * 8, LANES)


def unfold(sh, message, layers, start):
    height = message.shape[0]
    lane, _, across = sh.lane_grid(1)
    mask = (lane < sh.used) & lane_range(across, start, layers)
    parts = []
    for i, first in enumerate(range(0, sh.rows, height)):
        part = message[0 : min(height, sh.rows - first)]
        parts.append(pick(mask, shift(part, start + 2 - i * layers)))
    return jnp.concatenate(parts, axis=0) if len(parts) > 1 else parts[0]


def pack_xy(sh, ex, scratch, x_refs, y_refs, corner_refs):
    rows = sh.rows
    lane, _, across = sh.lane_grid(1)
    even_x, even_y = sh.here(0) % 2 == 0, sh.here(1) % 2 == 0
    span = ex.layers * sh.pitch
    x_up = x_down = y_up = y_down = jnp.zeros((rows, LANES), f32)
    inside = lane < sh.used
    y_above, y_below = sh.y + ex.up, ex.down
    for f in range(ex.fields):
        value = scratch[f]
        start = (sh.x + ex.up + 1) * sh.pitch
        x_up = x_up + shift(pick(lane_range(lane, start, span), value), f * span - start)
        start = (ex.down + 1) * sh.pitch
        x_down = x_down + shift(pick(lane_range(lane, start, span), value), f * span - start)
        mask = inside & lane_range(across, y_above, ex.layers)
        y_up = y_up + shift(pick(mask, value), f * ex.layers - y_above - 2)
        mask = inside & lane_range(across, y_below, ex.layers)
        y_down = y_down + shift(pick(mask, value), f * ex.layers - y_below - 2)
    packed = ex.fields * ex.layers
    y_up, y_down = fold(sh, y_up, packed), fold(sh, y_down, packed)
    for ref, message in zip(y_refs, pair(sh.y_links, even_y, y_up, y_down)):
        ref[...] = message
    for i, message in enumerate(pair(sh.x_links, even_x, x_up, x_down)):
        x_refs[i][...] = message
        upward, downward = fold(sh, message, ex.layers, y_above), fold(sh, message, ex.layers, y_below)
        for j, corner in enumerate(pair(sh.y_links, even_y, upward, downward)):
            corner_refs[i * sh.y_links + j][...] = corner


def merge_xy(sh, ex, scratch, rim, guard, y_refs, x_refs):
    lane, _, across = sh.lane_grid(1)
    inside = lane < sh.used
    low_mask = inside & lane_range(across, ex.up, ex.layers)
    high_mask = inside & lane_range(across, sh.y + ex.down, ex.layers)
    span = ex.layers * sh.pitch
    packed = ex.fields * ex.layers
    below_y, above_y = [unfold(sh, value, packed, -2) for value in sides(sh, 1, [ref[...] for ref in y_refs])]
    per_link = 1 + sh.y_links
    sums = []
    for link in range(sh.x_links):
        straight, diagonal = x_refs[link * per_link], x_refs[link * per_link + 1 : (link + 1) * per_link]
        total = straight[...]
        below, above = sides(sh, 1, [ref[...] for ref in diagonal])
        total = total + unfold(sh, below, ex.layers, ex.up)
        sums.append(total + unfold(sh, above, ex.layers, sh.y + ex.down))
    below_x, above_x = sides(sh, 0, sums)
    first = 1 if ex.up == -2 else 0
    last = ex.layers - 1 if ex.down + ex.layers == 2 else ex.layers
    for f in range(ex.fields):
        addend = pick(low_mask, shift(below_y, ex.up + 2 - ex.layers * f))
        addend = addend + pick(high_mask, shift(above_y, sh.y + ex.down + 2 - ex.layers * f))
        start = (ex.up + first + 1) * sh.pitch
        count = (ex.layers - first) * sh.pitch
        moved = shift(below_x, start - f * span - first * sh.pitch)
        addend = addend + pick(lane_range(lane, start, count), moved)
        start = (sh.x + ex.down + 1) * sh.pitch
        moved = shift(above_x, start - f * span)
        addend = addend + pick(lane_range(lane, start, last * sh.pitch), moved)
        scratch[f, guard : guard + sh.rows, :] += addend
        if rim is not None:
            low = pick(lane_range(lane, 0, sh.pitch), shift(below_x, -f * span))
            start = (sh.x + 1) * sh.pitch
            moved = shift(above_x, start - f * span - last * sh.pitch)
            high = pick(lane_range(lane, start, sh.pitch), moved)
            rim[f, guard : guard + sh.rows, :] = low + high


def clear_guards(sh, refs):
    for ref in refs:
        for f in range(ref.shape[0]):
            ref[f, :EDGE, :] = jnp.zeros((EDGE, LANES), f32)
            ref[f, sh.tall - EDGE :, :] = jnp.zeros((EDGE, LANES), f32)


def inner(ref, f):
    return ref[f, EDGE : ref.shape[1] - EDGE, :]


def z_stage(ref, f):
    end = ref.shape[1] - EDGE
    after = ref[f, EDGE + 1 : end + 1, :]
    before = ref[f, EDGE - 1 : end - 1, :]
    return inner(ref, f), before + after, after - before


def y_stage(value):
    after, before = shift(value, -1), shift(value, 1)
    return before + after, after - before


def yz_parts(ref):
    a, a_sum, a_dif = z_stage(ref, 0)
    b, b_sum, b_dif = z_stage(ref, 1)
    c, c_sum, c_dif = z_stage(ref, 2)
    pa, ma = y_stage(a)
    pas, mas = y_stage(a_sum)
    pad, _ = y_stage(a_dif)
    pb, mb = y_stage(b)
    pbs, mbs = y_stage(b_sum)
    _, mbd = y_stage(b_dif)
    pc, _ = y_stage(c)
    pcs, _ = y_stage(c_sum)
    pcd, mcd = y_stage(c_dif)
    own_x = ACROSS1 * (pa + a_sum) + ACROSS2 * pas
    even_x = ALONG1 * a + ALONG2 * (pa + a_sum) + SAME3 * pas
    odd_x = MIXED2 * (mb + c_dif) + MIXED3 * (mbs + pcd)
    own_y = ALONG1 * pb + ACROSS1 * b_sum + ALONG2 * pbs + MIXED2 * mcd
    even_y = ACROSS1 * b + ALONG2 * pb + ACROSS2 * b_sum + SAME3 * pbs + MIXED3 * mcd
    odd_y = MIXED2 * ma + MIXED3 * mas
    own_z = ALONG1 * c_sum + ACROSS1 * pc + ALONG2 * pcs + MIXED2 * mbd
    even_z = ACROSS1 * c + ACROSS2 * pc + ALONG2 * c_sum + SAME3 * pcs + MIXED3 * mbd
    odd_z = MIXED2 * a_dif + MIXED3 * pad
    return (own_x, even_x, odd_x), (own_y, even_y, odd_y), (own_z, even_z, odd_z)


def x_stage(sh, lane, own, plus, minus, rim_plus, rim_minus):
    after, before = shift(plus, -sh.pitch), shift(minus, sh.pitch)
    last = (sh.x + 1) * sh.pitch
    if rim_plus is None:
        return own + pick(lane < last, after) + pick(lane >= sh.pitch, before)
    return own + jnp.where(lane < last, after, rim_plus) + jnp.where(lane >= sh.pitch, before, rim_minus)


def stencil(sh, lane, ref, rim):
    parts = yz_parts(ref)
    rims = yz_parts(rim) if rim is not None else [None] * 3
    out = []
    for (own, even, odd), rim_part in zip(parts, rims):
        if rim_part is None:
            out.append(x_stage(sh, lane, own, even + odd, even - odd, None, None))
        else:
            _, rim_even, rim_odd = rim_part
            out.append(
                x_stage(sh, lane, own, even + odd, even - odd, rim_even + rim_odd, rim_even - rim_odd)
            )
    return out


def spring_parts(ref):
    k, k_sum, k_dif = z_stage(ref, 0)
    pk, mk = y_stage(k)
    pks, mks = y_stage(k_sum)
    pkd, mkd = y_stage(k_dif)
    zero = jnp.zeros_like(k)
    xx = (ACROSS1 * (pk + k_sum) + ACROSS2 * pks, ALONG1 * k + ALONG2 * (pk + k_sum) + SAME3 * pks, zero)
    yy = (
        ALONG1 * pk + ACROSS1 * k_sum + ALONG2 * pks,
        ACROSS1 * k + ALONG2 * pk + ACROSS2 * k_sum + SAME3 * pks,
        zero,
    )
    zz = (
        ALONG1 * k_sum + ACROSS1 * pk + ALONG2 * pks,
        ACROSS1 * k + ACROSS2 * pk + ALONG2 * k_sum + SAME3 * pks,
        zero,
    )
    xy = (zero, zero, MIXED2 * mk + MIXED3 * mks)
    xz = (zero, zero, MIXED2 * k_dif + MIXED3 * pkd)
    yz = (MIXED2 * mkd, MIXED3 * mkd, zero)
    return xx, yy, zz, xy, xz, yz


def own_block(sh, lane, springs):
    main, rim = springs
    k = inner(main, 0)
    out = []
    for index, ((own, even, odd), (_, rim_even, rim_odd)) in enumerate(
        zip(spring_parts(main), spring_parts(rim))
    ):
        total = x_stage(sh, lane, own, even + odd, even - odd, rim_even + rim_odd, rim_even - rim_odd)
        out.append(total + TOTAL * k if index < 3 else total)
    return out


def apply_block(d, v):
    return (
        d[0] * v[0] + d[3] * v[1] + d[4] * v[2],
        d[3] * v[0] + d[1] * v[1] + d[5] * v[2],
        d[4] * v[0] + d[5] * v[1] + d[2] * v[2],
    )


def image_of(sh, lane, v, kv, rims, springs_ref):
    k = springs_ref[6]
    k_before, k_after = shift(k, sh.pitch), shift(k, -sh.pitch)
    last = (sh.x + 1) * sh.pitch
    own = apply_block([springs_ref[f] for f in range(6)], [inner(v, m) for m in range(3)])
    rim_parts = [yz_parts(rims[0]), yz_parts(rims[1])] if rims else None
    out = []
    for m, (plain, scaled) in enumerate(zip(yz_parts(v), yz_parts(kv))):
        after = shift(k_before * (plain[1] + plain[2]) + (scaled[1] + scaled[2]), -sh.pitch)
        before = shift(k_after * (plain[1] - plain[2]) + (scaled[1] - scaled[2]), sh.pitch)
        if rims is None:
            after, before = pick(lane < last, after), pick(lane >= sh.pitch, before)
        else:
            plain_rim, scaled_rim = rim_parts[0][m], rim_parts[1][m]
            edge = k * (plain_rim[1] + plain_rim[2]) + (scaled_rim[1] + scaled_rim[2])
            after = jnp.where(lane < last, after, edge)
            edge = k * (plain_rim[1] - plain_rim[2]) + (scaled_rim[1] - scaled_rim[2])
            before = jnp.where(lane >= sh.pitch, before, edge)
        out.append(own[m] - (k * plain[0] + scaled[0] + after + before))
    return out


def level(sh):
    return lax.broadcasted_iota(jnp.int32, (sh.rows, LANES), 0) - EDGE


def extended_mask(sh):
    lane, _, across = sh.lane_grid(1)
    z = level(sh)
    return ((lane < sh.used) & (across >= -1) & (across <= sh.y)) & ((z >= -1) & (z <= sh.z))


def within(sh, axis, place, size):
    index = sh.here(axis)
    low = jnp.where(index > 0, -EDGE, 0)
    high = jnp.where(index < sh.sizes[axis] - 1, size + EDGE, size)
    return (place >= low) & (place < high)


def grid_masks(sh):
    lane, along, across = sh.lane_grid(1)
    lanes = (lane < sh.used) & within(sh, 1, across, sh.y)
    rows = within(sh, 2, level(sh), sh.z)
    return (lanes & within(sh, 0, along, sh.x)) & rows, lanes & rows


def put(ref, f, value):
    ref[f, EDGE : ref.shape[1] - EDGE, :] = value


def local_solve(sh, residual_ref, springs_ref, v, kv, factor):
    lane, _, _ = sh.lane_grid(1)
    mask = extended_mask(sh)
    for m in range(3):
        factor[m] = pick(mask, relax / jnp.where(mask, springs_ref[m], 1.0))
        z = residual_ref[m] * factor[m]
        put(v[0], m, z)
        put(kv[0], m, springs_ref[6] * z)
    for sweep in range(SWEEPS - 1):
        old, new = sweep % 2, (sweep + 1) % 2
        image = image_of(sh, lane, v[old], kv[old], None, springs_ref)
        for m in range(3):
            z = inner(v[old], m) + factor[m] * (residual_ref[m] - image[m])
            put(v[new], m, z)
            put(kv[new], m, springs_ref[6] * z)
    return (SWEEPS - 1) % 2


def coords(sh):
    lane, along, across = sh.lane_grid(sh.z)
    z = lax.broadcasted_iota(jnp.int32, (sh.z, LANES), 0)
    place = lambda index, size: (2 * index + 1).astype(f32) / size - 1.0
    return place(along, sh.x), place(across, sh.y), place(z, sh.z)


def cell_coords(sh):
    cell = lax.broadcasted_iota(jnp.int32, (sh.cells, sh.z), 0)
    z = lax.broadcasted_iota(jnp.int32, (sh.cells, sh.z), 1)
    x = cell // sh.y
    place = lambda index, size: (2 * index + 1).astype(f32) / size - 1.0
    return place(x, sh.x), place(cell - x * sh.y, sh.y), place(z, sh.z)


def cross(a, b):
    return (a[1] * b[2] - a[2] * b[1], a[2] * b[0] - a[0] * b[2], a[0] * b[1] - a[1] * b[0])


def fold_rows(value):
    total = value[0:8]
    for i in range(8, value.shape[0], 8):
        total = total + value[i : i + 8]
    return jnp.sum(total, axis=0, keepdims=True)


def lane_sums(rows_ref):
    ones = jnp.ones((8, LANES), f32)
    return lax.dot_general(
        ones, rows_ref[...], (((1,), (1,)), ((), ())), precision=highest, preferred_element_type=f32
    )


def coarse_sums(sh, nodes, field, places, count, sums):
    moments = tuple(field) + cross(places, field)
    for node in range(count):
        mask = nodes == node
        for m in range(6):
            sums[node * 6 + m : node * 6 + m + 1, :] = fold_rows(pick(mask, moments[m]))
    flat = (sh.here(0) * sh.sizes[1] + sh.here(1)) * sh.sizes[2] + sh.here(2)
    return pltpu.roll(lane_sums(sums), lax.rem(flat * (6 * count), LANES), 1)[0:1]


def coarse_values(sh, nodes, received, inverse_ref, values):
    unknowns, total = inverse_ref.shape
    row = lax.broadcasted_iota(jnp.int32, received.shape, 0)
    part = jnp.zeros((unknowns, LANES), f32)
    for i in range(0, total, LANES):
        owner = (i + lax.broadcasted_iota(jnp.int32, (1, LANES), 1)) // unknowns
        vector = jnp.sum(pick(row == owner, received), axis=0, keepdims=True)
        part = part + inverse_ref[:, i : i + LANES] * vector
    values[0:unknowns, :] = jnp.dot(
        part, jnp.ones((LANES, LANES), f32), precision=highest, preferred_element_type=f32
    )
    cells = []
    for m in range(6):
        cell = jnp.zeros((sh.z, LANES), f32)
        for node in range(unknowns // 6):
            cell = jnp.where(nodes == float(node), values[node * 6 + m : node * 6 + m + 1, :], cell)
        cells.append(cell)
    turned = cross(cells[3:], coords(sh))
    return [cells[m] + turned[m] for m in range(3)]


def selection(sh):
    lane, along, across = sh.lane_grid(sh.cells)
    inside = (along >= 0) & (along < sh.x) & (across >= 0) & (across < sh.y)
    row = lax.broadcasted_iota(jnp.int32, (sh.cells, LANES), 0)
    return (inside & (row == along * sh.y + across)).astype(f32)


def to_lanes(value, select):
    return lax.dot_general(
        value, select, (((0,), (0,)), ((), ())), precision=highest, preferred_element_type=f32
    )


def to_cells(value, select):
    return lax.dot_general(
        select, value, (((1,), (1,)), ((), ())), precision=highest, preferred_element_type=f32
    )


def send_lines(sh, lines, slots_ref):
    here = [sh.here(axis) for axis in range(3)]
    corner = [lines[8 * i : 8 * i + 8, :] for i in range(4)]
    top, bottom = lines[32:40, :], lines[40:48, :]
    for x in range(sh.sizes[0]):
        low_high = [jnp.where(x > here[0], corner[2 + high], corner[high]) for high in range(2)]
        for y in range(sh.sizes[1]):
            column = jnp.where(y > here[1], low_high[1], low_high[0])
            for z in range(sh.sizes[2]):
                slot = jnp.where(z == here[2] + 1, top, jnp.where(z == here[2] - 1, bottom, column))
                place = 8 * ((x * sh.sizes[1] + y) * sh.sizes[2] + z)
                slots_ref[place : place + 8, :] = slot


def slot_from(sh, received_ref, step):
    place, exists = 0, None
    for axis in range(3):
        index = sh.here(axis) + step[axis]
        inside = (index >= 0) & (index < sh.sizes[axis])
        exists = inside if exists is None else exists & inside
        place = place * sh.sizes[axis] + jnp.clip(index, 0, sh.sizes[axis] - 1)
    return scale(exists, received_ref[pl.ds(pl.multiple_of(place * 8, 8), 8), :])


def repeat_twice(count):
    row = lax.broadcasted_iota(jnp.int32, (2 * count, count), 0)
    column = lax.broadcasted_iota(jnp.int32, (2 * count, count), 1)
    return ((row >= 2 * column) & (row < 2 * column + 2)).astype(f32)


def ring(size_x, size_y, rows):
    row = lax.broadcasted_iota(jnp.int32, (rows, LANES), 0)
    sides_x, both = 2 * size_y, 2 * size_y + 2 * size_x
    corner = row - both
    x = jnp.where(row < size_y, -1, size_x)
    x = jnp.where(row < sides_x, x, jnp.where(row < sides_x + size_x, row - sides_x, row - sides_x - size_x))
    x = jnp.where(row < both, x, jnp.where(corner < 2, -1, size_x))
    y = jnp.where(row < size_y, row, row - size_y)
    y = jnp.where(row < sides_x, y, jnp.where(row < sides_x + size_x, -1, size_y))
    y = jnp.where(row < both, y, jnp.where((corner == 0) | (corner == 2), -1, size_y))
    return x, y, (row < sides_x) | (row >= both), row < both + 4


def face_shape(sh, label_x, label_y):
    rows = max(3 * sh.x + label_x, 3 * sh.y + label_y)
    return (-(-rows // 8) * 8, LANES)


def pack_faces(sh, natural_ref, stiff, label_x, label_y, x_refs, y_refs):
    even_x, even_y = sh.here(0) % 2 == 0, sh.here(1) % 2 == 0

    def face(at, count, stride, label_at, label_count, label_stride):
        rows = [natural_ref[m, pl.ds(at, count, stride=stride), :] for m in range(3)]
        return rows, stiff[pl.ds(label_at, label_count, stride=label_stride), :]

    above = face(sh.cells - sh.y, sh.y, 1, (label_x - 1) * label_y, label_y, 1)
    below = face(0, sh.y, 1, 0, label_y, 1)
    for refs, links, even, above, below in (
        (x_refs, sh.x_links, even_x, above, below),
        (
            y_refs,
            sh.y_links,
            even_y,
            face(sh.y - 1, sh.x, sh.y, label_y - 1, label_x, label_y),
            face(0, sh.x, sh.y, 0, label_x, label_y),
        ),
    ):
        for i, ref in enumerate(refs):
            ref[...] = jnp.zeros(ref.shape, f32)
            count = above[0][0].shape[0]
            for m in range(3):
                ref[m * count : (m + 1) * count, :] = pair(links, even, above[0][m], below[0][m])[i]
            labels, length = above[1].shape
            ref[3 * count : 3 * count + labels, 0:length] = pair(links, even, above[1], below[1])[i]


def merge_start(sh, refs, x_refs, y_refs, received_ref, sizes, cells, labels):
    residual, stiff, stiff_rim = refs
    label_x, label_y, label_z = sizes
    lane, along, across = sh.lane_grid(1)
    inside = lane < sh.used
    last = (sh.x + 1) * sh.pitch
    x_mask = {-1: lane < sh.pitch, 0: (lane >= sh.pitch) & (lane < last), 1: (lane >= last) & inside}
    y_mask = {-1: across < 0, 0: (across >= 0) & (across < sh.y), 1: across >= sh.y}
    cells[...] = jnp.zeros(cells.shape, f32)
    labels[...] = jnp.zeros(labels.shape, f32)
    count, label_count = cells.shape[1], labels.shape[0]
    at = label_at = 0
    for axis, face_refs, size, label_size in ((0, x_refs, sh.y, label_y), (1, y_refs, sh.x, label_x)):
        for message in sides(sh, axis, [ref[...] for ref in face_refs]):
            for m in range(3):
                cells[m, at : at + size, :] = message[m * size : (m + 1) * size]
            labels[label_at : label_at + label_size, :] = message[3 * size : 3 * size + label_size, 0:label_z]
            at, label_at = at + size, label_at + label_size
    for dx, dy in ((-1, -1), (-1, 1), (1, -1), (1, 1)):
        slot = slot_from(sh, received_ref, (dx, dy, 0))
        for m in range(3):
            cells[m, at : at + 1, :] = slot[m : m + 1]
        labels[label_at : label_at + 1, :] = slot[3:4, 0:label_z]
        at, label_at = at + 1, label_at + 1
    x, y, _, valid = ring(sh.x, sh.y, count)
    place = (valid & inside & (along == x) & (across == y)).astype(f32)
    own = slice(EDGE, EDGE + sh.z)
    tall_own = slice(2 * EDGE, 2 * EDGE + sh.z)
    for m in range(3):
        residual[m, own, :] += to_lanes(cells[m], place)
    by_z = lax.dot_general(
        repeat_twice(label_z), labels[...], (((1,), (1,)), ((), ())), precision=highest, preferred_element_type=f32
    )
    x, y, at_x, valid = ring(label_x, label_y, label_count)
    match = valid & inside & ((along >> 1) == x) & ((across >> 1) == y)
    columns = jnp.dot(by_z, (match & at_x).astype(f32), precision=highest, preferred_element_type=f32)
    stiff_rim[0, tall_own, :] = columns
    columns = columns + jnp.dot(by_z, (match & ~at_x).astype(f32), precision=highest, preferred_element_type=f32)
    stiff[0, tall_own, :] += columns
    for dz in (-1, 1):
        main = edge = jnp.zeros((8, LANES), f32)
        for dx in (-1, 0, 1):
            for dy in (-1, 0, 1):
                slot = slot_from(sh, received_ref, (dx, dy, dz))
                mask = x_mask[dx] & y_mask[dy]
                main = main + pick(mask, shift(slot, dx * sh.x * sh.pitch + dy * sh.y))
                if dx:
                    edge = edge + pick(mask, shift(slot, dx * (sh.x - 1) * sh.pitch + dy * sh.y))
        near = EDGE + sh.z if dz > 0 else EDGE - 1
        for m in range(3):
            residual[m, near : near + 1, :] = main[m : m + 1]
        for row in (EDGE + near, EDGE + near + dz):
            stiff[0, row : row + 1, :] = main[3:4]
            stiff_rim[0, row : row + 1, :] = edge[3:4]


def call(kernel, name, outs, ins, scratch=(), remote_ins=False):
    space = pltpu.HBM if remote_ins else pltpu.VMEM
    return pl.pallas_call(
        kernel,
        out_shape=[jax.ShapeDtypeStruct(shape, f32) for shape in outs],
        in_specs=[pl.BlockSpec(memory_space=space) for _ in ins],
        out_specs=[pl.BlockSpec(memory_space=pltpu.VMEM) for _ in outs],
        scratch_shapes=[pltpu.VMEM(shape, f32) if isinstance(shape, tuple) else shape for shape in scratch],
        compiler_params=pltpu.CompilerParams(vmem_limit_bytes=(62 if remote_ins else 48) * 1024 * 1024),
        name=name,
    )(*ins)


def permutation(sizes, moves):
    def partner(axis, link, index):
        size = sizes[axis]
        other = index ^ 1 if link == 0 else index + (1 if index % 2 else -1)
        if 0 <= other < size:
            return other
        return size - 1 - index if axis == 2 and size % 2 == 0 else index

    pairs = []
    for x in range(sizes[0]):
        for y in range(sizes[1]):
            for z in range(sizes[2]):
                place = [x, y, z]
                goal = [partner(a, moves[a], place[a]) if a in moves else place[a] for a in range(3)]
                if goal == place and 0 not in moves and sizes[0] % 2 == 0:
                    goal[0] = partner(0, 0, x)
                flat = [(p[0] * sizes[1] + p[1]) * sizes[2] + p[2] for p in (place, goal)]
                pairs.append(tuple(flat))
    return pairs


def send(sh, value, moves):
    return lax.ppermute(value, AXES, permutation(sh.sizes, moves))


def send_z(sh, messages):
    return [send(sh, message, {2: link}) for link, message in enumerate(messages)]


def send_faces(sh, x_messages, y_messages):
    from_y = [send(sh, message, {1: link}) for link, message in enumerate(y_messages)]
    from_x = [send(sh, message, {0: link}) for link, message in enumerate(x_messages)]
    return from_y, from_x


def to_all(slots):
    return lax.all_to_all(slots, AXES, 0, 0, tiled=True)


def exchange(sh, ex, name, field, z_messages):
    from_z = send_z(sh, z_messages)

    corners = sh.x_links * sh.y_links

    def packer(*refs):
        take = Taker(refs)
        field_ref, z_refs = take.one(), take(sh.z_links)
        x_refs, y_refs, corner_refs, scratch = take(sh.x_links), take(sh.y_links), take(corners), take.one()
        merge_z(sh, ex, field_ref, z_refs, scratch, 0)
        pack_xy(sh, ex, scratch, x_refs, y_refs, corner_refs)

    plane = (sh.rows, LANES)
    messages = call(
        packer,
        name,
        [plane] * sh.x_links
        + [folded_shape(sh, ex.fields * ex.layers)] * sh.y_links
        + [folded_shape(sh, ex.layers)] * corners,
        [field] + from_z,
        [(ex.fields,) + plane],
    )
    take = Taker(messages)
    x_messages, y_messages = take(sh.x_links), take(sh.y_links)
    from_y, straight = send_faces(sh, x_messages, y_messages)
    from_x = []
    for link in range(sh.x_links):
        from_x.append(straight[link])
        from_x.extend(send(sh, take.one(), {0: link, 1: other}) for other in range(sh.y_links))
    return from_z, from_y, from_x


class Taker:
    def __init__(self, refs):
        self.refs, self.at = refs, 0

    def __call__(self, count):
        self.at += count
        return self.refs[self.at - count : self.at]

    def one(self):
        return self(1)[0]


def merge_all(sh, ex, take, scratch, rim, guard):
    field = take.one()
    from_z, from_y = take(sh.z_links), take(sh.y_links)
    from_x = take(sh.x_links * (1 + sh.y_links))
    merge_z(sh, ex, field, from_z, scratch, guard)
    merge_xy(sh, ex, scratch, rim, guard, from_y, from_x)


def body(right_side, phase_labels, phase_moduli, coarse_nodes, coarse_inverse):
    sizes = tuple(lax.axis_size(axis) for axis in AXES)
    _, size_x, size_y, size_z = right_side.shape
    sh = Shape(size_x, size_y, size_z, phase_moduli.shape[0], sizes)
    unknowns = coarse_inverse.shape[0]
    node_count = unknowns // 6
    sum_rows = -(-unknowns // 8) * 8
    own = slice(EDGE, EDGE + sh.z)
    plane = (sh.rows, LANES)
    fields = (3,) + plane
    tall = (3, sh.tall, LANES)
    slots = (sh.devices, LANES)
    z_shape = lambda ex: [(8 * ex.fields, LANES)] * sh.z_links
    natural = right_side.reshape(3, sh.cells, sh.z)
    nodes_natural = coarse_nodes.reshape(sh.cells, sh.z)
    label_x, label_y, label_z = phase_labels.shape

    def block_places():
        lane, along, across = sh.lane_grid(label_x * label_y)
        inside = (along >= 0) & (along < sh.x) & (across >= 0) & (across < sh.y)
        block = lax.broadcasted_iota(jnp.int32, along.shape, 0)
        return (inside & (block == (along >> 1) * label_y + (across >> 1))).astype(f32)

    def end_layers(values, places):
        length = values.shape[1]
        row = lax.broadcasted_iota(jnp.int32, (8, length), 0)
        at = lax.broadcasted_iota(jnp.int32, (8, length), 1)
        ends = ((row == 0) & (at == length - 1)) | ((row == 1) & (at == 0))
        return jnp.dot(to_cells(values, ends.astype(f32)), places, precision=highest, preferred_element_type=f32)

    def begin(natural_in, labels_in, moduli_in, nodes_in, stiff, slots_ref, *rest):
        x_refs, y_refs = rest[: sh.x_links], rest[sh.x_links : sh.x_links + sh.y_links]
        natural_ref, labels_ref, moduli_ref, nodes_ref, sems, sums, lines = rest[sh.x_links + sh.y_links :]
        pairs = ((natural_in, natural_ref), (labels_in, labels_ref), (moduli_in, moduli_ref), (nodes_in, nodes_ref))
        copies = [pltpu.make_async_copy(a, b, sems.at[i]) for i, (a, b) in enumerate(pairs)]
        for copy in copies:
            copy.start()
        sums[...] = jnp.zeros(sums.shape, f32)
        lines[...] = jnp.zeros(lines.shape, f32)
        for copy in copies:
            copy.wait()
        for i in range(label_x):
            labels = labels_ref[i]
            moduli = jnp.zeros(labels.shape, f32)
            for phase in range(sh.phases):
                moduli = jnp.where(labels == phase, moduli_ref[phase], moduli)
            stiff[i * label_y : (i + 1) * label_y, :] = moduli
        cells = [natural_ref[m] for m in range(3)]
        line = coarse_sums(sh, nodes_ref[...], cells, cell_coords(sh), node_count, sums)
        for i, (cell, block) in enumerate(
            (
                (0, 0),
                (sh.y - 1, label_y - 1),
                ((sh.x - 1) * sh.y, (label_x - 1) * label_y),
                (sh.cells - 1, label_x * label_y - 1),
            )
        ):
            for m in range(3):
                lines[8 * i + m : 8 * i + m + 1, :] = natural_ref[m, cell : cell + 1, :]
            lines[8 * i + 3 : 8 * i + 4, 0:label_z] = stiff[block : block + 1, :]
        select = selection(sh)
        layers = [end_layers(cells[m], select) for m in range(3)] + [end_layers(stiff[...], block_places())]
        for i in range(2):
            for f in range(4):
                lines[8 * (4 + i) + f : 8 * (4 + i) + f + 1, :] = layers[f][i : i + 1]
        for i in range(6):
            lines[8 * i + 4 : 8 * i + 5, :] = line
        send_lines(sh, lines, slots_ref)
        pack_faces(sh, natural_ref, stiff, label_x, label_y, x_refs, y_refs)

    stiff_blocks, lines, *messages = call(
        begin,
        "begin",
        [(label_x * label_y, label_z), (8 * sh.devices, LANES)]
        + [face_shape(sh, label_x, label_y)] * (sh.x_links + sh.y_links),
        [natural, phase_labels, phase_moduli, nodes_natural],
        [
            natural.shape,
            pltpu.VMEM(phase_labels.shape, jnp.int32),
            pltpu.SMEM(phase_moduli.shape, f32),
            pltpu.VMEM(nodes_natural.shape, jnp.int32),
            pltpu.SemaphoreType.DMA((4,)),
            (LANES, LANES),
            (48, LANES),
        ],
        remote_ins=True,
    )

    def spread(natural_ref, nodes_ref, stiff, field_ref, lanes_ref):
        select = selection(sh)
        field_ref[...] = jnp.zeros(field_ref.shape, f32)
        for m in range(3):
            field_ref[m, own, :] = to_lanes(natural_ref[m], select)
        by_z = lax.dot_general(
            repeat_twice(label_z), stiff[...], (((1,), (1,)), ((), ())), precision=highest, preferred_element_type=f32
        )
        field_ref[3, own, :] = jnp.dot(by_z, block_places(), precision=highest, preferred_element_type=f32)
        lanes_ref[...] = to_lanes(nodes_ref[...].astype(f32) + 1.0, select) - 1.0

    start_field, nodes = call(
        spread, "spread", [(4,) + plane, (sh.z, LANES)], [natural, nodes_natural, stiff_blocks]
    )
    from_y, from_x = send_faces(sh, messages[: sh.x_links], messages[sh.x_links :])
    lines = to_all(lines)

    def add_coarse(nodes_ref, coarse, inverse_ref, values, solution_ref, z_refs, ex):
        added = coarse_values(sh, nodes_ref[...], coarse, inverse_ref, values)
        valid = nodes_ref[...] >= 0.0
        for m in range(3):
            solution_ref[m, own, :] += pick(valid, added[m])
        pack_z(sh, ex, lambda f, start, count: solution_ref[f, start : start + count, :], z_refs)

    def first_solve(*refs):
        take = Taker(refs)
        field_ref = take.one()
        y_refs, x_refs = take(sh.y_links), take(sh.x_links)
        nodes_ref, lines_ref, inverse_ref = take(3)
        solution_ref, springs_ref = take(2)
        z_refs = take(sh.z_links)
        residual, stiff, stiff_rim, v0, v1, kv0, kv1, factor, values, cells, labels = take(11)
        clear_guards(sh, (stiff, stiff_rim, v0, v1, kv0, kv1))
        residual[...] = field_ref[0:3]
        put(stiff, 0, field_ref[3])
        put(stiff_rim, 0, jnp.zeros(plane, f32))
        sizes = phase_labels.shape
        merge_start(sh, (residual, stiff, stiff_rim), x_refs, y_refs, lines_ref, sizes, cells, labels)
        springs_ref[6] = inner(stiff, 0)
        springs_ref[7] = inner(stiff_rim, 0)
        lane, _, _ = sh.lane_grid(1)
        for f, entry in enumerate(own_block(sh, lane, (stiff, stiff_rim))):
            springs_ref[f] = entry
        index = local_solve(sh, residual, springs_ref, (v0, v1), (kv0, kv1), factor)
        coarse = lines_ref[pl.ds(4, sh.devices, stride=8), :]
        for m in range(3):
            solution_ref[m] = inner((v0, v1)[index], m)
        add_coarse(nodes_ref, coarse, inverse_ref, values, solution_ref, z_refs, DEEP)

    solved, springs, *z_messages = call(
        first_solve,
        "first_solve",
        [fields, (8,) + plane] + z_shape(DEEP),
        [start_field, *from_y, *from_x, nodes, lines, coarse_inverse],
        [fields, (1, sh.tall, LANES), (1, sh.tall, LANES)]
        + [tall] * 4
        + [fields, (LANES, LANES)]
        + [
            (3, 8 * -(-(2 * sh.x + 2 * sh.y + 4) // 8), LANES),
            (8 * -(-(2 * label_x + 2 * label_y + 4) // 8), label_z),
        ],
    )
    from_z, from_y, from_x = exchange(sh, DEEP, "deep", solved, z_messages)

    def first_image(*refs):
        take = Taker(refs)
        merging = take(1 + sh.z_links + sh.y_links + sh.x_links * (1 + sh.y_links))
        nodes_ref, springs_ref = take(2)
        search_ref, image_ref, slots_ref = take(3)
        v, rim, kv, k_rim, sums = take(5)
        clear_guards(sh, (v, rim, kv, k_rim))
        merge_all(sh, DEEP, Taker(merging), v, rim, EDGE)
        lane, _, _ = sh.lane_grid(1)

        in_grid, in_rim = grid_masks(sh)
        for m in range(3):
            value = pick(in_grid, inner(v, m))
            put(v, m, value)
            search_ref[m] = value
            put(kv, m, springs_ref[6] * value)
            value = pick(in_rim, inner(rim, m))
            put(rim, m, value)
            put(k_rim, m, springs_ref[7] * value)
        image = image_of(sh, lane, v, kv, (rim, k_rim), springs_ref)
        keep = in_grid & extended_mask(sh)
        for m in range(3):
            image_ref[m] = pick(keep, image[m])
        sums[...] = jnp.zeros(sums.shape, f32)
        line = coarse_sums(sh, nodes_ref[...], [image_ref[m, own, :] for m in range(3)], coords(sh), node_count, sums)
        slots_ref[...] = jnp.broadcast_to(line, slots_ref.shape)

    search, image, sums = call(
        first_image,
        "first_image",
        [fields, fields, slots],
        [solved, *from_z, *from_y, *from_x, nodes, springs],
        [tall] * 4 + [(LANES, LANES)],
    )
    coarse = to_all(sums)

    def second_solve(image_ref, springs_ref, local_ref, v0, v1, kv0, kv1, factor):
        clear_guards(sh, (v0, v1, kv0, kv1))
        index = local_solve(sh, image_ref, springs_ref, (v0, v1), (kv0, kv1), factor)
        for m in range(3):
            local_ref[m] = inner((v0, v1)[index], m)

    (local,) = call(second_solve, "second_solve", [fields], [image, springs], [tall] * 4 + [fields])

    def second_add(local_ref, nodes_ref, coarse_ref, inverse_ref, *rest):
        solution_ref, z_refs, values = rest[0], rest[1:-1], rest[-1]
        solution_ref[...] = local_ref[...]
        add_coarse(nodes_ref, coarse_ref[...], inverse_ref, values, solution_ref, z_refs, NEAR)

    solved, *z_messages = call(
        second_add,
        "second_add",
        [fields] + z_shape(NEAR),
        [local, nodes, coarse, coarse_inverse],
        [(LANES, LANES)],
    )
    from_z, from_y, from_x = exchange(sh, NEAR, "near", solved, z_messages)

    def second_image(*refs):
        take = Taker(refs)
        merging = take(1 + sh.z_links + sh.y_links + sh.x_links * (1 + sh.y_links))
        nodes_ref, springs_ref, start_ref, search_ref, first_ref = take(5)
        second_ref, image_ref, slots_ref = take(3)
        v, kv, sums = take(3)
        clear_guards(sh, (v, kv))
        merge_all(sh, NEAR, Taker(merging), v, None, EDGE)
        lane, _, _ = sh.lane_grid(1)

        in_grid, _ = grid_masks(sh)
        for m in range(3):
            value = pick(in_grid, inner(v, m))
            put(v, m, value)
            second_ref[m] = value
            put(kv, m, springs_ref[6] * value)
        image = image_of(sh, lane, v, kv, None, springs_ref)
        for m in range(3):
            image_ref[m] = image[m]
        valid = nodes_ref[...] >= 0.0
        names = ("r", "z", "w", "q", "v")
        sources = (start_ref, search_ref, first_ref, second_ref, image_ref)
        get = {name: [source[m, own, :] for m in range(3)] for name, source in zip(names, sources)}
        sums[...] = jnp.zeros(sums.shape, f32)
        for i, (a, b) in enumerate(("rz", "zw", "rq", "wq", "zv", "qv")):
            product = sum(get[a][m] * get[b][m] for m in range(3))
            sums[i : i + 1, :] = fold_rows(pick(valid, product))
        slots_ref[...] = jnp.broadcast_to(lane_sums(sums)[0:1], slots_ref.shape)

    second, second_image_field, sums = call(
        second_image,
        "second_image",
        [fields, fields, slots],
        [solved, *from_z, *from_y, *from_x, nodes, springs, start_field, search, image],
        [tall] * 2 + [(LANES, LANES)],
    )
    totals = to_all(sums)

    def turn(search_ref, first_ref, second_ref, image_ref, out_ref):
        select = selection(sh)
        for i, ref in enumerate((search_ref, first_ref, second_ref, image_ref)):
            for m in range(3):
                out_ref[i, m] = to_cells(ref[m, own, :], select)

    (turned,) = call(turn, "turn", [(4,) + natural.shape], [search, image, second, second_image_field])

    def finish(totals_ref, natural_ref, turned_ref, field_ref, residual_ref):
        total = jnp.sum(totals_ref[...], axis=0, keepdims=True)
        rz, zw, rq, wq, zv, qv = [total[:, i : i + 1] for i in range(6)]
        step0 = rz / zw
        rho = rz - step0 * zw - step0 * rq + step0 * step0 * wq
        grow = 1.0 + rho / rz
        curvature = grow * grow * zw - grow * step0 * (zv + wq) + step0 * step0 * qv
        step1 = rho / curvature
        first = step0 + step1 * grow
        second = step0 * step1
        for m in range(3):
            field_ref[m] = first * turned_ref[0, m] - second * turned_ref[2, m]
            residual_ref[m] = natural_ref[m] - (first * turned_ref[1, m] - second * turned_ref[3, m])

    solution_field, residual = call(
        finish, "finish", [natural.shape, natural.shape], [totals, natural, turned]
    )
    return solution_field.reshape(right_side.shape), residual.reshape(right_side.shape)


def solution(mesh):
    in_specs = (
        P(None, "gx", "gy", "gz"),
        P("gx", "gy", "gz"),
        P(),
        P("gx", "gy", "gz"),
        P(("gx", "gy", "gz"), None),
    )
    out_specs = (P(None, "gx", "gy", "gz"), P(None, "gx", "gy", "gz"))
    return jax.shard_map(body, mesh=mesh, in_specs=in_specs, out_specs=out_specs, check_vma=False)
```

```python
import jax
import jax.numpy as jnp
from jax import lax
from jax.experimental import pallas as pl
from jax.experimental.pallas import tpu as pltpu
from jax.sharding import PartitionSpec as P

AXES = ("gx", "gy", "gz")
SWEEPS = 4
relax = 0.6
highest = lax.Precision.HIGHEST
f32 = jnp.float32
LANES = 128
EDGE = 8

ALONG1, ACROSS1 = 0.75, 0.5
ALONG2, ACROSS2, MIXED2 = 0.3125, 0.25, 0.0625
SAME3, MIXED3 = 7.0 / 36.0, 1.0 / 36.0
TOTAL = 2 * ALONG1 + 4 * ACROSS1 + 8 * ALONG2 + 4 * ACROSS2 + 8 * SAME3


class Exchange:
    def __init__(self, fields, layers, up, down):
        self.fields, self.layers, self.up, self.down = fields, layers, up, down


DEEP = Exchange(3, 3, -2, -1)
NEAR = Exchange(3, 2, -1, -1)


class Shape:
    def __init__(self, size_x, size_y, size_z, phases, mesh_sizes):
        self.x, self.y, self.z = size_x, size_y, size_z
        self.pitch = size_y + 4
        self.used = (size_x + 2) * self.pitch
        assert self.used <= LANES
        self.rows = size_z + 2 * EDGE
        self.tall = self.rows + 2 * EDGE
        self.phases = phases
        self.sizes = mesh_sizes
        self.devices = mesh_sizes[0] * mesh_sizes[1] * mesh_sizes[2]
        self.cells = size_x * size_y
        self.links = [1 if n <= 2 else 2 for n in mesh_sizes]
        self.x_links, self.y_links, self.z_links = self.links

    def lane_grid(self, rows):
        lane = lax.broadcasted_iota(jnp.int32, (rows, LANES), 1)
        column = jnp.zeros_like(lane)
        for j in range(1, self.x + 2):
            column = column + (lane >= j * self.pitch).astype(jnp.int32)
        offset = lane - column * self.pitch
        return lane, column - 1, offset - 2

    def here(self, axis):
        return lax.axis_index(AXES[axis])


def shift(value, amount):
    amount = amount % LANES
    return value if amount == 0 else pltpu.roll(value, amount, 1)


def pick(mask, value):
    return jnp.where(mask, value, 0.0)


def scale(flag, value):
    return value * flag.astype(f32)


def pair(links, even, upward, downward):
    first = jnp.where(even, upward, downward)
    return (first,) if links == 1 else (first, jnp.where(even, downward, upward))


def sides(sh, axis, received):
    index, size = sh.here(axis), sh.sizes[axis]
    even = index % 2 == 0
    first = received[0]
    second = received[1] if len(received) > 1 else jnp.zeros_like(first)
    below = jnp.where(even, second, first)
    above = jnp.where(even, first, second)
    return scale(index > 0, below), scale(index < size - 1, above)


def lane_range(lane, start, count):
    return (lane >= start) & (lane < start + count)


def pack_z(sh, ex, source, out_refs):
    even = sh.here(2) % 2 == 0
    zero = jnp.zeros((8 - ex.layers, LANES), f32)
    for f in range(ex.fields):
        upward = source(f, EDGE + sh.z + ex.up, ex.layers)
        downward = source(f, EDGE + ex.down, ex.layers)
        for ref, message in zip(out_refs, pair(sh.z_links, even, upward, downward)):
            ref[8 * f : 8 * f + ex.layers, :] = message
            ref[8 * f + ex.layers : 8 * f + 8, :] = zero


def merge_z(sh, ex, field_ref, received_refs, scratch, guard):
    below, above = sides(sh, 2, [ref[...] for ref in received_refs])
    for f in range(ex.fields):
        scratch[f, guard : guard + sh.rows, :] = field_ref[f]
        low = guard + EDGE + ex.up
        high = guard + EDGE + sh.z + ex.down
        scratch[f, low : low + ex.layers, :] += below[8 * f : 8 * f + ex.layers]
        scratch[f, high : high + ex.layers, :] += above[8 * f : 8 * f + ex.layers]


def fold(sh, value, layers, start=None):
    folds = sh.pitch // layers
    height = -(-sh.rows // (8 * folds)) * 8
    lane, _, across = sh.lane_grid(1)
    total = jnp.zeros((height, LANES), f32)
    for i, first in enumerate(range(0, sh.rows, height)):
        part = value[first : first + height]
        if start is not None:
            part = pick((lane < sh.used) & lane_range(across, start, layers), part)
        part = shift(part, i * layers - (0 if start is None else start + 2))
        if part.shape[0] < height:
            part = jnp.concatenate([part, jnp.zeros((height - part.shape[0], LANES), f32)], axis=0)
        total = total + part
    return total


def folded_shape(sh, layers):
    return (-(-sh.rows // (8 * (sh.pitch // layers))) * 8, LANES)


def unfold(sh, message, layers, start):
    height = message.shape[0]
    lane, _, across = sh.lane_grid(1)
    mask = (lane < sh.used) & lane_range(across, start, layers)
    parts = []
    for i, first in enumerate(range(0, sh.rows, height)):
        part = message[0 : min(height, sh.rows - first)]
        parts.append(pick(mask, shift(part, start + 2 - i * layers)))
    return jnp.concatenate(parts, axis=0) if len(parts) > 1 else parts[0]


def pack_xy(sh, ex, scratch, x_refs, y_refs, corner_refs):
    rows = sh.rows
    lane, _, across = sh.lane_grid(1)
    even_x, even_y = sh.here(0) % 2 == 0, sh.here(1) % 2 == 0
    span = ex.layers * sh.pitch
    x_up = x_down = y_up = y_down = jnp.zeros((rows, LANES), f32)
    inside = lane < sh.used
    y_above, y_below = sh.y + ex.up, ex.down
    for f in range(ex.fields):
        value = scratch[f]
        start = (sh.x + ex.up + 1) * sh.pitch
        x_up = x_up + shift(pick(lane_range(lane, start, span), value), f * span - start)
        start = (ex.down + 1) * sh.pitch
        x_down = x_down + shift(pick(lane_range(lane, start, span), value), f * span - start)
        mask = inside & lane_range(across, y_above, ex.layers)
        y_up = y_up + shift(pick(mask, value), f * ex.layers - y_above - 2)
        mask = inside & lane_range(across, y_below, ex.layers)
        y_down = y_down + shift(pick(mask, value), f * ex.layers - y_below - 2)
    packed = ex.fields * ex.layers
    y_up, y_down = fold(sh, y_up, packed), fold(sh, y_down, packed)
    for ref, message in zip(y_refs, pair(sh.y_links, even_y, y_up, y_down)):
        ref[...] = message
    for i, message in enumerate(pair(sh.x_links, even_x, x_up, x_down)):
        x_refs[i][...] = message
        upward, downward = fold(sh, message, ex.layers, y_above), fold(sh, message, ex.layers, y_below)
        for j, corner in enumerate(pair(sh.y_links, even_y, upward, downward)):
            corner_refs[i * sh.y_links + j][...] = corner


def merge_xy(sh, ex, scratch, rim, guard, y_refs, x_refs):
    lane, _, across = sh.lane_grid(1)
    inside = lane < sh.used
    low_mask = inside & lane_range(across, ex.up, ex.layers)
    high_mask = inside & lane_range(across, sh.y + ex.down, ex.layers)
    span = ex.layers * sh.pitch
    packed = ex.fields * ex.layers
    below_y, above_y = [unfold(sh, value, packed, -2) for value in sides(sh, 1, [ref[...] for ref in y_refs])]
    per_link = 1 + sh.y_links
    sums = []
    for link in range(sh.x_links):
        straight, diagonal = x_refs[link * per_link], x_refs[link * per_link + 1 : (link + 1) * per_link]
        total = straight[...]
        below, above = sides(sh, 1, [ref[...] for ref in diagonal])
        total = total + unfold(sh, below, ex.layers, ex.up)
        sums.append(total + unfold(sh, above, ex.layers, sh.y + ex.down))
    below_x, above_x = sides(sh, 0, sums)
    first = 1 if ex.up == -2 else 0
    last = ex.layers - 1 if ex.down + ex.layers == 2 else ex.layers
    for f in range(ex.fields):
        addend = pick(low_mask, shift(below_y, ex.up + 2 - ex.layers * f))
        addend = addend + pick(high_mask, shift(above_y, sh.y + ex.down + 2 - ex.layers * f))
        start = (ex.up + first + 1) * sh.pitch
        count = (ex.layers - first) * sh.pitch
        moved = shift(below_x, start - f * span - first * sh.pitch)
        addend = addend + pick(lane_range(lane, start, count), moved)
        start = (sh.x + ex.down + 1) * sh.pitch
        moved = shift(above_x, start - f * span)
        addend = addend + pick(lane_range(lane, start, last * sh.pitch), moved)
        scratch[f, guard : guard + sh.rows, :] += addend
        if rim is not None:
            low = pick(lane_range(lane, 0, sh.pitch), shift(below_x, -f * span))
            start = (sh.x + 1) * sh.pitch
            moved = shift(above_x, start - f * span - last * sh.pitch)
            high = pick(lane_range(lane, start, sh.pitch), moved)
            rim[f, guard : guard + sh.rows, :] = low + high


def clear_guards(sh, refs):
    for ref in refs:
        for f in range(ref.shape[0]):
            ref[f, :EDGE, :] = jnp.zeros((EDGE, LANES), f32)
            ref[f, ref.shape[1] - EDGE :, :] = jnp.zeros((EDGE, LANES), f32)


def inner(ref, f):
    return ref[f, EDGE : ref.shape[1] - EDGE, :]


def z_stage(ref, f):
    end = ref.shape[1] - EDGE
    after = ref[f, EDGE + 1 : end + 1, :]
    before = ref[f, EDGE - 1 : end - 1, :]
    return inner(ref, f), before + after, after - before


def y_stage(value):
    after, before = shift(value, -1), shift(value, 1)
    return before + after, after - before


def yz_parts(ref):
    a, a_sum, a_dif = z_stage(ref, 0)
    b, b_sum, b_dif = z_stage(ref, 1)
    c, c_sum, c_dif = z_stage(ref, 2)
    pa, ma = y_stage(a)
    pas, mas = y_stage(a_sum)
    pad, _ = y_stage(a_dif)
    pb, mb = y_stage(b)
    pbs, mbs = y_stage(b_sum)
    _, mbd = y_stage(b_dif)
    pc, _ = y_stage(c)
    pcs, _ = y_stage(c_sum)
    pcd, mcd = y_stage(c_dif)
    own_x = ACROSS1 * (pa + a_sum) + ACROSS2 * pas
    even_x = ALONG1 * a + ALONG2 * (pa + a_sum) + SAME3 * pas
    odd_x = MIXED2 * (mb + c_dif) + MIXED3 * (mbs + pcd)
    own_y = ALONG1 * pb + ACROSS1 * b_sum + ALONG2 * pbs + MIXED2 * mcd
    even_y = ACROSS1 * b + ALONG2 * pb + ACROSS2 * b_sum + SAME3 * pbs + MIXED3 * mcd
    odd_y = MIXED2 * ma + MIXED3 * mas
    own_z = ALONG1 * c_sum + ACROSS1 * pc + ALONG2 * pcs + MIXED2 * mbd
    even_z = ACROSS1 * c + ACROSS2 * pc + ALONG2 * c_sum + SAME3 * pcs + MIXED3 * mbd
    odd_z = MIXED2 * a_dif + MIXED3 * pad
    return (own_x, even_x, odd_x), (own_y, even_y, odd_y), (own_z, even_z, odd_z)


def x_stage(sh, lane, own, plus, minus, rim_plus, rim_minus):
    after, before = shift(plus, -sh.pitch), shift(minus, sh.pitch)
    last = (sh.x + 1) * sh.pitch
    if rim_plus is None:
        return own + pick(lane < last, after) + pick(lane >= sh.pitch, before)
    return own + jnp.where(lane < last, after, rim_plus) + jnp.where(lane >= sh.pitch, before, rim_minus)


def stencil(sh, lane, ref, rim):
    parts = yz_parts(ref)
    rims = yz_parts(rim) if rim is not None else [None] * 3
    out = []
    for (own, even, odd), rim_part in zip(parts, rims):
        if rim_part is None:
            out.append(x_stage(sh, lane, own, even + odd, even - odd, None, None))
        else:
            _, rim_even, rim_odd = rim_part
            out.append(
                x_stage(sh, lane, own, even + odd, even - odd, rim_even + rim_odd, rim_even - rim_odd)
            )
    return out


def spring_parts(ref):
    k, k_sum, k_dif = z_stage(ref, 0)
    pk, mk = y_stage(k)
    pks, mks = y_stage(k_sum)
    pkd, mkd = y_stage(k_dif)
    zero = jnp.zeros_like(k)
    xx = (ACROSS1 * (pk + k_sum) + ACROSS2 * pks, ALONG1 * k + ALONG2 * (pk + k_sum) + SAME3 * pks, zero)
    yy = (
        ALONG1 * pk + ACROSS1 * k_sum + ALONG2 * pks,
        ACROSS1 * k + ALONG2 * pk + ACROSS2 * k_sum + SAME3 * pks,
        zero,
    )
    zz = (
        ALONG1 * k_sum + ACROSS1 * pk + ALONG2 * pks,
        ACROSS1 * k + ACROSS2 * pk + ALONG2 * k_sum + SAME3 * pks,
        zero,
    )
    xy = (zero, zero, MIXED2 * mk + MIXED3 * mks)
    xz = (zero, zero, MIXED2 * k_dif + MIXED3 * pkd)
    yz = (MIXED2 * mkd, MIXED3 * mkd, zero)
    return xx, yy, zz, xy, xz, yz


def own_block(sh, lane, springs):
    main, rim = springs
    k = inner(main, 0)
    out = []
    for index, ((own, even, odd), (_, rim_even, rim_odd)) in enumerate(
        zip(spring_parts(main), spring_parts(rim))
    ):
        total = x_stage(sh, lane, own, even + odd, even - odd, rim_even + rim_odd, rim_even - rim_odd)
        out.append(total + TOTAL * k if index < 3 else total)
    return out


def apply_block(d, v):
    return (
        d[0] * v[0] + d[3] * v[1] + d[4] * v[2],
        d[3] * v[0] + d[1] * v[1] + d[5] * v[2],
        d[4] * v[0] + d[5] * v[1] + d[2] * v[2],
    )


def image_of(sh, lane, v, kv, rims, springs_ref):
    k = springs_ref[6]
    k_before, k_after = shift(k, sh.pitch), shift(k, -sh.pitch)
    last = (sh.x + 1) * sh.pitch
    own = apply_block([springs_ref[f] for f in range(6)], [inner(v, m) for m in range(3)])
    rim_parts = [yz_parts(rims[0]), yz_parts(rims[1])] if rims else None
    out = []
    for m, (plain, scaled) in enumerate(zip(yz_parts(v), yz_parts(kv))):
        after = shift(k_before * (plain[1] + plain[2]) + (scaled[1] + scaled[2]), -sh.pitch)
        before = shift(k_after * (plain[1] - plain[2]) + (scaled[1] - scaled[2]), sh.pitch)
        if rims is None:
            after, before = pick(lane < last, after), pick(lane >= sh.pitch, before)
        else:
            plain_rim, scaled_rim = rim_parts[0][m], rim_parts[1][m]
            edge = k * (plain_rim[1] + plain_rim[2]) + (scaled_rim[1] + scaled_rim[2])
            after = jnp.where(lane < last, after, edge)
            edge = k * (plain_rim[1] - plain_rim[2]) + (scaled_rim[1] - scaled_rim[2])
            before = jnp.where(lane >= sh.pitch, before, edge)
        out.append(own[m] - (k * plain[0] + scaled[0] + after + before))
    return out


def level(sh):
    return lax.broadcasted_iota(jnp.int32, (sh.rows, LANES), 0) - EDGE


def ends_level(sh):
    row = lax.broadcasted_iota(jnp.int32, (4 * EDGE, LANES), 0)
    return jnp.where(row < 2 * EDGE, row, row + sh.rows - 4 * EDGE) - EDGE


def ends(value):
    return jnp.concatenate([value[: 2 * EDGE], value[value.shape[0] - 2 * EDGE :]], axis=0)


def extended_mask(sh, z):
    lane, _, across = sh.lane_grid(1)
    return ((lane < sh.used) & (across >= -1) & (across <= sh.y)) & ((z >= -1) & (z <= sh.z))


def within(sh, axis, place, size):
    index = sh.here(axis)
    low = jnp.where(index > 0, -EDGE, 0)
    high = jnp.where(index < sh.sizes[axis] - 1, size + EDGE, size)
    return (place >= low) & (place < high)


def grid_masks(sh):
    lane, along, across = sh.lane_grid(1)
    lanes = (lane < sh.used) & within(sh, 1, across, sh.y)
    rows = within(sh, 2, level(sh), sh.z)
    return (lanes & within(sh, 0, along, sh.x)) & rows, lanes & rows


def put(ref, f, value):
    ref[f, EDGE : ref.shape[1] - EDGE, :] = value


def local_solve(sh, z, residual_ref, springs_ref, v, kv, factor):
    lane, _, _ = sh.lane_grid(1)
    mask = extended_mask(sh, z)
    for m in range(3):
        factor[m] = pick(mask, relax / jnp.where(mask, springs_ref[m], 1.0))
        value = residual_ref[m] * factor[m]
        put(v[0], m, value)
        put(kv[0], m, springs_ref[6] * value)
    for sweep in range(SWEEPS - 1):
        old, new = sweep % 2, (sweep + 1) % 2
        image = image_of(sh, lane, v[old], kv[old], None, springs_ref)
        for m in range(3):
            value = inner(v[old], m) + factor[m] * (residual_ref[m] - image[m])
            put(v[new], m, value)
            put(kv[new], m, springs_ref[6] * value)
    return (SWEEPS - 1) % 2


def own_level(sh):
    return lax.broadcasted_iota(jnp.int32, (sh.z, LANES), 0)


def coords(sh, z):
    _, along, across = sh.lane_grid(z.shape[0])
    along = jnp.where(along < 0, along + sh.x, jnp.where(along < sh.x, along, along - sh.x))
    across = jnp.where(across < 0, across + sh.y, jnp.where(across < sh.y, across, across - sh.y))
    place = lambda index, size: (2 * index + 1).astype(f32) / size - 1.0
    return place(along, sh.x), place(across, sh.y), place(z, sh.z)


def cell_coords(sh):
    cell = lax.broadcasted_iota(jnp.int32, (sh.cells, sh.z), 0)
    z = lax.broadcasted_iota(jnp.int32, (sh.cells, sh.z), 1)
    x = cell // sh.y
    place = lambda index, size: (2 * index + 1).astype(f32) / size - 1.0
    return place(x, sh.x), place(cell - x * sh.y, sh.y), place(z, sh.z)


def cross(a, b):
    return (a[1] * b[2] - a[2] * b[1], a[2] * b[0] - a[0] * b[2], a[0] * b[1] - a[1] * b[0])


def fold_rows(value):
    total = value[0:8]
    for i in range(8, value.shape[0], 8):
        total = total + value[i : i + 8]
    return jnp.sum(total, axis=0, keepdims=True)


def lane_sums(rows_ref):
    ones = jnp.ones((8, LANES), f32)
    return lax.dot_general(
        ones, rows_ref[...], (((1,), (1,)), ((), ())), precision=highest, preferred_element_type=f32
    )


def coarse_sums(nodes, field, places, count, sums):
    moments = tuple(field) + cross(places, field)
    for node in range(count):
        mask = nodes == node
        for m in range(6):
            sums[node * 6 + m : node * 6 + m + 1, :] = fold_rows(pick(mask, moments[m]))


def sums_line(sh, sums, unknowns):
    flat = (sh.here(0) * sh.sizes[1] + sh.here(1)) * sh.sizes[2] + sh.here(2)
    return pltpu.roll(lane_sums(sums), lax.rem(flat * unknowns, LANES), 1)[0:1]


def coarse_solution(received, inverse_ref, values):
    unknowns, total = inverse_ref.shape
    row = lax.broadcasted_iota(jnp.int32, received.shape, 0)
    part = jnp.zeros((unknowns, LANES), f32)
    for i in range(0, total, LANES):
        owner = (i + lax.broadcasted_iota(jnp.int32, (1, LANES), 1)) // unknowns
        vector = jnp.sum(pick(row == owner, received), axis=0, keepdims=True)
        part = part + inverse_ref[:, i : i + LANES] * vector
    values[0:unknowns, :] = jnp.dot(
        part, jnp.ones((LANES, LANES), f32), precision=highest, preferred_element_type=f32
    )


def coarse_shares(sums, inverse_ref, shares):
    unknowns, total = inverse_ref.shape
    column = jnp.dot(sums[...], jnp.ones((LANES, LANES), f32), precision=highest, preferred_element_type=f32)
    for i in range(0, total, LANES):
        share = inverse_ref[:, i : i + LANES] * column[0:unknowns]
        shares[i // LANES : i // LANES + 1, :] = jnp.sum(share, axis=0, keepdims=True)


def coarse_table(sh, shares_ref, unknowns, flat, table):
    rows = shares_ref.shape[0] // sh.devices
    lane = lax.broadcasted_iota(jnp.int32, (1, LANES), 1)
    for i in range(rows):
        flat[i : i + 1, :] = jnp.sum(shares_ref[pl.ds(i, sh.devices, stride=rows), :], axis=0, keepdims=True)
    for device in range(sh.devices):
        row, place = divmod(device * unknowns, LANES)
        part = shift(flat[row : row + 1, :], -place)
        if place + unknowns > LANES:
            part = jnp.where(lane < LANES - place, part, shift(flat[row + 1 : row + 2, :], -place))
        table[device : device + 1, :] = pick(lane < unknowns, part)


def region_values(sh, table, dz):
    lane, along, across = sh.lane_grid(1)
    x = sh.here(0) + jnp.where(along < 0, -1, jnp.where(along < sh.x, 0, 1))
    y = sh.here(1) + jnp.where(across < 0, -1, jnp.where(across < sh.y, 0, 1))
    z = sh.here(2) + dz
    exists = (lane < sh.used) & (x >= 0) & (x < sh.sizes[0]) & (y >= 0) & (y < sh.sizes[1])
    exists = exists & (z >= 0) & (z < sh.sizes[2])
    device = jnp.where(exists, (x * sh.sizes[1] + y) * sh.sizes[2] + z, -1)
    owner = lax.broadcasted_iota(jnp.int32, (sh.devices, LANES), 0) == device
    return lax.dot_general(
        table[...], owner.astype(f32), (((0,), (0,)), ((), ())), precision=highest, preferred_element_type=f32
    )


def coarse_cells(nodes, places, values, count):
    cells = []
    for m in range(6):
        cell = jnp.zeros(nodes.shape, f32)
        for node in range(count):
            cell = jnp.where(nodes == float(node), values[node * 6 + m : node * 6 + m + 1, :], cell)
        cells.append(cell)
    turned = cross(cells[3:], places)
    return [cells[m] + turned[m] for m in range(3)]


def selection(sh):
    lane, along, across = sh.lane_grid(sh.cells)
    inside = (along >= 0) & (along < sh.x) & (across >= 0) & (across < sh.y)
    row = lax.broadcasted_iota(jnp.int32, (sh.cells, LANES), 0)
    return (inside & (row == along * sh.y + across)).astype(f32)


def to_lanes(value, select):
    return lax.dot_general(
        value, select, (((0,), (0,)), ((), ())), precision=highest, preferred_element_type=f32
    )


def to_cells(value, select):
    return lax.dot_general(
        select, value, (((1,), (1,)), ((), ())), precision=highest, preferred_element_type=f32
    )


def send_lines(sh, lines, slots_ref):
    here = [sh.here(axis) for axis in range(3)]
    corner = [lines[8 * i : 8 * i + 8, :] for i in range(4)]
    top, bottom = lines[32:40, :], lines[40:48, :]
    for x in range(sh.sizes[0]):
        low_high = [jnp.where(x > here[0], corner[2 + high], corner[high]) for high in range(2)]
        for y in range(sh.sizes[1]):
            column = jnp.where(y > here[1], low_high[1], low_high[0])
            for z in range(sh.sizes[2]):
                slot = jnp.where(z == here[2] + 1, top, jnp.where(z == here[2] - 1, bottom, column))
                place = 8 * ((x * sh.sizes[1] + y) * sh.sizes[2] + z)
                slots_ref[place : place + 8, :] = slot


def slot_from(sh, received_ref, step):
    place, exists = 0, None
    for axis in range(3):
        index = sh.here(axis) + step[axis]
        inside = (index >= 0) & (index < sh.sizes[axis])
        exists = inside if exists is None else exists & inside
        place = place * sh.sizes[axis] + jnp.clip(index, 0, sh.sizes[axis] - 1)
    return scale(exists, received_ref[pl.ds(pl.multiple_of(place * 8, 8), 8), :])


def repeat_twice(count):
    row = lax.broadcasted_iota(jnp.int32, (2 * count, count), 0)
    column = lax.broadcasted_iota(jnp.int32, (2 * count, count), 1)
    return ((row >= 2 * column) & (row < 2 * column + 2)).astype(f32)


def ring(size_x, size_y, rows):
    row = lax.broadcasted_iota(jnp.int32, (rows, LANES), 0)
    sides_x, both = 2 * size_y, 2 * size_y + 2 * size_x
    corner = row - both
    x = jnp.where(row < size_y, -1, size_x)
    x = jnp.where(row < sides_x, x, jnp.where(row < sides_x + size_x, row - sides_x, row - sides_x - size_x))
    x = jnp.where(row < both, x, jnp.where(corner < 2, -1, size_x))
    y = jnp.where(row < size_y, row, row - size_y)
    y = jnp.where(row < sides_x, y, jnp.where(row < sides_x + size_x, -1, size_y))
    y = jnp.where(row < both, y, jnp.where((corner == 0) | (corner == 2), -1, size_y))
    return x, y, (row < sides_x) | (row >= both), row < both + 4


def face_shape(sh, label_x, label_y):
    rows = max(4 * sh.x + label_x, 4 * sh.y + label_y)
    return (-(-rows // 8) * 8, LANES)


def pack_faces(sh, natural_ref, stiff, label_x, label_y, x_refs, y_refs):
    even_x, even_y = sh.here(0) % 2 == 0, sh.here(1) % 2 == 0

    def face(at, count, stride, label_at, label_count, label_stride):
        rows = [natural_ref[m, pl.ds(at, count, stride=stride), :] for m in range(4)]
        return rows, stiff[pl.ds(label_at, label_count, stride=label_stride), :]

    above = face(sh.cells - sh.y, sh.y, 1, (label_x - 1) * label_y, label_y, 1)
    below = face(0, sh.y, 1, 0, label_y, 1)
    for refs, links, even, above, below in (
        (x_refs, sh.x_links, even_x, above, below),
        (
            y_refs,
            sh.y_links,
            even_y,
            face(sh.y - 1, sh.x, sh.y, label_y - 1, label_x, label_y),
            face(0, sh.x, sh.y, 0, label_x, label_y),
        ),
    ):
        for i, ref in enumerate(refs):
            ref[...] = jnp.zeros(ref.shape, f32)
            count = above[0][0].shape[0]
            for m in range(4):
                ref[m * count : (m + 1) * count, :] = pair(links, even, above[0][m], below[0][m])[i]
            labels, length = above[1].shape
            ref[4 * count : 4 * count + labels, 0:length] = pair(links, even, above[1], below[1])[i]


def merge_start(sh, refs, x_refs, y_refs, received_ref, sizes, cells, labels):
    residual, nodes, stiff, stiff_rim = refs
    label_x, label_y, label_z = sizes
    lane, along, across = sh.lane_grid(1)
    inside = lane < sh.used
    last = (sh.x + 1) * sh.pitch
    x_mask = {-1: lane < sh.pitch, 0: (lane >= sh.pitch) & (lane < last), 1: (lane >= last) & inside}
    y_mask = {-1: across < 0, 0: (across >= 0) & (across < sh.y), 1: across >= sh.y}
    cells[...] = jnp.zeros(cells.shape, f32)
    labels[...] = jnp.zeros(labels.shape, f32)
    count, label_count = cells.shape[1], labels.shape[0]
    at = label_at = 0
    for axis, face_refs, size, label_size in ((0, x_refs, sh.y, label_y), (1, y_refs, sh.x, label_x)):
        for message in sides(sh, axis, [ref[...] for ref in face_refs]):
            for m in range(4):
                cells[m, at : at + size, :] = message[m * size : (m + 1) * size]
            labels[label_at : label_at + label_size, :] = message[4 * size : 4 * size + label_size, 0:label_z]
            at, label_at = at + size, label_at + label_size
    for dx, dy in ((-1, -1), (-1, 1), (1, -1), (1, 1)):
        slot = slot_from(sh, received_ref, (dx, dy, 0))
        for m, row in enumerate((0, 1, 2, 5)):
            cells[m, at : at + 1, :] = slot[row : row + 1]
        labels[label_at : label_at + 1, :] = slot[3:4, 0:label_z]
        at, label_at = at + 1, label_at + 1
    x, y, _, valid = ring(sh.x, sh.y, count)
    place = (valid & inside & (along == x) & (across == y)).astype(f32)
    own = slice(EDGE, EDGE + sh.z)
    tall_own = slice(2 * EDGE, 2 * EDGE + sh.z)
    for m in range(3):
        residual[m, own, :] += to_lanes(cells[m], place)
    nodes[own, :] += to_lanes(cells[3], place)
    by_z = lax.dot_general(
        repeat_twice(label_z), labels[...], (((1,), (1,)), ((), ())), precision=highest, preferred_element_type=f32
    )
    x, y, at_x, valid = ring(label_x, label_y, label_count)
    match = valid & inside & ((along >> 1) == x) & ((across >> 1) == y)
    columns = jnp.dot(by_z, (match & at_x).astype(f32), precision=highest, preferred_element_type=f32)
    stiff_rim[0, tall_own, :] = columns
    columns = columns + jnp.dot(by_z, (match & ~at_x).astype(f32), precision=highest, preferred_element_type=f32)
    stiff[0, tall_own, :] += columns
    for dz in (-1, 1):
        main = edge = jnp.zeros((8, LANES), f32)
        for dx in (-1, 0, 1):
            for dy in (-1, 0, 1):
                slot = slot_from(sh, received_ref, (dx, dy, dz))
                mask = x_mask[dx] & y_mask[dy]
                main = main + pick(mask, shift(slot, dx * sh.x * sh.pitch + dy * sh.y))
                if dx:
                    edge = edge + pick(mask, shift(slot, dx * (sh.x - 1) * sh.pitch + dy * sh.y))
        near = EDGE + sh.z if dz > 0 else EDGE - 1
        for m in range(3):
            residual[m, near : near + 1, :] = main[m : m + 1]
        nodes[near : near + 1, :] = main[5:6]
        for row in (EDGE + near, EDGE + near + dz):
            stiff[0, row : row + 1, :] = main[3:4]
            stiff_rim[0, row : row + 1, :] = edge[3:4]


def call(kernel, name, outs, ins, scratch=(), remote_ins=False):
    space = pltpu.HBM if remote_ins else pltpu.VMEM
    return pl.pallas_call(
        kernel,
        out_shape=[jax.ShapeDtypeStruct(shape, f32) for shape in outs],
        in_specs=[pl.BlockSpec(memory_space=space) for _ in ins],
        out_specs=[pl.BlockSpec(memory_space=pltpu.VMEM) for _ in outs],
        scratch_shapes=[pltpu.VMEM(shape, f32) if isinstance(shape, tuple) else shape for shape in scratch],
        compiler_params=pltpu.CompilerParams(vmem_limit_bytes=(62 if remote_ins else 48) * 1024 * 1024),
        name=name,
    )(*ins)


def permutation(sizes, moves):
    def partner(axis, link, index):
        size = sizes[axis]
        other = index ^ 1 if link == 0 else index + (1 if index % 2 else -1)
        if 0 <= other < size:
            return other
        return size - 1 - index if axis == 2 and size % 2 == 0 else index

    pairs = []
    for x in range(sizes[0]):
        for y in range(sizes[1]):
            for z in range(sizes[2]):
                place = [x, y, z]
                goal = [partner(a, moves[a], place[a]) if a in moves else place[a] for a in range(3)]
                if goal == place and 0 not in moves and sizes[0] % 2 == 0:
                    goal[0] = partner(0, 0, x)
                flat = [(p[0] * sizes[1] + p[1]) * sizes[2] + p[2] for p in (place, goal)]
                pairs.append(tuple(flat))
    return pairs


def send(sh, value, moves):
    return lax.ppermute(value, AXES, permutation(sh.sizes, moves))


def send_z(sh, messages):
    return [send(sh, message, {2: link}) for link, message in enumerate(messages)]


def send_faces(sh, x_messages, y_messages):
    from_y = [send(sh, message, {1: link}) for link, message in enumerate(y_messages)]
    from_x = [send(sh, message, {0: link}) for link, message in enumerate(x_messages)]
    return from_y, from_x


def to_all(slots):
    return lax.all_to_all(slots, AXES, 0, 0, tiled=True)


def exchange(sh, ex, name, field, z_messages):
    from_z = send_z(sh, z_messages)

    corners = sh.x_links * sh.y_links

    def packer(*refs):
        take = Taker(refs)
        field_ref, z_refs = take.one(), take(sh.z_links)
        x_refs, y_refs, corner_refs, scratch = take(sh.x_links), take(sh.y_links), take(corners), take.one()
        merge_z(sh, ex, field_ref, z_refs, scratch, 0)
        pack_xy(sh, ex, scratch, x_refs, y_refs, corner_refs)

    plane = (sh.rows, LANES)
    messages = call(
        packer,
        name,
        [plane] * sh.x_links
        + [folded_shape(sh, ex.fields * ex.layers)] * sh.y_links
        + [folded_shape(sh, ex.layers)] * corners,
        [field] + from_z,
        [(ex.fields,) + plane],
    )
    take = Taker(messages)
    x_messages, y_messages = take(sh.x_links), take(sh.y_links)
    from_y, straight = send_faces(sh, x_messages, y_messages)
    from_x = []
    for link in range(sh.x_links):
        from_x.append(straight[link])
        from_x.extend(send(sh, take.one(), {0: link, 1: other}) for other in range(sh.y_links))
    return from_z, from_y, from_x


class Taker:
    def __init__(self, refs):
        self.refs, self.at = refs, 0

    def __call__(self, count):
        self.at += count
        return self.refs[self.at - count : self.at]

    def one(self):
        return self(1)[0]


def merge_all(sh, ex, take, scratch, rim, guard):
    field = take.one()
    from_z, from_y = take(sh.z_links), take(sh.y_links)
    from_x = take(sh.x_links * (1 + sh.y_links))
    merge_z(sh, ex, field, from_z, scratch, guard)
    merge_xy(sh, ex, scratch, rim, guard, from_y, from_x)


def body(right_side, phase_labels, phase_moduli, coarse_nodes, coarse_inverse):
    sizes = tuple(lax.axis_size(axis) for axis in AXES)
    _, size_x, size_y, size_z = right_side.shape
    sh = Shape(size_x, size_y, size_z, phase_moduli.shape[0], sizes)
    unknowns = coarse_inverse.shape[0]
    node_count = unknowns // 6
    sum_rows = -(-unknowns // 8) * 8
    share_rows = coarse_inverse.shape[1] // LANES
    own = slice(EDGE, EDGE + sh.z)
    plane = (sh.rows, LANES)
    fields = (3,) + plane
    tall = (3, sh.tall, LANES)
    slots = (sh.devices, LANES)
    z_shape = lambda ex: [(8 * ex.fields, LANES)] * sh.z_links
    natural = right_side.reshape(3, sh.cells, sh.z)
    nodes_natural = coarse_nodes.reshape(sh.cells, sh.z)
    label_x, label_y, label_z = phase_labels.shape

    def block_places():
        lane, along, across = sh.lane_grid(label_x * label_y)
        inside = (along >= 0) & (along < sh.x) & (across >= 0) & (across < sh.y)
        block = lax.broadcasted_iota(jnp.int32, along.shape, 0)
        return (inside & (block == (along >> 1) * label_y + (across >> 1))).astype(f32)

    def end_layers(values, places):
        length = values.shape[1]
        row = lax.broadcasted_iota(jnp.int32, (8, length), 0)
        at = lax.broadcasted_iota(jnp.int32, (8, length), 1)
        ends = ((row == 0) & (at == length - 1)) | ((row == 1) & (at == 0))
        return jnp.dot(to_cells(values, ends.astype(f32)), places, precision=highest, preferred_element_type=f32)

    def begin(natural_in, labels_in, moduli_in, nodes_in, stiff, slots_ref, *rest):
        x_refs, y_refs = rest[: sh.x_links], rest[sh.x_links : sh.x_links + sh.y_links]
        natural_ref, labels_ref, moduli_ref, nodes_ref, sems, sums, lines = rest[sh.x_links + sh.y_links :]
        pairs = ((natural_in, natural_ref.at[0:3]), (labels_in, labels_ref), (moduli_in, moduli_ref), (nodes_in, nodes_ref))
        copies = [pltpu.make_async_copy(a, b, sems.at[i]) for i, (a, b) in enumerate(pairs)]
        for copy in copies:
            copy.start()
        sums[...] = jnp.zeros(sums.shape, f32)
        lines[...] = jnp.zeros(lines.shape, f32)
        for copy in copies:
            copy.wait()
        for i in range(label_x):
            labels = labels_ref[i]
            moduli = jnp.zeros(labels.shape, f32)
            for phase in range(sh.phases):
                moduli = jnp.where(labels == phase, moduli_ref[phase], moduli)
            stiff[i * label_y : (i + 1) * label_y, :] = moduli
        natural_ref[3] = nodes_ref[...].astype(f32) + 1.0
        cells = [natural_ref[m] for m in range(3)]
        coarse_sums(nodes_ref[...], cells, cell_coords(sh), node_count, sums)
        line = sums_line(sh, sums, unknowns)
        for i, (cell, block) in enumerate(
            (
                (0, 0),
                (sh.y - 1, label_y - 1),
                ((sh.x - 1) * sh.y, (label_x - 1) * label_y),
                (sh.cells - 1, label_x * label_y - 1),
            )
        ):
            for m in range(3):
                lines[8 * i + m : 8 * i + m + 1, :] = natural_ref[m, cell : cell + 1, :]
            lines[8 * i + 3 : 8 * i + 4, 0:label_z] = stiff[block : block + 1, :]
            lines[8 * i + 5 : 8 * i + 6, :] = natural_ref[3, cell : cell + 1, :]
        select = selection(sh)
        layers = [end_layers(natural_ref[m], select) for m in range(4)] + [end_layers(stiff[...], block_places())]
        for i in range(2):
            for layer, row in zip(layers, (0, 1, 2, 5, 3)):
                lines[8 * (4 + i) + row : 8 * (4 + i) + row + 1, :] = layer[i : i + 1]
        for i in range(6):
            lines[8 * i + 4 : 8 * i + 5, :] = line
        send_lines(sh, lines, slots_ref)
        pack_faces(sh, natural_ref, stiff, label_x, label_y, x_refs, y_refs)

    stiff_blocks, lines, *messages = call(
        begin,
        "begin",
        [(label_x * label_y, label_z), (8 * sh.devices, LANES)]
        + [face_shape(sh, label_x, label_y)] * (sh.x_links + sh.y_links),
        [natural, phase_labels, phase_moduli, nodes_natural],
        [
            (4, sh.cells, sh.z),
            pltpu.VMEM(phase_labels.shape, jnp.int32),
            pltpu.SMEM(phase_moduli.shape, f32),
            pltpu.VMEM(nodes_natural.shape, jnp.int32),
            pltpu.SemaphoreType.DMA((4,)),
            (LANES, LANES),
            (48, LANES),
        ],
        remote_ins=True,
    )

    def spread(natural_ref, nodes_ref, stiff, field_ref, lanes_ref):
        select = selection(sh)
        field_ref[...] = jnp.zeros(field_ref.shape, f32)
        for m in range(3):
            field_ref[m, own, :] = to_lanes(natural_ref[m], select)
        by_z = lax.dot_general(
            repeat_twice(label_z), stiff[...], (((1,), (1,)), ((), ())), precision=highest, preferred_element_type=f32
        )
        field_ref[3, own, :] = jnp.dot(by_z, block_places(), precision=highest, preferred_element_type=f32)
        lanes_ref[...] = to_lanes(nodes_ref[...].astype(f32) + 1.0, select) - 1.0

    start_field, nodes = call(
        spread, "spread", [(4,) + plane, (sh.z, LANES)], [natural, nodes_natural, stiff_blocks]
    )
    from_y, from_x = send_faces(sh, messages[: sh.x_links], messages[sh.x_links :])
    lines = to_all(lines)

    short = (3, 6 * EDGE, LANES)
    short_fields = (3, 4 * EDGE, LANES)
    solve_scratch = [tall] * 4 + [fields]
    short_scratch = [short] * 4 + [short_fields]

    def end_rows(ref):
        def rows(f, start, count):
            place = start + EDGE if start < 2 * EDGE else start - sh.rows + 5 * EDGE
            return ref[f, place : place + count, :]

        return rows

    def first_ends(*refs):
        take = Taker(refs)
        field_ref = take.one()
        y_refs, x_refs = take(sh.y_links), take(sh.x_links)
        nodes_ref, lines_ref, inverse_ref = take(3)
        residual, wide_nodes, stiffness_ref, values = take(4)
        z_refs = take(sh.z_links)
        stiff, stiff_rim, cells, labels, short_stiff, short_rim, some_residual, springs = take(8)
        v0, v1, kv0, kv1, factor = take(5)
        clear_guards(sh, (stiff, stiff_rim, short_stiff, short_rim, v0, v1, kv0, kv1))
        residual[...] = field_ref[0:3]
        put(stiff, 0, field_ref[3])
        put(stiff_rim, 0, jnp.zeros(plane, f32))
        sizes = phase_labels.shape
        wide_nodes[...] = jnp.zeros(plane, f32)
        wide_nodes[own, :] = nodes_ref[...] + 1.0
        merge_start(sh, (residual, wide_nodes, stiff, stiff_rim), x_refs, y_refs, lines_ref, sizes, cells, labels)
        wide_nodes[...] = wide_nodes[...] - 1.0
        stiffness_ref[0] = inner(stiff, 0)
        stiffness_ref[1] = inner(stiff_rim, 0)
        coarse_solution(lines_ref[pl.ds(4, sh.devices, stride=8), :], inverse_ref, values)
        lane, _, _ = sh.lane_grid(1)
        put(short_stiff, 0, ends(stiffness_ref[0]))
        put(short_rim, 0, ends(stiffness_ref[1]))
        for f, entry in enumerate(own_block(sh, lane, (short_stiff, short_rim))):
            springs[f] = entry
        springs[6] = inner(short_stiff, 0)
        for m in range(3):
            some_residual[m] = ends(residual[m])
        index = local_solve(sh, ends_level(sh), some_residual, springs, (v0, v1), (kv0, kv1), factor)
        solution = (v0, v1)[index]
        z = lax.broadcasted_iota(jnp.int32, (2 * EDGE, LANES), 0)
        z = jnp.where(z < EDGE, z, z + sh.z - 2 * EDGE)
        some_nodes = jnp.concatenate([nodes_ref[0:EDGE, :], nodes_ref[sh.z - EDGE : sh.z, :]], axis=0)
        added = coarse_cells(some_nodes, coords(sh, z), values, node_count)
        for m in range(3):
            solution[m, 2 * EDGE : 4 * EDGE, :] += pick(some_nodes >= 0.0, added[m])
        pack_z(sh, DEEP, end_rows(solution), z_refs)

    residual, wide_nodes, stiffness, values, *z_messages = call(
        first_ends,
        "first_ends",
        [fields, plane, (2,) + plane, (sum_rows, LANES)] + z_shape(DEEP),
        [start_field, *from_y, *from_x, nodes, lines, coarse_inverse],
        [(1, sh.tall, LANES)] * 2
        + [
            (4, 8 * -(-(2 * sh.x + 2 * sh.y + 4) // 8), LANES),
            (8 * -(-(2 * label_x + 2 * label_y + 4) // 8), label_z),
        ]
        + [(1, 6 * EDGE, LANES)] * 2
        + [short_fields, (7, 4 * EDGE, LANES)]
        + short_scratch,
    )

    def first_solve(residual_ref, stiffness_ref, values, nodes_ref, solution_ref, springs_ref, *rest):
        stiff, stiff_rim, v0, v1, kv0, kv1, factor = rest
        clear_guards(sh, (stiff, stiff_rim, v0, v1, kv0, kv1))
        put(stiff, 0, stiffness_ref[0])
        put(stiff_rim, 0, stiffness_ref[1])
        springs_ref[6] = stiffness_ref[0]
        springs_ref[7] = stiffness_ref[1]
        lane, _, _ = sh.lane_grid(1)
        for f, entry in enumerate(own_block(sh, lane, (stiff, stiff_rim))):
            springs_ref[f] = entry
        index = local_solve(sh, level(sh), residual_ref, springs_ref, (v0, v1), (kv0, kv1), factor)
        for m in range(3):
            solution_ref[m] = inner((v0, v1)[index], m)
        added = coarse_cells(nodes_ref[...], coords(sh, own_level(sh)), values, node_count)
        for m in range(3):
            solution_ref[m, own, :] += pick(nodes_ref[...] >= 0.0, added[m])

    solved, springs = call(
        first_solve,
        "first_solve",
        [fields, (8,) + plane],
        [residual, stiffness, values, nodes],
        [(1, sh.tall, LANES)] * 2 + solve_scratch,
    )
    from_z, from_y, from_x = exchange(sh, DEEP, "deep", solved, z_messages)

    def first_image(*refs):
        take = Taker(refs)
        merging = take(1 + sh.z_links + sh.y_links + sh.x_links * (1 + sh.y_links))
        nodes_ref, springs_ref, inverse_ref = take(3)
        search_ref, image_ref, slots_ref = take(3)
        v, rim, kv, k_rim, sums, shares = take(6)
        clear_guards(sh, (v, rim, kv, k_rim))
        merge_all(sh, DEEP, Taker(merging), v, rim, EDGE)
        lane, _, _ = sh.lane_grid(1)

        in_grid, in_rim = grid_masks(sh)
        for m in range(3):
            value = pick(in_grid, inner(v, m))
            put(v, m, value)
            search_ref[m] = value
            put(kv, m, springs_ref[6] * value)
            value = pick(in_rim, inner(rim, m))
            put(rim, m, value)
            put(k_rim, m, springs_ref[7] * value)
        image = image_of(sh, lane, v, kv, (rim, k_rim), springs_ref)
        keep = in_grid & extended_mask(sh, level(sh))
        for m in range(3):
            image_ref[m] = pick(keep, image[m])
        sums[...] = jnp.zeros(sums.shape, f32)
        field = [image_ref[m, own, :] for m in range(3)]
        coarse_sums(nodes_ref[...], field, coords(sh, own_level(sh)), node_count, sums)
        coarse_shares(sums, inverse_ref, shares)
        for device in range(sh.devices):
            slots_ref[device * share_rows : (device + 1) * share_rows, :] = shares[0:share_rows, :]

    search, image, shares = call(
        first_image,
        "first_image",
        [fields, fields, (sh.devices * share_rows, LANES)],
        [solved, *from_z, *from_y, *from_x, nodes, springs, coarse_inverse],
        [tall] * 4 + [(LANES, LANES), (8 * -(-share_rows // 8), LANES)],
    )
    shares = to_all(shares.reshape(sh.devices, 1, share_rows * LANES)).reshape(shares.shape)

    def second_solve(image_ref, springs_ref, local_ref, v0, v1, kv0, kv1, factor):
        clear_guards(sh, (v0, v1, kv0, kv1))
        index = local_solve(sh, level(sh), image_ref, springs_ref, (v0, v1), (kv0, kv1), factor)
        for m in range(3):
            local_ref[m] = inner((v0, v1)[index], m)

    def second_ends(image_ref, springs_ref, *refs):
        take = Taker(refs)
        z_refs = take(sh.z_links)
        some_residual, springs, v0, v1, kv0, kv1, factor = take(7)
        clear_guards(sh, (v0, v1, kv0, kv1))
        for m in range(3):
            some_residual[m] = ends(image_ref[m])
        for f in range(7):
            springs[f] = ends(springs_ref[f])
        index = local_solve(sh, ends_level(sh), some_residual, springs, (v0, v1), (kv0, kv1), factor)
        pack_z(sh, NEAR, end_rows((v0, v1)[index]), z_refs)

    z_messages = call(
        second_ends,
        "second_ends",
        z_shape(NEAR),
        [image, springs],
        [short_fields, (7, 4 * EDGE, LANES)] + short_scratch,
    )
    (solved,) = call(second_solve, "second_solve", [fields], [image, springs], solve_scratch)
    from_z, from_y, from_x = exchange(sh, NEAR, "near", solved, z_messages)

    def second_image(*refs):
        take = Taker(refs)
        merging = take(1 + sh.z_links + sh.y_links + sh.x_links * (1 + sh.y_links))
        nodes_ref, springs_ref, start_ref, search_ref, first_ref, wide_nodes, shares_ref = take(7)
        second_ref, image_ref, slots_ref = take(3)
        v, kv, sums, flat, table, values = take(6)
        clear_guards(sh, (v, kv))
        merge_all(sh, NEAR, Taker(merging), v, None, EDGE)
        lane, _, _ = sh.lane_grid(1)
        in_grid, _ = grid_masks(sh)
        for m in range(3):
            put(v, m, pick(in_grid, inner(v, m)))
        coarse_table(sh, shares_ref, unknowns, flat, table)
        last = lax.broadcasted_iota(jnp.int32, (1, LANES), 0) + sh.z - 1
        for dz, first, z in ((0, EDGE, own_level(sh)), (-1, EDGE - 1, last), (1, EDGE + sh.z, last - sh.z + 1)):
            values[...] = region_values(sh, table, dz)
            rows = slice(first, first + z.shape[0])
            added = coarse_cells(wide_nodes[rows, :], coords(sh, z), values, node_count)
            for m in range(3):
                v[m, EDGE + rows.start : EDGE + rows.stop, :] += added[m]
        for m in range(3):
            value = inner(v, m)
            second_ref[m] = value
            put(kv, m, springs_ref[6] * value)
        image = image_of(sh, lane, v, kv, None, springs_ref)
        for m in range(3):
            image_ref[m] = image[m]
        valid = nodes_ref[...] >= 0.0
        names = ("r", "z", "w", "q", "v")
        sources = (start_ref, search_ref, first_ref, second_ref, image_ref)
        get = {name: [source[m, own, :] for m in range(3)] for name, source in zip(names, sources)}
        sums[...] = jnp.zeros(sums.shape, f32)
        for i, (a, b) in enumerate(("rz", "zw", "rq", "wq", "zv", "qv")):
            product = sum(get[a][m] * get[b][m] for m in range(3))
            sums[i : i + 1, :] = fold_rows(pick(valid, product))
        slots_ref[...] = jnp.broadcast_to(lane_sums(sums)[0:1], slots_ref.shape)

    second, second_image_field, sums = call(
        second_image,
        "second_image",
        [fields, fields, slots],
        [solved, *from_z, *from_y, *from_x, nodes, springs, start_field, search, image, wide_nodes, shares],
        [tall] * 2
        + [(LANES, LANES), (8 * -(-share_rows // 8) + 8, LANES), (sh.devices, LANES), (LANES, LANES)],
    )
    totals = to_all(sums)

    def turn(search_ref, first_ref, second_ref, image_ref, out_ref):
        select = selection(sh)
        for i, ref in enumerate((search_ref, first_ref, second_ref, image_ref)):
            for m in range(3):
                out_ref[i, m] = to_cells(ref[m, own, :], select)

    (turned,) = call(turn, "turn", [(4,) + natural.shape], [search, image, second, second_image_field])

    def finish(totals_ref, natural_ref, turned_ref, field_ref, residual_ref):
        total = jnp.sum(totals_ref[...], axis=0, keepdims=True)
        rz, zw, rq, wq, zv, qv = [total[:, i : i + 1] for i in range(6)]
        step0 = rz / zw
        rho = rz - step0 * zw - step0 * rq + step0 * step0 * wq
        grow = 1.0 + rho / rz
        curvature = grow * grow * zw - grow * step0 * (zv + wq) + step0 * step0 * qv
        step1 = rho / curvature
        first = step0 + step1 * grow
        second = step0 * step1
        for m in range(3):
            field_ref[m] = first * turned_ref[0, m] - second * turned_ref[2, m]
            residual_ref[m] = natural_ref[m] - (first * turned_ref[1, m] - second * turned_ref[3, m])

    solution_field, residual = call(
        finish, "finish", [natural.shape, natural.shape], [totals, natural, turned]
    )
    return solution_field.reshape(right_side.shape), residual.reshape(right_side.shape)


def solution(mesh):
    in_specs = (
        P(None, "gx", "gy", "gz"),
        P("gx", "gy", "gz"),
        P(),
        P("gx", "gy", "gz"),
        P(("gx", "gy", "gz"), None),
    )
    out_specs = (P(None, "gx", "gy", "gz"), P(None, "gx", "gy", "gz"))
    return jax.shard_map(body, mesh=mesh, in_specs=in_specs, out_specs=out_specs, check_vma=False)
```

```python
import jax
import jax.numpy as jnp
from jax import lax
from jax.experimental import pallas as pl
from jax.experimental.pallas import tpu as pltpu
from jax.sharding import PartitionSpec as P

AXES = ("gx", "gy", "gz")
SWEEPS = 4
relax = 0.6
highest = lax.Precision.HIGHEST
f32 = jnp.float32
LANES = 128
EDGE = 8

ALONG1, ACROSS1 = 0.75, 0.5
ALONG2, ACROSS2, MIXED2 = 0.3125, 0.25, 0.0625
SAME3, MIXED3 = 7.0 / 36.0, 1.0 / 36.0
TOTAL = 2 * ALONG1 + 4 * ACROSS1 + 8 * ALONG2 + 4 * ACROSS2 + 8 * SAME3


class Exchange:
    def __init__(self, fields, layers, up, down):
        self.fields, self.layers, self.up, self.down = fields, layers, up, down


DEEP = Exchange(3, 3, -2, -1)
NEAR = Exchange(3, 2, -1, -1)


class Shape:
    def __init__(self, size_x, size_y, size_z, phases, mesh_sizes):
        self.x, self.y, self.z = size_x, size_y, size_z
        self.pitch = size_y + 4
        self.used = (size_x + 2) * self.pitch
        assert self.used <= LANES
        self.rows = size_z + 2 * EDGE
        self.tall = self.rows + 2 * EDGE
        self.phases = phases
        self.sizes = mesh_sizes
        self.devices = mesh_sizes[0] * mesh_sizes[1] * mesh_sizes[2]
        self.cells = size_x * size_y
        self.links = [1 if n <= 2 else 2 for n in mesh_sizes]
        self.x_links, self.y_links, self.z_links = self.links

    def lane_grid(self, rows):
        lane = lax.broadcasted_iota(jnp.int32, (rows, LANES), 1)
        column = jnp.zeros_like(lane)
        for j in range(1, self.x + 2):
            column = column + (lane >= j * self.pitch).astype(jnp.int32)
        offset = lane - column * self.pitch
        return lane, column - 1, offset - 2

    def here(self, axis):
        return lax.axis_index(AXES[axis])


def shift(value, amount):
    amount = amount % LANES
    return value if amount == 0 else pltpu.roll(value, amount, 1)


def pick(mask, value):
    return jnp.where(mask, value, 0.0)


def scale(flag, value):
    return value * flag.astype(f32)


def pair(links, even, upward, downward):
    first = jnp.where(even, upward, downward)
    return (first,) if links == 1 else (first, jnp.where(even, downward, upward))


def sides(sh, axis, received):
    index, size = sh.here(axis), sh.sizes[axis]
    even = index % 2 == 0
    first = received[0]
    second = received[1] if len(received) > 1 else jnp.zeros_like(first)
    below = jnp.where(even, second, first)
    above = jnp.where(even, first, second)
    return scale(index > 0, below), scale(index < size - 1, above)


def lane_range(lane, start, count):
    return (lane >= start) & (lane < start + count)


def pack_z(sh, ex, source, out_refs):
    even = sh.here(2) % 2 == 0
    zero = jnp.zeros((8 - ex.layers, LANES), f32)
    for f in range(ex.fields):
        upward = source(f, EDGE + sh.z + ex.up, ex.layers)
        downward = source(f, EDGE + ex.down, ex.layers)
        for ref, message in zip(out_refs, pair(sh.z_links, even, upward, downward)):
            ref[8 * f : 8 * f + ex.layers, :] = message
            ref[8 * f + ex.layers : 8 * f + 8, :] = zero


def merge_z(sh, ex, field_ref, received_refs, scratch, guard):
    below, above = sides(sh, 2, [ref[...] for ref in received_refs])
    for f in range(ex.fields):
        scratch[f, guard : guard + sh.rows, :] = field_ref[f]
        low = guard + EDGE + ex.up
        high = guard + EDGE + sh.z + ex.down
        scratch[f, low : low + ex.layers, :] += below[8 * f : 8 * f + ex.layers]
        scratch[f, high : high + ex.layers, :] += above[8 * f : 8 * f + ex.layers]


def fold(sh, value, layers, start=None):
    folds = sh.pitch // layers
    height = -(-sh.rows // (8 * folds)) * 8
    lane, _, across = sh.lane_grid(1)
    total = jnp.zeros((height, LANES), f32)
    for i, first in enumerate(range(0, sh.rows, height)):
        part = value[first : first + height]
        if start is not None:
            part = pick((lane < sh.used) & lane_range(across, start, layers), part)
        part = shift(part, i * layers - (0 if start is None else start + 2))
        if part.shape[0] < height:
            part = jnp.concatenate([part, jnp.zeros((height - part.shape[0], LANES), f32)], axis=0)
        total = total + part
    return total


def folded_shape(sh, layers):
    return (-(-sh.rows // (8 * (sh.pitch // layers))) * 8, LANES)


def unfold(sh, message, layers, start):
    height = message.shape[0]
    lane, _, across = sh.lane_grid(1)
    mask = (lane < sh.used) & lane_range(across, start, layers)
    parts = []
    for i, first in enumerate(range(0, sh.rows, height)):
        part = message[0 : min(height, sh.rows - first)]
        parts.append(pick(mask, shift(part, start + 2 - i * layers)))
    return jnp.concatenate(parts, axis=0) if len(parts) > 1 else parts[0]


def pack_xy(sh, ex, scratch, x_refs, y_refs, corner_refs):
    rows = sh.rows
    lane, _, across = sh.lane_grid(1)
    even_x, even_y = sh.here(0) % 2 == 0, sh.here(1) % 2 == 0
    span = ex.layers * sh.pitch
    x_up = x_down = y_up = y_down = jnp.zeros((rows, LANES), f32)
    inside = lane < sh.used
    y_above, y_below = sh.y + ex.up, ex.down
    for f in range(ex.fields):
        value = scratch[f]
        start = (sh.x + ex.up + 1) * sh.pitch
        x_up = x_up + shift(pick(lane_range(lane, start, span), value), f * span - start)
        start = (ex.down + 1) * sh.pitch
        x_down = x_down + shift(pick(lane_range(lane, start, span), value), f * span - start)
        mask = inside & lane_range(across, y_above, ex.layers)
        y_up = y_up + shift(pick(mask, value), f * ex.layers - y_above - 2)
        mask = inside & lane_range(across, y_below, ex.layers)
        y_down = y_down + shift(pick(mask, value), f * ex.layers - y_below - 2)
    packed = ex.fields * ex.layers
    y_up, y_down = fold(sh, y_up, packed), fold(sh, y_down, packed)
    for ref, message in zip(y_refs, pair(sh.y_links, even_y, y_up, y_down)):
        ref[...] = message
    for i, message in enumerate(pair(sh.x_links, even_x, x_up, x_down)):
        x_refs[i][...] = message
        upward, downward = fold(sh, message, ex.layers, y_above), fold(sh, message, ex.layers, y_below)
        for j, corner in enumerate(pair(sh.y_links, even_y, upward, downward)):
            corner_refs[i * sh.y_links + j][...] = corner


def merge_xy(sh, ex, scratch, rim, guard, y_refs, x_refs):
    lane, _, across = sh.lane_grid(1)
    inside = lane < sh.used
    low_mask = inside & lane_range(across, ex.up, ex.layers)
    high_mask = inside & lane_range(across, sh.y + ex.down, ex.layers)
    span = ex.layers * sh.pitch
    packed = ex.fields * ex.layers
    below_y, above_y = [unfold(sh, value, packed, -2) for value in sides(sh, 1, [ref[...] for ref in y_refs])]
    per_link = 1 + sh.y_links
    sums = []
    for link in range(sh.x_links):
        straight, diagonal = x_refs[link * per_link], x_refs[link * per_link + 1 : (link + 1) * per_link]
        total = straight[...]
        below, above = sides(sh, 1, [ref[...] for ref in diagonal])
        total = total + unfold(sh, below, ex.layers, ex.up)
        sums.append(total + unfold(sh, above, ex.layers, sh.y + ex.down))
    below_x, above_x = sides(sh, 0, sums)
    first = 1 if ex.up == -2 else 0
    last = ex.layers - 1 if ex.down + ex.layers == 2 else ex.layers
    for f in range(ex.fields):
        addend = pick(low_mask, shift(below_y, ex.up + 2 - ex.layers * f))
        addend = addend + pick(high_mask, shift(above_y, sh.y + ex.down + 2 - ex.layers * f))
        start = (ex.up + first + 1) * sh.pitch
        count = (ex.layers - first) * sh.pitch
        moved = shift(below_x, start - f * span - first * sh.pitch)
        addend = addend + pick(lane_range(lane, start, count), moved)
        start = (sh.x + ex.down + 1) * sh.pitch
        moved = shift(above_x, start - f * span)
        addend = addend + pick(lane_range(lane, start, last * sh.pitch), moved)
        scratch[f, guard : guard + sh.rows, :] += addend
        if rim is not None:
            low = pick(lane_range(lane, 0, sh.pitch), shift(below_x, -f * span))
            start = (sh.x + 1) * sh.pitch
            moved = shift(above_x, start - f * span - last * sh.pitch)
            high = pick(lane_range(lane, start, sh.pitch), moved)
            rim[f, guard : guard + sh.rows, :] = low + high


def clear_guards(sh, refs):
    for ref in refs:
        for f in range(ref.shape[0]):
            ref[f, :EDGE, :] = jnp.zeros((EDGE, LANES), f32)
            ref[f, ref.shape[1] - EDGE :, :] = jnp.zeros((EDGE, LANES), f32)


def inner(ref, f):
    return ref[f, EDGE : ref.shape[1] - EDGE, :]


def z_stage(ref, f):
    end = ref.shape[1] - EDGE
    after = ref[f, EDGE + 1 : end + 1, :]
    before = ref[f, EDGE - 1 : end - 1, :]
    return inner(ref, f), before + after, after - before


def y_stage(value):
    after, before = shift(value, -1), shift(value, 1)
    return before + after, after - before


def yz_parts(ref):
    a, a_sum, a_dif = z_stage(ref, 0)
    b, b_sum, b_dif = z_stage(ref, 1)
    c, c_sum, c_dif = z_stage(ref, 2)
    pa, ma = y_stage(a)
    pas, mas = y_stage(a_sum)
    pad, _ = y_stage(a_dif)
    pb, mb = y_stage(b)
    pbs, mbs = y_stage(b_sum)
    _, mbd = y_stage(b_dif)
    pc, _ = y_stage(c)
    pcs, _ = y_stage(c_sum)
    pcd, mcd = y_stage(c_dif)
    own_x = ACROSS1 * (pa + a_sum) + ACROSS2 * pas
    even_x = ALONG1 * a + ALONG2 * (pa + a_sum) + SAME3 * pas
    odd_x = MIXED2 * (mb + c_dif) + MIXED3 * (mbs + pcd)
    own_y = ALONG1 * pb + ACROSS1 * b_sum + ALONG2 * pbs + MIXED2 * mcd
    even_y = ACROSS1 * b + ALONG2 * pb + ACROSS2 * b_sum + SAME3 * pbs + MIXED3 * mcd
    odd_y = MIXED2 * ma + MIXED3 * mas
    own_z = ALONG1 * c_sum + ACROSS1 * pc + ALONG2 * pcs + MIXED2 * mbd
    even_z = ACROSS1 * c + ACROSS2 * pc + ALONG2 * c_sum + SAME3 * pcs + MIXED3 * mbd
    odd_z = MIXED2 * a_dif + MIXED3 * pad
    return (own_x, even_x, odd_x), (own_y, even_y, odd_y), (own_z, even_z, odd_z)


def x_stage(sh, lane, own, plus, minus, rim_plus, rim_minus):
    after, before = shift(plus, -sh.pitch), shift(minus, sh.pitch)
    last = (sh.x + 1) * sh.pitch
    if rim_plus is None:
        return own + pick(lane < last, after) + pick(lane >= sh.pitch, before)
    return own + jnp.where(lane < last, after, rim_plus) + jnp.where(lane >= sh.pitch, before, rim_minus)


def stencil(sh, lane, ref, rim):
    parts = yz_parts(ref)
    rims = yz_parts(rim) if rim is not None else [None] * 3
    out = []
    for (own, even, odd), rim_part in zip(parts, rims):
        if rim_part is None:
            out.append(x_stage(sh, lane, own, even + odd, even - odd, None, None))
        else:
            _, rim_even, rim_odd = rim_part
            out.append(
                x_stage(sh, lane, own, even + odd, even - odd, rim_even + rim_odd, rim_even - rim_odd)
            )
    return out


def spring_parts(ref):
    k, k_sum, k_dif = z_stage(ref, 0)
    pk, mk = y_stage(k)
    pks, mks = y_stage(k_sum)
    pkd, mkd = y_stage(k_dif)
    zero = jnp.zeros_like(k)
    xx = (ACROSS1 * (pk + k_sum) + ACROSS2 * pks, ALONG1 * k + ALONG2 * (pk + k_sum) + SAME3 * pks, zero)
    yy = (
        ALONG1 * pk + ACROSS1 * k_sum + ALONG2 * pks,
        ACROSS1 * k + ALONG2 * pk + ACROSS2 * k_sum + SAME3 * pks,
        zero,
    )
    zz = (
        ALONG1 * k_sum + ACROSS1 * pk + ALONG2 * pks,
        ACROSS1 * k + ACROSS2 * pk + ALONG2 * k_sum + SAME3 * pks,
        zero,
    )
    xy = (zero, zero, MIXED2 * mk + MIXED3 * mks)
    xz = (zero, zero, MIXED2 * k_dif + MIXED3 * pkd)
    yz = (MIXED2 * mkd, MIXED3 * mkd, zero)
    return xx, yy, zz, xy, xz, yz


def own_block(sh, lane, springs):
    main, rim = springs
    k = inner(main, 0)
    out = []
    for index, ((own, even, odd), (_, rim_even, rim_odd)) in enumerate(
        zip(spring_parts(main), spring_parts(rim))
    ):
        total = x_stage(sh, lane, own, even + odd, even - odd, rim_even + rim_odd, rim_even - rim_odd)
        out.append(total + TOTAL * k if index < 3 else total)
    return out


def apply_block(d, v):
    return (
        d[0] * v[0] + d[3] * v[1] + d[4] * v[2],
        d[3] * v[0] + d[1] * v[1] + d[5] * v[2],
        d[4] * v[0] + d[5] * v[1] + d[2] * v[2],
    )


def image_of(sh, lane, v, kv, rims, springs_ref):
    k = springs_ref[6]
    k_before, k_after = shift(k, sh.pitch), shift(k, -sh.pitch)
    last = (sh.x + 1) * sh.pitch
    own = apply_block([springs_ref[f] for f in range(6)], [inner(v, m) for m in range(3)])
    rim_parts = [yz_parts(rims[0]), yz_parts(rims[1])] if rims else None
    out = []
    for m, (plain, scaled) in enumerate(zip(yz_parts(v), yz_parts(kv))):
        after = shift(k_before * (plain[1] + plain[2]) + (scaled[1] + scaled[2]), -sh.pitch)
        before = shift(k_after * (plain[1] - plain[2]) + (scaled[1] - scaled[2]), sh.pitch)
        if rims is None:
            after, before = pick(lane < last, after), pick(lane >= sh.pitch, before)
        else:
            plain_rim, scaled_rim = rim_parts[0][m], rim_parts[1][m]
            edge = k * (plain_rim[1] + plain_rim[2]) + (scaled_rim[1] + scaled_rim[2])
            after = jnp.where(lane < last, after, edge)
            edge = k * (plain_rim[1] - plain_rim[2]) + (scaled_rim[1] - scaled_rim[2])
            before = jnp.where(lane >= sh.pitch, before, edge)
        out.append(own[m] - (k * plain[0] + scaled[0] + after + before))
    return out


def level(sh):
    return lax.broadcasted_iota(jnp.int32, (sh.rows, LANES), 0) - EDGE


def ends_level(sh):
    row = lax.broadcasted_iota(jnp.int32, (4 * EDGE, LANES), 0)
    return jnp.where(row < 2 * EDGE, row, row + sh.rows - 4 * EDGE) - EDGE


def ends(value):
    return jnp.concatenate([value[: 2 * EDGE], value[value.shape[0] - 2 * EDGE :]], axis=0)


def extended_mask(sh, z):
    lane, _, across = sh.lane_grid(1)
    return ((lane < sh.used) & (across >= -1) & (across <= sh.y)) & ((z >= -1) & (z <= sh.z))


def within(sh, axis, place, size):
    index = sh.here(axis)
    low = jnp.where(index > 0, -EDGE, 0)
    high = jnp.where(index < sh.sizes[axis] - 1, size + EDGE, size)
    return (place >= low) & (place < high)


def grid_masks(sh):
    lane, along, across = sh.lane_grid(1)
    lanes = (lane < sh.used) & within(sh, 1, across, sh.y)
    rows = within(sh, 2, level(sh), sh.z)
    return (lanes & within(sh, 0, along, sh.x)) & rows, lanes & rows


def put(ref, f, value):
    ref[f, EDGE : ref.shape[1] - EDGE, :] = value


def local_solve(sh, z, residual_ref, springs_ref, v, kv, factor):
    lane, _, _ = sh.lane_grid(1)
    mask = extended_mask(sh, z)
    for m in range(3):
        factor[m] = pick(mask, relax / jnp.where(mask, springs_ref[m], 1.0))
        value = residual_ref[m] * factor[m]
        put(v[0], m, value)
        put(kv[0], m, springs_ref[6] * value)
    for sweep in range(SWEEPS - 1):
        old, new = sweep % 2, (sweep + 1) % 2
        image = image_of(sh, lane, v[old], kv[old], None, springs_ref)
        for m in range(3):
            value = inner(v[old], m) + factor[m] * (residual_ref[m] - image[m])
            put(v[new], m, value)
            put(kv[new], m, springs_ref[6] * value)
    return (SWEEPS - 1) % 2


def own_level(sh):
    return lax.broadcasted_iota(jnp.int32, (sh.z, LANES), 0)


def coords(sh, z):
    _, along, across = sh.lane_grid(z.shape[0])
    along = jnp.where(along < 0, along + sh.x, jnp.where(along < sh.x, along, along - sh.x))
    across = jnp.where(across < 0, across + sh.y, jnp.where(across < sh.y, across, across - sh.y))
    place = lambda index, size: (2 * index + 1).astype(f32) / size - 1.0
    return place(along, sh.x), place(across, sh.y), place(z, sh.z)


def cell_coords(sh):
    cell = lax.broadcasted_iota(jnp.int32, (sh.cells, sh.z), 0)
    z = lax.broadcasted_iota(jnp.int32, (sh.cells, sh.z), 1)
    x = cell // sh.y
    place = lambda index, size: (2 * index + 1).astype(f32) / size - 1.0
    return place(x, sh.x), place(cell - x * sh.y, sh.y), place(z, sh.z)


def cross(a, b):
    return (a[1] * b[2] - a[2] * b[1], a[2] * b[0] - a[0] * b[2], a[0] * b[1] - a[1] * b[0])


def fold_rows(value):
    total = value[0:8]
    for i in range(8, value.shape[0], 8):
        total = total + value[i : i + 8]
    return jnp.sum(total, axis=0, keepdims=True)


def lane_sums(rows_ref):
    ones = jnp.ones((8, LANES), f32)
    return lax.dot_general(
        ones, rows_ref[...], (((1,), (1,)), ((), ())), precision=highest, preferred_element_type=f32
    )


def coarse_sums(nodes, field, places, count, sums):
    moments = tuple(field) + cross(places, field)
    for node in range(count):
        mask = nodes == node
        for m in range(6):
            sums[node * 6 + m : node * 6 + m + 1, :] = fold_rows(pick(mask, moments[m]))


def sums_line(sh, sums, unknowns):
    flat = (sh.here(0) * sh.sizes[1] + sh.here(1)) * sh.sizes[2] + sh.here(2)
    return pltpu.roll(lane_sums(sums), lax.rem(flat * unknowns, LANES), 1)[0:1]


def coarse_solution(received, inverse_ref, values):
    unknowns, total = inverse_ref.shape
    row = lax.broadcasted_iota(jnp.int32, received.shape, 0)
    part = jnp.zeros((unknowns, LANES), f32)
    for i in range(0, total, LANES):
        owner = (i + lax.broadcasted_iota(jnp.int32, (1, LANES), 1)) // unknowns
        vector = jnp.sum(pick(row == owner, received), axis=0, keepdims=True)
        part = part + inverse_ref[:, i : i + LANES] * vector
    values[0:unknowns, :] = jnp.dot(
        part, jnp.ones((LANES, LANES), f32), precision=highest, preferred_element_type=f32
    )


def coarse_shares(sums, inverse_ref, shares):
    unknowns, total = inverse_ref.shape
    column = jnp.dot(sums[...], jnp.ones((LANES, LANES), f32), precision=highest, preferred_element_type=f32)
    for i in range(0, total, LANES):
        share = inverse_ref[:, i : i + LANES] * column[0:unknowns]
        shares[i // LANES : i // LANES + 1, :] = jnp.sum(share, axis=0, keepdims=True)


def coarse_table(sh, shares_ref, unknowns, flat, table):
    rows = shares_ref.shape[0] // sh.devices
    lane = lax.broadcasted_iota(jnp.int32, (1, LANES), 1)
    for i in range(rows):
        flat[i : i + 1, :] = jnp.sum(shares_ref[pl.ds(i, sh.devices, stride=rows), :], axis=0, keepdims=True)
    for device in range(sh.devices):
        row, place = divmod(device * unknowns, LANES)
        part = shift(flat[row : row + 1, :], -place)
        if place + unknowns > LANES:
            part = jnp.where(lane < LANES - place, part, shift(flat[row + 1 : row + 2, :], -place))
        table[device : device + 1, :] = pick(lane < unknowns, part)


def region_values(sh, table, dz):
    lane, along, across = sh.lane_grid(1)
    x = sh.here(0) + jnp.where(along < 0, -1, jnp.where(along < sh.x, 0, 1))
    y = sh.here(1) + jnp.where(across < 0, -1, jnp.where(across < sh.y, 0, 1))
    z = sh.here(2) + dz
    exists = (lane < sh.used) & (x >= 0) & (x < sh.sizes[0]) & (y >= 0) & (y < sh.sizes[1])
    exists = exists & (z >= 0) & (z < sh.sizes[2])
    device = jnp.where(exists, (x * sh.sizes[1] + y) * sh.sizes[2] + z, -1)
    owner = lax.broadcasted_iota(jnp.int32, (sh.devices, LANES), 0) == device
    return lax.dot_general(
        table[...], owner.astype(f32), (((0,), (0,)), ((), ())), precision=highest, preferred_element_type=f32
    )


def coarse_cells(nodes, places, values, count):
    cells = []
    for m in range(6):
        cell = jnp.zeros(nodes.shape, f32)
        for node in range(count):
            cell = jnp.where(nodes == float(node), values[node * 6 + m : node * 6 + m + 1, :], cell)
        cells.append(cell)
    turned = cross(cells[3:], places)
    return [cells[m] + turned[m] for m in range(3)]


def selection(sh):
    lane, along, across = sh.lane_grid(sh.cells)
    inside = (along >= 0) & (along < sh.x) & (across >= 0) & (across < sh.y)
    row = lax.broadcasted_iota(jnp.int32, (sh.cells, LANES), 0)
    return (inside & (row == along * sh.y + across)).astype(f32)


def to_lanes(value, select):
    return lax.dot_general(
        value, select, (((0,), (0,)), ((), ())), precision=highest, preferred_element_type=f32
    )


def to_cells(value, select):
    return lax.dot_general(
        select, value, (((1,), (1,)), ((), ())), precision=highest, preferred_element_type=f32
    )


def send_lines(sh, lines, slots_ref):
    here = [sh.here(axis) for axis in range(3)]
    corner = [lines[8 * i : 8 * i + 8, :] for i in range(4)]
    top, bottom = lines[32:40, :], lines[40:48, :]
    for x in range(sh.sizes[0]):
        low_high = [jnp.where(x > here[0], corner[2 + high], corner[high]) for high in range(2)]
        for y in range(sh.sizes[1]):
            column = jnp.where(y > here[1], low_high[1], low_high[0])
            for z in range(sh.sizes[2]):
                slot = jnp.where(z == here[2] + 1, top, jnp.where(z == here[2] - 1, bottom, column))
                place = 8 * ((x * sh.sizes[1] + y) * sh.sizes[2] + z)
                slots_ref[place : place + 8, :] = slot


def slot_from(sh, received_ref, step):
    place, exists = 0, None
    for axis in range(3):
        index = sh.here(axis) + step[axis]
        inside = (index >= 0) & (index < sh.sizes[axis])
        exists = inside if exists is None else exists & inside
        place = place * sh.sizes[axis] + jnp.clip(index, 0, sh.sizes[axis] - 1)
    return scale(exists, received_ref[pl.ds(pl.multiple_of(place * 8, 8), 8), :])


def repeat_twice(count):
    row = lax.broadcasted_iota(jnp.int32, (2 * count, count), 0)
    column = lax.broadcasted_iota(jnp.int32, (2 * count, count), 1)
    return ((row >= 2 * column) & (row < 2 * column + 2)).astype(f32)


def ring(size_x, size_y, rows):
    row = lax.broadcasted_iota(jnp.int32, (rows, LANES), 0)
    sides_x, both = 2 * size_y, 2 * size_y + 2 * size_x
    corner = row - both
    x = jnp.where(row < size_y, -1, size_x)
    x = jnp.where(row < sides_x, x, jnp.where(row < sides_x + size_x, row - sides_x, row - sides_x - size_x))
    x = jnp.where(row < both, x, jnp.where(corner < 2, -1, size_x))
    y = jnp.where(row < size_y, row, row - size_y)
    y = jnp.where(row < sides_x, y, jnp.where(row < sides_x + size_x, -1, size_y))
    y = jnp.where(row < both, y, jnp.where((corner == 0) | (corner == 2), -1, size_y))
    return x, y, (row < sides_x) | (row >= both), row < both + 4


def face_shape(sh, label_x, label_y):
    rows = max(4 * sh.x + label_x, 4 * sh.y + label_y)
    return (-(-rows // 8) * 8, LANES)


def pack_faces(sh, natural_ref, stiff, label_x, label_y, x_refs, y_refs):
    even_x, even_y = sh.here(0) % 2 == 0, sh.here(1) % 2 == 0

    def face(at, count, stride, label_at, label_count, label_stride):
        rows = [natural_ref[m, pl.ds(at, count, stride=stride), :] for m in range(4)]
        return rows, stiff[pl.ds(label_at, label_count, stride=label_stride), :]

    above = face(sh.cells - sh.y, sh.y, 1, (label_x - 1) * label_y, label_y, 1)
    below = face(0, sh.y, 1, 0, label_y, 1)
    for refs, links, even, above, below in (
        (x_refs, sh.x_links, even_x, above, below),
        (
            y_refs,
            sh.y_links,
            even_y,
            face(sh.y - 1, sh.x, sh.y, label_y - 1, label_x, label_y),
            face(0, sh.x, sh.y, 0, label_x, label_y),
        ),
    ):
        for i, ref in enumerate(refs):
            ref[...] = jnp.zeros(ref.shape, f32)
            count = above[0][0].shape[0]
            for m in range(4):
                ref[m * count : (m + 1) * count, :] = pair(links, even, above[0][m], below[0][m])[i]
            labels, length = above[1].shape
            ref[4 * count : 4 * count + labels, 0:length] = pair(links, even, above[1], below[1])[i]


def merge_start(sh, refs, x_refs, y_refs, received_ref, sizes, cells, labels):
    residual, nodes, stiff, stiff_rim = refs
    label_x, label_y, label_z = sizes
    lane, along, across = sh.lane_grid(1)
    inside = lane < sh.used
    last = (sh.x + 1) * sh.pitch
    x_mask = {-1: lane < sh.pitch, 0: (lane >= sh.pitch) & (lane < last), 1: (lane >= last) & inside}
    y_mask = {-1: across < 0, 0: (across >= 0) & (across < sh.y), 1: across >= sh.y}
    cells[...] = jnp.zeros(cells.shape, f32)
    labels[...] = jnp.zeros(labels.shape, f32)
    count, label_count = cells.shape[1], labels.shape[0]
    at = label_at = 0
    for axis, face_refs, size, label_size in ((0, x_refs, sh.y, label_y), (1, y_refs, sh.x, label_x)):
        for message in sides(sh, axis, [ref[...] for ref in face_refs]):
            for m in range(4):
                cells[m, at : at + size, :] = message[m * size : (m + 1) * size]
            labels[label_at : label_at + label_size, :] = message[4 * size : 4 * size + label_size, 0:label_z]
            at, label_at = at + size, label_at + label_size
    for dx, dy in ((-1, -1), (-1, 1), (1, -1), (1, 1)):
        slot = slot_from(sh, received_ref, (dx, dy, 0))
        for m, row in enumerate((0, 1, 2, 5)):
            cells[m, at : at + 1, :] = slot[row : row + 1]
        labels[label_at : label_at + 1, :] = slot[3:4, 0:label_z]
        at, label_at = at + 1, label_at + 1
    x, y, _, valid = ring(sh.x, sh.y, count)
    place = (valid & inside & (along == x) & (across == y)).astype(f32)
    own = slice(EDGE, EDGE + sh.z)
    tall_own = slice(2 * EDGE, 2 * EDGE + sh.z)
    for m in range(3):
        residual[m, own, :] += to_lanes(cells[m], place)
    nodes[own, :] += to_lanes(cells[3], place)
    by_z = lax.dot_general(
        repeat_twice(label_z), labels[...], (((1,), (1,)), ((), ())), precision=highest, preferred_element_type=f32
    )
    x, y, at_x, valid = ring(label_x, label_y, label_count)
    match = valid & inside & ((along >> 1) == x) & ((across >> 1) == y)
    columns = jnp.dot(by_z, (match & at_x).astype(f32), precision=highest, preferred_element_type=f32)
    stiff_rim[0, tall_own, :] = columns
    columns = columns + jnp.dot(by_z, (match & ~at_x).astype(f32), precision=highest, preferred_element_type=f32)
    stiff[0, tall_own, :] += columns
    for dz in (-1, 1):
        main = edge = jnp.zeros((8, LANES), f32)
        for dx in (-1, 0, 1):
            for dy in (-1, 0, 1):
                slot = slot_from(sh, received_ref, (dx, dy, dz))
                mask = x_mask[dx] & y_mask[dy]
                main = main + pick(mask, shift(slot, dx * sh.x * sh.pitch + dy * sh.y))
                if dx:
                    edge = edge + pick(mask, shift(slot, dx * (sh.x - 1) * sh.pitch + dy * sh.y))
        near = EDGE + sh.z if dz > 0 else EDGE - 1
        for m in range(3):
            residual[m, near : near + 1, :] = main[m : m + 1]
        nodes[near : near + 1, :] = main[5:6]
        for row in (EDGE + near, EDGE + near + dz):
            stiff[0, row : row + 1, :] = main[3:4]
            stiff_rim[0, row : row + 1, :] = edge[3:4]


def call(kernel, name, outs, ins, scratch=(), remote_ins=False):
    space = pltpu.HBM if remote_ins else pltpu.VMEM
    return pl.pallas_call(
        kernel,
        out_shape=[jax.ShapeDtypeStruct(shape, f32) for shape in outs],
        in_specs=[pl.BlockSpec(memory_space=space) for _ in ins],
        out_specs=[pl.BlockSpec(memory_space=pltpu.VMEM) for _ in outs],
        scratch_shapes=[pltpu.VMEM(shape, f32) if isinstance(shape, tuple) else shape for shape in scratch],
        compiler_params=pltpu.CompilerParams(vmem_limit_bytes=(62 if remote_ins else 48) * 1024 * 1024),
        name=name,
    )(*ins)


def permutation(sizes, moves):
    def partner(axis, link, index):
        size = sizes[axis]
        other = index ^ 1 if link == 0 else index + (1 if index % 2 else -1)
        if 0 <= other < size:
            return other
        return size - 1 - index if axis == 2 and size % 2 == 0 else index

    pairs = []
    for x in range(sizes[0]):
        for y in range(sizes[1]):
            for z in range(sizes[2]):
                place = [x, y, z]
                goal = [partner(a, moves[a], place[a]) if a in moves else place[a] for a in range(3)]
                if goal == place and 0 not in moves and sizes[0] % 2 == 0:
                    goal[0] = partner(0, 0, x)
                flat = [(p[0] * sizes[1] + p[1]) * sizes[2] + p[2] for p in (place, goal)]
                pairs.append(tuple(flat))
    return pairs


def send(sh, value, moves):
    return lax.ppermute(value, AXES, permutation(sh.sizes, moves))


def send_z(sh, messages):
    return [send(sh, message, {2: link}) for link, message in enumerate(messages)]


def send_faces(sh, x_messages, y_messages):
    from_y = [send(sh, message, {1: link}) for link, message in enumerate(y_messages)]
    from_x = [send(sh, message, {0: link}) for link, message in enumerate(x_messages)]
    return from_y, from_x


def to_all(slots):
    return lax.all_to_all(slots, AXES, 0, 0, tiled=True)


def exchange(sh, ex, name, field, z_messages):
    from_z = send_z(sh, z_messages)

    corners = sh.x_links * sh.y_links

    def packer(*refs):
        take = Taker(refs)
        field_ref, z_refs = take.one(), take(sh.z_links)
        x_refs, y_refs, corner_refs, scratch = take(sh.x_links), take(sh.y_links), take(corners), take.one()
        merge_z(sh, ex, field_ref, z_refs, scratch, 0)
        pack_xy(sh, ex, scratch, x_refs, y_refs, corner_refs)

    plane = (sh.rows, LANES)
    messages = call(
        packer,
        name,
        [plane] * sh.x_links
        + [folded_shape(sh, ex.fields * ex.layers)] * sh.y_links
        + [folded_shape(sh, ex.layers)] * corners,
        [field] + from_z,
        [(ex.fields,) + plane],
    )
    take = Taker(messages)
    x_messages, y_messages = take(sh.x_links), take(sh.y_links)
    from_y, straight = send_faces(sh, x_messages, y_messages)
    from_x = []
    for link in range(sh.x_links):
        from_x.append(straight[link])
        from_x.extend(send(sh, take.one(), {0: link, 1: other}) for other in range(sh.y_links))
    return from_z, from_y, from_x


class Taker:
    def __init__(self, refs):
        self.refs, self.at = refs, 0

    def __call__(self, count):
        self.at += count
        return self.refs[self.at - count : self.at]

    def one(self):
        return self(1)[0]


def merge_all(sh, ex, take, scratch, rim, guard):
    field = take.one()
    from_z, from_y = take(sh.z_links), take(sh.y_links)
    from_x = take(sh.x_links * (1 + sh.y_links))
    merge_z(sh, ex, field, from_z, scratch, guard)
    merge_xy(sh, ex, scratch, rim, guard, from_y, from_x)


def body(right_side, phase_labels, phase_moduli, coarse_nodes, coarse_inverse):
    sizes = tuple(lax.axis_size(axis) for axis in AXES)
    _, size_x, size_y, size_z = right_side.shape
    sh = Shape(size_x, size_y, size_z, phase_moduli.shape[0], sizes)
    unknowns = coarse_inverse.shape[0]
    node_count = unknowns // 6
    sum_rows = -(-unknowns // 8) * 8
    share_rows = coarse_inverse.shape[1] // LANES
    own = slice(EDGE, EDGE + sh.z)
    plane = (sh.rows, LANES)
    fields = (3,) + plane
    tall = (3, sh.tall, LANES)
    slots = (sh.devices, LANES)
    z_shape = lambda ex: [(8 * ex.fields, LANES)] * sh.z_links
    natural = right_side.reshape(3, sh.cells, sh.z)
    nodes_natural = coarse_nodes.reshape(sh.cells, sh.z)
    label_x, label_y, label_z = phase_labels.shape

    def block_places():
        lane, along, across = sh.lane_grid(label_x * label_y)
        inside = (along >= 0) & (along < sh.x) & (across >= 0) & (across < sh.y)
        block = lax.broadcasted_iota(jnp.int32, along.shape, 0)
        return (inside & (block == (along >> 1) * label_y + (across >> 1))).astype(f32)

    def end_layers(values, places):
        length = values.shape[1]
        row = lax.broadcasted_iota(jnp.int32, (8, length), 0)
        at = lax.broadcasted_iota(jnp.int32, (8, length), 1)
        ends = ((row == 0) & (at == length - 1)) | ((row == 1) & (at == 0))
        return jnp.dot(to_cells(values, ends.astype(f32)), places, precision=highest, preferred_element_type=f32)

    def begin(natural_in, labels_in, moduli_in, nodes_in, stiff, slots_ref, *rest):
        x_refs, y_refs = rest[: sh.x_links], rest[sh.x_links : sh.x_links + sh.y_links]
        natural_ref, labels_ref, moduli_ref, nodes_ref, sems, sums, lines = rest[sh.x_links + sh.y_links :]
        pairs = ((natural_in, natural_ref.at[0:3]), (labels_in, labels_ref), (moduli_in, moduli_ref), (nodes_in, nodes_ref))
        copies = [pltpu.make_async_copy(a, b, sems.at[i]) for i, (a, b) in enumerate(pairs)]
        for copy in copies:
            copy.start()
        sums[...] = jnp.zeros(sums.shape, f32)
        lines[...] = jnp.zeros(lines.shape, f32)
        for copy in copies:
            copy.wait()
        for i in range(label_x):
            labels = labels_ref[i]
            moduli = jnp.zeros(labels.shape, f32)
            for phase in range(sh.phases):
                moduli = jnp.where(labels == phase, moduli_ref[phase], moduli)
            stiff[i * label_y : (i + 1) * label_y, :] = moduli
        natural_ref[3] = nodes_ref[...].astype(f32) + 1.0
        cells = [natural_ref[m] for m in range(3)]
        coarse_sums(nodes_ref[...], cells, cell_coords(sh), node_count, sums)
        line = sums_line(sh, sums, unknowns)
        for i, (cell, block) in enumerate(
            (
                (0, 0),
                (sh.y - 1, label_y - 1),
                ((sh.x - 1) * sh.y, (label_x - 1) * label_y),
                (sh.cells - 1, label_x * label_y - 1),
            )
        ):
            for m in range(3):
                lines[8 * i + m : 8 * i + m + 1, :] = natural_ref[m, cell : cell + 1, :]
            lines[8 * i + 3 : 8 * i + 4, 0:label_z] = stiff[block : block + 1, :]
            lines[8 * i + 5 : 8 * i + 6, :] = natural_ref[3, cell : cell + 1, :]
        select = selection(sh)
        layers = [end_layers(natural_ref[m], select) for m in range(4)] + [end_layers(stiff[...], block_places())]
        for i in range(2):
            for layer, row in zip(layers, (0, 1, 2, 5, 3)):
                lines[8 * (4 + i) + row : 8 * (4 + i) + row + 1, :] = layer[i : i + 1]
        for i in range(6):
            lines[8 * i + 4 : 8 * i + 5, :] = line
        send_lines(sh, lines, slots_ref)
        pack_faces(sh, natural_ref, stiff, label_x, label_y, x_refs, y_refs)

    stiff_blocks, lines, *messages = call(
        begin,
        "begin",
        [(label_x * label_y, label_z), (8 * sh.devices, LANES)]
        + [face_shape(sh, label_x, label_y)] * (sh.x_links + sh.y_links),
        [natural, phase_labels, phase_moduli, nodes_natural],
        [
            (4, sh.cells, sh.z),
            pltpu.VMEM(phase_labels.shape, jnp.int32),
            pltpu.SMEM(phase_moduli.shape, f32),
            pltpu.VMEM(nodes_natural.shape, jnp.int32),
            pltpu.SemaphoreType.DMA((4,)),
            (LANES, LANES),
            (48, LANES),
        ],
        remote_ins=True,
    )

    def spread(natural_ref, nodes_ref, stiff, field_ref, lanes_ref):
        select = selection(sh)
        field_ref[...] = jnp.zeros(field_ref.shape, f32)
        for m in range(3):
            field_ref[m, own, :] = to_lanes(natural_ref[m], select)
        by_z = lax.dot_general(
            repeat_twice(label_z), stiff[...], (((1,), (1,)), ((), ())), precision=highest, preferred_element_type=f32
        )
        field_ref[3, own, :] = jnp.dot(by_z, block_places(), precision=highest, preferred_element_type=f32)
        lanes_ref[...] = to_lanes(nodes_ref[...].astype(f32) + 1.0, select) - 1.0

    start_field, nodes = call(
        spread, "spread", [(4,) + plane, (sh.z, LANES)], [natural, nodes_natural, stiff_blocks]
    )
    from_y, from_x = send_faces(sh, messages[: sh.x_links], messages[sh.x_links :])
    lines = to_all(lines)

    short = (3, 6 * EDGE, LANES)
    short_fields = (3, 4 * EDGE, LANES)
    solve_scratch = [tall] * 4 + [fields]
    short_scratch = [short] * 4 + [short_fields]

    def end_rows(ref):
        def rows(f, start, count):
            place = start + EDGE if start < 2 * EDGE else start - sh.rows + 5 * EDGE
            return ref[f, place : place + count, :]

        return rows

    def first_ends(*refs):
        take = Taker(refs)
        field_ref = take.one()
        y_refs, x_refs = take(sh.y_links), take(sh.x_links)
        nodes_ref, lines_ref, inverse_ref = take(3)
        residual, wide_nodes, stiffness_ref, values = take(4)
        z_refs = take(sh.z_links)
        stiff, stiff_rim, cells, labels, short_stiff, short_rim, some_residual, springs = take(8)
        v0, v1, kv0, kv1, factor = take(5)
        clear_guards(sh, (stiff, stiff_rim, short_stiff, short_rim, v0, v1, kv0, kv1))
        residual[...] = field_ref[0:3]
        put(stiff, 0, field_ref[3])
        put(stiff_rim, 0, jnp.zeros(plane, f32))
        sizes = phase_labels.shape
        wide_nodes[...] = jnp.zeros(plane, f32)
        wide_nodes[own, :] = nodes_ref[...] + 1.0
        merge_start(sh, (residual, wide_nodes, stiff, stiff_rim), x_refs, y_refs, lines_ref, sizes, cells, labels)
        wide_nodes[...] = wide_nodes[...] - 1.0
        stiffness_ref[0] = inner(stiff, 0)
        stiffness_ref[1] = inner(stiff_rim, 0)
        coarse_solution(lines_ref[pl.ds(4, sh.devices, stride=8), :], inverse_ref, values)
        lane, _, _ = sh.lane_grid(1)
        put(short_stiff, 0, ends(stiffness_ref[0]))
        put(short_rim, 0, ends(stiffness_ref[1]))
        for f, entry in enumerate(own_block(sh, lane, (short_stiff, short_rim))):
            springs[f] = entry
        springs[6] = inner(short_stiff, 0)
        for m in range(3):
            some_residual[m] = ends(residual[m])
        index = local_solve(sh, ends_level(sh), some_residual, springs, (v0, v1), (kv0, kv1), factor)
        solution = (v0, v1)[index]
        z = lax.broadcasted_iota(jnp.int32, (2 * EDGE, LANES), 0)
        z = jnp.where(z < EDGE, z, z + sh.z - 2 * EDGE)
        some_nodes = jnp.concatenate([nodes_ref[0:EDGE, :], nodes_ref[sh.z - EDGE : sh.z, :]], axis=0)
        added = coarse_cells(some_nodes, coords(sh, z), values, node_count)
        for m in range(3):
            solution[m, 2 * EDGE : 4 * EDGE, :] += pick(some_nodes >= 0.0, added[m])
        pack_z(sh, DEEP, end_rows(solution), z_refs)

    residual, wide_nodes, stiffness, values, *z_messages = call(
        first_ends,
        "first_ends",
        [fields, plane, (2,) + plane, (sum_rows, LANES)] + z_shape(DEEP),
        [start_field, *from_y, *from_x, nodes, lines, coarse_inverse],
        [(1, sh.tall, LANES)] * 2
        + [
            (4, 8 * -(-(2 * sh.x + 2 * sh.y + 4) // 8), LANES),
            (8 * -(-(2 * label_x + 2 * label_y + 4) // 8), label_z),
        ]
        + [(1, 6 * EDGE, LANES)] * 2
        + [short_fields, (7, 4 * EDGE, LANES)]
        + short_scratch,
    )

    def first_solve(residual_ref, stiffness_ref, values, nodes_ref, solution_ref, springs_ref, *rest):
        stiff, stiff_rim, v0, v1, kv0, kv1, factor = rest
        clear_guards(sh, (stiff, stiff_rim, v0, v1, kv0, kv1))
        put(stiff, 0, stiffness_ref[0])
        put(stiff_rim, 0, stiffness_ref[1])
        springs_ref[6] = stiffness_ref[0]
        springs_ref[7] = stiffness_ref[1]
        lane, _, _ = sh.lane_grid(1)
        for f, entry in enumerate(own_block(sh, lane, (stiff, stiff_rim))):
            springs_ref[f] = entry
        index = local_solve(sh, level(sh), residual_ref, springs_ref, (v0, v1), (kv0, kv1), factor)
        for m in range(3):
            solution_ref[m] = inner((v0, v1)[index], m)
        added = coarse_cells(nodes_ref[...], coords(sh, own_level(sh)), values, node_count)
        for m in range(3):
            solution_ref[m, own, :] += pick(nodes_ref[...] >= 0.0, added[m])

    solved, springs = call(
        first_solve,
        "first_solve",
        [fields, (8,) + plane],
        [residual, stiffness, values, nodes],
        [(1, sh.tall, LANES)] * 2 + solve_scratch,
    )
    from_z, from_y, from_x = exchange(sh, DEEP, "deep", solved, z_messages)

    def first_image(*refs):
        take = Taker(refs)
        merging = take(1 + sh.z_links + sh.y_links + sh.x_links * (1 + sh.y_links))
        nodes_ref, springs_ref, inverse_ref = take(3)
        search_ref, image_ref, slots_ref = take(3)
        v, rim, kv, k_rim, sums, shares = take(6)
        clear_guards(sh, (v, rim, kv, k_rim))
        merge_all(sh, DEEP, Taker(merging), v, rim, EDGE)
        lane, _, _ = sh.lane_grid(1)

        in_grid, in_rim = grid_masks(sh)
        for m in range(3):
            value = pick(in_grid, inner(v, m))
            put(v, m, value)
            search_ref[m] = value
            put(kv, m, springs_ref[6] * value)
            value = pick(in_rim, inner(rim, m))
            put(rim, m, value)
            put(k_rim, m, springs_ref[7] * value)
        image = image_of(sh, lane, v, kv, (rim, k_rim), springs_ref)
        keep = in_grid & extended_mask(sh, level(sh))
        for m in range(3):
            image_ref[m] = pick(keep, image[m])
        sums[...] = jnp.zeros(sums.shape, f32)
        field = [image_ref[m, own, :] for m in range(3)]
        coarse_sums(nodes_ref[...], field, coords(sh, own_level(sh)), node_count, sums)
        coarse_shares(sums, inverse_ref, shares)
        for device in range(sh.devices):
            slots_ref[device * share_rows : (device + 1) * share_rows, :] = shares[0:share_rows, :]

    search, image, shares = call(
        first_image,
        "first_image",
        [fields, fields, (sh.devices * share_rows, LANES)],
        [solved, *from_z, *from_y, *from_x, nodes, springs, coarse_inverse],
        [tall] * 4 + [(LANES, LANES), (8 * -(-share_rows // 8), LANES)],
    )
    shares = to_all(shares.reshape(sh.devices, 1, share_rows * LANES)).reshape(shares.shape)

    def second_solve(image_ref, springs_ref, local_ref, v0, v1, kv0, kv1, factor):
        clear_guards(sh, (v0, v1, kv0, kv1))
        index = local_solve(sh, level(sh), image_ref, springs_ref, (v0, v1), (kv0, kv1), factor)
        for m in range(3):
            local_ref[m] = inner((v0, v1)[index], m)

    def second_ends(image_ref, springs_ref, *refs):
        take = Taker(refs)
        z_refs = take(sh.z_links)
        some_residual, springs, v0, v1, kv0, kv1, factor = take(7)
        clear_guards(sh, (v0, v1, kv0, kv1))
        for m in range(3):
            some_residual[m] = ends(image_ref[m])
        for f in range(7):
            springs[f] = ends(springs_ref[f])
        index = local_solve(sh, ends_level(sh), some_residual, springs, (v0, v1), (kv0, kv1), factor)
        pack_z(sh, NEAR, end_rows((v0, v1)[index]), z_refs)

    z_messages = call(
        second_ends,
        "second_ends",
        z_shape(NEAR),
        [image, springs],
        [short_fields, (7, 4 * EDGE, LANES)] + short_scratch,
    )
    (solved,) = call(second_solve, "second_solve", [fields], [image, springs], solve_scratch)
    from_z, from_y, from_x = exchange(sh, NEAR, "near", solved, z_messages)

    def between(shares_ref, wide_nodes, nodes_ref, start_ref, search_ref, first_ref, coarse_ref, sums, *scratch):
        flat, table, values = scratch
        coarse_ref[...] = jnp.zeros(coarse_ref.shape, f32)
        sums[...] = jnp.zeros(sums.shape, f32)
        coarse_table(sh, shares_ref, unknowns, flat, table)
        last = lax.broadcasted_iota(jnp.int32, (1, LANES), 0) + sh.z - 1
        for dz, first, z in ((0, EDGE, own_level(sh)), (-1, EDGE - 1, last), (1, EDGE + sh.z, last - sh.z + 1)):
            values[...] = region_values(sh, table, dz)
            rows = slice(first, first + z.shape[0])
            added = coarse_cells(wide_nodes[rows, :], coords(sh, z), values, node_count)
            for m in range(3):
                coarse_ref[m, rows, :] = added[m]
        valid = nodes_ref[...] >= 0.0
        for i, other in enumerate((start_ref, first_ref)):
            product = sum(search_ref[m, own, :] * other[m, own, :] for m in range(3))
            sums[i : i + 1, :] = fold_rows(pick(valid, product))

    coarse_field, sums = call(
        between,
        "between",
        [fields, (8, LANES)],
        [shares, wide_nodes, nodes, start_field, search, image],
        [(8 * -(-share_rows // 8) + 8, LANES), (sh.devices, LANES), (LANES, LANES)],
    )

    def second_image(*refs):
        take = Taker(refs)
        merging = take(1 + sh.z_links + sh.y_links + sh.x_links * (1 + sh.y_links))
        nodes_ref, springs_ref, first_ref, coarse_ref, early_ref = take(5)
        second_ref, image_ref, slots_ref = take(3)
        v, kv, sums = take(3)
        clear_guards(sh, (v, kv))
        merge_all(sh, NEAR, Taker(merging), v, None, EDGE)
        lane, _, _ = sh.lane_grid(1)
        in_grid, _ = grid_masks(sh)
        for m in range(3):
            value = pick(in_grid, inner(v, m)) + coarse_ref[m]
            put(v, m, value)
            second_ref[m] = value
            put(kv, m, springs_ref[6] * value)
        image = image_of(sh, lane, v, kv, None, springs_ref)
        for m in range(3):
            image_ref[m] = image[m]
        valid = nodes_ref[...] >= 0.0
        sums[...] = jnp.zeros(sums.shape, f32)
        sums[0:8, :] = early_ref[...]
        for i, other in ((2, first_ref), (3, image_ref)):
            product = sum(second_ref[m, own, :] * other[m, own, :] for m in range(3))
            sums[i : i + 1, :] = fold_rows(pick(valid, product))
        slots_ref[...] = jnp.broadcast_to(lane_sums(sums)[0:1], slots_ref.shape)

    second, second_image_field, sums = call(
        second_image,
        "second_image",
        [fields, fields, slots],
        [solved, *from_z, *from_y, *from_x, nodes, springs, image, coarse_field, sums],
        [tall] * 2 + [(LANES, LANES)],
    )
    totals = to_all(sums)

    def turn(search_ref, first_ref, second_ref, image_ref, out_ref):
        select = selection(sh)
        for i, ref in enumerate((search_ref, first_ref, second_ref, image_ref)):
            for m in range(3):
                out_ref[i, m] = to_cells(ref[m, own, :], select)

    (turned,) = call(turn, "turn", [(4,) + natural.shape], [search, image, second, second_image_field])

    def finish(totals_ref, natural_ref, turned_ref, field_ref, residual_ref):
        total = jnp.sum(totals_ref[...], axis=0, keepdims=True)
        rz, zw, wq, qv = [total[:, i : i + 1] for i in range(4)]
        step0 = rz / zw
        rho = step0 * step0 * wq - step0 * zw
        grow = 1.0 + rho / rz
        curvature = grow * grow * zw - 2.0 * grow * step0 * wq + step0 * step0 * qv
        step1 = rho / curvature
        first = step0 + step1 * grow
        second = step0 * step1
        for m in range(3):
            field_ref[m] = first * turned_ref[0, m] - second * turned_ref[2, m]
            residual_ref[m] = natural_ref[m] - (first * turned_ref[1, m] - second * turned_ref[3, m])

    solution_field, residual = call(
        finish, "finish", [natural.shape, natural.shape], [totals, natural, turned]
    )
    return solution_field.reshape(right_side.shape), residual.reshape(right_side.shape)


def solution(mesh):
    in_specs = (
        P(None, "gx", "gy", "gz"),
        P("gx", "gy", "gz"),
        P(),
        P("gx", "gy", "gz"),
        P(("gx", "gy", "gz"), None),
    )
    out_specs = (P(None, "gx", "gy", "gz"), P(None, "gx", "gy", "gz"))
    return jax.shard_map(body, mesh=mesh, in_specs=in_specs, out_specs=out_specs, check_vma=False)
```

```python
import jax
import jax.numpy as jnp
from jax import lax
from jax.experimental import pallas as pl
from jax.experimental.pallas import tpu as pltpu
from jax.sharding import PartitionSpec as P

AXES = ("gx", "gy", "gz")
SWEEPS = 4
relax = 0.6
highest = lax.Precision.HIGHEST
small = lax.Precision.DEFAULT
f32 = jnp.float32
LANES = 128
EDGE = 8

ALONG1, ACROSS1 = 0.75, 0.5
ALONG2, ACROSS2, MIXED2 = 0.3125, 0.25, 0.0625
SAME3, MIXED3 = 7.0 / 36.0, 1.0 / 36.0
TOTAL = 2 * ALONG1 + 4 * ACROSS1 + 8 * ALONG2 + 4 * ACROSS2 + 8 * SAME3


class Exchange:
    def __init__(self, fields, layers, up, down):
        self.fields, self.layers, self.up, self.down = fields, layers, up, down


DEEP = Exchange(3, 3, -2, -1)
NEAR = Exchange(3, 2, -1, -1)


class Shape:
    def __init__(self, size_x, size_y, size_z, phases, mesh_sizes):
        self.x, self.y, self.z = size_x, size_y, size_z
        self.pitch = size_y + 4
        self.used = (size_x + 2) * self.pitch
        assert self.used <= LANES
        self.rows = size_z + 2 * EDGE
        self.tall = self.rows + 2 * EDGE
        self.phases = phases
        self.sizes = mesh_sizes
        self.devices = mesh_sizes[0] * mesh_sizes[1] * mesh_sizes[2]
        self.cells = size_x * size_y
        self.links = [1 if n <= 2 else 2 for n in mesh_sizes]
        self.x_links, self.y_links, self.z_links = self.links

    def lane_grid(self, rows):
        lane = lax.broadcasted_iota(jnp.int32, (rows, LANES), 1)
        column = jnp.zeros_like(lane)
        for j in range(1, self.x + 2):
            column = column + (lane >= j * self.pitch).astype(jnp.int32)
        offset = lane - column * self.pitch
        return lane, column - 1, offset - 2

    def here(self, axis):
        return lax.axis_index(AXES[axis])


def shift(value, amount):
    amount = amount % LANES
    return value if amount == 0 else pltpu.roll(value, amount, 1)


def pick(mask, value):
    return jnp.where(mask, value, 0.0)


def scale(flag, value):
    return value * flag.astype(f32)


def pair(links, even, upward, downward):
    first = jnp.where(even, upward, downward)
    return (first,) if links == 1 else (first, jnp.where(even, downward, upward))


def sides(sh, axis, received):
    index, size = sh.here(axis), sh.sizes[axis]
    even = index % 2 == 0
    first = received[0]
    second = received[1] if len(received) > 1 else jnp.zeros_like(first)
    below = jnp.where(even, second, first)
    above = jnp.where(even, first, second)
    return scale(index > 0, below), scale(index < size - 1, above)


def lane_range(lane, start, count):
    return (lane >= start) & (lane < start + count)


def pack_z(sh, ex, source, out_refs):
    even = sh.here(2) % 2 == 0
    for ref in out_refs:
        ref[...] = jnp.zeros(ref.shape, f32)
    for f in range(ex.fields):
        upward = source(f, EDGE + sh.z + ex.up, ex.layers)
        downward = source(f, EDGE + ex.down, ex.layers)
        for ref, message in zip(out_refs, pair(sh.z_links, even, upward, downward)):
            ref[8 * f : 8 * f + ex.layers, :] = message


def merge_z(sh, ex, field_ref, received_refs, scratch, guard):
    below, above = sides(sh, 2, [ref[...] for ref in received_refs])
    for f in range(ex.fields):
        scratch[f, guard : guard + sh.rows, :] = field_ref[f]
        low = guard + EDGE + ex.up
        high = guard + EDGE + sh.z + ex.down
        scratch[f, low : low + ex.layers, :] += below[8 * f : 8 * f + ex.layers]
        scratch[f, high : high + ex.layers, :] += above[8 * f : 8 * f + ex.layers]


def fold(sh, value, layers, start=None):
    folds = sh.pitch // layers
    height = -(-sh.rows // (8 * folds)) * 8
    lane, _, across = sh.lane_grid(1)
    total = jnp.zeros((height, LANES), f32)
    for i, first in enumerate(range(0, sh.rows, height)):
        part = value[first : first + height]
        if start is not None:
            part = pick((lane < sh.used) & lane_range(across, start, layers), part)
        part = shift(part, i * layers - (0 if start is None else start + 2))
        if part.shape[0] < height:
            part = jnp.concatenate([part, jnp.zeros((height - part.shape[0], LANES), f32)], axis=0)
        total = total + part
    return total


def folded_shape(sh, layers):
    return (-(-sh.rows // (8 * (sh.pitch // layers))) * 8, LANES)


def unfold(sh, message, layers, start):
    height = message.shape[0]
    lane, _, across = sh.lane_grid(1)
    mask = (lane < sh.used) & lane_range(across, start, layers)
    parts = []
    for i, first in enumerate(range(0, sh.rows, height)):
        part = message[0 : min(height, sh.rows - first)]
        parts.append(pick(mask, shift(part, start + 2 - i * layers)))
    return jnp.concatenate(parts, axis=0) if len(parts) > 1 else parts[0]


def pack_xy(sh, ex, scratch, x_refs, y_refs, corner_refs):
    rows = sh.rows
    lane, _, across = sh.lane_grid(1)
    even_x, even_y = sh.here(0) % 2 == 0, sh.here(1) % 2 == 0
    span = ex.layers * sh.pitch
    x_up = x_down = y_up = y_down = jnp.zeros((rows, LANES), f32)
    inside = lane < sh.used
    y_above, y_below = sh.y + ex.up, ex.down
    for f in range(ex.fields):
        value = scratch[f]
        start = (sh.x + ex.up + 1) * sh.pitch
        x_up = x_up + shift(pick(lane_range(lane, start, span), value), f * span - start)
        start = (ex.down + 1) * sh.pitch
        x_down = x_down + shift(pick(lane_range(lane, start, span), value), f * span - start)
        mask = inside & lane_range(across, y_above, ex.layers)
        y_up = y_up + shift(pick(mask, value), f * ex.layers - y_above - 2)
        mask = inside & lane_range(across, y_below, ex.layers)
        y_down = y_down + shift(pick(mask, value), f * ex.layers - y_below - 2)
    packed = ex.fields * ex.layers
    y_up, y_down = fold(sh, y_up, packed), fold(sh, y_down, packed)
    for ref, message in zip(y_refs, pair(sh.y_links, even_y, y_up, y_down)):
        ref[...] = message
    for i, message in enumerate(pair(sh.x_links, even_x, x_up, x_down)):
        x_refs[i][...] = message
        upward, downward = fold(sh, message, ex.layers, y_above), fold(sh, message, ex.layers, y_below)
        for j, corner in enumerate(pair(sh.y_links, even_y, upward, downward)):
            corner_refs[i * sh.y_links + j][...] = corner


def merge_xy(sh, ex, scratch, rim, guard, y_refs, x_refs):
    lane, _, across = sh.lane_grid(1)
    inside = lane < sh.used
    low_mask = inside & lane_range(across, ex.up, ex.layers)
    high_mask = inside & lane_range(across, sh.y + ex.down, ex.layers)
    span = ex.layers * sh.pitch
    packed = ex.fields * ex.layers
    below_y, above_y = [unfold(sh, value, packed, -2) for value in sides(sh, 1, [ref[...] for ref in y_refs])]
    per_link = 1 + sh.y_links
    sums = []
    for link in range(sh.x_links):
        straight, diagonal = x_refs[link * per_link], x_refs[link * per_link + 1 : (link + 1) * per_link]
        total = straight[...]
        below, above = sides(sh, 1, [ref[...] for ref in diagonal])
        total = total + unfold(sh, below, ex.layers, ex.up)
        sums.append(total + unfold(sh, above, ex.layers, sh.y + ex.down))
    below_x, above_x = sides(sh, 0, sums)
    first = 1 if ex.up == -2 else 0
    last = ex.layers - 1 if ex.down + ex.layers == 2 else ex.layers
    for f in range(ex.fields):
        addend = pick(low_mask, shift(below_y, ex.up + 2 - ex.layers * f))
        addend = addend + pick(high_mask, shift(above_y, sh.y + ex.down + 2 - ex.layers * f))
        start = (ex.up + first + 1) * sh.pitch
        count = (ex.layers - first) * sh.pitch
        moved = shift(below_x, start - f * span - first * sh.pitch)
        addend = addend + pick(lane_range(lane, start, count), moved)
        start = (sh.x + ex.down + 1) * sh.pitch
        moved = shift(above_x, start - f * span)
        addend = addend + pick(lane_range(lane, start, last * sh.pitch), moved)
        scratch[f, guard : guard + sh.rows, :] += addend
        if rim is not None:
            low = pick(lane_range(lane, 0, sh.pitch), shift(below_x, -f * span))
            start = (sh.x + 1) * sh.pitch
            moved = shift(above_x, start - f * span - last * sh.pitch)
            high = pick(lane_range(lane, start, sh.pitch), moved)
            rim[f, guard : guard + sh.rows, :] = low + high


def clear_guards(sh, refs):
    for ref in refs:
        for f in range(ref.shape[0]):
            ref[f, :EDGE, :] = jnp.zeros((EDGE, LANES), f32)
            ref[f, ref.shape[1] - EDGE :, :] = jnp.zeros((EDGE, LANES), f32)


def inner(ref, f):
    return ref[f, EDGE : ref.shape[1] - EDGE, :]


def z_stage(ref, f):
    end = ref.shape[1] - EDGE
    after = ref[f, EDGE + 1 : end + 1, :]
    before = ref[f, EDGE - 1 : end - 1, :]
    return inner(ref, f), before + after, after - before


def y_stage(value):
    after, before = shift(value, -1), shift(value, 1)
    return before + after, after - before


def yz_parts(ref):
    a, a_sum, a_dif = z_stage(ref, 0)
    b, b_sum, b_dif = z_stage(ref, 1)
    c, c_sum, c_dif = z_stage(ref, 2)
    pa, ma = y_stage(a)
    pas, mas = y_stage(a_sum)
    pad, _ = y_stage(a_dif)
    pb, mb = y_stage(b)
    pbs, mbs = y_stage(b_sum)
    _, mbd = y_stage(b_dif)
    pc, _ = y_stage(c)
    pcs, _ = y_stage(c_sum)
    pcd, mcd = y_stage(c_dif)
    own_x = ACROSS1 * (pa + a_sum) + ACROSS2 * pas
    even_x = ALONG1 * a + ALONG2 * (pa + a_sum) + SAME3 * pas
    odd_x = MIXED2 * (mb + c_dif) + MIXED3 * (mbs + pcd)
    own_y = ALONG1 * pb + ACROSS1 * b_sum + ALONG2 * pbs + MIXED2 * mcd
    even_y = ACROSS1 * b + ALONG2 * pb + ACROSS2 * b_sum + SAME3 * pbs + MIXED3 * mcd
    odd_y = MIXED2 * ma + MIXED3 * mas
    own_z = ALONG1 * c_sum + ACROSS1 * pc + ALONG2 * pcs + MIXED2 * mbd
    even_z = ACROSS1 * c + ACROSS2 * pc + ALONG2 * c_sum + SAME3 * pcs + MIXED3 * mbd
    odd_z = MIXED2 * a_dif + MIXED3 * pad
    return (own_x, even_x, odd_x), (own_y, even_y, odd_y), (own_z, even_z, odd_z)


def x_stage(sh, lane, own, plus, minus, rim_plus, rim_minus):
    after, before = shift(plus, -sh.pitch), shift(minus, sh.pitch)
    last = (sh.x + 1) * sh.pitch
    if rim_plus is None:
        return own + pick(lane < last, after) + pick(lane >= sh.pitch, before)
    return own + jnp.where(lane < last, after, rim_plus) + jnp.where(lane >= sh.pitch, before, rim_minus)


def stencil(sh, lane, ref, rim):
    parts = yz_parts(ref)
    rims = yz_parts(rim) if rim is not None else [None] * 3
    out = []
    for (own, even, odd), rim_part in zip(parts, rims):
        if rim_part is None:
            out.append(x_stage(sh, lane, own, even + odd, even - odd, None, None))
        else:
            _, rim_even, rim_odd = rim_part
            out.append(
                x_stage(sh, lane, own, even + odd, even - odd, rim_even + rim_odd, rim_even - rim_odd)
            )
    return out


def spring_parts(ref):
    k, k_sum, k_dif = z_stage(ref, 0)
    pk, mk = y_stage(k)
    pks, mks = y_stage(k_sum)
    pkd, mkd = y_stage(k_dif)
    zero = jnp.zeros_like(k)
    xx = (ACROSS1 * (pk + k_sum) + ACROSS2 * pks, ALONG1 * k + ALONG2 * (pk + k_sum) + SAME3 * pks, zero)
    yy = (
        ALONG1 * pk + ACROSS1 * k_sum + ALONG2 * pks,
        ACROSS1 * k + ALONG2 * pk + ACROSS2 * k_sum + SAME3 * pks,
        zero,
    )
    zz = (
        ALONG1 * k_sum + ACROSS1 * pk + ALONG2 * pks,
        ACROSS1 * k + ACROSS2 * pk + ALONG2 * k_sum + SAME3 * pks,
        zero,
    )
    xy = (zero, zero, MIXED2 * mk + MIXED3 * mks)
    xz = (zero, zero, MIXED2 * k_dif + MIXED3 * pkd)
    yz = (MIXED2 * mkd, MIXED3 * mkd, zero)
    return xx, yy, zz, xy, xz, yz


def own_block(sh, lane, springs):
    main, rim = springs
    k = inner(main, 0)
    out = []
    for index, ((own, even, odd), (_, rim_even, rim_odd)) in enumerate(
        zip(spring_parts(main), spring_parts(rim))
    ):
        total = x_stage(sh, lane, own, even + odd, even - odd, rim_even + rim_odd, rim_even - rim_odd)
        out.append(total + TOTAL * k if index < 3 else total)
    return out


def apply_block(d, v):
    return (
        d[0] * v[0] + d[3] * v[1] + d[4] * v[2],
        d[3] * v[0] + d[1] * v[1] + d[5] * v[2],
        d[4] * v[0] + d[5] * v[1] + d[2] * v[2],
    )


def image_of(sh, lane, v, kv, rims, springs_ref):
    k = springs_ref[6]
    k_before, k_after = shift(k, sh.pitch), shift(k, -sh.pitch)
    last = (sh.x + 1) * sh.pitch
    own = apply_block([springs_ref[f] for f in range(6)], [inner(v, m) for m in range(3)])
    rim_parts = [yz_parts(rims[0]), yz_parts(rims[1])] if rims else None
    out = []
    for m, (plain, scaled) in enumerate(zip(yz_parts(v), yz_parts(kv))):
        after = shift(k_before * (plain[1] + plain[2]) + (scaled[1] + scaled[2]), -sh.pitch)
        before = shift(k_after * (plain[1] - plain[2]) + (scaled[1] - scaled[2]), sh.pitch)
        if rims is None:
            after, before = pick(lane < last, after), pick(lane >= sh.pitch, before)
        else:
            plain_rim, scaled_rim = rim_parts[0][m], rim_parts[1][m]
            edge = k * (plain_rim[1] + plain_rim[2]) + (scaled_rim[1] + scaled_rim[2])
            after = jnp.where(lane < last, after, edge)
            edge = k * (plain_rim[1] - plain_rim[2]) + (scaled_rim[1] - scaled_rim[2])
            before = jnp.where(lane >= sh.pitch, before, edge)
        out.append(own[m] - (k * plain[0] + scaled[0] + after + before))
    return out


def level(sh):
    return lax.broadcasted_iota(jnp.int32, (sh.rows, LANES), 0) - EDGE


def ends_level(sh):
    row = lax.broadcasted_iota(jnp.int32, (4 * EDGE, LANES), 0)
    return jnp.where(row < 2 * EDGE, row, row + sh.rows - 4 * EDGE) - EDGE


def ends(value):
    return jnp.concatenate([value[: 2 * EDGE], value[value.shape[0] - 2 * EDGE :]], axis=0)


def extended_mask(sh, z):
    lane, _, across = sh.lane_grid(1)
    return ((lane < sh.used) & (across >= -1) & (across <= sh.y)) & ((z >= -1) & (z <= sh.z))


def within(sh, axis, place, size):
    index = sh.here(axis)
    low = jnp.where(index > 0, -EDGE, 0)
    high = jnp.where(index < sh.sizes[axis] - 1, size + EDGE, size)
    return (place >= low) & (place < high)


def grid_masks(sh):
    lane, along, across = sh.lane_grid(1)
    lanes = (lane < sh.used) & within(sh, 1, across, sh.y)
    rows = within(sh, 2, level(sh), sh.z)
    return (lanes & within(sh, 0, along, sh.x)) & rows, lanes & rows


def put(ref, f, value):
    ref[f, EDGE : ref.shape[1] - EDGE, :] = value


def local_solve(sh, z, residual_ref, springs_ref, v, kv, factor):
    lane, _, _ = sh.lane_grid(1)
    mask = extended_mask(sh, z)
    for m in range(3):
        factor[m] = pick(mask, relax / jnp.where(mask, springs_ref[m], 1.0))
        value = residual_ref[m] * factor[m]
        put(v[0], m, value)
        put(kv[0], m, springs_ref[6] * value)
    for sweep in range(SWEEPS - 1):
        old, new = sweep % 2, (sweep + 1) % 2
        image = image_of(sh, lane, v[old], kv[old], None, springs_ref)
        for m in range(3):
            value = inner(v[old], m) + factor[m] * (residual_ref[m] - image[m])
            put(v[new], m, value)
            put(kv[new], m, springs_ref[6] * value)
    return (SWEEPS - 1) % 2


def own_level(sh):
    return lax.broadcasted_iota(jnp.int32, (sh.z, LANES), 0)


def coords(sh, z):
    _, along, across = sh.lane_grid(z.shape[0])
    along = jnp.where(along < 0, along + sh.x, jnp.where(along < sh.x, along, along - sh.x))
    across = jnp.where(across < 0, across + sh.y, jnp.where(across < sh.y, across, across - sh.y))
    place = lambda index, size: (2 * index + 1).astype(f32) / size - 1.0
    return place(along, sh.x), place(across, sh.y), place(z, sh.z)


def cell_coords(sh):
    cell = lax.broadcasted_iota(jnp.int32, (sh.cells, sh.z), 0)
    z = lax.broadcasted_iota(jnp.int32, (sh.cells, sh.z), 1)
    x = cell // sh.y
    place = lambda index, size: (2 * index + 1).astype(f32) / size - 1.0
    return place(x, sh.x), place(cell - x * sh.y, sh.y), place(z, sh.z)


def cross(a, b):
    return (a[1] * b[2] - a[2] * b[1], a[2] * b[0] - a[0] * b[2], a[0] * b[1] - a[1] * b[0])


def fold_rows(value):
    total = value[0:8]
    for i in range(8, value.shape[0], 8):
        total = total + value[i : i + 8]
    return jnp.sum(total, axis=0, keepdims=True)


def lane_sums(rows_ref):
    ones = jnp.ones((8, LANES), f32)
    return lax.dot_general(
        ones, rows_ref[...], (((1,), (1,)), ((), ())), precision=highest, preferred_element_type=f32
    )


def coarse_sums(nodes, field, places, count, sums):
    moments = tuple(field) + cross(places, field)
    for node in range(count):
        mask = nodes == node
        for m in range(6):
            sums[node * 6 + m : node * 6 + m + 1, :] = fold_rows(pick(mask, moments[m]))


def sums_line(sh, sums, unknowns):
    flat = (sh.here(0) * sh.sizes[1] + sh.here(1)) * sh.sizes[2] + sh.here(2)
    return pltpu.roll(lane_sums(sums), lax.rem(flat * unknowns, LANES), 1)[0:1]


def coarse_solution(received, inverse_ref, values):
    unknowns, total = inverse_ref.shape
    row = lax.broadcasted_iota(jnp.int32, received.shape, 0)
    part = jnp.zeros((unknowns, LANES), f32)
    for i in range(0, total, LANES):
        owner = (i + lax.broadcasted_iota(jnp.int32, (1, LANES), 1)) // unknowns
        vector = jnp.sum(pick(row == owner, received), axis=0, keepdims=True)
        part = part + inverse_ref[:, i : i + LANES] * vector
    values[0:unknowns, :] = jnp.dot(
        part, jnp.ones((LANES, LANES), f32), precision=highest, preferred_element_type=f32
    )


def coarse_shares(sums, inverse_ref, shares):
    unknowns, total = inverse_ref.shape
    column = jnp.dot(sums[...], jnp.ones((LANES, LANES), f32), precision=highest, preferred_element_type=f32)
    for i in range(0, total, LANES):
        share = inverse_ref[:, i : i + LANES] * column[0:unknowns]
        shares[i // LANES : i // LANES + 1, :] = jnp.sum(share, axis=0, keepdims=True)


def coarse_table(sh, shares_ref, unknowns, flat, table):
    rows = shares_ref.shape[0] // sh.devices
    lane = lax.broadcasted_iota(jnp.int32, (1, LANES), 1)
    for i in range(rows):
        flat[i : i + 1, :] = jnp.sum(shares_ref[pl.ds(i, sh.devices, stride=rows), :], axis=0, keepdims=True)
    for device in range(sh.devices):
        row, place = divmod(device * unknowns, LANES)
        part = shift(flat[row : row + 1, :], -place)
        if place + unknowns > LANES:
            part = jnp.where(lane < LANES - place, part, shift(flat[row + 1 : row + 2, :], -place))
        table[device : device + 1, :] = pick(lane < unknowns, part)


def region_values(sh, table, dz):
    lane, along, across = sh.lane_grid(1)
    x = sh.here(0) + jnp.where(along < 0, -1, jnp.where(along < sh.x, 0, 1))
    y = sh.here(1) + jnp.where(across < 0, -1, jnp.where(across < sh.y, 0, 1))
    z = sh.here(2) + dz
    exists = (lane < sh.used) & (x >= 0) & (x < sh.sizes[0]) & (y >= 0) & (y < sh.sizes[1])
    exists = exists & (z >= 0) & (z < sh.sizes[2])
    device = jnp.where(exists, (x * sh.sizes[1] + y) * sh.sizes[2] + z, -1)
    owner = lax.broadcasted_iota(jnp.int32, (sh.devices, LANES), 0) == device
    return lax.dot_general(
        table[0 : sh.devices, :], owner.astype(f32), (((0,), (0,)), ((), ())), precision=highest, preferred_element_type=f32
    )


def coarse_cells(nodes, places, values, count):
    cells = []
    for m in range(6):
        cell = jnp.zeros(nodes.shape, f32)
        for node in range(count):
            cell = jnp.where(nodes == float(node), values[node * 6 + m : node * 6 + m + 1, :], cell)
        cells.append(cell)
    turned = cross(cells[3:], places)
    return [cells[m] + turned[m] for m in range(3)]


def selection(sh):
    lane, along, across = sh.lane_grid(sh.cells)
    inside = (along >= 0) & (along < sh.x) & (across >= 0) & (across < sh.y)
    row = lax.broadcasted_iota(jnp.int32, (sh.cells, LANES), 0)
    return (inside & (row == along * sh.y + across)).astype(f32)


def to_lanes(value, select, precision=highest):
    return lax.dot_general(
        value, select, (((0,), (0,)), ((), ())), precision=precision, preferred_element_type=f32
    )


def to_cells(value, select):
    return lax.dot_general(
        select, value, (((1,), (1,)), ((), ())), precision=highest, preferred_element_type=f32
    )


def send_lines(sh, lines, slots_ref):
    here = [sh.here(axis) for axis in range(3)]
    corner = [lines[8 * i : 8 * i + 8, :] for i in range(4)]
    top, bottom = lines[32:40, :], lines[40:48, :]
    for x in range(sh.sizes[0]):
        low_high = [jnp.where(x > here[0], corner[2 + high], corner[high]) for high in range(2)]
        for y in range(sh.sizes[1]):
            column = jnp.where(y > here[1], low_high[1], low_high[0])
            for z in range(sh.sizes[2]):
                slot = jnp.where(z == here[2] + 1, top, jnp.where(z == here[2] - 1, bottom, column))
                place = 8 * ((x * sh.sizes[1] + y) * sh.sizes[2] + z)
                slots_ref[place : place + 8, :] = slot


def slot_from(sh, received_ref, step):
    place, exists = 0, None
    for axis in range(3):
        index = sh.here(axis) + step[axis]
        inside = (index >= 0) & (index < sh.sizes[axis])
        exists = inside if exists is None else exists & inside
        place = place * sh.sizes[axis] + jnp.clip(index, 0, sh.sizes[axis] - 1)
    return scale(exists, received_ref[pl.ds(pl.multiple_of(place * 8, 8), 8), :])


def repeat_twice(count):
    row = lax.broadcasted_iota(jnp.int32, (2 * count, count), 0)
    column = lax.broadcasted_iota(jnp.int32, (2 * count, count), 1)
    return ((row >= 2 * column) & (row < 2 * column + 2)).astype(f32)


def ring(size_x, size_y, rows):
    row = lax.broadcasted_iota(jnp.int32, (rows, LANES), 0)
    sides_x, both = 2 * size_y, 2 * size_y + 2 * size_x
    corner = row - both
    x = jnp.where(row < size_y, -1, size_x)
    x = jnp.where(row < sides_x, x, jnp.where(row < sides_x + size_x, row - sides_x, row - sides_x - size_x))
    x = jnp.where(row < both, x, jnp.where(corner < 2, -1, size_x))
    y = jnp.where(row < size_y, row, row - size_y)
    y = jnp.where(row < sides_x, y, jnp.where(row < sides_x + size_x, -1, size_y))
    y = jnp.where(row < both, y, jnp.where((corner == 0) | (corner == 2), -1, size_y))
    return x, y, (row < sides_x) | (row >= both), row < both + 4


def face_shape(sh, label_x, label_y):
    rows = max(4 * sh.x + label_x, 4 * sh.y + label_y)
    return (-(-rows // 8) * 8, LANES)


def pack_faces(sh, natural_ref, stiff, label_x, label_y, x_refs, y_refs):
    even_x, even_y = sh.here(0) % 2 == 0, sh.here(1) % 2 == 0

    def face(at, count, stride, label_at, label_count, label_stride):
        rows = [natural_ref[m, pl.ds(at, count, stride=stride), :] for m in range(4)]
        return rows, stiff[pl.ds(label_at, label_count, stride=label_stride), :]

    above = face(sh.cells - sh.y, sh.y, 1, (label_x - 1) * label_y, label_y, 1)
    below = face(0, sh.y, 1, 0, label_y, 1)
    for refs, links, even, above, below in (
        (x_refs, sh.x_links, even_x, above, below),
        (
            y_refs,
            sh.y_links,
            even_y,
            face(sh.y - 1, sh.x, sh.y, label_y - 1, label_x, label_y),
            face(0, sh.x, sh.y, 0, label_x, label_y),
        ),
    ):
        for i, ref in enumerate(refs):
            ref[...] = jnp.zeros(ref.shape, f32)
            count = above[0][0].shape[0]
            for m in range(4):
                ref[m * count : (m + 1) * count, :] = pair(links, even, above[0][m], below[0][m])[i]
            labels, length = above[1].shape
            ref[4 * count : 4 * count + labels, 0:length] = pair(links, even, above[1], below[1])[i]


def merge_start(sh, refs, x_refs, y_refs, received_ref, sizes, cells, labels):
    residual, nodes, stiff, stiff_rim = refs
    label_x, label_y, label_z = sizes
    lane, along, across = sh.lane_grid(1)
    inside = lane < sh.used
    last = (sh.x + 1) * sh.pitch
    x_mask = {-1: lane < sh.pitch, 0: (lane >= sh.pitch) & (lane < last), 1: (lane >= last) & inside}
    y_mask = {-1: across < 0, 0: (across >= 0) & (across < sh.y), 1: across >= sh.y}
    cells[...] = jnp.zeros(cells.shape, f32)
    labels[...] = jnp.zeros(labels.shape, f32)
    count, label_count = cells.shape[1], labels.shape[0]
    at = label_at = 0
    for axis, face_refs, size, label_size in ((0, x_refs, sh.y, label_y), (1, y_refs, sh.x, label_x)):
        for message in sides(sh, axis, [ref[...] for ref in face_refs]):
            for m in range(4):
                cells[m, at : at + size, :] = message[m * size : (m + 1) * size]
            labels[label_at : label_at + label_size, :] = message[4 * size : 4 * size + label_size, 0:label_z]
            at, label_at = at + size, label_at + label_size
    for dx, dy in ((-1, -1), (-1, 1), (1, -1), (1, 1)):
        slot = slot_from(sh, received_ref, (dx, dy, 0))
        for m, row in enumerate((0, 1, 2, 5)):
            cells[m, at : at + 1, :] = slot[row : row + 1]
        labels[label_at : label_at + 1, :] = slot[3:4, 0:label_z]
        at, label_at = at + 1, label_at + 1
    x, y, _, valid = ring(sh.x, sh.y, count)
    place = (valid & inside & (along == x) & (across == y)).astype(f32)
    own = slice(EDGE, EDGE + sh.z)
    tall_own = slice(2 * EDGE, 2 * EDGE + sh.z)
    for m in range(3):
        residual[m, own, :] += to_lanes(cells[m], place)
    nodes[own, :] += to_lanes(cells[3], place, small)
    by_z = lax.dot_general(
        repeat_twice(label_z), labels[...], (((1,), (1,)), ((), ())), precision=highest, preferred_element_type=f32
    )
    x, y, at_x, valid = ring(label_x, label_y, label_count)
    match = valid & inside & ((along >> 1) == x) & ((across >> 1) == y)
    columns = jnp.dot(by_z, (match & at_x).astype(f32), precision=highest, preferred_element_type=f32)
    stiff_rim[0, tall_own, :] = columns
    columns = columns + jnp.dot(by_z, (match & ~at_x).astype(f32), precision=highest, preferred_element_type=f32)
    stiff[0, tall_own, :] += columns
    for dz in (-1, 1):
        main = edge = jnp.zeros((8, LANES), f32)
        for dx in (-1, 0, 1):
            for dy in (-1, 0, 1):
                slot = slot_from(sh, received_ref, (dx, dy, dz))
                mask = x_mask[dx] & y_mask[dy]
                main = main + pick(mask, shift(slot, dx * sh.x * sh.pitch + dy * sh.y))
                if dx:
                    edge = edge + pick(mask, shift(slot, dx * (sh.x - 1) * sh.pitch + dy * sh.y))
        near = EDGE + sh.z if dz > 0 else EDGE - 1
        for m in range(3):
            residual[m, near : near + 1, :] = main[m : m + 1]
        nodes[near : near + 1, :] = main[5:6]
        for row in (EDGE + near, EDGE + near + dz):
            stiff[0, row : row + 1, :] = main[3:4]
            stiff_rim[0, row : row + 1, :] = edge[3:4]


def call(kernel, name, outs, ins, scratch=(), remote_ins=False, remote_outs=()):
    space = pltpu.HBM if remote_ins else pltpu.VMEM
    return pl.pallas_call(
        kernel,
        out_shape=[jax.ShapeDtypeStruct(shape, f32) for shape in outs],
        in_specs=[pl.BlockSpec(memory_space=space) for _ in ins],
        out_specs=[
            pl.BlockSpec(memory_space=pltpu.HBM if i in remote_outs else pltpu.VMEM) for i in range(len(outs))
        ],
        scratch_shapes=[pltpu.VMEM(shape, f32) if isinstance(shape, tuple) else shape for shape in scratch],
        compiler_params=pltpu.CompilerParams(vmem_limit_bytes=(62 if remote_ins else 48) * 1024 * 1024),
        name=name,
    )(*ins)


def permutation(sizes, moves):
    def partner(axis, link, index):
        size = sizes[axis]
        other = index ^ 1 if link == 0 else index + (1 if index % 2 else -1)
        if 0 <= other < size:
            return other
        return size - 1 - index if axis == 2 and size % 2 == 0 else index

    pairs = []
    for x in range(sizes[0]):
        for y in range(sizes[1]):
            for z in range(sizes[2]):
                place = [x, y, z]
                goal = [partner(a, moves[a], place[a]) if a in moves else place[a] for a in range(3)]
                if goal == place and 0 not in moves and sizes[0] % 2 == 0:
                    goal[0] = partner(0, 0, x)
                flat = [(p[0] * sizes[1] + p[1]) * sizes[2] + p[2] for p in (place, goal)]
                pairs.append(tuple(flat))
    return pairs


def send(sh, value, moves):
    return lax.ppermute(value, AXES, permutation(sh.sizes, moves))


def send_z(sh, messages):
    return [send(sh, message, {2: link}) for link, message in enumerate(messages)]


def send_faces(sh, x_messages, y_messages):
    from_y = [send(sh, message, {1: link}) for link, message in enumerate(y_messages)]
    from_x = [send(sh, message, {0: link}) for link, message in enumerate(x_messages)]
    return from_y, from_x


def to_all(slots):
    return lax.all_to_all(slots, AXES, 0, 0, tiled=True)


def exchange(sh, ex, name, field, z_messages):
    from_z = send_z(sh, z_messages)

    corners = sh.x_links * sh.y_links

    def packer(*refs):
        take = Taker(refs)
        field_ref, z_refs = take.one(), take(sh.z_links)
        x_refs, y_refs, corner_refs, scratch = take(sh.x_links), take(sh.y_links), take(corners), take.one()
        merge_z(sh, ex, field_ref, z_refs, scratch, 0)
        pack_xy(sh, ex, scratch, x_refs, y_refs, corner_refs)

    plane = (sh.rows, LANES)
    messages = call(
        packer,
        name,
        [plane] * sh.x_links
        + [folded_shape(sh, ex.fields * ex.layers)] * sh.y_links
        + [folded_shape(sh, ex.layers)] * corners,
        [field] + from_z,
        [(ex.fields,) + plane],
    )
    take = Taker(messages)
    x_messages, y_messages = take(sh.x_links), take(sh.y_links)
    from_y, straight = send_faces(sh, x_messages, y_messages)
    from_x = []
    for link in range(sh.x_links):
        from_x.append(straight[link])
        from_x.extend(send(sh, take.one(), {0: link, 1: other}) for other in range(sh.y_links))
    return from_z, from_y, from_x


class Taker:
    def __init__(self, refs):
        self.refs, self.at = refs, 0

    def __call__(self, count):
        self.at += count
        return self.refs[self.at - count : self.at]

    def one(self):
        return self(1)[0]


def merge_all(sh, ex, take, scratch, rim, guard):
    field = take.one()
    from_z, from_y = take(sh.z_links), take(sh.y_links)
    from_x = take(sh.x_links * (1 + sh.y_links))
    merge_z(sh, ex, field, from_z, scratch, guard)
    merge_xy(sh, ex, scratch, rim, guard, from_y, from_x)


def body(right_side, phase_labels, phase_moduli, coarse_nodes, coarse_inverse):
    sizes = tuple(lax.axis_size(axis) for axis in AXES)
    _, size_x, size_y, size_z = right_side.shape
    sh = Shape(size_x, size_y, size_z, phase_moduli.shape[0], sizes)
    unknowns = coarse_inverse.shape[0]
    node_count = unknowns // 6
    sum_rows = -(-unknowns // 8) * 8 + 8
    share_rows = coarse_inverse.shape[1] // LANES
    own = slice(EDGE, EDGE + sh.z)
    plane = (sh.rows, LANES)
    fields = (3,) + plane
    tall = (3, sh.tall, LANES)
    slots = (sh.devices, LANES)
    z_shape = lambda ex: [(8 * ex.fields, LANES)] * sh.z_links
    natural = right_side.reshape(3, sh.cells, sh.z)
    nodes_natural = coarse_nodes.reshape(sh.cells, sh.z)
    label_x, label_y, label_z = phase_labels.shape

    def block_places():
        lane, along, across = sh.lane_grid(label_x * label_y)
        inside = (along >= 0) & (along < sh.x) & (across >= 0) & (across < sh.y)
        block = lax.broadcasted_iota(jnp.int32, along.shape, 0)
        return (inside & (block == (along >> 1) * label_y + (across >> 1))).astype(f32)

    def end_layers(values, places):
        length = values.shape[1]
        row = lax.broadcasted_iota(jnp.int32, (8, length), 0)
        at = lax.broadcasted_iota(jnp.int32, (8, length), 1)
        ends = ((row == 0) & (at == length - 1)) | ((row == 1) & (at == 0))
        return jnp.dot(to_cells(values, ends.astype(f32)), places, precision=highest, preferred_element_type=f32)

    def begin(natural_in, labels_in, moduli_in, nodes_in, stiff, slots_ref, *rest):
        x_refs, y_refs = rest[: sh.x_links], rest[sh.x_links : sh.x_links + sh.y_links]
        natural_ref, labels_ref, moduli_ref, nodes_ref, sems, sums, lines = rest[sh.x_links + sh.y_links :]
        pairs = ((natural_in, natural_ref.at[0:3, 0 : sh.cells, :]), (labels_in, labels_ref.at[0:label_x]), (moduli_in, moduli_ref), (nodes_in, nodes_ref))
        copies = [pltpu.make_async_copy(a, b, sems.at[i]) for i, (a, b) in enumerate(pairs)]
        for copy in copies:
            copy.start()
        sums[...] = jnp.zeros(sums.shape, f32)
        lines[...] = jnp.zeros(lines.shape, f32)
        for copy in copies:
            copy.wait()
        for i in range(label_x):
            labels = labels_ref[i]
            moduli = jnp.zeros(labels.shape, f32)
            for phase in range(sh.phases):
                moduli = jnp.where(labels == phase, moduli_ref[phase], moduli)
            stiff[i * label_y : (i + 1) * label_y, :] = moduli
        natural_ref[3, 0 : sh.cells, :] = nodes_ref[...].astype(f32) + 1.0
        cells = [natural_ref[m, 0 : sh.cells, :] for m in range(4)]
        coarse_sums(nodes_ref[...], cells[:3], cell_coords(sh), node_count, sums)
        line = sums_line(sh, sums, unknowns)
        for i, (cell, block) in enumerate(
            (
                (0, 0),
                (sh.y - 1, label_y - 1),
                ((sh.x - 1) * sh.y, (label_x - 1) * label_y),
                (sh.cells - 1, label_x * label_y - 1),
            )
        ):
            for m in range(3):
                lines[8 * i + m : 8 * i + m + 1, :] = natural_ref[m, cell : cell + 1, :]
            lines[8 * i + 3 : 8 * i + 4, 0:label_z] = stiff[block : block + 1, :]
            lines[8 * i + 5 : 8 * i + 6, :] = natural_ref[3, cell : cell + 1, :]
        select = selection(sh)
        layers = [end_layers(cells[m], select) for m in range(4)] + [end_layers(stiff[0 : label_x * label_y, :], block_places())]
        for i in range(2):
            for layer, row in zip(layers, (0, 1, 2, 5, 3)):
                lines[8 * (4 + i) + row : 8 * (4 + i) + row + 1, :] = layer[i : i + 1]
        for i in range(6):
            lines[8 * i + 4 : 8 * i + 5, :] = line
        send_lines(sh, lines, slots_ref)
        pack_faces(sh, natural_ref, stiff, label_x, label_y, x_refs, y_refs)

    block_rows = (8 * -(-(label_x + 8) * label_y // 8), label_z)
    stiff_blocks, lines, *messages = call(
        begin,
        "begin",
        [block_rows, (8 * sh.devices, LANES)]
        + [face_shape(sh, label_x, label_y)] * (sh.x_links + sh.y_links),
        [natural, phase_labels, phase_moduli, nodes_natural],
        [
            (4, sh.cells + 8, sh.z),
            pltpu.VMEM((label_x + 2, label_y, label_z), jnp.int32),
            pltpu.SMEM(phase_moduli.shape, f32),
            pltpu.VMEM(nodes_natural.shape, jnp.int32),
            pltpu.SemaphoreType.DMA((4,)),
            (LANES, LANES),
            (56, LANES),
        ],
        remote_ins=True,
    )

    def spread(natural_ref, nodes_ref, stiff, field_ref, lanes_ref):
        select = selection(sh)
        field_ref[...] = jnp.zeros(field_ref.shape, f32)
        for m in range(3):
            field_ref[m, own, :] = to_lanes(natural_ref[m], select)
        by_z = lax.dot_general(
            repeat_twice(label_z),
            stiff[0 : label_x * label_y, :],
            (((1,), (1,)), ((), ())),
            precision=highest,
            preferred_element_type=f32,
        )
        field_ref[3, own, :] = jnp.dot(by_z, block_places(), precision=highest, preferred_element_type=f32)
        lanes_ref[...] = to_lanes(nodes_ref[...].astype(f32) + 1.0, select, small) - 1.0

    start_field, nodes = call(
        spread, "spread", [(4,) + plane, (sh.z, LANES)], [natural, nodes_natural, stiff_blocks]
    )
    from_y, from_x = send_faces(sh, messages[: sh.x_links], messages[sh.x_links :])
    lines = to_all(lines)

    short = (3, 6 * EDGE, LANES)
    short_fields = (3, 4 * EDGE, LANES)
    solve_scratch = [tall] * 4 + [fields]
    short_scratch = [short] * 4 + [short_fields]

    def end_rows(ref):
        def rows(f, start, count):
            place = start + EDGE if start < 2 * EDGE else start - sh.rows + 5 * EDGE
            return ref[f, place : place + count, :]

        return rows

    def first_ends(*refs):
        take = Taker(refs)
        field_ref = take.one()
        y_refs, x_refs = take(sh.y_links), take(sh.x_links)
        nodes_ref, lines_ref, inverse_ref = take(3)
        residual, wide_nodes, stiffness_ref, values = take(4)
        z_refs = take(sh.z_links)
        stiff, stiff_rim, cells, labels, short_stiff, short_rim, some_residual, springs = take(8)
        v0, v1, kv0, kv1, factor = take(5)
        clear_guards(sh, (stiff, stiff_rim, short_stiff, short_rim, v0, v1, kv0, kv1))
        residual[...] = field_ref[0:3]
        put(stiff, 0, field_ref[3])
        put(stiff_rim, 0, jnp.zeros(plane, f32))
        sizes = phase_labels.shape
        wide_nodes[...] = jnp.zeros(plane, f32)
        wide_nodes[own, :] = nodes_ref[...] + 1.0
        merge_start(sh, (residual, wide_nodes, stiff, stiff_rim), x_refs, y_refs, lines_ref, sizes, cells, labels)
        wide_nodes[...] = wide_nodes[...] - 1.0
        stiffness_ref[0] = inner(stiff, 0)
        stiffness_ref[1] = inner(stiff_rim, 0)
        coarse_solution(lines_ref[pl.ds(4, sh.devices, stride=8), :], inverse_ref, values)
        lane, _, _ = sh.lane_grid(1)
        put(short_stiff, 0, ends(stiffness_ref[0]))
        put(short_rim, 0, ends(stiffness_ref[1]))
        for f, entry in enumerate(own_block(sh, lane, (short_stiff, short_rim))):
            springs[f] = entry
        springs[6] = inner(short_stiff, 0)
        for m in range(3):
            some_residual[m] = ends(residual[m])
        index = local_solve(sh, ends_level(sh), some_residual, springs, (v0, v1), (kv0, kv1), factor)
        solution = (v0, v1)[index]
        z = lax.broadcasted_iota(jnp.int32, (2 * EDGE, LANES), 0)
        z = jnp.where(z < EDGE, z, z + sh.z - 2 * EDGE)
        some_nodes = jnp.concatenate([nodes_ref[0:EDGE, :], nodes_ref[sh.z - EDGE : sh.z, :]], axis=0)
        added = coarse_cells(some_nodes, coords(sh, z), values, node_count)
        for m in range(3):
            solution[m, 2 * EDGE : 4 * EDGE, :] += pick(some_nodes >= 0.0, added[m])
        pack_z(sh, DEEP, end_rows(solution), z_refs)

    residual, wide_nodes, stiffness, values, *z_messages = call(
        first_ends,
        "first_ends",
        [fields, plane, (2,) + plane, (sum_rows, LANES)] + z_shape(DEEP),
        [start_field, *from_y, *from_x, nodes, lines, coarse_inverse],
        [(1, sh.tall, LANES)] * 2
        + [
            (4, 8 * -(-(2 * sh.x + 2 * sh.y + 4) // 8) + 8, LANES),
            (8 * -(-(2 * label_x + 2 * label_y + 4) // 8) + 8, label_z),
        ]
        + [(1, 6 * EDGE, LANES)] * 2
        + [short_fields, (7, 4 * EDGE, LANES)]
        + short_scratch,
    )

    def first_solve(residual_ref, stiffness_ref, values, nodes_ref, solution_ref, springs_ref, *rest):
        stiff, stiff_rim, v0, v1, kv0, kv1, factor = rest
        clear_guards(sh, (stiff, stiff_rim, v0, v1, kv0, kv1))
        put(stiff, 0, stiffness_ref[0])
        put(stiff_rim, 0, stiffness_ref[1])
        springs_ref[6] = stiffness_ref[0]
        springs_ref[7] = stiffness_ref[1]
        lane, _, _ = sh.lane_grid(1)
        for f, entry in enumerate(own_block(sh, lane, (stiff, stiff_rim))):
            springs_ref[f] = entry
        index = local_solve(sh, level(sh), residual_ref, springs_ref, (v0, v1), (kv0, kv1), factor)
        for m in range(3):
            solution_ref[m] = inner((v0, v1)[index], m)
        added = coarse_cells(nodes_ref[...], coords(sh, own_level(sh)), values, node_count)
        for m in range(3):
            solution_ref[m, own, :] += pick(nodes_ref[...] >= 0.0, added[m])

    solved, springs = call(
        first_solve,
        "first_solve",
        [fields, (8,) + plane],
        [residual, stiffness, values, nodes],
        [(1, sh.tall, LANES)] * 2 + solve_scratch,
    )
    from_z, from_y, from_x = exchange(sh, DEEP, "deep", solved, z_messages)

    def first_image(*refs):
        take = Taker(refs)
        merging = take(1 + sh.z_links + sh.y_links + sh.x_links * (1 + sh.y_links))
        nodes_ref, springs_ref, inverse_ref = take(3)
        search_ref, image_ref, slots_out = take(3)
        z_refs = take(sh.z_links)
        v, rim, kv, k_rim, sums, shares, slots_ref, sem = take(8)
        some_residual, some_springs, v0, v1, kv0, kv1, factor = take(7)
        clear_guards(sh, (v0, v1, kv0, kv1))
        clear_guards(sh, (v, rim, kv, k_rim))
        merge_all(sh, DEEP, Taker(merging), v, rim, EDGE)
        lane, _, _ = sh.lane_grid(1)

        in_grid, in_rim = grid_masks(sh)
        for m in range(3):
            value = pick(in_grid, inner(v, m))
            put(v, m, value)
            search_ref[m] = value
            put(kv, m, springs_ref[6] * value)
            value = pick(in_rim, inner(rim, m))
            put(rim, m, value)
            put(k_rim, m, springs_ref[7] * value)
        image = image_of(sh, lane, v, kv, (rim, k_rim), springs_ref)
        keep = in_grid & extended_mask(sh, level(sh))
        for m in range(3):
            image_ref[m] = pick(keep, image[m])
        sums[...] = jnp.zeros(sums.shape, f32)
        field = [image_ref[m, own, :] for m in range(3)]
        coarse_sums(nodes_ref[...], field, coords(sh, own_level(sh)), node_count, sums)
        coarse_shares(sums, inverse_ref, shares)
        for device in range(sh.devices):
            slots_ref[device * share_rows : (device + 1) * share_rows, :] = shares[0:share_rows, :]
        copy = pltpu.make_async_copy(slots_ref.at[0 : slots_out.shape[0], :], slots_out, sem)
        copy.start()
        for m in range(3):
            some_residual[m] = ends(image_ref[m])
        for f in range(7):
            some_springs[f] = ends(springs_ref[f])
        index = local_solve(sh, ends_level(sh), some_residual, some_springs, (v0, v1), (kv0, kv1), factor)
        pack_z(sh, NEAR, end_rows((v0, v1)[index]), z_refs)
        copy.wait()

    all_slots = (sh.devices * share_rows, LANES)
    search, image, shares, *z_messages = call(
        first_image,
        "first_image",
        [fields, fields, all_slots] + z_shape(NEAR),
        [solved, *from_z, *from_y, *from_x, nodes, springs, coarse_inverse],
        [tall] * 4
        + [(LANES, LANES), (8 * -(-share_rows // 8) + 8, LANES)]
        + [(8 * -(-all_slots[0] // 8) + 8, LANES), pltpu.SemaphoreType.DMA]
        + [short_fields, (7, 4 * EDGE, LANES)]
        + short_scratch,
        remote_outs=(2,),
    )
    shares = to_all(shares.reshape(sh.devices, 1, share_rows * LANES)).reshape(shares.shape)

    def second_solve(image_ref, springs_ref, local_ref, v0, v1, kv0, kv1, factor):
        clear_guards(sh, (v0, v1, kv0, kv1))
        index = local_solve(sh, level(sh), image_ref, springs_ref, (v0, v1), (kv0, kv1), factor)
        for m in range(3):
            local_ref[m] = inner((v0, v1)[index], m)

    (solved,) = call(second_solve, "second_solve", [fields], [image, springs], solve_scratch)
    from_z, from_y, from_x = exchange(sh, NEAR, "near", solved, z_messages)

    def between(shares_ref, wide_nodes, nodes_ref, start_ref, search_ref, first_ref, coarse_ref, sums, *scratch):
        flat, table, values = scratch
        coarse_ref[...] = jnp.zeros(coarse_ref.shape, f32)
        coarse_table(sh, shares_ref, unknowns, flat, table)
        last = lax.broadcasted_iota(jnp.int32, (1, LANES), 0) + sh.z - 1
        for dz, first, z in ((0, EDGE, own_level(sh)), (-1, EDGE - 1, last), (1, EDGE + sh.z, last - sh.z + 1)):
            values[...] = region_values(sh, table, dz)
            rows = slice(first, first + z.shape[0])
            added = coarse_cells(wide_nodes[rows, :], coords(sh, z), values, node_count)
            for m in range(3):
                coarse_ref[m, rows, :] = added[m]
        valid = nodes_ref[...] >= 0.0
        row = lax.broadcasted_iota(jnp.int32, sums.shape, 0)
        total = jnp.zeros(sums.shape, f32)
        for i, other in enumerate((start_ref, first_ref)):
            product = sum(search_ref[m, own, :] * other[m, own, :] for m in range(3))
            total = jnp.where(row == i, fold_rows(pick(valid, product)), total)
        sums[...] = total

    coarse_field, sums = call(
        between,
        "between",
        [fields, (8, LANES)],
        [shares, wide_nodes, nodes, start_field, search, image],
        [(8 * -(-share_rows // 8) + 8, LANES), (8 * -(-sh.devices // 8) + 8, LANES), (LANES, LANES)],
    )

    def second_image(*refs):
        take = Taker(refs)
        merging = take(1 + sh.z_links + sh.y_links + sh.x_links * (1 + sh.y_links))
        nodes_ref, springs_ref, first_ref, coarse_ref, early_ref = take(5)
        second_ref, image_ref, slots_ref = take(3)
        v, kv, sums = take(3)
        clear_guards(sh, (v, kv))
        merge_all(sh, NEAR, Taker(merging), v, None, EDGE)
        lane, _, _ = sh.lane_grid(1)
        in_grid, _ = grid_masks(sh)
        for m in range(3):
            value = pick(in_grid, inner(v, m)) + coarse_ref[m]
            put(v, m, value)
            second_ref[m] = value
            put(kv, m, springs_ref[6] * value)
        image = image_of(sh, lane, v, kv, None, springs_ref)
        for m in range(3):
            image_ref[m] = image[m]
        valid = nodes_ref[...] >= 0.0
        sums[...] = jnp.zeros(sums.shape, f32)
        sums[0:8, :] = early_ref[...]
        for i, other in ((2, first_ref), (3, image_ref)):
            product = sum(second_ref[m, own, :] * other[m, own, :] for m in range(3))
            sums[i : i + 1, :] = fold_rows(pick(valid, product))
        slots_ref[...] = jnp.broadcast_to(lane_sums(sums)[0:1], slots_ref.shape)

    second, second_image_field, sums = call(
        second_image,
        "second_image",
        [fields, fields, slots],
        [solved, *from_z, *from_y, *from_x, nodes, springs, image, coarse_field, sums],
        [tall] * 2 + [(LANES, LANES)],
    )
    totals = to_all(sums)

    def turn(search_ref, first_ref, second_ref, image_ref, out_ref):
        select = selection(sh)
        for i, ref in enumerate((search_ref, first_ref, second_ref, image_ref)):
            for m in range(3):
                out_ref[i, m] = to_cells(ref[m, own, :], select)

    (turned,) = call(turn, "turn", [(4,) + natural.shape], [search, image, second, second_image_field])

    def finish(totals_ref, natural_ref, turned_ref, field_ref, residual_ref):
        total = jnp.sum(totals_ref[...], axis=0, keepdims=True)
        rz, zw, wq, qv = [total[:, i : i + 1] for i in range(4)]
        step0 = rz / zw
        rho = step0 * step0 * wq - step0 * zw
        grow = 1.0 + rho / rz
        curvature = grow * grow * zw - 2.0 * grow * step0 * wq + step0 * step0 * qv
        step1 = rho / curvature
        first = step0 + step1 * grow
        second = step0 * step1
        for m in range(3):
            field_ref[m] = first * turned_ref[0, m] - second * turned_ref[2, m]
            residual_ref[m] = natural_ref[m] - (first * turned_ref[1, m] - second * turned_ref[3, m])

    solution_field, residual = call(
        finish, "finish", [natural.shape, natural.shape], [totals, natural, turned]
    )
    return solution_field.reshape(right_side.shape), residual.reshape(right_side.shape)


def solution(mesh):
    in_specs = (
        P(None, "gx", "gy", "gz"),
        P("gx", "gy", "gz"),
        P(),
        P("gx", "gy", "gz"),
        P(("gx", "gy", "gz"), None),
    )
    out_specs = (P(None, "gx", "gy", "gz"), P(None, "gx", "gy", "gz"))
    return jax.shard_map(body, mesh=mesh, in_specs=in_specs, out_specs=out_specs, check_vma=False)
```

```python
import jax
import jax.numpy as jnp
from jax import lax
from jax.experimental import pallas as pl
from jax.experimental.pallas import tpu as pltpu
from jax.sharding import PartitionSpec as P

AXES = ("gx", "gy", "gz")
SWEEPS = 4
relax = 0.6
highest = lax.Precision.HIGHEST
small = lax.Precision.DEFAULT
f32 = jnp.float32
LANES = 128
EDGE = 8

ALONG1, ACROSS1 = 0.75, 0.5
ALONG2, ACROSS2, MIXED2 = 0.3125, 0.25, 0.0625
SAME3, MIXED3 = 7.0 / 36.0, 1.0 / 36.0
TOTAL = 2 * ALONG1 + 4 * ACROSS1 + 8 * ALONG2 + 4 * ACROSS2 + 8 * SAME3


class Exchange:
    def __init__(self, fields, layers, up, down):
        self.fields, self.layers, self.up, self.down = fields, layers, up, down


DEEP = Exchange(3, 3, -2, -1)
NEAR = Exchange(3, 2, -1, -1)


class Shape:
    def __init__(self, size_x, size_y, size_z, phases, mesh_sizes):
        self.x, self.y, self.z = size_x, size_y, size_z
        self.pitch = size_y + 4
        self.used = (size_x + 2) * self.pitch
        assert self.used <= LANES
        self.rows = size_z + 2 * EDGE
        self.tall = self.rows + 2 * EDGE
        self.phases = phases
        self.sizes = mesh_sizes
        self.devices = mesh_sizes[0] * mesh_sizes[1] * mesh_sizes[2]
        self.cells = size_x * size_y
        self.links = [1 if n <= 2 else 2 for n in mesh_sizes]
        self.x_links, self.y_links, self.z_links = self.links

    def lane_grid(self, rows):
        lane = lax.broadcasted_iota(jnp.int32, (rows, LANES), 1)
        column = jnp.zeros_like(lane)
        for j in range(1, self.x + 2):
            column = column + (lane >= j * self.pitch).astype(jnp.int32)
        offset = lane - column * self.pitch
        return lane, column - 1, offset - 2

    def here(self, axis):
        return lax.axis_index(AXES[axis])


def shift(value, amount):
    amount = amount % LANES
    return value if amount == 0 else pltpu.roll(value, amount, 1)


def pick(mask, value):
    return jnp.where(mask, value, 0.0)


def scale(flag, value):
    return value * flag.astype(f32)


def pair(links, even, upward, downward):
    first = jnp.where(even, upward, downward)
    return (first,) if links == 1 else (first, jnp.where(even, downward, upward))


def sides(sh, axis, received):
    index, size = sh.here(axis), sh.sizes[axis]
    even = index % 2 == 0
    first = received[0]
    second = received[1] if len(received) > 1 else jnp.zeros_like(first)
    below = jnp.where(even, second, first)
    above = jnp.where(even, first, second)
    return scale(index > 0, below), scale(index < size - 1, above)


def lane_range(lane, start, count):
    return (lane >= start) & (lane < start + count)


def pack_z(sh, ex, source, out_refs):
    even = sh.here(2) % 2 == 0
    for ref in out_refs:
        ref[...] = jnp.zeros(ref.shape, f32)
    for f in range(ex.fields):
        upward = source(f, EDGE + sh.z + ex.up, ex.layers)
        downward = source(f, EDGE + ex.down, ex.layers)
        for ref, message in zip(out_refs, pair(sh.z_links, even, upward, downward)):
            ref[8 * f : 8 * f + ex.layers, :] = message


def merge_z(sh, ex, field_ref, received_refs, scratch, guard):
    below, above = sides(sh, 2, [ref[...] for ref in received_refs])
    for f in range(ex.fields):
        scratch[f, guard : guard + sh.rows, :] = field_ref[f]
        low = guard + EDGE + ex.up
        high = guard + EDGE + sh.z + ex.down
        scratch[f, low : low + ex.layers, :] += below[8 * f : 8 * f + ex.layers]
        scratch[f, high : high + ex.layers, :] += above[8 * f : 8 * f + ex.layers]


def fold(sh, value, layers, start=None):
    folds = sh.pitch // layers
    height = -(-sh.rows // (8 * folds)) * 8
    lane, _, across = sh.lane_grid(1)
    total = jnp.zeros((height, LANES), f32)
    for i, first in enumerate(range(0, sh.rows, height)):
        part = value[first : first + height]
        if start is not None:
            part = pick((lane < sh.used) & lane_range(across, start, layers), part)
        part = shift(part, i * layers - (0 if start is None else start + 2))
        if part.shape[0] < height:
            part = jnp.concatenate([part, jnp.zeros((height - part.shape[0], LANES), f32)], axis=0)
        total = total + part
    return total


def folded_shape(sh, layers):
    return (-(-sh.rows // (8 * (sh.pitch // layers))) * 8, LANES)


def unfold(sh, message, layers, start):
    height = message.shape[0]
    lane, _, across = sh.lane_grid(1)
    mask = (lane < sh.used) & lane_range(across, start, layers)
    parts = []
    for i, first in enumerate(range(0, sh.rows, height)):
        part = message[0 : min(height, sh.rows - first)]
        parts.append(pick(mask, shift(part, start + 2 - i * layers)))
    return jnp.concatenate(parts, axis=0) if len(parts) > 1 else parts[0]


def pack_xy(sh, ex, scratch, x_refs, y_refs, corner_refs):
    rows = sh.rows
    lane, _, across = sh.lane_grid(1)
    even_x, even_y = sh.here(0) % 2 == 0, sh.here(1) % 2 == 0
    span = ex.layers * sh.pitch
    x_up = x_down = y_up = y_down = jnp.zeros((rows, LANES), f32)
    inside = lane < sh.used
    y_above, y_below = sh.y + ex.up, ex.down
    for f in range(ex.fields):
        value = scratch[f]
        start = (sh.x + ex.up + 1) * sh.pitch
        x_up = x_up + shift(pick(lane_range(lane, start, span), value), f * span - start)
        start = (ex.down + 1) * sh.pitch
        x_down = x_down + shift(pick(lane_range(lane, start, span), value), f * span - start)
        mask = inside & lane_range(across, y_above, ex.layers)
        y_up = y_up + shift(pick(mask, value), f * ex.layers - y_above - 2)
        mask = inside & lane_range(across, y_below, ex.layers)
        y_down = y_down + shift(pick(mask, value), f * ex.layers - y_below - 2)
    packed = ex.fields * ex.layers
    y_up, y_down = fold(sh, y_up, packed), fold(sh, y_down, packed)
    for ref, message in zip(y_refs, pair(sh.y_links, even_y, y_up, y_down)):
        ref[...] = message
    for i, message in enumerate(pair(sh.x_links, even_x, x_up, x_down)):
        x_refs[i][...] = message
        upward, downward = fold(sh, message, ex.layers, y_above), fold(sh, message, ex.layers, y_below)
        for j, corner in enumerate(pair(sh.y_links, even_y, upward, downward)):
            corner_refs[i * sh.y_links + j][...] = corner


def merge_xy(sh, ex, scratch, rim, guard, y_refs, x_refs):
    lane, _, across = sh.lane_grid(1)
    inside = lane < sh.used
    low_mask = inside & lane_range(across, ex.up, ex.layers)
    high_mask = inside & lane_range(across, sh.y + ex.down, ex.layers)
    span = ex.layers * sh.pitch
    packed = ex.fields * ex.layers
    below_y, above_y = [unfold(sh, value, packed, -2) for value in sides(sh, 1, [ref[...] for ref in y_refs])]
    per_link = 1 + sh.y_links
    sums = []
    for link in range(sh.x_links):
        straight, diagonal = x_refs[link * per_link], x_refs[link * per_link + 1 : (link + 1) * per_link]
        total = straight[...]
        below, above = sides(sh, 1, [ref[...] for ref in diagonal])
        total = total + unfold(sh, below, ex.layers, ex.up)
        sums.append(total + unfold(sh, above, ex.layers, sh.y + ex.down))
    below_x, above_x = sides(sh, 0, sums)
    first = 1 if ex.up == -2 else 0
    last = ex.layers - 1 if ex.down + ex.layers == 2 else ex.layers
    for f in range(ex.fields):
        addend = pick(low_mask, shift(below_y, ex.up + 2 - ex.layers * f))
        addend = addend + pick(high_mask, shift(above_y, sh.y + ex.down + 2 - ex.layers * f))
        start = (ex.up + first + 1) * sh.pitch
        count = (ex.layers - first) * sh.pitch
        moved = shift(below_x, start - f * span - first * sh.pitch)
        addend = addend + pick(lane_range(lane, start, count), moved)
        start = (sh.x + ex.down + 1) * sh.pitch
        moved = shift(above_x, start - f * span)
        addend = addend + pick(lane_range(lane, start, last * sh.pitch), moved)
        scratch[f, guard : guard + sh.rows, :] += addend
        if rim is not None:
            low = pick(lane_range(lane, 0, sh.pitch), shift(below_x, -f * span))
            start = (sh.x + 1) * sh.pitch
            moved = shift(above_x, start - f * span - last * sh.pitch)
            high = pick(lane_range(lane, start, sh.pitch), moved)
            rim[f, guard : guard + sh.rows, :] = low + high


def clear_guards(sh, refs):
    for ref in refs:
        for f in range(ref.shape[0]):
            ref[f, :EDGE, :] = jnp.zeros((EDGE, LANES), f32)
            ref[f, ref.shape[1] - EDGE :, :] = jnp.zeros((EDGE, LANES), f32)


def inner(ref, f):
    return ref[f, EDGE : ref.shape[1] - EDGE, :]


def z_stage(ref, f):
    end = ref.shape[1] - EDGE
    after = ref[f, EDGE + 1 : end + 1, :]
    before = ref[f, EDGE - 1 : end - 1, :]
    return inner(ref, f), before + after, after - before


def y_stage(value):
    after, before = shift(value, -1), shift(value, 1)
    return before + after, after - before


COLUMNS = [(dx, dy) for dx in (-1, 0, 1) for dy in (-1, 0, 1) if dx or dy]


def column_parts(ref, sign=None):
    a, a_sum, a_dif = z_stage(ref, 0)
    b, b_sum, b_dif = z_stage(ref, 1)
    c, c_sum, c_dif = z_stage(ref, 2)
    parts = {(0, 0): (ACROSS1 * a_sum, ACROSS1 * b_sum, ALONG1 * c_sum)}
    mixed_x, mixed_y = MIXED2 * b + MIXED3 * b_sum, MIXED2 * a + MIXED3 * a_sum
    x_c_dif = c_dif
    if sign is not None:
        mixed_x, mixed_y, x_c_dif, a_dif = sign * mixed_x, sign * mixed_y, sign * c_dif, sign * a_dif
    both_z = ACROSS1 * c + ALONG2 * c_sum
    along, across = ALONG1 * a + ALONG2 * a_sum, ACROSS1 * b + ACROSS2 * b_sum
    for dx in (-1, 1):
        parts[dx, 0] = (along + dx * MIXED2 * x_c_dif, across, both_z + dx * MIXED2 * a_dif)
    along, across = ALONG1 * b + ALONG2 * b_sum, ACROSS1 * a + ACROSS2 * a_sum
    for dy in (-1, 1):
        parts[0, dy] = (across, along + dy * MIXED2 * c_dif, both_z + dy * MIXED2 * b_dif)
    same_x, same_y = ALONG2 * a + SAME3 * a_sum, ALONG2 * b + SAME3 * b_sum
    same_z = ACROSS2 * c + SAME3 * c_sum
    for dx in (-1, 1):
        for dy in (-1, 1):
            parts[dx, dy] = (
                (same_x + dx * dy * mixed_x) + dx * MIXED3 * x_c_dif,
                (same_y + dx * dy * mixed_y) + dy * MIXED3 * c_dif,
                (same_z + dx * MIXED3 * a_dif) + dy * MIXED3 * b_dif,
            )
    return parts


def put_columns(sh, springs_ref):
    for i, (dx, dy) in enumerate(COLUMNS):
        springs_ref[8 + i] = shift(springs_ref[6], dx * sh.pitch + dy)


def x_stage(sh, lane, own, plus, minus, rim_plus, rim_minus):
    after, before = shift(plus, -sh.pitch), shift(minus, sh.pitch)
    last = (sh.x + 1) * sh.pitch
    if rim_plus is None:
        return own + pick(lane < last, after) + pick(lane >= sh.pitch, before)
    return own + jnp.where(lane < last, after, rim_plus) + jnp.where(lane >= sh.pitch, before, rim_minus)


def spring_parts(ref):
    k, k_sum, k_dif = z_stage(ref, 0)
    pk, mk = y_stage(k)
    pks, mks = y_stage(k_sum)
    pkd, mkd = y_stage(k_dif)
    zero = jnp.zeros_like(k)
    xx = (ACROSS1 * (pk + k_sum) + ACROSS2 * pks, ALONG1 * k + ALONG2 * (pk + k_sum) + SAME3 * pks, zero)
    yy = (
        ALONG1 * pk + ACROSS1 * k_sum + ALONG2 * pks,
        ACROSS1 * k + ALONG2 * pk + ACROSS2 * k_sum + SAME3 * pks,
        zero,
    )
    zz = (
        ALONG1 * k_sum + ACROSS1 * pk + ALONG2 * pks,
        ACROSS1 * k + ACROSS2 * pk + ALONG2 * k_sum + SAME3 * pks,
        zero,
    )
    xy = (zero, zero, MIXED2 * mk + MIXED3 * mks)
    xz = (zero, zero, MIXED2 * k_dif + MIXED3 * pkd)
    yz = (MIXED2 * mkd, MIXED3 * mkd, zero)
    return xx, yy, zz, xy, xz, yz


def own_block(sh, lane, springs):
    main, rim = springs
    k = inner(main, 0)
    out = []
    for index, ((own, even, odd), (_, rim_even, rim_odd)) in enumerate(
        zip(spring_parts(main), spring_parts(rim))
    ):
        total = x_stage(sh, lane, own, even + odd, even - odd, rim_even + rim_odd, rim_even - rim_odd)
        out.append(total + TOTAL * k if index < 3 else total)
    return out


def apply_block(d, v):
    return (
        d[0] * v[0] + d[3] * v[1] + d[4] * v[2],
        d[3] * v[0] + d[1] * v[1] + d[5] * v[2],
        d[4] * v[0] + d[5] * v[1] + d[2] * v[2],
    )


def image_of(sh, lane, v, kv, rims, springs_ref):
    k = springs_ref[6]
    last = (sh.x + 1) * sh.pitch
    own = apply_block([springs_ref[f] for f in range(6)], [inner(v, m) for m in range(3)])
    plain, scaled = column_parts(v), column_parts(kv)
    total = [k * plain[0, 0][m] + scaled[0, 0][m] for m in range(3)]
    for dx in (0, -1, 1):
        for m in range(3):
            side = None
            for i, column in enumerate(COLUMNS):
                if column[0] == dx:
                    moved = springs_ref[8 + i] * plain[column][m] + scaled[column][m]
                    moved = shift(moved, -(dx * sh.pitch + column[1]))
                    side = moved if side is None else side + moved
            if dx:
                side = pick(lane < last if dx > 0 else lane >= sh.pitch, side)
            total[m] = total[m] + side
    if rims is not None:
        sign = jnp.where(lane < sh.pitch, -1.0, 1.0)
        plain, scaled = column_parts(rims[0], sign), column_parts(rims[1], sign)
        at_rim = (lane < sh.pitch) | (lane >= last)
        for m in range(3):
            side = None
            for dy in (-1, 0, 1):
                moved = shift(k, dy) * plain[1, dy][m] + scaled[1, dy][m]
                moved = shift(moved, -dy)
                side = moved if side is None else side + moved
            total[m] = total[m] + pick(at_rim, side)
    return [own[m] - total[m] for m in range(3)]


def level(sh):
    return lax.broadcasted_iota(jnp.int32, (sh.rows, LANES), 0) - EDGE


def ends_level(sh):
    row = lax.broadcasted_iota(jnp.int32, (4 * EDGE, LANES), 0)
    return jnp.where(row < 2 * EDGE, row, row + sh.rows - 4 * EDGE) - EDGE


def ends(value):
    return jnp.concatenate([value[: 2 * EDGE], value[value.shape[0] - 2 * EDGE :]], axis=0)


def extended_mask(sh, z):
    lane, _, across = sh.lane_grid(1)
    return ((lane < sh.used) & (across >= -1) & (across <= sh.y)) & ((z >= -1) & (z <= sh.z))


def within(sh, axis, place, size):
    index = sh.here(axis)
    low = jnp.where(index > 0, -EDGE, 0)
    high = jnp.where(index < sh.sizes[axis] - 1, size + EDGE, size)
    return (place >= low) & (place < high)


def grid_masks(sh):
    lane, along, across = sh.lane_grid(1)
    lanes = (lane < sh.used) & within(sh, 1, across, sh.y)
    rows = within(sh, 2, level(sh), sh.z)
    return (lanes & within(sh, 0, along, sh.x)) & rows, lanes & rows


def put(ref, f, value):
    ref[f, EDGE : ref.shape[1] - EDGE, :] = value


def local_solve(sh, z, residual_ref, springs_ref, v, kv, factor):
    lane, _, _ = sh.lane_grid(1)
    mask = extended_mask(sh, z)
    for m in range(3):
        factor[m] = pick(mask, relax / jnp.where(mask, springs_ref[m], 1.0))
        value = residual_ref[m] * factor[m]
        put(v[0], m, value)
        put(kv[0], m, springs_ref[6] * value)
    for sweep in range(SWEEPS - 1):
        old, new = sweep % 2, (sweep + 1) % 2
        image = image_of(sh, lane, v[old], kv[old], None, springs_ref)
        for m in range(3):
            value = inner(v[old], m) + factor[m] * (residual_ref[m] - image[m])
            put(v[new], m, value)
            put(kv[new], m, springs_ref[6] * value)
    return (SWEEPS - 1) % 2


def own_level(sh):
    return lax.broadcasted_iota(jnp.int32, (sh.z, LANES), 0)


def coords(sh, z):
    _, along, across = sh.lane_grid(z.shape[0])
    along = jnp.where(along < 0, along + sh.x, jnp.where(along < sh.x, along, along - sh.x))
    across = jnp.where(across < 0, across + sh.y, jnp.where(across < sh.y, across, across - sh.y))
    place = lambda index, size: (2 * index + 1).astype(f32) / size - 1.0
    return place(along, sh.x), place(across, sh.y), place(z, sh.z)


def cell_coords(sh):
    cell = lax.broadcasted_iota(jnp.int32, (sh.cells, sh.z), 0)
    z = lax.broadcasted_iota(jnp.int32, (sh.cells, sh.z), 1)
    x = cell // sh.y
    place = lambda index, size: (2 * index + 1).astype(f32) / size - 1.0
    return place(x, sh.x), place(cell - x * sh.y, sh.y), place(z, sh.z)


def cross(a, b):
    return (a[1] * b[2] - a[2] * b[1], a[2] * b[0] - a[0] * b[2], a[0] * b[1] - a[1] * b[0])


def fold_rows(value):
    total = value[0:8]
    for i in range(8, value.shape[0], 8):
        total = total + value[i : i + 8]
    return jnp.sum(total, axis=0, keepdims=True)


def lane_sums(rows_ref):
    ones = jnp.ones((8, LANES), f32)
    return lax.dot_general(
        ones, rows_ref[...], (((1,), (1,)), ((), ())), precision=highest, preferred_element_type=f32
    )


def coarse_sums(nodes, field, places, count, sums):
    moments = tuple(field) + cross(places, field)
    for node in range(count):
        mask = nodes == node
        for m in range(6):
            sums[node * 6 + m : node * 6 + m + 1, :] = fold_rows(pick(mask, moments[m]))


def sums_line(sh, sums, unknowns):
    flat = (sh.here(0) * sh.sizes[1] + sh.here(1)) * sh.sizes[2] + sh.here(2)
    return pltpu.roll(lane_sums(sums), lax.rem(flat * unknowns, LANES), 1)[0:1]


def coarse_solution(received, inverse_ref, values):
    unknowns, total = inverse_ref.shape
    row = lax.broadcasted_iota(jnp.int32, received.shape, 0)
    part = jnp.zeros((unknowns, LANES), f32)
    for i in range(0, total, LANES):
        owner = (i + lax.broadcasted_iota(jnp.int32, (1, LANES), 1)) // unknowns
        vector = jnp.sum(pick(row == owner, received), axis=0, keepdims=True)
        part = part + inverse_ref[:, i : i + LANES] * vector
    values[0:unknowns, :] = jnp.dot(
        part, jnp.ones((LANES, LANES), f32), precision=highest, preferred_element_type=f32
    )


def coarse_shares(sums, inverse_ref, shares):
    unknowns, total = inverse_ref.shape
    column = jnp.dot(sums[...], jnp.ones((LANES, LANES), f32), precision=highest, preferred_element_type=f32)
    for i in range(0, total, LANES):
        share = inverse_ref[:, i : i + LANES] * column[0:unknowns]
        shares[i // LANES : i // LANES + 1, :] = jnp.sum(share, axis=0, keepdims=True)


def coarse_table(sh, shares_ref, unknowns, flat, table):
    rows = shares_ref.shape[0] // sh.devices
    lane = lax.broadcasted_iota(jnp.int32, (1, LANES), 1)
    for i in range(rows):
        flat[i : i + 1, :] = jnp.sum(shares_ref[pl.ds(i, sh.devices, stride=rows), :], axis=0, keepdims=True)
    for device in range(sh.devices):
        row, place = divmod(device * unknowns, LANES)
        part = shift(flat[row : row + 1, :], -place)
        if place + unknowns > LANES:
            part = jnp.where(lane < LANES - place, part, shift(flat[row + 1 : row + 2, :], -place))
        table[device : device + 1, :] = pick(lane < unknowns, part)


def region_values(sh, table, dz):
    lane, along, across = sh.lane_grid(1)
    x = sh.here(0) + jnp.where(along < 0, -1, jnp.where(along < sh.x, 0, 1))
    y = sh.here(1) + jnp.where(across < 0, -1, jnp.where(across < sh.y, 0, 1))
    z = sh.here(2) + dz
    exists = (lane < sh.used) & (x >= 0) & (x < sh.sizes[0]) & (y >= 0) & (y < sh.sizes[1])
    exists = exists & (z >= 0) & (z < sh.sizes[2])
    device = jnp.where(exists, (x * sh.sizes[1] + y) * sh.sizes[2] + z, -1)
    owner = lax.broadcasted_iota(jnp.int32, (sh.devices, LANES), 0) == device
    return lax.dot_general(
        table[0 : sh.devices, :], owner.astype(f32), (((0,), (0,)), ((), ())), precision=highest, preferred_element_type=f32
    )


def coarse_cells(nodes, places, values, count):
    cells = []
    for m in range(6):
        cell = jnp.zeros(nodes.shape, f32)
        for node in range(count):
            cell = jnp.where(nodes == float(node), values[node * 6 + m : node * 6 + m + 1, :], cell)
        cells.append(cell)
    turned = cross(cells[3:], places)
    return [cells[m] + turned[m] for m in range(3)]


def selection(sh):
    lane, along, across = sh.lane_grid(sh.cells)
    inside = (along >= 0) & (along < sh.x) & (across >= 0) & (across < sh.y)
    row = lax.broadcasted_iota(jnp.int32, (sh.cells, LANES), 0)
    return (inside & (row == along * sh.y + across)).astype(f32)


def to_lanes(value, select, precision=highest):
    return lax.dot_general(
        value, select, (((0,), (0,)), ((), ())), precision=precision, preferred_element_type=f32
    )


def to_cells(value, select):
    return lax.dot_general(
        select, value, (((1,), (1,)), ((), ())), precision=highest, preferred_element_type=f32
    )


def send_lines(sh, lines, slots_ref):
    here = [sh.here(axis) for axis in range(3)]
    corner = [lines[8 * i : 8 * i + 8, :] for i in range(4)]
    top, bottom = lines[32:40, :], lines[40:48, :]
    for x in range(sh.sizes[0]):
        low_high = [jnp.where(x > here[0], corner[2 + high], corner[high]) for high in range(2)]
        for y in range(sh.sizes[1]):
            column = jnp.where(y > here[1], low_high[1], low_high[0])
            for z in range(sh.sizes[2]):
                slot = jnp.where(z == here[2] + 1, top, jnp.where(z == here[2] - 1, bottom, column))
                place = 8 * ((x * sh.sizes[1] + y) * sh.sizes[2] + z)
                slots_ref[place : place + 8, :] = slot


def slot_from(sh, received_ref, step):
    place, exists = 0, None
    for axis in range(3):
        index = sh.here(axis) + step[axis]
        inside = (index >= 0) & (index < sh.sizes[axis])
        exists = inside if exists is None else exists & inside
        place = place * sh.sizes[axis] + jnp.clip(index, 0, sh.sizes[axis] - 1)
    return scale(exists, received_ref[pl.ds(pl.multiple_of(place * 8, 8), 8), :])


def repeat_twice(count):
    row = lax.broadcasted_iota(jnp.int32, (2 * count, count), 0)
    column = lax.broadcasted_iota(jnp.int32, (2 * count, count), 1)
    return ((row >= 2 * column) & (row < 2 * column + 2)).astype(f32)


def ring(size_x, size_y, rows):
    row = lax.broadcasted_iota(jnp.int32, (rows, LANES), 0)
    sides_x, both = 2 * size_y, 2 * size_y + 2 * size_x
    corner = row - both
    x = jnp.where(row < size_y, -1, size_x)
    x = jnp.where(row < sides_x, x, jnp.where(row < sides_x + size_x, row - sides_x, row - sides_x - size_x))
    x = jnp.where(row < both, x, jnp.where(corner < 2, -1, size_x))
    y = jnp.where(row < size_y, row, row - size_y)
    y = jnp.where(row < sides_x, y, jnp.where(row < sides_x + size_x, -1, size_y))
    y = jnp.where(row < both, y, jnp.where((corner == 0) | (corner == 2), -1, size_y))
    return x, y, (row < sides_x) | (row >= both), row < both + 4


def face_shape(sh, label_x, label_y):
    rows = max(4 * sh.x + label_x, 4 * sh.y + label_y)
    return (-(-rows // 8) * 8, LANES)


def pack_faces(sh, natural_ref, stiff, label_x, label_y, x_refs, y_refs):
    even_x, even_y = sh.here(0) % 2 == 0, sh.here(1) % 2 == 0

    def face(at, count, stride, label_at, label_count, label_stride):
        rows = [natural_ref[m, pl.ds(at, count, stride=stride), :] for m in range(4)]
        return rows, stiff[pl.ds(label_at, label_count, stride=label_stride), :]

    above = face(sh.cells - sh.y, sh.y, 1, (label_x - 1) * label_y, label_y, 1)
    below = face(0, sh.y, 1, 0, label_y, 1)
    for refs, links, even, above, below in (
        (x_refs, sh.x_links, even_x, above, below),
        (
            y_refs,
            sh.y_links,
            even_y,
            face(sh.y - 1, sh.x, sh.y, label_y - 1, label_x, label_y),
            face(0, sh.x, sh.y, 0, label_x, label_y),
        ),
    ):
        for i, ref in enumerate(refs):
            ref[...] = jnp.zeros(ref.shape, f32)
            count = above[0][0].shape[0]
            for m in range(4):
                ref[m * count : (m + 1) * count, :] = pair(links, even, above[0][m], below[0][m])[i]
            labels, length = above[1].shape
            ref[4 * count : 4 * count + labels, 0:length] = pair(links, even, above[1], below[1])[i]


def merge_start(sh, refs, x_refs, y_refs, received_ref, sizes, cells, labels):
    residual, nodes, stiff, stiff_rim = refs
    label_x, label_y, label_z = sizes
    lane, along, across = sh.lane_grid(1)
    inside = lane < sh.used
    last = (sh.x + 1) * sh.pitch
    x_mask = {-1: lane < sh.pitch, 0: (lane >= sh.pitch) & (lane < last), 1: (lane >= last) & inside}
    y_mask = {-1: across < 0, 0: (across >= 0) & (across < sh.y), 1: across >= sh.y}
    cells[...] = jnp.zeros(cells.shape, f32)
    labels[...] = jnp.zeros(labels.shape, f32)
    count, label_count = cells.shape[1], labels.shape[0]
    at = label_at = 0
    for axis, face_refs, size, label_size in ((0, x_refs, sh.y, label_y), (1, y_refs, sh.x, label_x)):
        for message in sides(sh, axis, [ref[...] for ref in face_refs]):
            for m in range(4):
                cells[m, at : at + size, :] = message[m * size : (m + 1) * size]
            labels[label_at : label_at + label_size, :] = message[4 * size : 4 * size + label_size, 0:label_z]
            at, label_at = at + size, label_at + label_size
    for dx, dy in ((-1, -1), (-1, 1), (1, -1), (1, 1)):
        slot = slot_from(sh, received_ref, (dx, dy, 0))
        for m, row in enumerate((0, 1, 2, 5)):
            cells[m, at : at + 1, :] = slot[row : row + 1]
        labels[label_at : label_at + 1, :] = slot[3:4, 0:label_z]
        at, label_at = at + 1, label_at + 1
    x, y, _, valid = ring(sh.x, sh.y, count)
    place = (valid & inside & (along == x) & (across == y)).astype(f32)
    own = slice(EDGE, EDGE + sh.z)
    tall_own = slice(2 * EDGE, 2 * EDGE + sh.z)
    for m in range(3):
        residual[m, own, :] += to_lanes(cells[m], place)
    nodes[own, :] += to_lanes(cells[3], place, small)
    by_z = lax.dot_general(
        repeat_twice(label_z), labels[...], (((1,), (1,)), ((), ())), precision=highest, preferred_element_type=f32
    )
    x, y, at_x, valid = ring(label_x, label_y, label_count)
    match = valid & inside & ((along >> 1) == x) & ((across >> 1) == y)
    columns = jnp.dot(by_z, (match & at_x).astype(f32), precision=highest, preferred_element_type=f32)
    stiff_rim[0, tall_own, :] = columns
    columns = columns + jnp.dot(by_z, (match & ~at_x).astype(f32), precision=highest, preferred_element_type=f32)
    stiff[0, tall_own, :] += columns
    for dz in (-1, 1):
        main = edge = jnp.zeros((8, LANES), f32)
        for dx in (-1, 0, 1):
            for dy in (-1, 0, 1):
                slot = slot_from(sh, received_ref, (dx, dy, dz))
                mask = x_mask[dx] & y_mask[dy]
                main = main + pick(mask, shift(slot, dx * sh.x * sh.pitch + dy * sh.y))
                if dx:
                    edge = edge + pick(mask, shift(slot, dx * (sh.x - 1) * sh.pitch + dy * sh.y))
        near = EDGE + sh.z if dz > 0 else EDGE - 1
        for m in range(3):
            residual[m, near : near + 1, :] = main[m : m + 1]
        nodes[near : near + 1, :] = main[5:6]
        for row in (EDGE + near, EDGE + near + dz):
            stiff[0, row : row + 1, :] = main[3:4]
            stiff_rim[0, row : row + 1, :] = edge[3:4]


def call(kernel, name, outs, ins, scratch=(), remote_ins=False, remote_outs=()):
    space = pltpu.HBM if remote_ins else pltpu.VMEM
    return pl.pallas_call(
        kernel,
        out_shape=[jax.ShapeDtypeStruct(shape, f32) for shape in outs],
        in_specs=[pl.BlockSpec(memory_space=space) for _ in ins],
        out_specs=[
            pl.BlockSpec(memory_space=pltpu.HBM if i in remote_outs else pltpu.VMEM) for i in range(len(outs))
        ],
        scratch_shapes=[pltpu.VMEM(shape, f32) if isinstance(shape, tuple) else shape for shape in scratch],
        compiler_params=pltpu.CompilerParams(vmem_limit_bytes=(56 if remote_ins else 48) * 1024 * 1024),
        name=name,
    )(*ins)


def permutation(sizes, moves):
    def partner(axis, link, index):
        size = sizes[axis]
        other = index ^ 1 if link == 0 else index + (1 if index % 2 else -1)
        if 0 <= other < size:
            return other
        return size - 1 - index if axis == 2 and size % 2 == 0 else index

    pairs = []
    for x in range(sizes[0]):
        for y in range(sizes[1]):
            for z in range(sizes[2]):
                place = [x, y, z]
                goal = [partner(a, moves[a], place[a]) if a in moves else place[a] for a in range(3)]
                if goal == place and 0 not in moves and sizes[0] % 2 == 0:
                    goal[0] = partner(0, 0, x)
                flat = [(p[0] * sizes[1] + p[1]) * sizes[2] + p[2] for p in (place, goal)]
                pairs.append(tuple(flat))
    return pairs


def send(sh, value, moves):
    return lax.ppermute(value, AXES, permutation(sh.sizes, moves))


def send_z(sh, messages):
    return [send(sh, message, {2: link}) for link, message in enumerate(messages)]


def send_faces(sh, x_messages, y_messages):
    from_y = [send(sh, message, {1: link}) for link, message in enumerate(y_messages)]
    from_x = [send(sh, message, {0: link}) for link, message in enumerate(x_messages)]
    return from_y, from_x


def to_all(slots):
    return lax.all_to_all(slots, AXES, 0, 0, tiled=True)


def exchange(sh, ex, name, field, z_messages):
    from_z = send_z(sh, z_messages)

    corners = sh.x_links * sh.y_links

    def packer(*refs):
        take = Taker(refs)
        field_ref, z_refs = take.one(), take(sh.z_links)
        x_refs, y_refs, corner_refs, scratch = take(sh.x_links), take(sh.y_links), take(corners), take.one()
        merge_z(sh, ex, field_ref, z_refs, scratch, 0)
        pack_xy(sh, ex, scratch, x_refs, y_refs, corner_refs)

    plane = (sh.rows, LANES)
    messages = call(
        packer,
        name,
        [plane] * sh.x_links
        + [folded_shape(sh, ex.fields * ex.layers)] * sh.y_links
        + [folded_shape(sh, ex.layers)] * corners,
        [field] + from_z,
        [(ex.fields,) + plane],
    )
    take = Taker(messages)
    x_messages, y_messages = take(sh.x_links), take(sh.y_links)
    from_y, straight = send_faces(sh, x_messages, y_messages)
    from_x = []
    for link in range(sh.x_links):
        from_x.append(straight[link])
        from_x.extend(send(sh, take.one(), {0: link, 1: other}) for other in range(sh.y_links))
    return from_z, from_y, from_x


class Taker:
    def __init__(self, refs):
        self.refs, self.at = refs, 0

    def __call__(self, count):
        self.at += count
        return self.refs[self.at - count : self.at]

    def one(self):
        return self(1)[0]


def merge_all(sh, ex, take, scratch, rim, guard):
    field = take.one()
    from_z, from_y = take(sh.z_links), take(sh.y_links)
    from_x = take(sh.x_links * (1 + sh.y_links))
    merge_z(sh, ex, field, from_z, scratch, guard)
    merge_xy(sh, ex, scratch, rim, guard, from_y, from_x)


def body(right_side, phase_labels, phase_moduli, coarse_nodes, coarse_inverse):
    sizes = tuple(lax.axis_size(axis) for axis in AXES)
    _, size_x, size_y, size_z = right_side.shape
    sh = Shape(size_x, size_y, size_z, phase_moduli.shape[0], sizes)
    unknowns = coarse_inverse.shape[0]
    node_count = unknowns // 6
    sum_rows = -(-unknowns // 8) * 8 + 8
    share_rows = coarse_inverse.shape[1] // LANES
    own = slice(EDGE, EDGE + sh.z)
    plane = (sh.rows, LANES)
    fields = (3,) + plane
    tall = (3, sh.tall, LANES)
    slots = (sh.devices, LANES)
    z_shape = lambda ex: [(8 * ex.fields, LANES)] * sh.z_links
    natural = right_side.reshape(3, sh.cells, sh.z)
    nodes_natural = coarse_nodes.reshape(sh.cells, sh.z)
    label_x, label_y, label_z = phase_labels.shape

    def block_places():
        lane, along, across = sh.lane_grid(label_x * label_y)
        inside = (along >= 0) & (along < sh.x) & (across >= 0) & (across < sh.y)
        block = lax.broadcasted_iota(jnp.int32, along.shape, 0)
        return (inside & (block == (along >> 1) * label_y + (across >> 1))).astype(f32)

    def end_layers(values, places):
        length = values.shape[1]
        row = lax.broadcasted_iota(jnp.int32, (8, length), 0)
        at = lax.broadcasted_iota(jnp.int32, (8, length), 1)
        ends = ((row == 0) & (at == length - 1)) | ((row == 1) & (at == 0))
        return jnp.dot(to_cells(values, ends.astype(f32)), places, precision=highest, preferred_element_type=f32)

    def begin(natural_in, labels_in, moduli_in, nodes_in, stiff, slots_ref, *rest):
        x_refs, y_refs = rest[: sh.x_links], rest[sh.x_links : sh.x_links + sh.y_links]
        natural_ref, labels_ref, moduli_ref, nodes_ref, sems, sums, lines = rest[sh.x_links + sh.y_links :]
        pairs = ((natural_in, natural_ref.at[0:3, 0 : sh.cells, :]), (labels_in, labels_ref.at[0:label_x]), (moduli_in, moduli_ref), (nodes_in, nodes_ref))
        copies = [pltpu.make_async_copy(a, b, sems.at[i]) for i, (a, b) in enumerate(pairs)]
        for copy in copies:
            copy.start()
        sums[...] = jnp.zeros(sums.shape, f32)
        lines[...] = jnp.zeros(lines.shape, f32)
        for copy in copies:
            copy.wait()
        for i in range(label_x):
            labels = labels_ref[i]
            moduli = jnp.zeros(labels.shape, f32)
            for phase in range(sh.phases):
                moduli = jnp.where(labels == phase, moduli_ref[phase], moduli)
            stiff[i * label_y : (i + 1) * label_y, :] = moduli
        natural_ref[3, 0 : sh.cells, :] = nodes_ref[...].astype(f32) + 1.0
        cells = [natural_ref[m, 0 : sh.cells, :] for m in range(4)]
        coarse_sums(nodes_ref[...], cells[:3], cell_coords(sh), node_count, sums)
        line = sums_line(sh, sums, unknowns)
        for i, (cell, block) in enumerate(
            (
                (0, 0),
                (sh.y - 1, label_y - 1),
                ((sh.x - 1) * sh.y, (label_x - 1) * label_y),
                (sh.cells - 1, label_x * label_y - 1),
            )
        ):
            for m in range(3):
                lines[8 * i + m : 8 * i + m + 1, :] = natural_ref[m, cell : cell + 1, :]
            lines[8 * i + 3 : 8 * i + 4, 0:label_z] = stiff[block : block + 1, :]
            lines[8 * i + 5 : 8 * i + 6, :] = natural_ref[3, cell : cell + 1, :]
        select = selection(sh)
        layers = [end_layers(cells[m], select) for m in range(4)] + [end_layers(stiff[0 : label_x * label_y, :], block_places())]
        for i in range(2):
            for layer, row in zip(layers, (0, 1, 2, 5, 3)):
                lines[8 * (4 + i) + row : 8 * (4 + i) + row + 1, :] = layer[i : i + 1]
        for i in range(6):
            lines[8 * i + 4 : 8 * i + 5, :] = line
        send_lines(sh, lines, slots_ref)
        pack_faces(sh, natural_ref, stiff, label_x, label_y, x_refs, y_refs)

    block_rows = (8 * -(-(label_x + 8) * label_y // 8), label_z)
    stiff_blocks, lines, *messages = call(
        begin,
        "begin",
        [block_rows, (8 * sh.devices, LANES)]
        + [face_shape(sh, label_x, label_y)] * (sh.x_links + sh.y_links),
        [natural, phase_labels, phase_moduli, nodes_natural],
        [
            (4, sh.cells + 8, sh.z),
            pltpu.VMEM((label_x + 2, label_y, label_z), jnp.int32),
            pltpu.SMEM(phase_moduli.shape, f32),
            pltpu.VMEM(nodes_natural.shape, jnp.int32),
            pltpu.SemaphoreType.DMA((4,)),
            (LANES, LANES),
            (56, LANES),
        ],
        remote_ins=True,
    )

    def spread(natural_ref, nodes_ref, stiff, inverse_in, field_ref, lanes_ref, inverse_ref):
        inverse_ref[...] = inverse_in[...]
        select = selection(sh)
        field_ref[...] = jnp.zeros(field_ref.shape, f32)
        for m in range(3):
            field_ref[m, own, :] = to_lanes(natural_ref[m], select)
        by_z = lax.dot_general(
            repeat_twice(label_z),
            stiff[0 : label_x * label_y, :],
            (((1,), (1,)), ((), ())),
            precision=highest,
            preferred_element_type=f32,
        )
        field_ref[3, own, :] = jnp.dot(by_z, block_places(), precision=highest, preferred_element_type=f32)
        lanes_ref[...] = to_lanes(nodes_ref[...].astype(f32) + 1.0, select, small) - 1.0

    start_field, nodes, inverse = call(
        spread,
        "spread",
        [(4,) + plane, (sh.z, LANES), coarse_inverse.shape],
        [natural, nodes_natural, stiff_blocks, coarse_inverse],
    )
    from_y, from_x = send_faces(sh, messages[: sh.x_links], messages[sh.x_links :])
    lines = to_all(lines)

    short = (3, 6 * EDGE, LANES)
    short_fields = (3, 4 * EDGE, LANES)
    solve_scratch = [tall] * 4 + [fields]
    short_scratch = [short] * 4 + [short_fields]

    def end_rows(ref):
        def rows(f, start, count):
            place = start + EDGE if start < 2 * EDGE else start - sh.rows + 5 * EDGE
            return ref[f, place : place + count, :]

        return rows

    def first_ends(*refs):
        take = Taker(refs)
        field_ref = take.one()
        y_refs, x_refs = take(sh.y_links), take(sh.x_links)
        nodes_ref, lines_ref, inverse_ref = take(3)
        residual, wide_nodes, stiffness_ref, values = take(4)
        z_refs = take(sh.z_links)
        stiff, stiff_rim, cells, labels, short_stiff, short_rim, some_residual, springs = take(8)
        v0, v1, kv0, kv1, factor = take(5)
        clear_guards(sh, (stiff, stiff_rim, short_stiff, short_rim, v0, v1, kv0, kv1))
        residual[...] = field_ref[0:3]
        put(stiff, 0, field_ref[3])
        put(stiff_rim, 0, jnp.zeros(plane, f32))
        sizes = phase_labels.shape
        wide_nodes[...] = jnp.zeros(plane, f32)
        wide_nodes[own, :] = nodes_ref[...] + 1.0
        merge_start(sh, (residual, wide_nodes, stiff, stiff_rim), x_refs, y_refs, lines_ref, sizes, cells, labels)
        wide_nodes[...] = wide_nodes[...] - 1.0
        stiffness_ref[0] = inner(stiff, 0)
        stiffness_ref[1] = inner(stiff_rim, 0)
        coarse_solution(lines_ref[pl.ds(4, sh.devices, stride=8), :], inverse_ref, values)
        lane, _, _ = sh.lane_grid(1)
        put(short_stiff, 0, ends(stiffness_ref[0]))
        put(short_rim, 0, ends(stiffness_ref[1]))
        for f, entry in enumerate(own_block(sh, lane, (short_stiff, short_rim))):
            springs[f] = entry
        springs[6] = inner(short_stiff, 0)
        put_columns(sh, springs)
        for m in range(3):
            some_residual[m] = ends(residual[m])
        index = local_solve(sh, ends_level(sh), some_residual, springs, (v0, v1), (kv0, kv1), factor)
        solution = (v0, v1)[index]
        z = lax.broadcasted_iota(jnp.int32, (2 * EDGE, LANES), 0)
        z = jnp.where(z < EDGE, z, z + sh.z - 2 * EDGE)
        some_nodes = jnp.concatenate([nodes_ref[0:EDGE, :], nodes_ref[sh.z - EDGE : sh.z, :]], axis=0)
        added = coarse_cells(some_nodes, coords(sh, z), values, node_count)
        for m in range(3):
            solution[m, 2 * EDGE : 4 * EDGE, :] += pick(some_nodes >= 0.0, added[m])
        pack_z(sh, DEEP, end_rows(solution), z_refs)

    residual, wide_nodes, stiffness, values, *z_messages = call(
        first_ends,
        "first_ends",
        [fields, plane, (2,) + plane, (sum_rows, LANES)] + z_shape(DEEP),
        [start_field, *from_y, *from_x, nodes, lines, inverse],
        [(1, sh.tall, LANES)] * 2
        + [
            (4, 8 * -(-(2 * sh.x + 2 * sh.y + 4) // 8) + 8, LANES),
            (8 * -(-(2 * label_x + 2 * label_y + 4) // 8) + 8, label_z),
        ]
        + [(1, 6 * EDGE, LANES)] * 2
        + [short_fields, (16, 4 * EDGE, LANES)]
        + short_scratch,
    )

    def first_solve(residual_ref, stiffness_ref, values, nodes_ref, solution_ref, springs_ref, *rest):
        stiff, stiff_rim, v0, v1, kv0, kv1, factor = rest
        clear_guards(sh, (stiff, stiff_rim, v0, v1, kv0, kv1))
        put(stiff, 0, stiffness_ref[0])
        put(stiff_rim, 0, stiffness_ref[1])
        springs_ref[6] = stiffness_ref[0]
        springs_ref[7] = stiffness_ref[1]
        put_columns(sh, springs_ref)
        lane, _, _ = sh.lane_grid(1)
        for f, entry in enumerate(own_block(sh, lane, (stiff, stiff_rim))):
            springs_ref[f] = entry
        index = local_solve(sh, level(sh), residual_ref, springs_ref, (v0, v1), (kv0, kv1), factor)
        for m in range(3):
            solution_ref[m] = inner((v0, v1)[index], m)
        added = coarse_cells(nodes_ref[...], coords(sh, own_level(sh)), values, node_count)
        for m in range(3):
            solution_ref[m, own, :] += pick(nodes_ref[...] >= 0.0, added[m])

    solved, springs = call(
        first_solve,
        "first_solve",
        [fields, (16,) + plane],
        [residual, stiffness, values, nodes],
        [(1, sh.tall, LANES)] * 2 + solve_scratch,
    )
    from_z, from_y, from_x = exchange(sh, DEEP, "deep", solved, z_messages)

    def first_image(*refs):
        take = Taker(refs)
        merging = take(1 + sh.z_links + sh.y_links + sh.x_links * (1 + sh.y_links))
        nodes_ref, springs_ref, inverse_ref = take(3)
        search_ref, image_ref, slots_out = take(3)
        z_refs = take(sh.z_links)
        v, rim, kv, k_rim, sums, shares, slots_ref, sem = take(8)
        some_residual, some_springs, v0, v1, kv0, kv1, factor = take(7)
        clear_guards(sh, (v0, v1, kv0, kv1))
        clear_guards(sh, (v, rim, kv, k_rim))
        merge_all(sh, DEEP, Taker(merging), v, rim, EDGE)
        lane, _, _ = sh.lane_grid(1)

        in_grid, in_rim = grid_masks(sh)
        for m in range(3):
            value = pick(in_grid, inner(v, m))
            put(v, m, value)
            search_ref[m] = value
            put(kv, m, springs_ref[6] * value)
            value = pick(in_rim, inner(rim, m))
            put(rim, m, value)
            put(k_rim, m, springs_ref[7] * value)
        image = image_of(sh, lane, v, kv, (rim, k_rim), springs_ref)
        keep = in_grid & extended_mask(sh, level(sh))
        for m in range(3):
            image_ref[m] = pick(keep, image[m])
        sums[...] = jnp.zeros(sums.shape, f32)
        field = [image_ref[m, own, :] for m in range(3)]
        coarse_sums(nodes_ref[...], field, coords(sh, own_level(sh)), node_count, sums)
        coarse_shares(sums, inverse_ref, shares)
        for device in range(sh.devices):
            slots_ref[device * share_rows : (device + 1) * share_rows, :] = shares[0:share_rows, :]
        copy = pltpu.make_async_copy(slots_ref.at[0 : slots_out.shape[0], :], slots_out, sem)
        copy.start()
        for m in range(3):
            some_residual[m] = ends(image_ref[m])
        for f in range(16):
            some_springs[f] = ends(springs_ref[f])
        index = local_solve(sh, ends_level(sh), some_residual, some_springs, (v0, v1), (kv0, kv1), factor)
        pack_z(sh, NEAR, end_rows((v0, v1)[index]), z_refs)
        copy.wait()

    all_slots = (sh.devices * share_rows, LANES)
    search, image, shares, *z_messages = call(
        first_image,
        "first_image",
        [fields, fields, all_slots] + z_shape(NEAR),
        [solved, *from_z, *from_y, *from_x, nodes, springs, inverse],
        [tall] * 4
        + [(LANES, LANES), (8 * -(-share_rows // 8) + 8, LANES)]
        + [(8 * -(-all_slots[0] // 8) + 8, LANES), pltpu.SemaphoreType.DMA]
        + [short_fields, (16, 4 * EDGE, LANES)]
        + short_scratch,
        remote_outs=(2,),
    )
    shares = to_all(shares.reshape(sh.devices, 1, share_rows * LANES)).reshape(shares.shape)

    def second_solve(image_ref, springs_ref, local_ref, v0, v1, kv0, kv1, factor):
        clear_guards(sh, (v0, v1, kv0, kv1))
        index = local_solve(sh, level(sh), image_ref, springs_ref, (v0, v1), (kv0, kv1), factor)
        for m in range(3):
            local_ref[m] = inner((v0, v1)[index], m)

    (solved,) = call(second_solve, "second_solve", [fields], [image, springs], solve_scratch)
    from_z, from_y, from_x = exchange(sh, NEAR, "near", solved, z_messages)

    def between(shares_ref, wide_nodes, nodes_ref, start_ref, search_ref, first_ref, coarse_ref, sums, *scratch):
        flat, table, values = scratch
        coarse_ref[...] = jnp.zeros(coarse_ref.shape, f32)
        coarse_table(sh, shares_ref, unknowns, flat, table)
        last = lax.broadcasted_iota(jnp.int32, (1, LANES), 0) + sh.z - 1
        for dz, first, z in ((0, EDGE, own_level(sh)), (-1, EDGE - 1, last), (1, EDGE + sh.z, last - sh.z + 1)):
            values[...] = region_values(sh, table, dz)
            rows = slice(first, first + z.shape[0])
            added = coarse_cells(wide_nodes[rows, :], coords(sh, z), values, node_count)
            for m in range(3):
                coarse_ref[m, rows, :] = added[m]
        valid = nodes_ref[...] >= 0.0
        row = lax.broadcasted_iota(jnp.int32, sums.shape, 0)
        total = jnp.zeros(sums.shape, f32)
        for i, other in enumerate((start_ref, first_ref)):
            product = sum(search_ref[m, own, :] * other[m, own, :] for m in range(3))
            total = jnp.where(row == i, fold_rows(pick(valid, product)), total)
        sums[...] = total

    coarse_field, sums = call(
        between,
        "between",
        [fields, (8, LANES)],
        [shares, wide_nodes, nodes, start_field, search, image],
        [(8 * -(-share_rows // 8) + 8, LANES), (8 * -(-sh.devices // 8) + 8, LANES), (LANES, LANES)],
    )

    def second_image(*refs):
        take = Taker(refs)
        merging = take(1 + sh.z_links + sh.y_links + sh.x_links * (1 + sh.y_links))
        nodes_ref, springs_ref, first_ref, coarse_ref, early_ref = take(5)
        second_ref, image_ref, slots_ref = take(3)
        v, kv, sums = take(3)
        clear_guards(sh, (v, kv))
        merge_all(sh, NEAR, Taker(merging), v, None, EDGE)
        lane, _, _ = sh.lane_grid(1)
        in_grid, _ = grid_masks(sh)
        for m in range(3):
            value = pick(in_grid, inner(v, m)) + coarse_ref[m]
            put(v, m, value)
            second_ref[m] = value
            put(kv, m, springs_ref[6] * value)
        image = image_of(sh, lane, v, kv, None, springs_ref)
        for m in range(3):
            image_ref[m] = image[m]
        valid = nodes_ref[...] >= 0.0
        sums[...] = jnp.zeros(sums.shape, f32)
        sums[0:8, :] = early_ref[...]
        for i, other in ((2, first_ref), (3, image_ref)):
            product = sum(second_ref[m, own, :] * other[m, own, :] for m in range(3))
            sums[i : i + 1, :] = fold_rows(pick(valid, product))
        slots_ref[...] = jnp.broadcast_to(lane_sums(sums)[0:1], slots_ref.shape)

    second, second_image_field, sums = call(
        second_image,
        "second_image",
        [fields, fields, slots],
        [solved, *from_z, *from_y, *from_x, nodes, springs, image, coarse_field, sums],
        [tall] * 2 + [(LANES, LANES)],
    )
    totals = to_all(sums)

    def turn(search_ref, first_ref, second_ref, image_ref, out_ref):
        select = selection(sh)
        for i, ref in enumerate((search_ref, first_ref, second_ref, image_ref)):
            for m in range(3):
                out_ref[i, m] = to_cells(ref[m, own, :], select)

    (turned,) = call(turn, "turn", [(4,) + natural.shape], [search, image, second, second_image_field])

    def finish(totals_ref, natural_ref, turned_ref, field_ref, residual_ref):
        total = jnp.sum(totals_ref[...], axis=0, keepdims=True)
        rz, zw, wq, qv = [total[:, i : i + 1] for i in range(4)]
        step0 = rz / zw
        rho = step0 * step0 * wq - step0 * zw
        grow = 1.0 + rho / rz
        curvature = grow * grow * zw - 2.0 * grow * step0 * wq + step0 * step0 * qv
        step1 = rho / curvature
        first = step0 + step1 * grow
        second = step0 * step1
        for m in range(3):
            field_ref[m] = first * turned_ref[0, m] - second * turned_ref[2, m]
            residual_ref[m] = natural_ref[m] - (first * turned_ref[1, m] - second * turned_ref[3, m])

    solution_field, residual = call(
        finish, "finish", [natural.shape, natural.shape], [totals, natural, turned]
    )
    return solution_field.reshape(right_side.shape), residual.reshape(right_side.shape)


def solution(mesh):
    in_specs = (
        P(None, "gx", "gy", "gz"),
        P("gx", "gy", "gz"),
        P(),
        P("gx", "gy", "gz"),
        P(("gx", "gy", "gz"), None),
    )
    out_specs = (P(None, "gx", "gy", "gz"), P(None, "gx", "gy", "gz"))
    return jax.shard_map(body, mesh=mesh, in_specs=in_specs, out_specs=out_specs, check_vma=False)
```

```python
import jax
import jax.numpy as jnp
from jax import lax
from jax.experimental import pallas as pl
from jax.experimental.pallas import tpu as pltpu
from jax.sharding import PartitionSpec as P

AXES = ("gx", "gy", "gz")
SWEEPS = 4
relax = 0.6
highest = lax.Precision.HIGHEST
small = lax.Precision.DEFAULT
f32 = jnp.float32
LANES = 128
EDGE = 8

ALONG1, ACROSS1 = 0.75, 0.5
ALONG2, ACROSS2, MIXED2 = 0.3125, 0.25, 0.0625
SAME3, MIXED3 = 7.0 / 36.0, 1.0 / 36.0
TOTAL = 2 * ALONG1 + 4 * ACROSS1 + 8 * ALONG2 + 4 * ACROSS2 + 8 * SAME3


class Exchange:
    def __init__(self, fields, layers, up, down):
        self.fields, self.layers, self.up, self.down = fields, layers, up, down


DEEP = Exchange(3, 3, -2, -1)
NEAR = Exchange(3, 2, -1, -1)


class Shape:
    def __init__(self, size_x, size_y, size_z, phases, mesh_sizes):
        self.x, self.y, self.z = size_x, size_y, size_z
        self.pitch = size_y + 4
        self.used = (size_x + 2) * self.pitch
        assert self.used <= LANES
        self.rows = size_z + 2 * EDGE
        self.tall = self.rows + 2 * EDGE
        self.phases = phases
        self.sizes = mesh_sizes
        self.devices = mesh_sizes[0] * mesh_sizes[1] * mesh_sizes[2]
        self.cells = size_x * size_y
        self.links = [1 if n <= 2 else 2 for n in mesh_sizes]
        self.x_links, self.y_links, self.z_links = self.links

    def lane_grid(self, rows):
        lane = lax.broadcasted_iota(jnp.int32, (rows, LANES), 1)
        column = jnp.zeros_like(lane)
        for j in range(1, self.x + 2):
            column = column + (lane >= j * self.pitch).astype(jnp.int32)
        offset = lane - column * self.pitch
        return lane, column - 1, offset - 2

    def here(self, axis):
        return lax.axis_index(AXES[axis])


def shift(value, amount):
    amount = amount % LANES
    return value if amount == 0 else pltpu.roll(value, amount, 1)


def pick(mask, value):
    return jnp.where(mask, value, 0.0)


def scale(flag, value):
    return value * flag.astype(f32)


def pair(links, even, upward, downward):
    first = jnp.where(even, upward, downward)
    return (first,) if links == 1 else (first, jnp.where(even, downward, upward))


def sides(sh, axis, received):
    index, size = sh.here(axis), sh.sizes[axis]
    even = index % 2 == 0
    first = received[0]
    second = received[1] if len(received) > 1 else jnp.zeros_like(first)
    below = jnp.where(even, second, first)
    above = jnp.where(even, first, second)
    return scale(index > 0, below), scale(index < size - 1, above)


def lane_range(lane, start, count):
    return (lane >= start) & (lane < start + count)


def pack_z(sh, ex, source, out_refs):
    even = sh.here(2) % 2 == 0
    for ref in out_refs:
        ref[...] = jnp.zeros(ref.shape, f32)
    for f in range(ex.fields):
        upward = source(f, EDGE + sh.z + ex.up, ex.layers)
        downward = source(f, EDGE + ex.down, ex.layers)
        for ref, message in zip(out_refs, pair(sh.z_links, even, upward, downward)):
            ref[8 * f : 8 * f + ex.layers, :] = message


def merge_z(sh, ex, field_ref, received_refs, scratch, guard):
    below, above = sides(sh, 2, [ref[...] for ref in received_refs])
    for f in range(ex.fields):
        scratch[f, guard : guard + sh.rows, :] = field_ref[f]
        low = guard + EDGE + ex.up
        high = guard + EDGE + sh.z + ex.down
        scratch[f, low : low + ex.layers, :] += below[8 * f : 8 * f + ex.layers]
        scratch[f, high : high + ex.layers, :] += above[8 * f : 8 * f + ex.layers]


def fold(sh, value, layers, start=None):
    folds = sh.pitch // layers
    height = -(-sh.rows // (8 * folds)) * 8
    lane, _, across = sh.lane_grid(1)
    total = jnp.zeros((height, LANES), f32)
    for i, first in enumerate(range(0, sh.rows, height)):
        part = value[first : first + height]
        if start is not None:
            part = pick((lane < sh.used) & lane_range(across, start, layers), part)
        part = shift(part, i * layers - (0 if start is None else start + 2))
        if part.shape[0] < height:
            part = jnp.concatenate([part, jnp.zeros((height - part.shape[0], LANES), f32)], axis=0)
        total = total + part
    return total


def folded_shape(sh, layers):
    return (-(-sh.rows // (8 * (sh.pitch // layers))) * 8, LANES)


def unfold(sh, message, layers, start):
    height = message.shape[0]
    lane, _, across = sh.lane_grid(1)
    mask = (lane < sh.used) & lane_range(across, start, layers)
    parts = []
    for i, first in enumerate(range(0, sh.rows, height)):
        part = message[0 : min(height, sh.rows - first)]
        parts.append(pick(mask, shift(part, start + 2 - i * layers)))
    return jnp.concatenate(parts, axis=0) if len(parts) > 1 else parts[0]


def pack_xy(sh, ex, scratch, x_refs, y_refs, corner_refs):
    rows = sh.rows
    lane, _, across = sh.lane_grid(1)
    even_x, even_y = sh.here(0) % 2 == 0, sh.here(1) % 2 == 0
    span = ex.layers * sh.pitch
    x_up = x_down = y_up = y_down = jnp.zeros((rows, LANES), f32)
    inside = lane < sh.used
    y_above, y_below = sh.y + ex.up, ex.down
    for f in range(ex.fields):
        value = scratch[f]
        start = (sh.x + ex.up + 1) * sh.pitch
        x_up = x_up + shift(pick(lane_range(lane, start, span), value), f * span - start)
        start = (ex.down + 1) * sh.pitch
        x_down = x_down + shift(pick(lane_range(lane, start, span), value), f * span - start)
        mask = inside & lane_range(across, y_above, ex.layers)
        y_up = y_up + shift(pick(mask, value), f * ex.layers - y_above - 2)
        mask = inside & lane_range(across, y_below, ex.layers)
        y_down = y_down + shift(pick(mask, value), f * ex.layers - y_below - 2)
    packed = ex.fields * ex.layers
    y_up, y_down = fold(sh, y_up, packed), fold(sh, y_down, packed)
    for ref, message in zip(y_refs, pair(sh.y_links, even_y, y_up, y_down)):
        ref[...] = message
    for i, message in enumerate(pair(sh.x_links, even_x, x_up, x_down)):
        x_refs[i][...] = message
        upward, downward = fold(sh, message, ex.layers, y_above), fold(sh, message, ex.layers, y_below)
        for j, corner in enumerate(pair(sh.y_links, even_y, upward, downward)):
            corner_refs[i * sh.y_links + j][...] = corner


def merge_xy(sh, ex, scratch, rim, guard, y_refs, x_refs):
    lane, _, across = sh.lane_grid(1)
    inside = lane < sh.used
    low_mask = inside & lane_range(across, ex.up, ex.layers)
    high_mask = inside & lane_range(across, sh.y + ex.down, ex.layers)
    span = ex.layers * sh.pitch
    packed = ex.fields * ex.layers
    below_y, above_y = [unfold(sh, value, packed, -2) for value in sides(sh, 1, [ref[...] for ref in y_refs])]
    per_link = 1 + sh.y_links
    sums = []
    for link in range(sh.x_links):
        straight, diagonal = x_refs[link * per_link], x_refs[link * per_link + 1 : (link + 1) * per_link]
        total = straight[...]
        below, above = sides(sh, 1, [ref[...] for ref in diagonal])
        total = total + unfold(sh, below, ex.layers, ex.up)
        sums.append(total + unfold(sh, above, ex.layers, sh.y + ex.down))
    below_x, above_x = sides(sh, 0, sums)
    first = 1 if ex.up == -2 else 0
    last = ex.layers - 1 if ex.down + ex.layers == 2 else ex.layers
    for f in range(ex.fields):
        addend = pick(low_mask, shift(below_y, ex.up + 2 - ex.layers * f))
        addend = addend + pick(high_mask, shift(above_y, sh.y + ex.down + 2 - ex.layers * f))
        start = (ex.up + first + 1) * sh.pitch
        count = (ex.layers - first) * sh.pitch
        moved = shift(below_x, start - f * span - first * sh.pitch)
        addend = addend + pick(lane_range(lane, start, count), moved)
        start = (sh.x + ex.down + 1) * sh.pitch
        moved = shift(above_x, start - f * span)
        addend = addend + pick(lane_range(lane, start, last * sh.pitch), moved)
        scratch[f, guard : guard + sh.rows, :] += addend
        if rim is not None:
            low = pick(lane_range(lane, 0, sh.pitch), shift(below_x, -f * span))
            start = (sh.x + 1) * sh.pitch
            moved = shift(above_x, start - f * span - last * sh.pitch)
            high = pick(lane_range(lane, start, sh.pitch), moved)
            rim[f, guard : guard + sh.rows, :] = low + high


def clear_guards(sh, refs):
    for ref in refs:
        for f in range(ref.shape[0]):
            ref[f, :EDGE, :] = jnp.zeros((EDGE, LANES), f32)
            ref[f, ref.shape[1] - EDGE :, :] = jnp.zeros((EDGE, LANES), f32)


def inner(ref, f):
    return ref[f, EDGE : ref.shape[1] - EDGE, :]


def z_stage(ref, f):
    end = ref.shape[1] - EDGE
    after = ref[f, EDGE + 1 : end + 1, :]
    before = ref[f, EDGE - 1 : end - 1, :]
    return inner(ref, f), before + after, after - before


def y_stage(value):
    after, before = shift(value, -1), shift(value, 1)
    return before + after, after - before


COLUMNS = [(dx, dy) for dx in (-1, 0, 1) for dy in (-1, 0, 1) if dx or dy]


def column_parts(ref, sign=None):
    a, a_sum, a_dif = z_stage(ref, 0)
    b, b_sum, b_dif = z_stage(ref, 1)
    c, c_sum, c_dif = z_stage(ref, 2)
    parts = {(0, 0): (ACROSS1 * a_sum, ACROSS1 * b_sum, ALONG1 * c_sum)}
    mixed_x, mixed_y = MIXED2 * b + MIXED3 * b_sum, MIXED2 * a + MIXED3 * a_sum
    x_c_dif = c_dif
    if sign is not None:
        mixed_x, mixed_y, x_c_dif, a_dif = sign * mixed_x, sign * mixed_y, sign * c_dif, sign * a_dif
    both_z = ACROSS1 * c + ALONG2 * c_sum
    along, across = ALONG1 * a + ALONG2 * a_sum, ACROSS1 * b + ACROSS2 * b_sum
    for dx in (-1, 1):
        parts[dx, 0] = (along + dx * MIXED2 * x_c_dif, across, both_z + dx * MIXED2 * a_dif)
    along, across = ALONG1 * b + ALONG2 * b_sum, ACROSS1 * a + ACROSS2 * a_sum
    for dy in (-1, 1):
        parts[0, dy] = (across, along + dy * MIXED2 * c_dif, both_z + dy * MIXED2 * b_dif)
    same_x, same_y = ALONG2 * a + SAME3 * a_sum, ALONG2 * b + SAME3 * b_sum
    same_z = ACROSS2 * c + SAME3 * c_sum
    for dx in (-1, 1):
        for dy in (-1, 1):
            parts[dx, dy] = (
                (same_x + dx * dy * mixed_x) + dx * MIXED3 * x_c_dif,
                (same_y + dx * dy * mixed_y) + dy * MIXED3 * c_dif,
                (same_z + dx * MIXED3 * a_dif) + dy * MIXED3 * b_dif,
            )
    return parts


def put_columns(sh, springs_ref, columns):
    for i, (dx, dy) in enumerate(COLUMNS):
        columns[i] = shift(springs_ref[6], dx * sh.pitch + dy)


def x_stage(sh, lane, own, plus, minus, rim_plus, rim_minus):
    after, before = shift(plus, -sh.pitch), shift(minus, sh.pitch)
    last = (sh.x + 1) * sh.pitch
    if rim_plus is None:
        return own + pick(lane < last, after) + pick(lane >= sh.pitch, before)
    return own + jnp.where(lane < last, after, rim_plus) + jnp.where(lane >= sh.pitch, before, rim_minus)


def spring_parts(ref):
    k, k_sum, k_dif = z_stage(ref, 0)
    pk, mk = y_stage(k)
    pks, mks = y_stage(k_sum)
    pkd, mkd = y_stage(k_dif)
    zero = jnp.zeros_like(k)
    xx = (ACROSS1 * (pk + k_sum) + ACROSS2 * pks, ALONG1 * k + ALONG2 * (pk + k_sum) + SAME3 * pks, zero)
    yy = (
        ALONG1 * pk + ACROSS1 * k_sum + ALONG2 * pks,
        ACROSS1 * k + ALONG2 * pk + ACROSS2 * k_sum + SAME3 * pks,
        zero,
    )
    zz = (
        ALONG1 * k_sum + ACROSS1 * pk + ALONG2 * pks,
        ACROSS1 * k + ACROSS2 * pk + ALONG2 * k_sum + SAME3 * pks,
        zero,
    )
    xy = (zero, zero, MIXED2 * mk + MIXED3 * mks)
    xz = (zero, zero, MIXED2 * k_dif + MIXED3 * pkd)
    yz = (MIXED2 * mkd, MIXED3 * mkd, zero)
    return xx, yy, zz, xy, xz, yz


def own_block(sh, lane, springs):
    main, rim = springs
    k = inner(main, 0)
    out = []
    for index, ((own, even, odd), (_, rim_even, rim_odd)) in enumerate(
        zip(spring_parts(main), spring_parts(rim))
    ):
        total = x_stage(sh, lane, own, even + odd, even - odd, rim_even + rim_odd, rim_even - rim_odd)
        out.append(total + TOTAL * k if index < 3 else total)
    return out


def apply_block(d, v):
    return (
        d[0] * v[0] + d[3] * v[1] + d[4] * v[2],
        d[3] * v[0] + d[1] * v[1] + d[5] * v[2],
        d[4] * v[0] + d[5] * v[1] + d[2] * v[2],
    )


def image_of(sh, lane, v, kv, rims, springs_ref, columns):
    k = springs_ref[6]
    last = (sh.x + 1) * sh.pitch
    own = apply_block([springs_ref[f] for f in range(6)], [inner(v, m) for m in range(3)])
    plain, scaled = column_parts(v), column_parts(kv)
    total = [k * plain[0, 0][m] + scaled[0, 0][m] for m in range(3)]
    for dx in (0, -1, 1):
        for m in range(3):
            side = None
            for i, column in enumerate(COLUMNS):
                if column[0] == dx:
                    moved = columns[i] * plain[column][m] + scaled[column][m]
                    moved = shift(moved, -(dx * sh.pitch + column[1]))
                    side = moved if side is None else side + moved
            if dx:
                side = pick(lane < last if dx > 0 else lane >= sh.pitch, side)
            total[m] = total[m] + side
    if rims is not None:
        sign = jnp.where(lane < sh.pitch, -1.0, 1.0)
        plain, scaled = column_parts(rims[0], sign), column_parts(rims[1], sign)
        at_rim = (lane < sh.pitch) | (lane >= last)
        for m in range(3):
            side = None
            for dy in (-1, 0, 1):
                moved = shift(k, dy) * plain[1, dy][m] + scaled[1, dy][m]
                moved = shift(moved, -dy)
                side = moved if side is None else side + moved
            total[m] = total[m] + pick(at_rim, side)
    return [own[m] - total[m] for m in range(3)]


def level(sh):
    return lax.broadcasted_iota(jnp.int32, (sh.rows, LANES), 0) - EDGE


def ends_level(sh):
    row = lax.broadcasted_iota(jnp.int32, (4 * EDGE, LANES), 0)
    return jnp.where(row < 2 * EDGE, row, row + sh.rows - 4 * EDGE) - EDGE


def ends(value):
    return jnp.concatenate([value[: 2 * EDGE], value[value.shape[0] - 2 * EDGE :]], axis=0)


def extended_mask(sh, z):
    lane, _, across = sh.lane_grid(1)
    return ((lane < sh.used) & (across >= -1) & (across <= sh.y)) & ((z >= -1) & (z <= sh.z))


def within(sh, axis, place, size):
    index = sh.here(axis)
    low = jnp.where(index > 0, -EDGE, 0)
    high = jnp.where(index < sh.sizes[axis] - 1, size + EDGE, size)
    return (place >= low) & (place < high)


def grid_masks(sh):
    lane, along, across = sh.lane_grid(1)
    lanes = (lane < sh.used) & within(sh, 1, across, sh.y)
    rows = within(sh, 2, level(sh), sh.z)
    return (lanes & within(sh, 0, along, sh.x)) & rows, lanes & rows


def put(ref, f, value):
    ref[f, EDGE : ref.shape[1] - EDGE, :] = value


def local_solve(sh, z, residual_ref, springs_ref, columns, v, kv, factor):
    lane, _, _ = sh.lane_grid(1)
    mask = extended_mask(sh, z)
    put_columns(sh, springs_ref, columns)
    for m in range(3):
        factor[m] = pick(mask, relax / jnp.where(mask, springs_ref[m], 1.0))
        value = residual_ref[m] * factor[m]
        put(v[0], m, value)
        put(kv[0], m, springs_ref[6] * value)
    for sweep in range(SWEEPS - 1):
        old, new = sweep % 2, (sweep + 1) % 2
        image = image_of(sh, lane, v[old], kv[old], None, springs_ref, columns)
        for m in range(3):
            value = inner(v[old], m) + factor[m] * (residual_ref[m] - image[m])
            put(v[new], m, value)
            put(kv[new], m, springs_ref[6] * value)
    return (SWEEPS - 1) % 2


def own_level(sh):
    return lax.broadcasted_iota(jnp.int32, (sh.z, LANES), 0)


def coords(sh, z):
    _, along, across = sh.lane_grid(z.shape[0])
    along = jnp.where(along < 0, along + sh.x, jnp.where(along < sh.x, along, along - sh.x))
    across = jnp.where(across < 0, across + sh.y, jnp.where(across < sh.y, across, across - sh.y))
    place = lambda index, size: (2 * index + 1).astype(f32) / size - 1.0
    return place(along, sh.x), place(across, sh.y), place(z, sh.z)


def cell_coords(sh):
    cell = lax.broadcasted_iota(jnp.int32, (sh.cells, sh.z), 0)
    z = lax.broadcasted_iota(jnp.int32, (sh.cells, sh.z), 1)
    x = cell // sh.y
    place = lambda index, size: (2 * index + 1).astype(f32) / size - 1.0
    return place(x, sh.x), place(cell - x * sh.y, sh.y), place(z, sh.z)


def cross(a, b):
    return (a[1] * b[2] - a[2] * b[1], a[2] * b[0] - a[0] * b[2], a[0] * b[1] - a[1] * b[0])


def fold_rows(value):
    total = value[0:8]
    for i in range(8, value.shape[0], 8):
        total = total + value[i : i + 8]
    return jnp.sum(total, axis=0, keepdims=True)


def lane_sums(rows_ref):
    ones = jnp.ones((8, LANES), f32)
    return lax.dot_general(
        ones, rows_ref[...], (((1,), (1,)), ((), ())), precision=highest, preferred_element_type=f32
    )


def coarse_sums(nodes, field, places, count, sums):
    moments = tuple(field) + cross(places, field)
    for node in range(count):
        mask = nodes == node
        for m in range(6):
            sums[node * 6 + m : node * 6 + m + 1, :] = fold_rows(pick(mask, moments[m]))


def sums_line(sh, sums, unknowns):
    flat = (sh.here(0) * sh.sizes[1] + sh.here(1)) * sh.sizes[2] + sh.here(2)
    return pltpu.roll(lane_sums(sums), lax.rem(flat * unknowns, LANES), 1)[0:1]


def coarse_solution(received, inverse_ref, values):
    unknowns, total = inverse_ref.shape
    row = lax.broadcasted_iota(jnp.int32, received.shape, 0)
    part = jnp.zeros((unknowns, LANES), f32)
    for i in range(0, total, LANES):
        owner = (i + lax.broadcasted_iota(jnp.int32, (1, LANES), 1)) // unknowns
        vector = jnp.sum(pick(row == owner, received), axis=0, keepdims=True)
        part = part + inverse_ref[:, i : i + LANES] * vector
    values[0:unknowns, :] = jnp.dot(
        part, jnp.ones((LANES, LANES), f32), precision=highest, preferred_element_type=f32
    )


def coarse_shares(sums, inverse_ref, shares):
    unknowns, total = inverse_ref.shape
    column = jnp.dot(sums[...], jnp.ones((LANES, LANES), f32), precision=highest, preferred_element_type=f32)
    for i in range(0, total, LANES):
        share = inverse_ref[:, i : i + LANES] * column[0:unknowns]
        shares[i // LANES : i // LANES + 1, :] = jnp.sum(share, axis=0, keepdims=True)


def coarse_table(sh, shares_ref, unknowns, flat, table):
    rows = shares_ref.shape[0] // sh.devices
    lane = lax.broadcasted_iota(jnp.int32, (1, LANES), 1)
    for i in range(rows):
        flat[i : i + 1, :] = jnp.sum(shares_ref[pl.ds(i, sh.devices, stride=rows), :], axis=0, keepdims=True)
    for device in range(sh.devices):
        row, place = divmod(device * unknowns, LANES)
        part = shift(flat[row : row + 1, :], -place)
        if place + unknowns > LANES:
            part = jnp.where(lane < LANES - place, part, shift(flat[row + 1 : row + 2, :], -place))
        table[device : device + 1, :] = pick(lane < unknowns, part)


def region_values(sh, table, dz):
    lane, along, across = sh.lane_grid(1)
    x = sh.here(0) + jnp.where(along < 0, -1, jnp.where(along < sh.x, 0, 1))
    y = sh.here(1) + jnp.where(across < 0, -1, jnp.where(across < sh.y, 0, 1))
    z = sh.here(2) + dz
    exists = (lane < sh.used) & (x >= 0) & (x < sh.sizes[0]) & (y >= 0) & (y < sh.sizes[1])
    exists = exists & (z >= 0) & (z < sh.sizes[2])
    device = jnp.where(exists, (x * sh.sizes[1] + y) * sh.sizes[2] + z, -1)
    owner = lax.broadcasted_iota(jnp.int32, (sh.devices, LANES), 0) == device
    return lax.dot_general(
        table[0 : sh.devices, :], owner.astype(f32), (((0,), (0,)), ((), ())), precision=highest, preferred_element_type=f32
    )


def coarse_cells(nodes, places, values, count):
    cells = []
    for m in range(6):
        cell = jnp.zeros(nodes.shape, f32)
        for node in range(count):
            cell = jnp.where(nodes == float(node), values[node * 6 + m : node * 6 + m + 1, :], cell)
        cells.append(cell)
    turned = cross(cells[3:], places)
    return [cells[m] + turned[m] for m in range(3)]


def selection(sh):
    lane, along, across = sh.lane_grid(sh.cells)
    inside = (along >= 0) & (along < sh.x) & (across >= 0) & (across < sh.y)
    row = lax.broadcasted_iota(jnp.int32, (sh.cells, LANES), 0)
    return (inside & (row == along * sh.y + across)).astype(f32)


def to_lanes(value, select, precision=highest):
    return lax.dot_general(
        value, select, (((0,), (0,)), ((), ())), precision=precision, preferred_element_type=f32
    )


def to_cells(value, select):
    return lax.dot_general(
        select, value, (((1,), (1,)), ((), ())), precision=highest, preferred_element_type=f32
    )


def send_lines(sh, lines, slots_ref):
    here = [sh.here(axis) for axis in range(3)]
    corner = [lines[8 * i : 8 * i + 8, :] for i in range(4)]
    top, bottom = lines[32:40, :], lines[40:48, :]
    for x in range(sh.sizes[0]):
        low_high = [jnp.where(x > here[0], corner[2 + high], corner[high]) for high in range(2)]
        for y in range(sh.sizes[1]):
            column = jnp.where(y > here[1], low_high[1], low_high[0])
            for z in range(sh.sizes[2]):
                slot = jnp.where(z == here[2] + 1, top, jnp.where(z == here[2] - 1, bottom, column))
                place = 8 * ((x * sh.sizes[1] + y) * sh.sizes[2] + z)
                slots_ref[place : place + 8, :] = slot


def slot_from(sh, received_ref, step):
    place, exists = 0, None
    for axis in range(3):
        index = sh.here(axis) + step[axis]
        inside = (index >= 0) & (index < sh.sizes[axis])
        exists = inside if exists is None else exists & inside
        place = place * sh.sizes[axis] + jnp.clip(index, 0, sh.sizes[axis] - 1)
    return scale(exists, received_ref[pl.ds(pl.multiple_of(place * 8, 8), 8), :])


def repeat_twice(count):
    row = lax.broadcasted_iota(jnp.int32, (2 * count, count), 0)
    column = lax.broadcasted_iota(jnp.int32, (2 * count, count), 1)
    return ((row >= 2 * column) & (row < 2 * column + 2)).astype(f32)


def ring(size_x, size_y, rows):
    row = lax.broadcasted_iota(jnp.int32, (rows, LANES), 0)
    sides_x, both = 2 * size_y, 2 * size_y + 2 * size_x
    corner = row - both
    x = jnp.where(row < size_y, -1, size_x)
    x = jnp.where(row < sides_x, x, jnp.where(row < sides_x + size_x, row - sides_x, row - sides_x - size_x))
    x = jnp.where(row < both, x, jnp.where(corner < 2, -1, size_x))
    y = jnp.where(row < size_y, row, row - size_y)
    y = jnp.where(row < sides_x, y, jnp.where(row < sides_x + size_x, -1, size_y))
    y = jnp.where(row < both, y, jnp.where((corner == 0) | (corner == 2), -1, size_y))
    return x, y, (row < sides_x) | (row >= both), row < both + 4


def face_shape(sh, label_x, label_y):
    rows = max(4 * sh.x + label_x, 4 * sh.y + label_y)
    return (-(-rows // 8) * 8, LANES)


def pack_faces(sh, natural_ref, stiff, label_x, label_y, x_refs, y_refs):
    even_x, even_y = sh.here(0) % 2 == 0, sh.here(1) % 2 == 0

    def face(at, count, stride, label_at, label_count, label_stride):
        rows = [natural_ref[m, pl.ds(at, count, stride=stride), :] for m in range(4)]
        return rows, stiff[pl.ds(label_at, label_count, stride=label_stride), :]

    above = face(sh.cells - sh.y, sh.y, 1, (label_x - 1) * label_y, label_y, 1)
    below = face(0, sh.y, 1, 0, label_y, 1)
    for refs, links, even, above, below in (
        (x_refs, sh.x_links, even_x, above, below),
        (
            y_refs,
            sh.y_links,
            even_y,
            face(sh.y - 1, sh.x, sh.y, label_y - 1, label_x, label_y),
            face(0, sh.x, sh.y, 0, label_x, label_y),
        ),
    ):
        for i, ref in enumerate(refs):
            ref[...] = jnp.zeros(ref.shape, f32)
            count = above[0][0].shape[0]
            for m in range(4):
                ref[m * count : (m + 1) * count, :] = pair(links, even, above[0][m], below[0][m])[i]
            labels, length = above[1].shape
            ref[4 * count : 4 * count + labels, 0:length] = pair(links, even, above[1], below[1])[i]


def merge_start(sh, refs, x_refs, y_refs, received_ref, sizes, cells, labels):
    residual, nodes, stiff, stiff_rim = refs
    label_x, label_y, label_z = sizes
    lane, along, across = sh.lane_grid(1)
    inside = lane < sh.used
    last = (sh.x + 1) * sh.pitch
    x_mask = {-1: lane < sh.pitch, 0: (lane >= sh.pitch) & (lane < last), 1: (lane >= last) & inside}
    y_mask = {-1: across < 0, 0: (across >= 0) & (across < sh.y), 1: across >= sh.y}
    cells[...] = jnp.zeros(cells.shape, f32)
    labels[...] = jnp.zeros(labels.shape, f32)
    count, label_count = cells.shape[1], labels.shape[0]
    at = label_at = 0
    for axis, face_refs, size, label_size in ((0, x_refs, sh.y, label_y), (1, y_refs, sh.x, label_x)):
        for message in sides(sh, axis, [ref[...] for ref in face_refs]):
            for m in range(4):
                cells[m, at : at + size, :] = message[m * size : (m + 1) * size]
            labels[label_at : label_at + label_size, :] = message[4 * size : 4 * size + label_size, 0:label_z]
            at, label_at = at + size, label_at + label_size
    for dx, dy in ((-1, -1), (-1, 1), (1, -1), (1, 1)):
        slot = slot_from(sh, received_ref, (dx, dy, 0))
        for m, row in enumerate((0, 1, 2, 5)):
            cells[m, at : at + 1, :] = slot[row : row + 1]
        labels[label_at : label_at + 1, :] = slot[3:4, 0:label_z]
        at, label_at = at + 1, label_at + 1
    x, y, _, valid = ring(sh.x, sh.y, count)
    place = (valid & inside & (along == x) & (across == y)).astype(f32)
    own = slice(EDGE, EDGE + sh.z)
    tall_own = slice(2 * EDGE, 2 * EDGE + sh.z)
    for m in range(3):
        residual[m, own, :] += to_lanes(cells[m], place)
    nodes[own, :] += to_lanes(cells[3], place, small)
    by_z = lax.dot_general(
        repeat_twice(label_z), labels[...], (((1,), (1,)), ((), ())), precision=highest, preferred_element_type=f32
    )
    x, y, at_x, valid = ring(label_x, label_y, label_count)
    match = valid & inside & ((along >> 1) == x) & ((across >> 1) == y)
    columns = jnp.dot(by_z, (match & at_x).astype(f32), precision=highest, preferred_element_type=f32)
    stiff_rim[0, tall_own, :] = columns
    columns = columns + jnp.dot(by_z, (match & ~at_x).astype(f32), precision=highest, preferred_element_type=f32)
    stiff[0, tall_own, :] += columns
    for dz in (-1, 1):
        main = edge = jnp.zeros((8, LANES), f32)
        for dx in (-1, 0, 1):
            for dy in (-1, 0, 1):
                slot = slot_from(sh, received_ref, (dx, dy, dz))
                mask = x_mask[dx] & y_mask[dy]
                main = main + pick(mask, shift(slot, dx * sh.x * sh.pitch + dy * sh.y))
                if dx:
                    edge = edge + pick(mask, shift(slot, dx * (sh.x - 1) * sh.pitch + dy * sh.y))
        near = EDGE + sh.z if dz > 0 else EDGE - 1
        for m in range(3):
            residual[m, near : near + 1, :] = main[m : m + 1]
        nodes[near : near + 1, :] = main[5:6]
        for row in (EDGE + near, EDGE + near + dz):
            stiff[0, row : row + 1, :] = main[3:4]
            stiff_rim[0, row : row + 1, :] = edge[3:4]


def call(kernel, name, outs, ins, scratch=(), remote_ins=False, remote_outs=()):
    space = pltpu.HBM if remote_ins else pltpu.VMEM
    return pl.pallas_call(
        kernel,
        out_shape=[jax.ShapeDtypeStruct(shape, f32) for shape in outs],
        in_specs=[pl.BlockSpec(memory_space=space) for _ in ins],
        out_specs=[
            pl.BlockSpec(memory_space=pltpu.HBM if i in remote_outs else pltpu.VMEM) for i in range(len(outs))
        ],
        scratch_shapes=[pltpu.VMEM(shape, f32) if isinstance(shape, tuple) else shape for shape in scratch],
        compiler_params=pltpu.CompilerParams(vmem_limit_bytes=(56 if remote_ins else 48) * 1024 * 1024),
        name=name,
    )(*ins)


def permutation(sizes, moves):
    def partner(axis, link, index):
        size = sizes[axis]
        other = index ^ 1 if link == 0 else index + (1 if index % 2 else -1)
        if 0 <= other < size:
            return other
        return size - 1 - index if axis == 2 and size % 2 == 0 else index

    pairs = []
    for x in range(sizes[0]):
        for y in range(sizes[1]):
            for z in range(sizes[2]):
                place = [x, y, z]
                goal = [partner(a, moves[a], place[a]) if a in moves else place[a] for a in range(3)]
                if any(goal[a] == place[a] for a in moves) and sizes[2] % 2 == 0:
                    goal = [x, y, partner(2, 0, z)]
                flat = [(p[0] * sizes[1] + p[1]) * sizes[2] + p[2] for p in (place, goal)]
                pairs.append(tuple(flat))
    return pairs


def send(sh, value, moves):
    return lax.ppermute(value, AXES, permutation(sh.sizes, moves))


def send_z(sh, messages):
    return [send(sh, message, {2: link}) for link, message in enumerate(messages)]


def send_faces(sh, x_messages, y_messages):
    from_x = [send(sh, message, {0: link}) for link, message in enumerate(x_messages)]
    from_y = [send(sh, message, {1: link}) for link, message in enumerate(y_messages)]
    return from_y, from_x


def to_all(slots):
    return lax.all_to_all(slots, AXES, 0, 0, tiled=True)


def exchange(sh, ex, name, field, z_messages):
    from_z = send_z(sh, z_messages)

    corners = sh.x_links * sh.y_links

    def packer(*refs):
        take = Taker(refs)
        field_ref, z_refs = take.one(), take(sh.z_links)
        x_refs, y_refs, corner_refs, scratch = take(sh.x_links), take(sh.y_links), take(corners), take.one()
        merge_z(sh, ex, field_ref, z_refs, scratch, 0)
        pack_xy(sh, ex, scratch, x_refs, y_refs, corner_refs)

    plane = (sh.rows, LANES)
    messages = call(
        packer,
        name,
        [plane] * sh.x_links
        + [folded_shape(sh, ex.fields * ex.layers)] * sh.y_links
        + [folded_shape(sh, ex.layers)] * corners,
        [field] + from_z,
        [(ex.fields,) + plane],
    )
    take = Taker(messages)
    x_messages, y_messages = take(sh.x_links), take(sh.y_links)
    from_y, straight = send_faces(sh, x_messages, y_messages)
    from_x = []
    for link in range(sh.x_links):
        from_x.append(straight[link])
        from_x.extend(send(sh, take.one(), {0: link, 1: other}) for other in range(sh.y_links))
    return from_z, from_y, from_x


class Taker:
    def __init__(self, refs):
        self.refs, self.at = refs, 0

    def __call__(self, count):
        self.at += count
        return self.refs[self.at - count : self.at]

    def one(self):
        return self(1)[0]


def merge_all(sh, ex, take, scratch, rim, guard):
    field = take.one()
    from_z, from_y = take(sh.z_links), take(sh.y_links)
    from_x = take(sh.x_links * (1 + sh.y_links))
    merge_z(sh, ex, field, from_z, scratch, guard)
    merge_xy(sh, ex, scratch, rim, guard, from_y, from_x)


def body(right_side, phase_labels, phase_moduli, coarse_nodes, coarse_inverse):
    sizes = tuple(lax.axis_size(axis) for axis in AXES)
    _, size_x, size_y, size_z = right_side.shape
    sh = Shape(size_x, size_y, size_z, phase_moduli.shape[0], sizes)
    unknowns = coarse_inverse.shape[0]
    node_count = unknowns // 6
    sum_rows = -(-unknowns // 8) * 8 + 8
    share_rows = coarse_inverse.shape[1] // LANES
    own = slice(EDGE, EDGE + sh.z)
    plane = (sh.rows, LANES)
    fields = (3,) + plane
    tall = (3, sh.tall, LANES)
    slots = (sh.devices, LANES)
    z_shape = lambda ex: [(8 * ex.fields, LANES)] * sh.z_links
    natural = right_side.reshape(3, sh.cells, sh.z)
    nodes_natural = coarse_nodes.reshape(sh.cells, sh.z)
    label_x, label_y, label_z = phase_labels.shape

    def block_places():
        lane, along, across = sh.lane_grid(label_x * label_y)
        inside = (along >= 0) & (along < sh.x) & (across >= 0) & (across < sh.y)
        block = lax.broadcasted_iota(jnp.int32, along.shape, 0)
        return (inside & (block == (along >> 1) * label_y + (across >> 1))).astype(f32)

    def end_layers(values, places):
        length = values.shape[1]
        row = lax.broadcasted_iota(jnp.int32, (8, length), 0)
        at = lax.broadcasted_iota(jnp.int32, (8, length), 1)
        ends = ((row == 0) & (at == length - 1)) | ((row == 1) & (at == 0))
        return jnp.dot(to_cells(values, ends.astype(f32)), places, precision=highest, preferred_element_type=f32)

    def begin(natural_in, labels_in, moduli_in, nodes_in, stiff, slots_ref, *rest):
        x_refs, y_refs = rest[: sh.x_links], rest[sh.x_links : sh.x_links + sh.y_links]
        natural_ref, labels_ref, moduli_ref, nodes_ref, sems, sums, lines = rest[sh.x_links + sh.y_links :]
        pairs = ((natural_in, natural_ref.at[0:3, 0 : sh.cells, :]), (labels_in, labels_ref.at[0:label_x]), (moduli_in, moduli_ref), (nodes_in, nodes_ref))
        copies = [pltpu.make_async_copy(a, b, sems.at[i]) for i, (a, b) in enumerate(pairs)]
        for copy in copies:
            copy.start()
        sums[...] = jnp.zeros(sums.shape, f32)
        lines[...] = jnp.zeros(lines.shape, f32)
        for copy in copies:
            copy.wait()
        for i in range(label_x):
            labels = labels_ref[i]
            moduli = jnp.zeros(labels.shape, f32)
            for phase in range(sh.phases):
                moduli = jnp.where(labels == phase, moduli_ref[phase], moduli)
            stiff[i * label_y : (i + 1) * label_y, :] = moduli
        natural_ref[3, 0 : sh.cells, :] = nodes_ref[...].astype(f32) + 1.0
        cells = [natural_ref[m, 0 : sh.cells, :] for m in range(4)]
        coarse_sums(nodes_ref[...], cells[:3], cell_coords(sh), node_count, sums)
        line = sums_line(sh, sums, unknowns)
        for i, (cell, block) in enumerate(
            (
                (0, 0),
                (sh.y - 1, label_y - 1),
                ((sh.x - 1) * sh.y, (label_x - 1) * label_y),
                (sh.cells - 1, label_x * label_y - 1),
            )
        ):
            for m in range(3):
                lines[8 * i + m : 8 * i + m + 1, :] = natural_ref[m, cell : cell + 1, :]
            lines[8 * i + 3 : 8 * i + 4, 0:label_z] = stiff[block : block + 1, :]
            lines[8 * i + 5 : 8 * i + 6, :] = natural_ref[3, cell : cell + 1, :]
        select = selection(sh)
        layers = [end_layers(cells[m], select) for m in range(4)] + [end_layers(stiff[0 : label_x * label_y, :], block_places())]
        for i in range(2):
            for layer, row in zip(layers, (0, 1, 2, 5, 3)):
                lines[8 * (4 + i) + row : 8 * (4 + i) + row + 1, :] = layer[i : i + 1]
        for i in range(6):
            lines[8 * i + 4 : 8 * i + 5, :] = line
        send_lines(sh, lines, slots_ref)
        pack_faces(sh, natural_ref, stiff, label_x, label_y, x_refs, y_refs)

    block_rows = (8 * -(-(label_x + 8) * label_y // 8), label_z)
    stiff_blocks, lines, *messages = call(
        begin,
        "begin",
        [block_rows, (8 * sh.devices, LANES)]
        + [face_shape(sh, label_x, label_y)] * (sh.x_links + sh.y_links),
        [natural, phase_labels, phase_moduli, nodes_natural],
        [
            (4, sh.cells + 8, sh.z),
            pltpu.VMEM((label_x + 2, label_y, label_z), jnp.int32),
            pltpu.SMEM(phase_moduli.shape, f32),
            pltpu.VMEM(nodes_natural.shape, jnp.int32),
            pltpu.SemaphoreType.DMA((4,)),
            (LANES, LANES),
            (56, LANES),
        ],
        remote_ins=True,
    )

    def spread(natural_ref, nodes_ref, stiff, inverse_in, field_ref, lanes_ref, inverse_ref):
        inverse_ref[...] = inverse_in[...]
        select = selection(sh)
        field_ref[...] = jnp.zeros(field_ref.shape, f32)
        for m in range(3):
            field_ref[m, own, :] = to_lanes(natural_ref[m], select)
        by_z = lax.dot_general(
            repeat_twice(label_z),
            stiff[0 : label_x * label_y, :],
            (((1,), (1,)), ((), ())),
            precision=highest,
            preferred_element_type=f32,
        )
        field_ref[3, own, :] = jnp.dot(by_z, block_places(), precision=highest, preferred_element_type=f32)
        lanes_ref[...] = to_lanes(nodes_ref[...].astype(f32) + 1.0, select, small) - 1.0

    start_field, nodes, inverse = call(
        spread,
        "spread",
        [(4,) + plane, (sh.z, LANES), coarse_inverse.shape],
        [natural, nodes_natural, stiff_blocks, coarse_inverse],
    )
    from_y, from_x = send_faces(sh, messages[: sh.x_links], messages[sh.x_links :])
    lines = to_all(lines)

    short = (3, 6 * EDGE, LANES)
    short_fields = (3, 4 * EDGE, LANES)
    solve_scratch = [tall] * 4 + [fields, (8,) + plane]
    short_scratch = [short] * 4 + [short_fields, (8, 4 * EDGE, LANES)]

    def end_rows(ref):
        def rows(f, start, count):
            place = start + EDGE if start < 2 * EDGE else start - sh.rows + 5 * EDGE
            return ref[f, place : place + count, :]

        return rows

    def first_ends(*refs):
        take = Taker(refs)
        field_ref = take.one()
        y_refs, x_refs = take(sh.y_links), take(sh.x_links)
        nodes_ref, lines_ref, inverse_ref = take(3)
        residual, wide_nodes, stiffness_ref, values = take(4)
        z_refs = take(sh.z_links)
        stiff, stiff_rim, cells, labels, short_stiff, short_rim, some_residual, springs = take(8)
        v0, v1, kv0, kv1, factor, columns = take(6)
        clear_guards(sh, (stiff, stiff_rim, short_stiff, short_rim, v0, v1, kv0, kv1))
        residual[...] = field_ref[0:3]
        put(stiff, 0, field_ref[3])
        put(stiff_rim, 0, jnp.zeros(plane, f32))
        sizes = phase_labels.shape
        wide_nodes[...] = jnp.zeros(plane, f32)
        wide_nodes[own, :] = nodes_ref[...] + 1.0
        merge_start(sh, (residual, wide_nodes, stiff, stiff_rim), x_refs, y_refs, lines_ref, sizes, cells, labels)
        wide_nodes[...] = wide_nodes[...] - 1.0
        stiffness_ref[0] = inner(stiff, 0)
        stiffness_ref[1] = inner(stiff_rim, 0)
        coarse_solution(lines_ref[pl.ds(4, sh.devices, stride=8), :], inverse_ref, values)
        lane, _, _ = sh.lane_grid(1)
        put(short_stiff, 0, ends(stiffness_ref[0]))
        put(short_rim, 0, ends(stiffness_ref[1]))
        for f, entry in enumerate(own_block(sh, lane, (short_stiff, short_rim))):
            springs[f] = entry
        springs[6] = inner(short_stiff, 0)
        for m in range(3):
            some_residual[m] = ends(residual[m])
        index = local_solve(sh, ends_level(sh), some_residual, springs, columns, (v0, v1), (kv0, kv1), factor)
        solution = (v0, v1)[index]
        z = lax.broadcasted_iota(jnp.int32, (2 * EDGE, LANES), 0)
        z = jnp.where(z < EDGE, z, z + sh.z - 2 * EDGE)
        some_nodes = jnp.concatenate([nodes_ref[0:EDGE, :], nodes_ref[sh.z - EDGE : sh.z, :]], axis=0)
        added = coarse_cells(some_nodes, coords(sh, z), values, node_count)
        for m in range(3):
            solution[m, 2 * EDGE : 4 * EDGE, :] += pick(some_nodes >= 0.0, added[m])
        pack_z(sh, DEEP, end_rows(solution), z_refs)

    residual, wide_nodes, stiffness, values, *z_messages = call(
        first_ends,
        "first_ends",
        [fields, plane, (2,) + plane, (sum_rows, LANES)] + z_shape(DEEP),
        [start_field, *from_y, *from_x, nodes, lines, inverse],
        [(1, sh.tall, LANES)] * 2
        + [
            (4, 8 * -(-(2 * sh.x + 2 * sh.y + 4) // 8) + 8, LANES),
            (8 * -(-(2 * label_x + 2 * label_y + 4) // 8) + 8, label_z),
        ]
        + [(1, 6 * EDGE, LANES)] * 2
        + [short_fields, (7, 4 * EDGE, LANES)]
        + short_scratch,
    )

    def first_solve(residual_ref, stiffness_ref, values, nodes_ref, solution_ref, springs_ref, *rest):
        stiff, stiff_rim, v0, v1, kv0, kv1, factor, columns = rest
        clear_guards(sh, (stiff, stiff_rim, v0, v1, kv0, kv1))
        put(stiff, 0, stiffness_ref[0])
        put(stiff_rim, 0, stiffness_ref[1])
        springs_ref[6] = stiffness_ref[0]
        springs_ref[7] = stiffness_ref[1]
        lane, _, _ = sh.lane_grid(1)
        for f, entry in enumerate(own_block(sh, lane, (stiff, stiff_rim))):
            springs_ref[f] = entry
        index = local_solve(sh, level(sh), residual_ref, springs_ref, columns, (v0, v1), (kv0, kv1), factor)
        for m in range(3):
            solution_ref[m] = inner((v0, v1)[index], m)
        added = coarse_cells(nodes_ref[...], coords(sh, own_level(sh)), values, node_count)
        for m in range(3):
            solution_ref[m, own, :] += pick(nodes_ref[...] >= 0.0, added[m])

    solved, springs = call(
        first_solve,
        "first_solve",
        [fields, (8,) + plane],
        [residual, stiffness, values, nodes],
        [(1, sh.tall, LANES)] * 2 + solve_scratch,
    )
    from_z, from_y, from_x = exchange(sh, DEEP, "deep", solved, z_messages)

    def first_image(*refs):
        take = Taker(refs)
        merging = take(1 + sh.z_links + sh.y_links + sh.x_links * (1 + sh.y_links))
        nodes_ref, springs_ref, inverse_ref = take(3)
        search_ref, image_ref, slots_out = take(3)
        z_refs = take(sh.z_links)
        v, rim, kv, k_rim, sums, shares, slots_ref, sem = take(8)
        some_residual, some_springs, v0, v1, kv0, kv1, factor, some_columns, columns = take(9)
        clear_guards(sh, (v0, v1, kv0, kv1))
        clear_guards(sh, (v, rim, kv, k_rim))
        merge_all(sh, DEEP, Taker(merging), v, rim, EDGE)
        lane, _, _ = sh.lane_grid(1)

        in_grid, in_rim = grid_masks(sh)
        for m in range(3):
            value = pick(in_grid, inner(v, m))
            put(v, m, value)
            search_ref[m] = value
            put(kv, m, springs_ref[6] * value)
            value = pick(in_rim, inner(rim, m))
            put(rim, m, value)
            put(k_rim, m, springs_ref[7] * value)
        put_columns(sh, springs_ref, columns)
        image = image_of(sh, lane, v, kv, (rim, k_rim), springs_ref, columns)
        keep = in_grid & extended_mask(sh, level(sh))
        for m in range(3):
            image_ref[m] = pick(keep, image[m])
        sums[...] = jnp.zeros(sums.shape, f32)
        field = [image_ref[m, own, :] for m in range(3)]
        coarse_sums(nodes_ref[...], field, coords(sh, own_level(sh)), node_count, sums)
        coarse_shares(sums, inverse_ref, shares)
        for device in range(sh.devices):
            slots_ref[device * share_rows : (device + 1) * share_rows, :] = shares[0:share_rows, :]
        copy = pltpu.make_async_copy(slots_ref.at[0 : slots_out.shape[0], :], slots_out, sem)
        copy.start()
        for m in range(3):
            some_residual[m] = ends(image_ref[m])
        for f in range(7):
            some_springs[f] = ends(springs_ref[f])
        index = local_solve(sh, ends_level(sh), some_residual, some_springs, some_columns, (v0, v1), (kv0, kv1), factor)
        pack_z(sh, NEAR, end_rows((v0, v1)[index]), z_refs)
        copy.wait()

    all_slots = (sh.devices * share_rows, LANES)
    search, image, shares, *z_messages = call(
        first_image,
        "first_image",
        [fields, fields, all_slots] + z_shape(NEAR),
        [solved, *from_z, *from_y, *from_x, nodes, springs, inverse],
        [tall] * 4
        + [(LANES, LANES), (8 * -(-share_rows // 8) + 8, LANES)]
        + [(8 * -(-all_slots[0] // 8) + 8, LANES), pltpu.SemaphoreType.DMA]
        + [short_fields, (7, 4 * EDGE, LANES)]
        + short_scratch
        + [(8,) + plane],
        remote_outs=(2,),
    )
    shares = to_all(shares.reshape(sh.devices, 1, share_rows * LANES)).reshape(shares.shape)

    def second_solve(image_ref, springs_ref, local_ref, v0, v1, kv0, kv1, factor, columns):
        clear_guards(sh, (v0, v1, kv0, kv1))
        index = local_solve(sh, level(sh), image_ref, springs_ref, columns, (v0, v1), (kv0, kv1), factor)
        for m in range(3):
            local_ref[m] = inner((v0, v1)[index], m)

    (solved,) = call(second_solve, "second_solve", [fields], [image, springs], solve_scratch)
    from_z, from_y, from_x = exchange(sh, NEAR, "near", solved, z_messages)

    def between(shares_ref, wide_nodes, nodes_ref, start_ref, search_ref, first_ref, coarse_ref, sums, *scratch):
        flat, table, values = scratch
        coarse_ref[...] = jnp.zeros(coarse_ref.shape, f32)
        coarse_table(sh, shares_ref, unknowns, flat, table)
        last = lax.broadcasted_iota(jnp.int32, (1, LANES), 0) + sh.z - 1
        for dz, first, z in ((0, EDGE, own_level(sh)), (-1, EDGE - 1, last), (1, EDGE + sh.z, last - sh.z + 1)):
            values[...] = region_values(sh, table, dz)
            rows = slice(first, first + z.shape[0])
            added = coarse_cells(wide_nodes[rows, :], coords(sh, z), values, node_count)
            for m in range(3):
                coarse_ref[m, rows, :] = added[m]
        valid = nodes_ref[...] >= 0.0
        row = lax.broadcasted_iota(jnp.int32, sums.shape, 0)
        total = jnp.zeros(sums.shape, f32)
        for i, other in enumerate((start_ref, first_ref)):
            product = sum(search_ref[m, own, :] * other[m, own, :] for m in range(3))
            total = jnp.where(row == i, fold_rows(pick(valid, product)), total)
        sums[...] = total

    coarse_field, sums = call(
        between,
        "between",
        [fields, (8, LANES)],
        [shares, wide_nodes, nodes, start_field, search, image],
        [(8 * -(-share_rows // 8) + 8, LANES), (8 * -(-sh.devices // 8) + 8, LANES), (LANES, LANES)],
    )

    def second_image(*refs):
        take = Taker(refs)
        merging = take(1 + sh.z_links + sh.y_links + sh.x_links * (1 + sh.y_links))
        nodes_ref, springs_ref, first_ref, coarse_ref, early_ref = take(5)
        second_ref, image_ref, slots_ref = take(3)
        v, kv, sums, columns = take(4)
        clear_guards(sh, (v, kv))
        put_columns(sh, springs_ref, columns)
        merge_all(sh, NEAR, Taker(merging), v, None, EDGE)
        lane, _, _ = sh.lane_grid(1)
        in_grid, _ = grid_masks(sh)
        for m in range(3):
            value = pick(in_grid, inner(v, m)) + coarse_ref[m]
            put(v, m, value)
            second_ref[m] = value
            put(kv, m, springs_ref[6] * value)
        image = image_of(sh, lane, v, kv, None, springs_ref, columns)
        for m in range(3):
            image_ref[m] = image[m]
        valid = nodes_ref[...] >= 0.0
        sums[...] = jnp.zeros(sums.shape, f32)
        sums[0:8, :] = early_ref[...]
        for i, other in ((2, first_ref), (3, image_ref)):
            product = sum(second_ref[m, own, :] * other[m, own, :] for m in range(3))
            sums[i : i + 1, :] = fold_rows(pick(valid, product))
        slots_ref[...] = jnp.broadcast_to(lane_sums(sums)[0:1], slots_ref.shape)

    second, second_image_field, sums = call(
        second_image,
        "second_image",
        [fields, fields, slots],
        [solved, *from_z, *from_y, *from_x, nodes, springs, image, coarse_field, sums],
        [tall] * 2 + [(LANES, LANES), (8,) + plane],
    )
    totals = to_all(sums)

    def turn(search_ref, first_ref, second_ref, image_ref, out_ref):
        select = selection(sh)
        for i, ref in enumerate((search_ref, first_ref, second_ref, image_ref)):
            for m in range(3):
                out_ref[i, m] = to_cells(ref[m, own, :], select)

    (turned,) = call(turn, "turn", [(4,) + natural.shape], [search, image, second, second_image_field])

    def finish(totals_ref, natural_ref, turned_ref, field_ref, residual_ref):
        total = jnp.sum(totals_ref[...], axis=0, keepdims=True)
        rz, zw, wq, qv = [total[:, i : i + 1] for i in range(4)]
        step0 = rz / zw
        rho = step0 * step0 * wq - step0 * zw
        grow = 1.0 + rho / rz
        curvature = grow * grow * zw - 2.0 * grow * step0 * wq + step0 * step0 * qv
        step1 = rho / curvature
        first = step0 + step1 * grow
        second = step0 * step1
        for m in range(3):
            field_ref[m] = first * turned_ref[0, m] - second * turned_ref[2, m]
            residual_ref[m] = natural_ref[m] - (first * turned_ref[1, m] - second * turned_ref[3, m])

    solution_field, residual = call(
        finish, "finish", [natural.shape, natural.shape], [totals, natural, turned]
    )
    return solution_field.reshape(right_side.shape), residual.reshape(right_side.shape)


def solution(mesh):
    in_specs = (
        P(None, "gx", "gy", "gz"),
        P("gx", "gy", "gz"),
        P(),
        P("gx", "gy", "gz"),
        P(("gx", "gy", "gz"), None),
    )
    out_specs = (P(None, "gx", "gy", "gz"), P(None, "gx", "gy", "gz"))
    return jax.shard_map(body, mesh=mesh, in_specs=in_specs, out_specs=out_specs, check_vma=False)
```

```python
import jax
import jax.numpy as jnp
from jax import lax
from jax.experimental import pallas as pl
from jax.experimental.pallas import tpu as pltpu
from jax.sharding import PartitionSpec as P

AXES = ("gx", "gy", "gz")
SWEEPS = 4
relax = 0.6
highest = lax.Precision.HIGHEST
small = lax.Precision.DEFAULT
f32 = jnp.float32
LANES = 128
EDGE = 8

SCALE = 36.0
ALONG1, ACROSS1 = 27.0, 18.0
ALONG2, ACROSS2, MIXED2 = 11.25, 9.0, 2.25
SAME3 = 7.0
TOTAL = 2 * ALONG1 + 4 * ACROSS1 + 8 * ALONG2 + 4 * ACROSS2 + 8 * SAME3


class Exchange:
    def __init__(self, fields, layers, up, down):
        self.fields, self.layers, self.up, self.down = fields, layers, up, down


DEEP = Exchange(3, 3, -2, -1)
NEAR = Exchange(3, 2, -1, -1)


class Shape:
    def __init__(self, size_x, size_y, size_z, phases, mesh_sizes):
        self.x, self.y, self.z = size_x, size_y, size_z
        self.pitch = size_y + 4
        self.used = (size_x + 2) * self.pitch
        assert self.used <= LANES
        self.rows = size_z + 2 * EDGE
        self.tall = self.rows + 2 * EDGE
        self.phases = phases
        self.sizes = mesh_sizes
        self.devices = mesh_sizes[0] * mesh_sizes[1] * mesh_sizes[2]
        self.cells = size_x * size_y
        self.links = [1 if n <= 2 else 2 for n in mesh_sizes]
        self.x_links, self.y_links, self.z_links = self.links

    def lane_grid(self, rows):
        lane = lax.broadcasted_iota(jnp.int32, (rows, LANES), 1)
        column = jnp.zeros_like(lane)
        for j in range(1, self.x + 2):
            column = column + (lane >= j * self.pitch).astype(jnp.int32)
        offset = lane - column * self.pitch
        return lane, column - 1, offset - 2

    def here(self, axis):
        return lax.axis_index(AXES[axis])


def shift(value, amount):
    amount = amount % LANES
    return value if amount == 0 else pltpu.roll(value, amount, 1)


def pick(mask, value):
    return jnp.where(mask, value, 0.0)


def scale(flag, value):
    return value * flag.astype(f32)


def pair(links, even, upward, downward):
    first = jnp.where(even, upward, downward)
    return (first,) if links == 1 else (first, jnp.where(even, downward, upward))


def sides(sh, axis, received):
    index, size = sh.here(axis), sh.sizes[axis]
    even = index % 2 == 0
    first = received[0]
    second = received[1] if len(received) > 1 else jnp.zeros_like(first)
    below = jnp.where(even, second, first)
    above = jnp.where(even, first, second)
    return scale(index > 0, below), scale(index < size - 1, above)


def lane_range(lane, start, count):
    return (lane >= start) & (lane < start + count)


def pack_z(sh, ex, source, out_refs):
    even = sh.here(2) % 2 == 0
    for ref in out_refs:
        ref[...] = jnp.zeros(ref.shape, f32)
    for f in range(ex.fields):
        upward = source(f, EDGE + sh.z + ex.up, ex.layers)
        downward = source(f, EDGE + ex.down, ex.layers)
        for ref, message in zip(out_refs, pair(sh.z_links, even, upward, downward)):
            ref[8 * f : 8 * f + ex.layers, :] = message


def merge_z(sh, ex, field_ref, received_refs, scratch, guard):
    below, above = sides(sh, 2, [ref[...] for ref in received_refs])
    for f in range(ex.fields):
        scratch[f, guard : guard + sh.rows, :] = field_ref[f]
        low = guard + EDGE + ex.up
        high = guard + EDGE + sh.z + ex.down
        scratch[f, low : low + ex.layers, :] += below[8 * f : 8 * f + ex.layers]
        scratch[f, high : high + ex.layers, :] += above[8 * f : 8 * f + ex.layers]


def fold(sh, value, layers, start=None):
    folds = sh.pitch // layers
    height = -(-sh.rows // (8 * folds)) * 8
    lane, _, across = sh.lane_grid(1)
    total = jnp.zeros((height, LANES), f32)
    for i, first in enumerate(range(0, sh.rows, height)):
        part = value[first : first + height]
        if start is not None:
            part = pick((lane < sh.used) & lane_range(across, start, layers), part)
        part = shift(part, i * layers - (0 if start is None else start + 2))
        if part.shape[0] < height:
            part = jnp.concatenate([part, jnp.zeros((height - part.shape[0], LANES), f32)], axis=0)
        total = total + part
    return total


def folded_shape(sh, layers):
    return (-(-sh.rows // (8 * (sh.pitch // layers))) * 8, LANES)


def unfold(sh, message, layers, start):
    height = message.shape[0]
    lane, _, across = sh.lane_grid(1)
    mask = (lane < sh.used) & lane_range(across, start, layers)
    parts = []
    for i, first in enumerate(range(0, sh.rows, height)):
        part = message[0 : min(height, sh.rows - first)]
        parts.append(pick(mask, shift(part, start + 2 - i * layers)))
    return jnp.concatenate(parts, axis=0) if len(parts) > 1 else parts[0]


def pack_xy(sh, ex, scratch, x_refs, y_refs, corner_refs):
    rows = sh.rows
    lane, _, across = sh.lane_grid(1)
    even_x, even_y = sh.here(0) % 2 == 0, sh.here(1) % 2 == 0
    span = ex.layers * sh.pitch
    x_up = x_down = y_up = y_down = jnp.zeros((rows, LANES), f32)
    inside = lane < sh.used
    y_above, y_below = sh.y + ex.up, ex.down
    for f in range(ex.fields):
        value = scratch[f]
        start = (sh.x + ex.up + 1) * sh.pitch
        x_up = x_up + shift(pick(lane_range(lane, start, span), value), f * span - start)
        start = (ex.down + 1) * sh.pitch
        x_down = x_down + shift(pick(lane_range(lane, start, span), value), f * span - start)
        mask = inside & lane_range(across, y_above, ex.layers)
        y_up = y_up + shift(pick(mask, value), f * ex.layers - y_above - 2)
        mask = inside & lane_range(across, y_below, ex.layers)
        y_down = y_down + shift(pick(mask, value), f * ex.layers - y_below - 2)
    packed = ex.fields * ex.layers
    y_up, y_down = fold(sh, y_up, packed), fold(sh, y_down, packed)
    for ref, message in zip(y_refs, pair(sh.y_links, even_y, y_up, y_down)):
        ref[...] = message
    for i, message in enumerate(pair(sh.x_links, even_x, x_up, x_down)):
        x_refs[i][...] = message
        upward, downward = fold(sh, message, ex.layers, y_above), fold(sh, message, ex.layers, y_below)
        for j, corner in enumerate(pair(sh.y_links, even_y, upward, downward)):
            corner_refs[i * sh.y_links + j][...] = corner


def merge_xy(sh, ex, scratch, rim, guard, y_refs, x_refs):
    lane, _, across = sh.lane_grid(1)
    inside = lane < sh.used
    low_mask = inside & lane_range(across, ex.up, ex.layers)
    high_mask = inside & lane_range(across, sh.y + ex.down, ex.layers)
    span = ex.layers * sh.pitch
    packed = ex.fields * ex.layers
    below_y, above_y = [unfold(sh, value, packed, -2) for value in sides(sh, 1, [ref[...] for ref in y_refs])]
    per_link = 1 + sh.y_links
    sums = []
    for link in range(sh.x_links):
        straight, diagonal = x_refs[link * per_link], x_refs[link * per_link + 1 : (link + 1) * per_link]
        total = straight[...]
        below, above = sides(sh, 1, [ref[...] for ref in diagonal])
        total = total + unfold(sh, below, ex.layers, ex.up)
        sums.append(total + unfold(sh, above, ex.layers, sh.y + ex.down))
    below_x, above_x = sides(sh, 0, sums)
    first = 1 if ex.up == -2 else 0
    last = ex.layers - 1 if ex.down + ex.layers == 2 else ex.layers
    for f in range(ex.fields):
        addend = pick(low_mask, shift(below_y, ex.up + 2 - ex.layers * f))
        addend = addend + pick(high_mask, shift(above_y, sh.y + ex.down + 2 - ex.layers * f))
        start = (ex.up + first + 1) * sh.pitch
        count = (ex.layers - first) * sh.pitch
        moved = shift(below_x, start - f * span - first * sh.pitch)
        addend = addend + pick(lane_range(lane, start, count), moved)
        start = (sh.x + ex.down + 1) * sh.pitch
        moved = shift(above_x, start - f * span)
        addend = addend + pick(lane_range(lane, start, last * sh.pitch), moved)
        scratch[f, guard : guard + sh.rows, :] += addend
        if rim is not None:
            low = pick(lane_range(lane, 0, sh.pitch), shift(below_x, -f * span))
            start = (sh.x + 1) * sh.pitch
            moved = shift(above_x, start - f * span - last * sh.pitch)
            high = pick(lane_range(lane, start, sh.pitch), moved)
            rim[f, guard : guard + sh.rows, :] = low + high


def clear_guards(sh, refs):
    for ref in refs:
        for f in range(ref.shape[0]):
            ref[f, :EDGE, :] = jnp.zeros((EDGE, LANES), f32)
            ref[f, ref.shape[1] - EDGE :, :] = jnp.zeros((EDGE, LANES), f32)


def inner(ref, f):
    return ref[f, EDGE : ref.shape[1] - EDGE, :]


def z_stage(ref, f):
    end = ref.shape[1] - EDGE
    after = ref[f, EDGE + 1 : end + 1, :]
    before = ref[f, EDGE - 1 : end - 1, :]
    return inner(ref, f), before + after, after - before


COLUMNS = [(dx, dy) for dx in (-1, 0, 1) for dy in (-1, 0, 1) if dx or dy]


def column_parts(ref, sign=None):
    a, a_sum, a_dif = z_stage(ref, 0)
    b, b_sum, b_dif = z_stage(ref, 1)
    c, c_sum, c_dif = z_stage(ref, 2)
    mixed_x, mixed_y = MIXED2 * b + b_sum, MIXED2 * a + a_sum
    x_c_dif = c_dif
    if sign is not None:
        mixed_x, mixed_y, x_c_dif, a_dif = sign * mixed_x, sign * mixed_y, sign * c_dif, sign * a_dif
    both_z = ACROSS1 * c + ALONG2 * c_sum
    along_x, across_x = ALONG1 * a + ALONG2 * a_sum, ACROSS1 * a + ACROSS2 * a_sum
    along_y, across_y = ALONG1 * b + ALONG2 * b_sum, ACROSS1 * b + ACROSS2 * b_sum
    tilt_a, tilt_b, tilt_c, tilt_x = MIXED2 * a_dif, MIXED2 * b_dif, MIXED2 * c_dif, MIXED2 * x_c_dif
    same_x, same_y = ALONG2 * a + SAME3 * a_sum, ALONG2 * b + SAME3 * b_sum
    same_z = ACROSS2 * c + SAME3 * c_sum
    plus_x, plus_y, plus_z = same_x + mixed_x, same_y + mixed_y, same_z + a_dif
    minus_x, minus_y, minus_z = same_x - mixed_x, same_y - mixed_y, same_z - a_dif
    return {
        (0, 0): (ACROSS1 * a_sum, ACROSS1 * b_sum, ALONG1 * c_sum),
        (1, 0): (along_x + tilt_x, across_y, both_z + tilt_a),
        (-1, 0): (along_x - tilt_x, across_y, both_z - tilt_a),
        (0, 1): (across_x, along_y + tilt_c, both_z + tilt_b),
        (0, -1): (across_x, along_y - tilt_c, both_z - tilt_b),
        (1, 1): (plus_x + x_c_dif, plus_y + c_dif, plus_z + b_dif),
        (1, -1): (minus_x + x_c_dif, minus_y - c_dif, plus_z - b_dif),
        (-1, 1): (minus_x - x_c_dif, minus_y + c_dif, minus_z + b_dif),
        (-1, -1): (plus_x - x_c_dif, plus_y - c_dif, minus_z - b_dif),
    }


def put_columns(sh, k, rim, columns):
    lane, _, _ = sh.lane_grid(1)
    for i, (dx, dy) in enumerate(COLUMNS):
        value = shift(k, dx * sh.pitch + dy)
        if dx and rim is not None:
            edge = lane < sh.pitch if dx > 0 else lane >= (sh.x + 1) * sh.pitch
            value = jnp.where(edge, shift(rim, dy), value)
        put(columns, i, value)


def own_block(stiff, columns):
    k, k_sum, _ = z_stage(stiff, 0)
    at = {(-dx, -dy): z_stage(columns, i) for i, (dx, dy) in enumerate(COLUMNS)}
    total = lambda j, *places: sum(at[place][j] for place in places)
    in_x, in_y = ((1, 0), (-1, 0)), ((0, 1), (0, -1))
    same, other = ((1, 1), (-1, -1)), ((1, -1), (-1, 1))
    x, x_sum, y, y_sum = total(0, *in_x), total(1, *in_x), total(0, *in_y), total(1, *in_y)
    same_0, same_1, other_0, other_1 = total(0, *same), total(1, *same), total(0, *other), total(1, *other)
    corner, corner_sum = same_0 + other_0, SAME3 * (same_1 + other_1)
    shared = ALONG2 * corner + corner_sum + ACROSS1 * k_sum + TOTAL * k
    turn_x = at[1, 1][2] - at[-1, -1][2]
    turn_y = at[1, -1][2] - at[-1, 1][2]
    return (
        ALONG1 * x + ALONG2 * x_sum + ACROSS1 * y + ACROSS2 * y_sum + shared,
        ALONG1 * y + ALONG2 * y_sum + ACROSS1 * x + ACROSS2 * x_sum + shared,
        ACROSS1 * (x + y) + ALONG2 * (x_sum + y_sum) + ACROSS2 * corner + corner_sum + ALONG1 * k_sum + TOTAL * k,
        MIXED2 * (same_0 - other_0) + (same_1 - other_1),
        MIXED2 * (at[1, 0][2] - at[-1, 0][2]) + (turn_x + turn_y),
        MIXED2 * (at[0, 1][2] - at[0, -1][2]) + (turn_x - turn_y),
    )


def apply_block(d, v):
    return (
        d[0] * v[0] + d[3] * v[1] + d[4] * v[2],
        d[3] * v[0] + d[1] * v[1] + d[5] * v[2],
        d[4] * v[0] + d[5] * v[1] + d[2] * v[2],
    )


def image_of(sh, lane, v, kv, rims, springs_ref, columns):
    k = springs_ref[6]
    last = (sh.x + 1) * sh.pitch
    own = apply_block([springs_ref[f] for f in range(6)], [inner(v, m) for m in range(3)])
    plain, scaled = column_parts(v), column_parts(kv)
    total = [k * plain[0, 0][m] + scaled[0, 0][m] for m in range(3)]
    for dx in (0, -1, 1):
        for m in range(3):
            side = None
            for i, column in enumerate(COLUMNS):
                if column[0] == dx:
                    moved = inner(columns, i) * plain[column][m] + scaled[column][m]
                    moved = shift(moved, -(dx * sh.pitch + column[1]))
                    side = moved if side is None else side + moved
            if dx:
                side = pick(lane < last if dx > 0 else lane >= sh.pitch, side)
            total[m] = total[m] + side
    if rims is not None:
        sign = jnp.where(lane < sh.pitch, -1.0, 1.0)
        plain, scaled = column_parts(rims[0], sign), column_parts(rims[1], sign)
        at_rim = (lane < sh.pitch) | (lane >= last)
        for m in range(3):
            side = None
            for dy in (-1, 0, 1):
                moved = shift(k, dy) * plain[1, dy][m] + scaled[1, dy][m]
                moved = shift(moved, -dy)
                side = moved if side is None else side + moved
            total[m] = total[m] + pick(at_rim, side)
    return [own[m] - total[m] for m in range(3)]


def level(sh):
    return lax.broadcasted_iota(jnp.int32, (sh.rows, LANES), 0) - EDGE


def ends_level(sh):
    row = lax.broadcasted_iota(jnp.int32, (4 * EDGE, LANES), 0)
    return jnp.where(row < 2 * EDGE, row, row + sh.rows - 4 * EDGE) - EDGE


def ends(value):
    return jnp.concatenate([value[: 2 * EDGE], value[value.shape[0] - 2 * EDGE :]], axis=0)


def extended_mask(sh, z):
    lane, _, across = sh.lane_grid(1)
    return ((lane < sh.used) & (across >= -1) & (across <= sh.y)) & ((z >= -1) & (z <= sh.z))


def within(sh, axis, place, size):
    index = sh.here(axis)
    low = jnp.where(index > 0, -EDGE, 0)
    high = jnp.where(index < sh.sizes[axis] - 1, size + EDGE, size)
    return (place >= low) & (place < high)


def grid_masks(sh):
    lane, along, across = sh.lane_grid(1)
    lanes = (lane < sh.used) & within(sh, 1, across, sh.y)
    rows = within(sh, 2, level(sh), sh.z)
    return (lanes & within(sh, 0, along, sh.x)) & rows, lanes & rows


def put(ref, f, value):
    ref[f, EDGE : ref.shape[1] - EDGE, :] = value


def local_solve(sh, z, residual_ref, springs_ref, columns, v, kv, factor):
    lane, _, _ = sh.lane_grid(1)
    mask = extended_mask(sh, z)
    for m in range(3):
        factor[m] = pick(mask, relax / jnp.where(mask, springs_ref[m], 1.0))
        value = residual_ref[m] * factor[m]
        put(v[0], m, value)
        put(kv[0], m, springs_ref[6] * value)
    for sweep in range(SWEEPS - 1):
        old, new = sweep % 2, (sweep + 1) % 2
        image = image_of(sh, lane, v[old], kv[old], None, springs_ref, columns)
        for m in range(3):
            value = inner(v[old], m) + factor[m] * (residual_ref[m] - image[m])
            put(v[new], m, value)
            put(kv[new], m, springs_ref[6] * value)
    return (SWEEPS - 1) % 2


def own_level(sh):
    return lax.broadcasted_iota(jnp.int32, (sh.z, LANES), 0)


def coords(sh, z):
    _, along, across = sh.lane_grid(z.shape[0])
    along = jnp.where(along < 0, along + sh.x, jnp.where(along < sh.x, along, along - sh.x))
    across = jnp.where(across < 0, across + sh.y, jnp.where(across < sh.y, across, across - sh.y))
    place = lambda index, size: (2 * index + 1).astype(f32) / size - 1.0
    return place(along, sh.x), place(across, sh.y), place(z, sh.z)


def cell_coords(sh):
    cell = lax.broadcasted_iota(jnp.int32, (sh.cells, sh.z), 0)
    z = lax.broadcasted_iota(jnp.int32, (sh.cells, sh.z), 1)
    x = cell // sh.y
    place = lambda index, size: (2 * index + 1).astype(f32) / size - 1.0
    return place(x, sh.x), place(cell - x * sh.y, sh.y), place(z, sh.z)


def cross(a, b):
    return (a[1] * b[2] - a[2] * b[1], a[2] * b[0] - a[0] * b[2], a[0] * b[1] - a[1] * b[0])


def fold_rows(value):
    total = value[0:8]
    for i in range(8, value.shape[0], 8):
        total = total + value[i : i + 8]
    return jnp.sum(total, axis=0, keepdims=True)


def lane_sums(rows_ref):
    ones = jnp.ones((8, LANES), f32)
    return lax.dot_general(
        ones, rows_ref[...], (((1,), (1,)), ((), ())), precision=highest, preferred_element_type=f32
    )


def coarse_sums(nodes, field, places, count, sums):
    moments = tuple(field) + cross(places, field)
    for node in range(count):
        mask = nodes == node
        for m in range(6):
            sums[node * 6 + m : node * 6 + m + 1, :] = fold_rows(pick(mask, moments[m]))


def sums_line(sh, sums, unknowns):
    flat = (sh.here(0) * sh.sizes[1] + sh.here(1)) * sh.sizes[2] + sh.here(2)
    return pltpu.roll(lane_sums(sums), lax.rem(flat * unknowns, LANES), 1)[0:1]


def coarse_solution(received, inverse_ref, values):
    unknowns, total = inverse_ref.shape
    row = lax.broadcasted_iota(jnp.int32, received.shape, 0)
    part = jnp.zeros((unknowns, LANES), f32)
    for i in range(0, total, LANES):
        owner = (i + lax.broadcasted_iota(jnp.int32, (1, LANES), 1)) // unknowns
        vector = jnp.sum(pick(row == owner, received), axis=0, keepdims=True)
        part = part + inverse_ref[:, i : i + LANES] * vector
    values[0:unknowns, :] = jnp.dot(
        part, jnp.ones((LANES, LANES), f32), precision=highest, preferred_element_type=f32
    )


def coarse_shares(sums, inverse_ref, shares):
    unknowns, total = inverse_ref.shape
    column = jnp.dot(sums[...], jnp.ones((LANES, LANES), f32), precision=highest, preferred_element_type=f32)
    for i in range(0, total, LANES):
        share = inverse_ref[:, i : i + LANES] * column[0:unknowns]
        shares[i // LANES : i // LANES + 1, :] = jnp.sum(share, axis=0, keepdims=True)


def coarse_table(sh, shares_ref, unknowns, flat, table):
    rows = shares_ref.shape[0] // sh.devices
    lane = lax.broadcasted_iota(jnp.int32, (1, LANES), 1)
    for i in range(rows):
        flat[i : i + 1, :] = jnp.sum(shares_ref[pl.ds(i, sh.devices, stride=rows), :], axis=0, keepdims=True)
    for device in range(sh.devices):
        row, place = divmod(device * unknowns, LANES)
        part = shift(flat[row : row + 1, :], -place)
        if place + unknowns > LANES:
            part = jnp.where(lane < LANES - place, part, shift(flat[row + 1 : row + 2, :], -place))
        table[device : device + 1, :] = pick(lane < unknowns, part)


def region_values(sh, table, dz):
    lane, along, across = sh.lane_grid(1)
    x = sh.here(0) + jnp.where(along < 0, -1, jnp.where(along < sh.x, 0, 1))
    y = sh.here(1) + jnp.where(across < 0, -1, jnp.where(across < sh.y, 0, 1))
    z = sh.here(2) + dz
    exists = (lane < sh.used) & (x >= 0) & (x < sh.sizes[0]) & (y >= 0) & (y < sh.sizes[1])
    exists = exists & (z >= 0) & (z < sh.sizes[2])
    device = jnp.where(exists, (x * sh.sizes[1] + y) * sh.sizes[2] + z, -1)
    owner = lax.broadcasted_iota(jnp.int32, (sh.devices, LANES), 0) == device
    return lax.dot_general(
        table[0 : sh.devices, :], owner.astype(f32), (((0,), (0,)), ((), ())), precision=highest, preferred_element_type=f32
    )


def coarse_cells(nodes, places, values, count):
    cells = []
    for m in range(6):
        cell = jnp.zeros(nodes.shape, f32)
        for node in range(count):
            cell = jnp.where(nodes == float(node), values[node * 6 + m : node * 6 + m + 1, :], cell)
        cells.append(cell)
    turned = cross(cells[3:], places)
    return [cells[m] + turned[m] for m in range(3)]


def selection(sh):
    lane, along, across = sh.lane_grid(sh.cells)
    inside = (along >= 0) & (along < sh.x) & (across >= 0) & (across < sh.y)
    row = lax.broadcasted_iota(jnp.int32, (sh.cells, LANES), 0)
    return (inside & (row == along * sh.y + across)).astype(f32)


def to_lanes(value, select, precision=highest):
    return lax.dot_general(
        value, select, (((0,), (0,)), ((), ())), precision=precision, preferred_element_type=f32
    )


def to_cells(value, select):
    return lax.dot_general(
        select, value, (((1,), (1,)), ((), ())), precision=highest, preferred_element_type=f32
    )


def send_lines(sh, lines, slots_ref):
    here = [sh.here(axis) for axis in range(3)]
    corner = [lines[8 * i : 8 * i + 8, :] for i in range(4)]
    top, bottom = lines[32:40, :], lines[40:48, :]
    for x in range(sh.sizes[0]):
        low_high = [jnp.where(x > here[0], corner[2 + high], corner[high]) for high in range(2)]
        for y in range(sh.sizes[1]):
            column = jnp.where(y > here[1], low_high[1], low_high[0])
            for z in range(sh.sizes[2]):
                slot = jnp.where(z == here[2] + 1, top, jnp.where(z == here[2] - 1, bottom, column))
                place = 8 * ((x * sh.sizes[1] + y) * sh.sizes[2] + z)
                slots_ref[place : place + 8, :] = slot


def slot_from(sh, received_ref, step):
    place, exists = 0, None
    for axis in range(3):
        index = sh.here(axis) + step[axis]
        inside = (index >= 0) & (index < sh.sizes[axis])
        exists = inside if exists is None else exists & inside
        place = place * sh.sizes[axis] + jnp.clip(index, 0, sh.sizes[axis] - 1)
    return scale(exists, received_ref[pl.ds(pl.multiple_of(place * 8, 8), 8), :])


def repeat_twice(count):
    row = lax.broadcasted_iota(jnp.int32, (2 * count, count), 0)
    column = lax.broadcasted_iota(jnp.int32, (2 * count, count), 1)
    return ((row >= 2 * column) & (row < 2 * column + 2)).astype(f32)


def ring(size_x, size_y, rows):
    row = lax.broadcasted_iota(jnp.int32, (rows, LANES), 0)
    sides_x, both = 2 * size_y, 2 * size_y + 2 * size_x
    corner = row - both
    x = jnp.where(row < size_y, -1, size_x)
    x = jnp.where(row < sides_x, x, jnp.where(row < sides_x + size_x, row - sides_x, row - sides_x - size_x))
    x = jnp.where(row < both, x, jnp.where(corner < 2, -1, size_x))
    y = jnp.where(row < size_y, row, row - size_y)
    y = jnp.where(row < sides_x, y, jnp.where(row < sides_x + size_x, -1, size_y))
    y = jnp.where(row < both, y, jnp.where((corner == 0) | (corner == 2), -1, size_y))
    return x, y, (row < sides_x) | (row >= both), row < both + 4


def face_shape(sh, label_x, label_y):
    rows = max(4 * sh.x + label_x, 4 * sh.y + label_y)
    return (-(-rows // 8) * 8, LANES)


def pack_faces(sh, natural_ref, stiff, label_x, label_y, x_refs, y_refs):
    even_x, even_y = sh.here(0) % 2 == 0, sh.here(1) % 2 == 0

    def face(at, count, stride, label_at, label_count, label_stride):
        rows = [natural_ref[m, pl.ds(at, count, stride=stride), :] for m in range(4)]
        return rows, stiff[pl.ds(label_at, label_count, stride=label_stride), :]

    above = face(sh.cells - sh.y, sh.y, 1, (label_x - 1) * label_y, label_y, 1)
    below = face(0, sh.y, 1, 0, label_y, 1)
    for refs, links, even, above, below in (
        (x_refs, sh.x_links, even_x, above, below),
        (
            y_refs,
            sh.y_links,
            even_y,
            face(sh.y - 1, sh.x, sh.y, label_y - 1, label_x, label_y),
            face(0, sh.x, sh.y, 0, label_x, label_y),
        ),
    ):
        for i, ref in enumerate(refs):
            ref[...] = jnp.zeros(ref.shape, f32)
            count = above[0][0].shape[0]
            for m in range(4):
                ref[m * count : (m + 1) * count, :] = pair(links, even, above[0][m], below[0][m])[i]
            labels, length = above[1].shape
            ref[4 * count : 4 * count + labels, 0:length] = pair(links, even, above[1], below[1])[i]


def merge_start(sh, refs, x_refs, y_refs, received_ref, sizes, cells, labels):
    residual, nodes, stiff, stiff_rim = refs
    label_x, label_y, label_z = sizes
    lane, along, across = sh.lane_grid(1)
    inside = lane < sh.used
    last = (sh.x + 1) * sh.pitch
    x_mask = {-1: lane < sh.pitch, 0: (lane >= sh.pitch) & (lane < last), 1: (lane >= last) & inside}
    y_mask = {-1: across < 0, 0: (across >= 0) & (across < sh.y), 1: across >= sh.y}
    cells[...] = jnp.zeros(cells.shape, f32)
    labels[...] = jnp.zeros(labels.shape, f32)
    count, label_count = cells.shape[1], labels.shape[0]
    at = label_at = 0
    for axis, face_refs, size, label_size in ((0, x_refs, sh.y, label_y), (1, y_refs, sh.x, label_x)):
        for message in sides(sh, axis, [ref[...] for ref in face_refs]):
            for m in range(4):
                cells[m, at : at + size, :] = message[m * size : (m + 1) * size]
            labels[label_at : label_at + label_size, :] = message[4 * size : 4 * size + label_size, 0:label_z]
            at, label_at = at + size, label_at + label_size
    for dx, dy in ((-1, -1), (-1, 1), (1, -1), (1, 1)):
        slot = slot_from(sh, received_ref, (dx, dy, 0))
        for m, row in enumerate((0, 1, 2, 5)):
            cells[m, at : at + 1, :] = slot[row : row + 1]
        labels[label_at : label_at + 1, :] = slot[3:4, 0:label_z]
        at, label_at = at + 1, label_at + 1
    x, y, _, valid = ring(sh.x, sh.y, count)
    place = (valid & inside & (along == x) & (across == y)).astype(f32)
    own = slice(EDGE, EDGE + sh.z)
    tall_own = slice(2 * EDGE, 2 * EDGE + sh.z)
    for m in range(3):
        residual[m, own, :] += to_lanes(cells[m], place)
    nodes[own, :] += to_lanes(cells[3], place, small)
    by_z = lax.dot_general(
        repeat_twice(label_z), labels[...], (((1,), (1,)), ((), ())), precision=highest, preferred_element_type=f32
    )
    x, y, at_x, valid = ring(label_x, label_y, label_count)
    match = valid & inside & ((along >> 1) == x) & ((across >> 1) == y)
    columns = jnp.dot(by_z, (match & at_x).astype(f32), precision=highest, preferred_element_type=f32)
    stiff_rim[0, tall_own, :] = columns
    columns = columns + jnp.dot(by_z, (match & ~at_x).astype(f32), precision=highest, preferred_element_type=f32)
    stiff[0, tall_own, :] += columns
    for dz in (-1, 1):
        main = edge = jnp.zeros((8, LANES), f32)
        for dx in (-1, 0, 1):
            for dy in (-1, 0, 1):
                slot = slot_from(sh, received_ref, (dx, dy, dz))
                mask = x_mask[dx] & y_mask[dy]
                main = main + pick(mask, shift(slot, dx * sh.x * sh.pitch + dy * sh.y))
                if dx:
                    edge = edge + pick(mask, shift(slot, dx * (sh.x - 1) * sh.pitch + dy * sh.y))
        near = EDGE + sh.z if dz > 0 else EDGE - 1
        for m in range(3):
            residual[m, near : near + 1, :] = main[m : m + 1]
        nodes[near : near + 1, :] = main[5:6]
        for row in (EDGE + near, EDGE + near + dz):
            stiff[0, row : row + 1, :] = main[3:4]
            stiff_rim[0, row : row + 1, :] = edge[3:4]


def call(kernel, name, outs, ins, scratch=(), remote_ins=False, remote_outs=()):
    space = pltpu.HBM if remote_ins else pltpu.VMEM
    return pl.pallas_call(
        kernel,
        out_shape=[jax.ShapeDtypeStruct(shape, f32) for shape in outs],
        in_specs=[pl.BlockSpec(memory_space=space) for _ in ins],
        out_specs=[
            pl.BlockSpec(memory_space=pltpu.HBM if i in remote_outs else pltpu.VMEM) for i in range(len(outs))
        ],
        scratch_shapes=[pltpu.VMEM(shape, f32) if isinstance(shape, tuple) else shape for shape in scratch],
        compiler_params=pltpu.CompilerParams(vmem_limit_bytes=(56 if remote_ins else 48) * 1024 * 1024),
        name=name,
    )(*ins)


def permutation(sizes, moves):
    def partner(axis, link, index):
        size = sizes[axis]
        other = index ^ 1 if link == 0 else index + (1 if index % 2 else -1)
        if 0 <= other < size:
            return other
        return size - 1 - index if axis == 2 and size % 2 == 0 else index

    pairs = []
    for x in range(sizes[0]):
        for y in range(sizes[1]):
            for z in range(sizes[2]):
                place = [x, y, z]
                goal = [partner(a, moves[a], place[a]) if a in moves else place[a] for a in range(3)]
                if any(goal[a] == place[a] for a in moves) and sizes[2] % 2 == 0:
                    goal = [x, y, partner(2, 0, z)]
                flat = [(p[0] * sizes[1] + p[1]) * sizes[2] + p[2] for p in (place, goal)]
                pairs.append(tuple(flat))
    return pairs


def send(sh, value, moves):
    return lax.ppermute(value, AXES, permutation(sh.sizes, moves))


def send_z(sh, messages):
    return [send(sh, message, {2: link}) for link, message in enumerate(messages)]


def send_faces(sh, x_messages, y_messages):
    from_x = [send(sh, message, {0: link}) for link, message in enumerate(x_messages)]
    from_y = [send(sh, message, {1: link}) for link, message in enumerate(y_messages)]
    return from_y, from_x


def to_all(slots):
    return lax.all_to_all(slots, AXES, 0, 0, tiled=True)


def exchange(sh, ex, name, field, z_messages):
    from_z = send_z(sh, z_messages)

    corners = sh.x_links * sh.y_links

    def packer(*refs):
        take = Taker(refs)
        field_ref, z_refs = take.one(), take(sh.z_links)
        x_refs, y_refs, corner_refs, scratch = take(sh.x_links), take(sh.y_links), take(corners), take.one()
        merge_z(sh, ex, field_ref, z_refs, scratch, 0)
        pack_xy(sh, ex, scratch, x_refs, y_refs, corner_refs)

    plane = (sh.rows, LANES)
    messages = call(
        packer,
        name,
        [plane] * sh.x_links
        + [folded_shape(sh, ex.fields * ex.layers)] * sh.y_links
        + [folded_shape(sh, ex.layers)] * corners,
        [field] + from_z,
        [(ex.fields,) + plane],
    )
    take = Taker(messages)
    x_messages, y_messages = take(sh.x_links), take(sh.y_links)
    from_y, straight = send_faces(sh, x_messages, y_messages)
    from_x = []
    for link in range(sh.x_links):
        from_x.append(straight[link])
        from_x.extend(send(sh, take.one(), {0: link, 1: other}) for other in range(sh.y_links))
    return from_z, from_y, from_x


class Taker:
    def __init__(self, refs):
        self.refs, self.at = refs, 0

    def __call__(self, count):
        self.at += count
        return self.refs[self.at - count : self.at]

    def one(self):
        return self(1)[0]


def merge_all(sh, ex, take, scratch, rim, guard):
    field = take.one()
    from_z, from_y = take(sh.z_links), take(sh.y_links)
    from_x = take(sh.x_links * (1 + sh.y_links))
    merge_z(sh, ex, field, from_z, scratch, guard)
    merge_xy(sh, ex, scratch, rim, guard, from_y, from_x)


def body(right_side, phase_labels, phase_moduli, coarse_nodes, coarse_inverse):
    sizes = tuple(lax.axis_size(axis) for axis in AXES)
    _, size_x, size_y, size_z = right_side.shape
    sh = Shape(size_x, size_y, size_z, phase_moduli.shape[0], sizes)
    unknowns = coarse_inverse.shape[0]
    node_count = unknowns // 6
    sum_rows = -(-unknowns // 8) * 8 + 8
    share_rows = coarse_inverse.shape[1] // LANES
    own = slice(EDGE, EDGE + sh.z)
    plane = (sh.rows, LANES)
    fields = (3,) + plane
    tall = (3, sh.tall, LANES)
    slots = (sh.devices, LANES)
    z_shape = lambda ex: [(8 * ex.fields, LANES)] * sh.z_links
    natural = right_side.reshape(3, sh.cells, sh.z)
    nodes_natural = coarse_nodes.reshape(sh.cells, sh.z)
    label_x, label_y, label_z = phase_labels.shape

    def block_places():
        lane, along, across = sh.lane_grid(label_x * label_y)
        inside = (along >= 0) & (along < sh.x) & (across >= 0) & (across < sh.y)
        block = lax.broadcasted_iota(jnp.int32, along.shape, 0)
        return (inside & (block == (along >> 1) * label_y + (across >> 1))).astype(f32)

    def end_layers(values, places):
        length = values.shape[1]
        row = lax.broadcasted_iota(jnp.int32, (8, length), 0)
        at = lax.broadcasted_iota(jnp.int32, (8, length), 1)
        ends = ((row == 0) & (at == length - 1)) | ((row == 1) & (at == 0))
        return jnp.dot(to_cells(values, ends.astype(f32)), places, precision=highest, preferred_element_type=f32)

    def begin(natural_in, labels_in, moduli_in, nodes_in, stiff, slots_ref, *rest):
        x_refs, y_refs = rest[: sh.x_links], rest[sh.x_links : sh.x_links + sh.y_links]
        natural_ref, labels_ref, moduli_ref, nodes_ref, sems, sums, lines = rest[sh.x_links + sh.y_links :]
        pairs = ((natural_in, natural_ref.at[0:3, 0 : sh.cells, :]), (labels_in, labels_ref.at[0:label_x]), (moduli_in, moduli_ref), (nodes_in, nodes_ref))
        copies = [pltpu.make_async_copy(a, b, sems.at[i]) for i, (a, b) in enumerate(pairs)]
        for copy in copies:
            copy.start()
        sums[...] = jnp.zeros(sums.shape, f32)
        lines[...] = jnp.zeros(lines.shape, f32)
        for copy in copies:
            copy.wait()
        for i in range(label_x):
            labels = labels_ref[i]
            moduli = jnp.zeros(labels.shape, f32)
            for phase in range(sh.phases):
                moduli = jnp.where(labels == phase, moduli_ref[phase], moduli)
            stiff[i * label_y : (i + 1) * label_y, :] = moduli * (1.0 / SCALE)
        natural_ref[3, 0 : sh.cells, :] = nodes_ref[...].astype(f32) + 1.0
        cells = [natural_ref[m, 0 : sh.cells, :] for m in range(4)]
        coarse_sums(nodes_ref[...], cells[:3], cell_coords(sh), node_count, sums)
        line = sums_line(sh, sums, unknowns)
        for i, (cell, block) in enumerate(
            (
                (0, 0),
                (sh.y - 1, label_y - 1),
                ((sh.x - 1) * sh.y, (label_x - 1) * label_y),
                (sh.cells - 1, label_x * label_y - 1),
            )
        ):
            for m in range(3):
                lines[8 * i + m : 8 * i + m + 1, :] = natural_ref[m, cell : cell + 1, :]
            lines[8 * i + 3 : 8 * i + 4, 0:label_z] = stiff[block : block + 1, :]
            lines[8 * i + 5 : 8 * i + 6, :] = natural_ref[3, cell : cell + 1, :]
        select = selection(sh)
        layers = [end_layers(cells[m], select) for m in range(4)] + [end_layers(stiff[0 : label_x * label_y, :], block_places())]
        for i in range(2):
            for layer, row in zip(layers, (0, 1, 2, 5, 3)):
                lines[8 * (4 + i) + row : 8 * (4 + i) + row + 1, :] = layer[i : i + 1]
        for i in range(6):
            lines[8 * i + 4 : 8 * i + 5, :] = line
        send_lines(sh, lines, slots_ref)
        pack_faces(sh, natural_ref, stiff, label_x, label_y, x_refs, y_refs)

    block_rows = (8 * -(-(label_x + 8) * label_y // 8), label_z)
    stiff_blocks, lines, *messages = call(
        begin,
        "begin",
        [block_rows, (8 * sh.devices, LANES)]
        + [face_shape(sh, label_x, label_y)] * (sh.x_links + sh.y_links),
        [natural, phase_labels, phase_moduli, nodes_natural],
        [
            (4, sh.cells + 8, sh.z),
            pltpu.VMEM((label_x + 2, label_y, label_z), jnp.int32),
            pltpu.SMEM(phase_moduli.shape, f32),
            pltpu.VMEM(nodes_natural.shape, jnp.int32),
            pltpu.SemaphoreType.DMA((4,)),
            (LANES, LANES),
            (56, LANES),
        ],
        remote_ins=True,
    )

    def spread(natural_ref, nodes_ref, stiff, inverse_in, field_ref, lanes_ref, inverse_ref):
        inverse_ref[...] = inverse_in[...]
        select = selection(sh)
        field_ref[...] = jnp.zeros(field_ref.shape, f32)
        for m in range(3):
            field_ref[m, own, :] = to_lanes(natural_ref[m], select)
        by_z = lax.dot_general(
            repeat_twice(label_z),
            stiff[0 : label_x * label_y, :],
            (((1,), (1,)), ((), ())),
            precision=highest,
            preferred_element_type=f32,
        )
        field_ref[3, own, :] = jnp.dot(by_z, block_places(), precision=highest, preferred_element_type=f32)
        lanes_ref[...] = to_lanes(nodes_ref[...].astype(f32) + 1.0, select, small) - 1.0

    start_field, nodes, inverse = call(
        spread,
        "spread",
        [(4,) + plane, (sh.z, LANES), coarse_inverse.shape],
        [natural, nodes_natural, stiff_blocks, coarse_inverse],
    )
    from_y, from_x = send_faces(sh, messages[: sh.x_links], messages[sh.x_links :])
    lines = to_all(lines)

    short = (3, 6 * EDGE, LANES)
    short_fields = (3, 4 * EDGE, LANES)
    tall_columns = (len(COLUMNS), sh.tall, LANES)
    solve_scratch = [tall] * 4 + [fields, tall_columns]
    short_scratch = [short] * 4 + [short_fields, (len(COLUMNS), 6 * EDGE, LANES)]

    def end_rows(ref):
        def rows(f, start, count):
            place = start + EDGE if start < 2 * EDGE else start - sh.rows + 5 * EDGE
            return ref[f, place : place + count, :]

        return rows

    def first_ends(*refs):
        take = Taker(refs)
        field_ref = take.one()
        y_refs, x_refs = take(sh.y_links), take(sh.x_links)
        nodes_ref, lines_ref, inverse_ref = take(3)
        residual, wide_nodes, stiffness_ref, values = take(4)
        z_refs = take(sh.z_links)
        stiff, stiff_rim, cells, labels, short_stiff, some_residual, springs = take(7)
        v0, v1, kv0, kv1, factor, columns = take(6)
        clear_guards(sh, (stiff, stiff_rim, short_stiff, v0, v1, kv0, kv1, columns))
        residual[...] = field_ref[0:3]
        put(stiff, 0, field_ref[3])
        put(stiff_rim, 0, jnp.zeros(plane, f32))
        sizes = phase_labels.shape
        wide_nodes[...] = jnp.zeros(plane, f32)
        wide_nodes[own, :] = nodes_ref[...] + 1.0
        merge_start(sh, (residual, wide_nodes, stiff, stiff_rim), x_refs, y_refs, lines_ref, sizes, cells, labels)
        wide_nodes[...] = wide_nodes[...] - 1.0
        stiffness_ref[0] = inner(stiff, 0)
        stiffness_ref[1] = inner(stiff_rim, 0)
        coarse_solution(lines_ref[pl.ds(4, sh.devices, stride=8), :], inverse_ref, values)
        lane, _, _ = sh.lane_grid(1)
        put(short_stiff, 0, ends(stiffness_ref[0]))
        put_columns(sh, ends(stiffness_ref[0]), ends(stiffness_ref[1]), columns)
        for f, entry in enumerate(own_block(short_stiff, columns)):
            springs[f] = entry
        springs[6] = inner(short_stiff, 0)
        for m in range(3):
            some_residual[m] = ends(residual[m])
        index = local_solve(sh, ends_level(sh), some_residual, springs, columns, (v0, v1), (kv0, kv1), factor)
        solution = (v0, v1)[index]
        z = lax.broadcasted_iota(jnp.int32, (2 * EDGE, LANES), 0)
        z = jnp.where(z < EDGE, z, z + sh.z - 2 * EDGE)
        some_nodes = jnp.concatenate([nodes_ref[0:EDGE, :], nodes_ref[sh.z - EDGE : sh.z, :]], axis=0)
        added = coarse_cells(some_nodes, coords(sh, z), values, node_count)
        for m in range(3):
            solution[m, 2 * EDGE : 4 * EDGE, :] += pick(some_nodes >= 0.0, added[m])
        pack_z(sh, DEEP, end_rows(solution), z_refs)

    residual, wide_nodes, stiffness, values, *z_messages = call(
        first_ends,
        "first_ends",
        [fields, plane, (2,) + plane, (sum_rows, LANES)] + z_shape(DEEP),
        [start_field, *from_y, *from_x, nodes, lines, inverse],
        [(1, sh.tall, LANES)] * 2
        + [
            (4, 8 * -(-(2 * sh.x + 2 * sh.y + 4) // 8) + 8, LANES),
            (8 * -(-(2 * label_x + 2 * label_y + 4) // 8) + 8, label_z),
        ]
        + [(1, 6 * EDGE, LANES)]
        + [short_fields, (7, 4 * EDGE, LANES)]
        + short_scratch,
    )

    def first_solve(residual_ref, stiffness_ref, values, nodes_ref, solution_ref, springs_ref, *rest):
        stiff, v0, v1, kv0, kv1, factor, columns = rest
        clear_guards(sh, (stiff, v0, v1, kv0, kv1, columns))
        put(stiff, 0, stiffness_ref[0])
        put_columns(sh, stiffness_ref[0], stiffness_ref[1], columns)
        springs_ref[6] = stiffness_ref[0]
        springs_ref[7] = stiffness_ref[1]
        lane, _, _ = sh.lane_grid(1)
        for f, entry in enumerate(own_block(stiff, columns)):
            springs_ref[f] = entry
        index = local_solve(sh, level(sh), residual_ref, springs_ref, columns, (v0, v1), (kv0, kv1), factor)
        for m in range(3):
            solution_ref[m] = inner((v0, v1)[index], m)
        added = coarse_cells(nodes_ref[...], coords(sh, own_level(sh)), values, node_count)
        for m in range(3):
            solution_ref[m, own, :] += pick(nodes_ref[...] >= 0.0, added[m])

    solved, springs = call(
        first_solve,
        "first_solve",
        [fields, (8,) + plane],
        [residual, stiffness, values, nodes],
        [(1, sh.tall, LANES)] + solve_scratch,
    )
    from_z, from_y, from_x = exchange(sh, DEEP, "deep", solved, z_messages)

    def first_image(*refs):
        take = Taker(refs)
        merging = take(1 + sh.z_links + sh.y_links + sh.x_links * (1 + sh.y_links))
        nodes_ref, springs_ref, inverse_ref = take(3)
        search_ref, image_ref, slots_out = take(3)
        z_refs = take(sh.z_links)
        v, rim, kv, k_rim, sums, shares, slots_ref, sem = take(8)
        some_residual, some_springs, v0, v1, kv0, kv1, factor, some_columns, columns = take(9)
        clear_guards(sh, (v0, v1, kv0, kv1))
        clear_guards(sh, (v, rim, kv, k_rim))
        merge_all(sh, DEEP, Taker(merging), v, rim, EDGE)
        lane, _, _ = sh.lane_grid(1)

        in_grid, in_rim = grid_masks(sh)
        for m in range(3):
            value = pick(in_grid, inner(v, m))
            put(v, m, value)
            search_ref[m] = value
            put(kv, m, springs_ref[6] * value)
            value = pick(in_rim, inner(rim, m))
            put(rim, m, value)
            put(k_rim, m, springs_ref[7] * value)
        put_columns(sh, springs_ref[6], None, columns)
        image = image_of(sh, lane, v, kv, (rim, k_rim), springs_ref, columns)
        keep = in_grid & extended_mask(sh, level(sh))
        for m in range(3):
            image_ref[m] = pick(keep, image[m])
        sums[...] = jnp.zeros(sums.shape, f32)
        field = [image_ref[m, own, :] for m in range(3)]
        coarse_sums(nodes_ref[...], field, coords(sh, own_level(sh)), node_count, sums)
        coarse_shares(sums, inverse_ref, shares)
        for device in range(sh.devices):
            slots_ref[device * share_rows : (device + 1) * share_rows, :] = shares[0:share_rows, :]
        copy = pltpu.make_async_copy(slots_ref.at[0 : slots_out.shape[0], :], slots_out, sem)
        copy.start()
        for m in range(3):
            some_residual[m] = ends(image_ref[m])
        for f in range(7):
            some_springs[f] = ends(springs_ref[f])
        put_columns(sh, some_springs[6], None, some_columns)
        index = local_solve(sh, ends_level(sh), some_residual, some_springs, some_columns, (v0, v1), (kv0, kv1), factor)
        pack_z(sh, NEAR, end_rows((v0, v1)[index]), z_refs)
        copy.wait()

    all_slots = (sh.devices * share_rows, LANES)
    search, image, shares, *z_messages = call(
        first_image,
        "first_image",
        [fields, fields, all_slots] + z_shape(NEAR),
        [solved, *from_z, *from_y, *from_x, nodes, springs, inverse],
        [tall] * 4
        + [(LANES, LANES), (8 * -(-share_rows // 8) + 8, LANES)]
        + [(8 * -(-all_slots[0] // 8) + 8, LANES), pltpu.SemaphoreType.DMA]
        + [short_fields, (7, 4 * EDGE, LANES)]
        + short_scratch
        + [tall_columns],
        remote_outs=(2,),
    )
    shares = to_all(shares.reshape(sh.devices, 1, share_rows * LANES)).reshape(shares.shape)

    def second_solve(image_ref, springs_ref, local_ref, v0, v1, kv0, kv1, factor, columns):
        clear_guards(sh, (v0, v1, kv0, kv1))
        put_columns(sh, springs_ref[6], None, columns)
        index = local_solve(sh, level(sh), image_ref, springs_ref, columns, (v0, v1), (kv0, kv1), factor)
        for m in range(3):
            local_ref[m] = inner((v0, v1)[index], m)

    (solved,) = call(second_solve, "second_solve", [fields], [image, springs], solve_scratch)
    from_z, from_y, from_x = exchange(sh, NEAR, "near", solved, z_messages)

    def between(shares_ref, wide_nodes, nodes_ref, start_ref, search_ref, first_ref, coarse_ref, sums, *scratch):
        flat, table, values = scratch
        coarse_ref[...] = jnp.zeros(coarse_ref.shape, f32)
        coarse_table(sh, shares_ref, unknowns, flat, table)
        last = lax.broadcasted_iota(jnp.int32, (1, LANES), 0) + sh.z - 1
        for dz, first, z in ((0, EDGE, own_level(sh)), (-1, EDGE - 1, last), (1, EDGE + sh.z, last - sh.z + 1)):
            values[...] = region_values(sh, table, dz)
            rows = slice(first, first + z.shape[0])
            added = coarse_cells(wide_nodes[rows, :], coords(sh, z), values, node_count)
            for m in range(3):
                coarse_ref[m, rows, :] = added[m]
        valid = nodes_ref[...] >= 0.0
        row = lax.broadcasted_iota(jnp.int32, sums.shape, 0)
        total = jnp.zeros(sums.shape, f32)
        for i, other in enumerate((start_ref, first_ref)):
            product = sum(search_ref[m, own, :] * other[m, own, :] for m in range(3))
            total = jnp.where(row == i, fold_rows(pick(valid, product)), total)
        sums[...] = total

    coarse_field, sums = call(
        between,
        "between",
        [fields, (8, LANES)],
        [shares, wide_nodes, nodes, start_field, search, image],
        [(8 * -(-share_rows // 8) + 8, LANES), (8 * -(-sh.devices // 8) + 8, LANES), (LANES, LANES)],
    )

    def second_image(*refs):
        take = Taker(refs)
        merging = take(1 + sh.z_links + sh.y_links + sh.x_links * (1 + sh.y_links))
        nodes_ref, springs_ref, first_ref, coarse_ref, early_ref = take(5)
        second_ref, image_ref, slots_ref = take(3)
        v, kv, sums, columns = take(4)
        clear_guards(sh, (v, kv))
        put_columns(sh, springs_ref[6], None, columns)
        merge_all(sh, NEAR, Taker(merging), v, None, EDGE)
        lane, _, _ = sh.lane_grid(1)
        in_grid, _ = grid_masks(sh)
        for m in range(3):
            value = pick(in_grid, inner(v, m)) + coarse_ref[m]
            put(v, m, value)
            second_ref[m] = value
            put(kv, m, springs_ref[6] * value)
        image = image_of(sh, lane, v, kv, None, springs_ref, columns)
        for m in range(3):
            image_ref[m] = image[m]
        valid = nodes_ref[...] >= 0.0
        sums[...] = jnp.zeros(sums.shape, f32)
        sums[0:8, :] = early_ref[...]
        for i, other in ((2, first_ref), (3, image_ref)):
            product = sum(second_ref[m, own, :] * other[m, own, :] for m in range(3))
            sums[i : i + 1, :] = fold_rows(pick(valid, product))
        slots_ref[...] = jnp.broadcast_to(lane_sums(sums)[0:1], slots_ref.shape)

    second, second_image_field, sums = call(
        second_image,
        "second_image",
        [fields, fields, slots],
        [solved, *from_z, *from_y, *from_x, nodes, springs, image, coarse_field, sums],
        [tall] * 2 + [(LANES, LANES), tall_columns],
    )
    totals = to_all(sums)

    def turn(search_ref, first_ref, second_ref, image_ref, out_ref):
        select = selection(sh)
        for i, ref in enumerate((search_ref, first_ref, second_ref, image_ref)):
            for m in range(3):
                out_ref[i, m] = to_cells(ref[m, own, :], select)

    (turned,) = call(turn, "turn", [(4,) + natural.shape], [search, image, second, second_image_field])

    def finish(totals_ref, natural_ref, turned_ref, field_ref, residual_ref):
        total = jnp.sum(totals_ref[...], axis=0, keepdims=True)
        rz, zw, wq, qv = [total[:, i : i + 1] for i in range(4)]
        step0 = rz / zw
        rho = step0 * step0 * wq - step0 * zw
        grow = 1.0 + rho / rz
        curvature = grow * grow * zw - 2.0 * grow * step0 * wq + step0 * step0 * qv
        step1 = rho / curvature
        first = step0 + step1 * grow
        second = step0 * step1
        for m in range(3):
            field_ref[m] = first * turned_ref[0, m] - second * turned_ref[2, m]
            residual_ref[m] = natural_ref[m] - (first * turned_ref[1, m] - second * turned_ref[3, m])

    solution_field, residual = call(
        finish, "finish", [natural.shape, natural.shape], [totals, natural, turned]
    )
    return solution_field.reshape(right_side.shape), residual.reshape(right_side.shape)


def solution(mesh):
    in_specs = (
        P(None, "gx", "gy", "gz"),
        P("gx", "gy", "gz"),
        P(),
        P("gx", "gy", "gz"),
        P(("gx", "gy", "gz"), None),
    )
    out_specs = (P(None, "gx", "gy", "gz"), P(None, "gx", "gy", "gz"))
    return jax.shard_map(body, mesh=mesh, in_specs=in_specs, out_specs=out_specs, check_vma=False)
```

```python
import jax
import jax.numpy as jnp
from jax import lax
from jax.experimental import pallas as pl
from jax.experimental.pallas import tpu as pltpu
from jax.sharding import PartitionSpec as P

AXES = ("gx", "gy", "gz")
SWEEPS = 4
relax = 0.6
highest = lax.Precision.HIGHEST
small = lax.Precision.DEFAULT
f32 = jnp.float32
LANES = 128
EDGE = 8

SCALE = 36.0
ALONG1, ACROSS1 = 27.0, 18.0
ALONG2, ACROSS2, MIXED2 = 11.25, 9.0, 2.25
SAME3 = 7.0
TOTAL = 2 * ALONG1 + 4 * ACROSS1 + 8 * ALONG2 + 4 * ACROSS2 + 8 * SAME3


class Exchange:
    def __init__(self, fields, layers, up, down):
        self.fields, self.layers, self.up, self.down = fields, layers, up, down


DEEP = Exchange(3, 3, -2, -1)
NEAR = Exchange(3, 2, -1, -1)


class Shape:
    def __init__(self, size_x, size_y, size_z, phases, mesh_sizes):
        self.x, self.y, self.z = size_x, size_y, size_z
        self.pitch = size_y + 4
        self.used = (size_x + 2) * self.pitch
        assert self.used <= LANES
        self.rows = size_z + 2 * EDGE
        self.tall = self.rows + 2 * EDGE
        self.phases = phases
        self.sizes = mesh_sizes
        self.devices = mesh_sizes[0] * mesh_sizes[1] * mesh_sizes[2]
        self.cells = size_x * size_y
        self.links = [1 if n <= 2 else 2 for n in mesh_sizes]
        self.x_links, self.y_links, self.z_links = self.links

    def lane_grid(self, rows):
        lane = lax.broadcasted_iota(jnp.int32, (rows, LANES), 1)
        column = jnp.zeros_like(lane)
        for j in range(1, self.x + 2):
            column = column + (lane >= j * self.pitch).astype(jnp.int32)
        offset = lane - column * self.pitch
        return lane, column - 1, offset - 2

    def here(self, axis):
        return lax.axis_index(AXES[axis])


def shift(value, amount):
    amount = amount % LANES
    return value if amount == 0 else pltpu.roll(value, amount, 1)


def shift_either(flag, value, first, second):
    return pltpu.roll(value, jnp.where(flag, first % LANES, second % LANES), 1)


def pick(mask, value):
    return jnp.where(mask, value, 0.0)


def scale(flag, value):
    return value * flag.astype(f32)


def pair(links, even, upward, downward):
    first = jnp.where(even, upward, downward)
    return (first,) if links == 1 else (first, jnp.where(even, downward, upward))


def sides(sh, axis, received):
    index, size = sh.here(axis), sh.sizes[axis]
    even = index % 2 == 0
    first = received[0]
    second = received[1] if len(received) > 1 else jnp.zeros_like(first)
    below = jnp.where(even, second, first)
    above = jnp.where(even, first, second)
    return scale(index > 0, below), scale(index < size - 1, above)


def lane_range(lane, start, count):
    return (lane >= start) & (lane < start + count)


def pack_z(sh, ex, source, out_refs):
    even = sh.here(2) % 2 == 0
    for ref in out_refs:
        ref[...] = jnp.zeros(ref.shape, f32)
    for f in range(ex.fields):
        upward = source(f, EDGE + sh.z + ex.up, ex.layers)
        downward = source(f, EDGE + ex.down, ex.layers)
        for ref, message in zip(out_refs, pair(sh.z_links, even, upward, downward)):
            ref[8 * f : 8 * f + ex.layers, :] = message


def merge_z(sh, ex, field_ref, received_refs, scratch, guard):
    below, above = sides(sh, 2, [ref[...] for ref in received_refs])
    for f in range(ex.fields):
        scratch[f, guard : guard + sh.rows, :] = field_ref[f]
        low = guard + EDGE + ex.up
        high = guard + EDGE + sh.z + ex.down
        scratch[f, low : low + ex.layers, :] += below[8 * f : 8 * f + ex.layers]
        scratch[f, high : high + ex.layers, :] += above[8 * f : 8 * f + ex.layers]


def fold(sh, value, layers, start=None):
    folds = sh.pitch // layers
    height = -(-sh.rows // (8 * folds)) * 8
    lane, _, across = sh.lane_grid(1)
    total = jnp.zeros((height, LANES), f32)
    for i, first in enumerate(range(0, sh.rows, height)):
        part = value[first : first + height]
        if start is not None:
            part = pick((lane < sh.used) & lane_range(across, start, layers), part)
        part = shift(part, i * layers - (0 if start is None else start + 2))
        if part.shape[0] < height:
            part = jnp.concatenate([part, jnp.zeros((height - part.shape[0], LANES), f32)], axis=0)
        total = total + part
    return total


def folded_shape(sh, layers):
    return (-(-sh.rows // (8 * (sh.pitch // layers))) * 8, LANES)


def unfold(sh, message, layers, start):
    height = message.shape[0]
    lane, _, across = sh.lane_grid(1)
    mask = (lane < sh.used) & lane_range(across, start, layers)
    parts = []
    for i, first in enumerate(range(0, sh.rows, height)):
        part = message[0 : min(height, sh.rows - first)]
        parts.append(pick(mask, shift(part, start + 2 - i * layers)))
    return jnp.concatenate(parts, axis=0) if len(parts) > 1 else parts[0]


def pack_xy(sh, ex, scratch, x_refs, y_refs, corner_refs):
    rows = sh.rows
    lane, _, across = sh.lane_grid(1)
    even_x, even_y = sh.here(0) % 2 == 0, sh.here(1) % 2 == 0
    span = ex.layers * sh.pitch
    x_up = x_down = y_up = y_down = jnp.zeros((rows, LANES), f32)
    inside = lane < sh.used
    y_above, y_below = sh.y + ex.up, ex.down
    for f in range(ex.fields):
        value = scratch[f]
        high, low = (sh.x + ex.up + 1) * sh.pitch, (ex.down + 1) * sh.pitch
        if sh.x_links == 1:
            part = pick(lane_range(lane, jnp.where(even_x, high, low), span), value)
            x_up = x_down = x_up + shift_either(even_x, part, f * span - high, f * span - low)
        else:
            x_up = x_up + shift(pick(lane_range(lane, high, span), value), f * span - high)
            x_down = x_down + shift(pick(lane_range(lane, low, span), value), f * span - low)
        mask = inside & lane_range(across, y_above, ex.layers)
        y_up = y_up + shift(pick(mask, value), f * ex.layers - y_above - 2)
        mask = inside & lane_range(across, y_below, ex.layers)
        y_down = y_down + shift(pick(mask, value), f * ex.layers - y_below - 2)
    packed = ex.fields * ex.layers
    y_up, y_down = fold(sh, y_up, packed), fold(sh, y_down, packed)
    for ref, message in zip(y_refs, pair(sh.y_links, even_y, y_up, y_down)):
        ref[...] = message
    for i, message in enumerate([x_up] if sh.x_links == 1 else pair(sh.x_links, even_x, x_up, x_down)):
        x_refs[i][...] = message
        upward, downward = fold(sh, message, ex.layers, y_above), fold(sh, message, ex.layers, y_below)
        for j, corner in enumerate(pair(sh.y_links, even_y, upward, downward)):
            corner_refs[i * sh.y_links + j][...] = corner


def merge_xy(sh, ex, scratch, rim, guard, y_refs, x_refs):
    lane, _, across = sh.lane_grid(1)
    inside = lane < sh.used
    low_mask = inside & lane_range(across, ex.up, ex.layers)
    high_mask = inside & lane_range(across, sh.y + ex.down, ex.layers)
    span = ex.layers * sh.pitch
    packed = ex.fields * ex.layers
    below_y, above_y = [unfold(sh, value, packed, -2) for value in sides(sh, 1, [ref[...] for ref in y_refs])]
    per_link = 1 + sh.y_links
    sums = []
    for link in range(sh.x_links):
        straight, diagonal = x_refs[link * per_link], x_refs[link * per_link + 1 : (link + 1) * per_link]
        total = straight[...]
        below, above = sides(sh, 1, [ref[...] for ref in diagonal])
        total = total + unfold(sh, below, ex.layers, ex.up)
        sums.append(total + unfold(sh, above, ex.layers, sh.y + ex.down))
    single = sh.x_links == 1
    even = sh.here(0) % 2 == 0
    if single:
        message = scale(jnp.where(even, sh.here(0) < sh.sizes[0] - 1, sh.here(0) > 0), sums[0])
    else:
        below_x, above_x = sides(sh, 0, sums)
    first = 1 if ex.up == -2 else 0
    last = ex.layers - 1 if ex.down + ex.layers == 2 else ex.layers
    low, low_count = (ex.up + first + 1) * sh.pitch, (ex.layers - first) * sh.pitch
    high, high_count = (sh.x + ex.down + 1) * sh.pitch, last * sh.pitch
    edge = (sh.x + 1) * sh.pitch
    for f in range(ex.fields):
        addend = pick(low_mask, shift(below_y, ex.up + 2 - ex.layers * f))
        addend = addend + pick(high_mask, shift(above_y, sh.y + ex.down + 2 - ex.layers * f))
        from_low, from_high = low - f * span - first * sh.pitch, high - f * span
        if single:
            mask = lane_range(lane, jnp.where(even, high, low), jnp.where(even, high_count, low_count))
            addend = addend + pick(mask, shift_either(even, message, from_high, from_low))
        else:
            addend = addend + pick(lane_range(lane, low, low_count), shift(below_x, from_low))
            addend = addend + pick(lane_range(lane, high, high_count), shift(above_x, from_high))
        scratch[f, guard : guard + sh.rows, :] += addend
        if rim is not None:
            from_high = edge - f * span - last * sh.pitch
            if single:
                mask = lane_range(lane, jnp.where(even, edge, 0), sh.pitch)
                both = pick(mask, shift_either(even, message, from_high, -f * span))
            else:
                both = pick(lane_range(lane, 0, sh.pitch), shift(below_x, -f * span))
                both = both + pick(lane_range(lane, edge, sh.pitch), shift(above_x, from_high))
            rim[f, guard : guard + sh.rows, :] = both


def clear_guards(sh, refs):
    for ref in refs:
        for f in range(ref.shape[0]):
            ref[f, :EDGE, :] = jnp.zeros((EDGE, LANES), f32)
            ref[f, ref.shape[1] - EDGE :, :] = jnp.zeros((EDGE, LANES), f32)


def inner(ref, f):
    return ref[f, EDGE : ref.shape[1] - EDGE, :]


def z_stage(ref, f):
    end = ref.shape[1] - EDGE
    after = ref[f, EDGE + 1 : end + 1, :]
    before = ref[f, EDGE - 1 : end - 1, :]
    return inner(ref, f), before + after, after - before


COLUMNS = [(dx, dy) for dx in (-1, 0, 1) for dy in (-1, 0, 1) if dx or dy]


def column_parts(ref, sign=None):
    a, a_sum, a_dif = z_stage(ref, 0)
    b, b_sum, b_dif = z_stage(ref, 1)
    c, c_sum, c_dif = z_stage(ref, 2)
    mixed_x, mixed_y = MIXED2 * b + b_sum, MIXED2 * a + a_sum
    x_c_dif = c_dif
    if sign is not None:
        mixed_x, mixed_y, x_c_dif, a_dif = sign * mixed_x, sign * mixed_y, sign * c_dif, sign * a_dif
    both_z = ACROSS1 * c + ALONG2 * c_sum
    along_x, across_x = ALONG1 * a + ALONG2 * a_sum, ACROSS1 * a + ACROSS2 * a_sum
    along_y, across_y = ALONG1 * b + ALONG2 * b_sum, ACROSS1 * b + ACROSS2 * b_sum
    tilt_a, tilt_b, tilt_c, tilt_x = MIXED2 * a_dif, MIXED2 * b_dif, MIXED2 * c_dif, MIXED2 * x_c_dif
    same_x, same_y = ALONG2 * a + SAME3 * a_sum, ALONG2 * b + SAME3 * b_sum
    same_z = ACROSS2 * c + SAME3 * c_sum
    plus_x, plus_y, plus_z = same_x + mixed_x, same_y + mixed_y, same_z + a_dif
    minus_x, minus_y, minus_z = same_x - mixed_x, same_y - mixed_y, same_z - a_dif
    return {
        (0, 0): (ACROSS1 * a_sum, ACROSS1 * b_sum, ALONG1 * c_sum),
        (1, 0): (along_x + tilt_x, across_y, both_z + tilt_a),
        (-1, 0): (along_x - tilt_x, across_y, both_z - tilt_a),
        (0, 1): (across_x, along_y + tilt_c, both_z + tilt_b),
        (0, -1): (across_x, along_y - tilt_c, both_z - tilt_b),
        (1, 1): (plus_x + x_c_dif, plus_y + c_dif, plus_z + b_dif),
        (1, -1): (minus_x + x_c_dif, minus_y - c_dif, plus_z - b_dif),
        (-1, 1): (minus_x - x_c_dif, minus_y + c_dif, minus_z + b_dif),
        (-1, -1): (plus_x - x_c_dif, plus_y - c_dif, minus_z - b_dif),
    }


def put_columns(sh, k, rim, columns):
    lane, _, _ = sh.lane_grid(1)
    for i, (dx, dy) in enumerate(COLUMNS):
        value = shift(k, dx * sh.pitch + dy)
        if dx and rim is not None:
            edge = lane < sh.pitch if dx > 0 else lane >= (sh.x + 1) * sh.pitch
            value = jnp.where(edge, shift(rim, dy), value)
        put(columns, i, value)


def own_block(stiff, columns):
    k, k_sum, _ = z_stage(stiff, 0)
    at = {(-dx, -dy): z_stage(columns, i) for i, (dx, dy) in enumerate(COLUMNS)}
    total = lambda j, *places: sum(at[place][j] for place in places)
    in_x, in_y = ((1, 0), (-1, 0)), ((0, 1), (0, -1))
    same, other = ((1, 1), (-1, -1)), ((1, -1), (-1, 1))
    x, x_sum, y, y_sum = total(0, *in_x), total(1, *in_x), total(0, *in_y), total(1, *in_y)
    same_0, same_1, other_0, other_1 = total(0, *same), total(1, *same), total(0, *other), total(1, *other)
    corner, corner_sum = same_0 + other_0, SAME3 * (same_1 + other_1)
    shared = ALONG2 * corner + corner_sum + ACROSS1 * k_sum + TOTAL * k
    turn_x = at[1, 1][2] - at[-1, -1][2]
    turn_y = at[1, -1][2] - at[-1, 1][2]
    return (
        ALONG1 * x + ALONG2 * x_sum + ACROSS1 * y + ACROSS2 * y_sum + shared,
        ALONG1 * y + ALONG2 * y_sum + ACROSS1 * x + ACROSS2 * x_sum + shared,
        ACROSS1 * (x + y) + ALONG2 * (x_sum + y_sum) + ACROSS2 * corner + corner_sum + ALONG1 * k_sum + TOTAL * k,
        MIXED2 * (same_0 - other_0) + (same_1 - other_1),
        MIXED2 * (at[1, 0][2] - at[-1, 0][2]) + (turn_x + turn_y),
        MIXED2 * (at[0, 1][2] - at[0, -1][2]) + (turn_x - turn_y),
    )


def apply_block(d, v):
    return (
        d[0] * v[0] + d[3] * v[1] + d[4] * v[2],
        d[3] * v[0] + d[1] * v[1] + d[5] * v[2],
        d[4] * v[0] + d[5] * v[1] + d[2] * v[2],
    )


def image_of(sh, lane, v, kv, rims, springs_ref, columns):
    k = springs_ref[6]
    last = (sh.x + 1) * sh.pitch
    own = apply_block([springs_ref[f] for f in range(6)], [inner(v, m) for m in range(3)])
    plain, scaled = column_parts(v), column_parts(kv)
    total = [k * plain[0, 0][m] + scaled[0, 0][m] for m in range(3)]
    for dx in (0, -1, 1):
        for m in range(3):
            side = None
            for i, column in enumerate(COLUMNS):
                if column[0] == dx:
                    moved = inner(columns, i) * plain[column][m] + scaled[column][m]
                    moved = shift(moved, -(dx * sh.pitch + column[1]))
                    side = moved if side is None else side + moved
            if dx:
                side = pick(lane < last if dx > 0 else lane >= sh.pitch, side)
            total[m] = total[m] + side
    if rims is not None:
        sign = jnp.where(lane < sh.pitch, -1.0, 1.0)
        plain, scaled = column_parts(rims[0], sign), column_parts(rims[1], sign)
        at_rim = (lane < sh.pitch) | (lane >= last)
        for m in range(3):
            side = None
            for dy in (-1, 0, 1):
                moved = shift(k, dy) * plain[1, dy][m] + scaled[1, dy][m]
                moved = shift(moved, -dy)
                side = moved if side is None else side + moved
            total[m] = total[m] + pick(at_rim, side)
    return [own[m] - total[m] for m in range(3)]


def level(sh):
    return lax.broadcasted_iota(jnp.int32, (sh.rows, LANES), 0) - EDGE


def ends_level(sh):
    row = lax.broadcasted_iota(jnp.int32, (4 * EDGE, LANES), 0)
    return jnp.where(row < 2 * EDGE, row, row + sh.rows - 4 * EDGE) - EDGE


def ends(value):
    return jnp.concatenate([value[: 2 * EDGE], value[value.shape[0] - 2 * EDGE :]], axis=0)


def extended_mask(sh, z):
    lane, _, across = sh.lane_grid(1)
    return ((lane < sh.used) & (across >= -1) & (across <= sh.y)) & ((z >= -1) & (z <= sh.z))


def within(sh, axis, place, size):
    index = sh.here(axis)
    low = jnp.where(index > 0, -EDGE, 0)
    high = jnp.where(index < sh.sizes[axis] - 1, size + EDGE, size)
    return (place >= low) & (place < high)


def grid_masks(sh):
    lane, along, across = sh.lane_grid(1)
    lanes = (lane < sh.used) & within(sh, 1, across, sh.y)
    rows = within(sh, 2, level(sh), sh.z)
    return (lanes & within(sh, 0, along, sh.x)) & rows, lanes & rows


def put(ref, f, value):
    ref[f, EDGE : ref.shape[1] - EDGE, :] = value


def local_solve(sh, z, residual_ref, springs_ref, columns, v, kv, factor):
    lane, _, _ = sh.lane_grid(1)
    mask = extended_mask(sh, z)
    for m in range(3):
        factor[m] = pick(mask, relax / jnp.where(mask, springs_ref[m], 1.0))
        value = residual_ref[m] * factor[m]
        put(v[0], m, value)
        put(kv[0], m, springs_ref[6] * value)
    for sweep in range(SWEEPS - 1):
        old, new = sweep % 2, (sweep + 1) % 2
        image = image_of(sh, lane, v[old], kv[old], None, springs_ref, columns)
        for m in range(3):
            value = inner(v[old], m) + factor[m] * (residual_ref[m] - image[m])
            put(v[new], m, value)
            put(kv[new], m, springs_ref[6] * value)
    return (SWEEPS - 1) % 2


def own_level(sh):
    return lax.broadcasted_iota(jnp.int32, (sh.z, LANES), 0)


def coords(sh, z):
    _, along, across = sh.lane_grid(z.shape[0])
    along = jnp.where(along < 0, along + sh.x, jnp.where(along < sh.x, along, along - sh.x))
    across = jnp.where(across < 0, across + sh.y, jnp.where(across < sh.y, across, across - sh.y))
    place = lambda index, size: (2 * index + 1).astype(f32) / size - 1.0
    return place(along, sh.x), place(across, sh.y), place(z, sh.z)


def cell_coords(sh):
    cell = lax.broadcasted_iota(jnp.int32, (sh.cells, sh.z), 0)
    z = lax.broadcasted_iota(jnp.int32, (sh.cells, sh.z), 1)
    x = cell // sh.y
    place = lambda index, size: (2 * index + 1).astype(f32) / size - 1.0
    return place(x, sh.x), place(cell - x * sh.y, sh.y), place(z, sh.z)


def cross(a, b):
    return (a[1] * b[2] - a[2] * b[1], a[2] * b[0] - a[0] * b[2], a[0] * b[1] - a[1] * b[0])


def fold_rows(value):
    total = value[0:8]
    for i in range(8, value.shape[0], 8):
        total = total + value[i : i + 8]
    return jnp.sum(total, axis=0, keepdims=True)


def lane_sums(rows_ref):
    ones = jnp.ones((8, LANES), f32)
    return lax.dot_general(
        ones, rows_ref[...], (((1,), (1,)), ((), ())), precision=highest, preferred_element_type=f32
    )


def coarse_sums(nodes, field, places, count, sums):
    moments = tuple(field) + cross(places, field)
    for node in range(count):
        mask = nodes == node
        for m in range(6):
            sums[node * 6 + m : node * 6 + m + 1, :] = fold_rows(pick(mask, moments[m]))


def sums_line(sh, sums, unknowns):
    flat = (sh.here(0) * sh.sizes[1] + sh.here(1)) * sh.sizes[2] + sh.here(2)
    return pltpu.roll(lane_sums(sums), lax.rem(flat * unknowns, LANES), 1)[0:1]


def coarse_solution(received, inverse_ref, values):
    unknowns, total = inverse_ref.shape
    row = lax.broadcasted_iota(jnp.int32, received.shape, 0)
    part = jnp.zeros((unknowns, LANES), f32)
    for i in range(0, total, LANES):
        owner = (i + lax.broadcasted_iota(jnp.int32, (1, LANES), 1)) // unknowns
        vector = jnp.sum(pick(row == owner, received), axis=0, keepdims=True)
        part = part + inverse_ref[:, i : i + LANES] * vector
    values[0:unknowns, :] = jnp.dot(
        part, jnp.ones((LANES, LANES), f32), precision=highest, preferred_element_type=f32
    )


def coarse_shares(sums, inverse_ref, shares):
    unknowns, total = inverse_ref.shape
    column = jnp.dot(sums[...], jnp.ones((LANES, LANES), f32), precision=highest, preferred_element_type=f32)
    for i in range(0, total, LANES):
        share = inverse_ref[:, i : i + LANES] * column[0:unknowns]
        shares[i // LANES : i // LANES + 1, :] = jnp.sum(share, axis=0, keepdims=True)


def coarse_table(sh, shares_ref, unknowns, flat, table):
    rows = shares_ref.shape[0] // sh.devices
    lane = lax.broadcasted_iota(jnp.int32, (1, LANES), 1)
    for i in range(rows):
        flat[i : i + 1, :] = jnp.sum(shares_ref[pl.ds(i, sh.devices, stride=rows), :], axis=0, keepdims=True)
    for device in range(sh.devices):
        row, place = divmod(device * unknowns, LANES)
        part = shift(flat[row : row + 1, :], -place)
        if place + unknowns > LANES:
            part = jnp.where(lane < LANES - place, part, shift(flat[row + 1 : row + 2, :], -place))
        table[device : device + 1, :] = pick(lane < unknowns, part)


def region_values(sh, table, dz):
    lane, along, across = sh.lane_grid(1)
    x = sh.here(0) + jnp.where(along < 0, -1, jnp.where(along < sh.x, 0, 1))
    y = sh.here(1) + jnp.where(across < 0, -1, jnp.where(across < sh.y, 0, 1))
    z = sh.here(2) + dz
    exists = (lane < sh.used) & (x >= 0) & (x < sh.sizes[0]) & (y >= 0) & (y < sh.sizes[1])
    exists = exists & (z >= 0) & (z < sh.sizes[2])
    device = jnp.where(exists, (x * sh.sizes[1] + y) * sh.sizes[2] + z, -1)
    owner = lax.broadcasted_iota(jnp.int32, (sh.devices, LANES), 0) == device
    return lax.dot_general(
        table[0 : sh.devices, :], owner.astype(f32), (((0,), (0,)), ((), ())), precision=highest, preferred_element_type=f32
    )


def coarse_cells(nodes, places, values, count):
    cells = []
    for m in range(6):
        cell = jnp.zeros(nodes.shape, f32)
        for node in range(count):
            cell = jnp.where(nodes == float(node), values[node * 6 + m : node * 6 + m + 1, :], cell)
        cells.append(cell)
    turned = cross(cells[3:], places)
    return [cells[m] + turned[m] for m in range(3)]


def selection(sh):
    lane, along, across = sh.lane_grid(sh.cells)
    inside = (along >= 0) & (along < sh.x) & (across >= 0) & (across < sh.y)
    row = lax.broadcasted_iota(jnp.int32, (sh.cells, LANES), 0)
    return (inside & (row == along * sh.y + across)).astype(f32)


def to_lanes(value, select, precision=highest):
    return lax.dot_general(
        value, select, (((0,), (0,)), ((), ())), precision=precision, preferred_element_type=f32
    )


def to_cells(value, select):
    return lax.dot_general(
        select, value, (((1,), (1,)), ((), ())), precision=highest, preferred_element_type=f32
    )


def send_lines(sh, lines, slots_ref):
    here = [sh.here(axis) for axis in range(3)]
    corner = [lines[8 * i : 8 * i + 8, :] for i in range(4)]
    top, bottom = lines[32:40, :], lines[40:48, :]
    for x in range(sh.sizes[0]):
        low_high = [jnp.where(x > here[0], corner[2 + high], corner[high]) for high in range(2)]
        for y in range(sh.sizes[1]):
            column = jnp.where(y > here[1], low_high[1], low_high[0])
            for z in range(sh.sizes[2]):
                slot = jnp.where(z == here[2] + 1, top, jnp.where(z == here[2] - 1, bottom, column))
                place = 8 * ((x * sh.sizes[1] + y) * sh.sizes[2] + z)
                slots_ref[place : place + 8, :] = slot


def slot_from(sh, received_ref, step):
    place, exists = 0, None
    for axis in range(3):
        index = sh.here(axis) + step[axis]
        inside = (index >= 0) & (index < sh.sizes[axis])
        exists = inside if exists is None else exists & inside
        place = place * sh.sizes[axis] + jnp.clip(index, 0, sh.sizes[axis] - 1)
    return scale(exists, received_ref[pl.ds(pl.multiple_of(place * 8, 8), 8), :])


def repeat_twice(count):
    row = lax.broadcasted_iota(jnp.int32, (2 * count, count), 0)
    column = lax.broadcasted_iota(jnp.int32, (2 * count, count), 1)
    return ((row >= 2 * column) & (row < 2 * column + 2)).astype(f32)


def ring(size_x, size_y, rows):
    row = lax.broadcasted_iota(jnp.int32, (rows, LANES), 0)
    sides_x, both = 2 * size_y, 2 * size_y + 2 * size_x
    corner = row - both
    x = jnp.where(row < size_y, -1, size_x)
    x = jnp.where(row < sides_x, x, jnp.where(row < sides_x + size_x, row - sides_x, row - sides_x - size_x))
    x = jnp.where(row < both, x, jnp.where(corner < 2, -1, size_x))
    y = jnp.where(row < size_y, row, row - size_y)
    y = jnp.where(row < sides_x, y, jnp.where(row < sides_x + size_x, -1, size_y))
    y = jnp.where(row < both, y, jnp.where((corner == 0) | (corner == 2), -1, size_y))
    return x, y, (row < sides_x) | (row >= both), row < both + 4


def face_shape(sh, label_x, label_y):
    rows = max(4 * sh.x + label_x, 4 * sh.y + label_y)
    return (-(-rows // 8) * 8, LANES)


def pack_faces(sh, natural_ref, stiff, label_x, label_y, x_refs, y_refs):
    even_x, even_y = sh.here(0) % 2 == 0, sh.here(1) % 2 == 0

    def face(at, count, stride, label_at, label_count, label_stride):
        rows = [natural_ref[m, pl.ds(at, count, stride=stride), :] for m in range(4)]
        return rows, stiff[pl.ds(label_at, label_count, stride=label_stride), :]

    above = face(sh.cells - sh.y, sh.y, 1, (label_x - 1) * label_y, label_y, 1)
    below = face(0, sh.y, 1, 0, label_y, 1)
    for refs, links, even, above, below in (
        (x_refs, sh.x_links, even_x, above, below),
        (
            y_refs,
            sh.y_links,
            even_y,
            face(sh.y - 1, sh.x, sh.y, label_y - 1, label_x, label_y),
            face(0, sh.x, sh.y, 0, label_x, label_y),
        ),
    ):
        for i, ref in enumerate(refs):
            ref[...] = jnp.zeros(ref.shape, f32)
            count = above[0][0].shape[0]
            for m in range(4):
                ref[m * count : (m + 1) * count, :] = pair(links, even, above[0][m], below[0][m])[i]
            labels, length = above[1].shape
            ref[4 * count : 4 * count + labels, 0:length] = pair(links, even, above[1], below[1])[i]


def merge_start(sh, refs, x_refs, y_refs, received_ref, sizes, cells, labels):
    residual, nodes, stiff, stiff_rim = refs
    label_x, label_y, label_z = sizes
    lane, along, across = sh.lane_grid(1)
    inside = lane < sh.used
    last = (sh.x + 1) * sh.pitch
    x_mask = {-1: lane < sh.pitch, 0: (lane >= sh.pitch) & (lane < last), 1: (lane >= last) & inside}
    y_mask = {-1: across < 0, 0: (across >= 0) & (across < sh.y), 1: across >= sh.y}
    cells[...] = jnp.zeros(cells.shape, f32)
    labels[...] = jnp.zeros(labels.shape, f32)
    count, label_count = cells.shape[1], labels.shape[0]
    at = label_at = 0
    for axis, face_refs, size, label_size in ((0, x_refs, sh.y, label_y), (1, y_refs, sh.x, label_x)):
        for message in sides(sh, axis, [ref[...] for ref in face_refs]):
            for m in range(4):
                cells[m, at : at + size, :] = message[m * size : (m + 1) * size]
            labels[label_at : label_at + label_size, :] = message[4 * size : 4 * size + label_size, 0:label_z]
            at, label_at = at + size, label_at + label_size
    for dx, dy in ((-1, -1), (-1, 1), (1, -1), (1, 1)):
        slot = slot_from(sh, received_ref, (dx, dy, 0))
        for m, row in enumerate((0, 1, 2, 5)):
            cells[m, at : at + 1, :] = slot[row : row + 1]
        labels[label_at : label_at + 1, :] = slot[3:4, 0:label_z]
        at, label_at = at + 1, label_at + 1
    x, y, _, valid = ring(sh.x, sh.y, count)
    place = (valid & inside & (along == x) & (across == y)).astype(f32)
    own = slice(EDGE, EDGE + sh.z)
    tall_own = slice(2 * EDGE, 2 * EDGE + sh.z)
    for m in range(3):
        residual[m, own, :] += to_lanes(cells[m], place)
    nodes[own, :] += to_lanes(cells[3], place, small)
    by_z = lax.dot_general(
        repeat_twice(label_z), labels[...], (((1,), (1,)), ((), ())), precision=highest, preferred_element_type=f32
    )
    x, y, at_x, valid = ring(label_x, label_y, label_count)
    match = valid & inside & ((along >> 1) == x) & ((across >> 1) == y)
    columns = jnp.dot(by_z, (match & at_x).astype(f32), precision=highest, preferred_element_type=f32)
    stiff_rim[0, tall_own, :] = columns
    columns = columns + jnp.dot(by_z, (match & ~at_x).astype(f32), precision=highest, preferred_element_type=f32)
    stiff[0, tall_own, :] += columns
    for dz in (-1, 1):
        main = edge = jnp.zeros((8, LANES), f32)
        for dx in (-1, 0, 1):
            for dy in (-1, 0, 1):
                slot = slot_from(sh, received_ref, (dx, dy, dz))
                mask = x_mask[dx] & y_mask[dy]
                main = main + pick(mask, shift(slot, dx * sh.x * sh.pitch + dy * sh.y))
                if dx:
                    edge = edge + pick(mask, shift(slot, dx * (sh.x - 1) * sh.pitch + dy * sh.y))
        near = EDGE + sh.z if dz > 0 else EDGE - 1
        for m in range(3):
            residual[m, near : near + 1, :] = main[m : m + 1]
        nodes[near : near + 1, :] = main[5:6]
        for row in (EDGE + near, EDGE + near + dz):
            stiff[0, row : row + 1, :] = main[3:4]
            stiff_rim[0, row : row + 1, :] = edge[3:4]


def call(kernel, name, outs, ins, scratch=(), remote_ins=False, remote_outs=()):
    space = pltpu.HBM if remote_ins else pltpu.VMEM
    return pl.pallas_call(
        kernel,
        out_shape=[jax.ShapeDtypeStruct(shape, f32) for shape in outs],
        in_specs=[pl.BlockSpec(memory_space=space) for _ in ins],
        out_specs=[
            pl.BlockSpec(memory_space=pltpu.HBM if i in remote_outs else pltpu.VMEM) for i in range(len(outs))
        ],
        scratch_shapes=[pltpu.VMEM(shape, f32) if isinstance(shape, tuple) else shape for shape in scratch],
        compiler_params=pltpu.CompilerParams(vmem_limit_bytes=(56 if remote_ins else 48) * 1024 * 1024),
        name=name,
    )(*ins)


def permutation(sizes, moves):
    def partner(axis, link, index):
        size = sizes[axis]
        other = index ^ 1 if link == 0 else index + (1 if index % 2 else -1)
        if 0 <= other < size:
            return other
        return size - 1 - index if axis == 2 and size % 2 == 0 else index

    pairs = []
    for x in range(sizes[0]):
        for y in range(sizes[1]):
            for z in range(sizes[2]):
                place = [x, y, z]
                goal = [partner(a, moves[a], place[a]) if a in moves else place[a] for a in range(3)]
                if any(goal[a] == place[a] for a in moves) and sizes[2] % 2 == 0:
                    goal = [x, y, partner(2, 0, z)]
                flat = [(p[0] * sizes[1] + p[1]) * sizes[2] + p[2] for p in (place, goal)]
                pairs.append(tuple(flat))
    return pairs


def send(sh, value, moves):
    return lax.ppermute(value, AXES, permutation(sh.sizes, moves))


def send_z(sh, messages):
    return [send(sh, message, {2: link}) for link, message in enumerate(messages)]


def send_faces(sh, x_messages, y_messages):
    from_x = [send(sh, message, {0: link}) for link, message in enumerate(x_messages)]
    from_y = [send(sh, message, {1: link}) for link, message in enumerate(y_messages)]
    return from_y, from_x


def to_all(slots):
    return lax.all_to_all(slots, AXES, 0, 0, tiled=True)


def exchange(sh, ex, name, field, z_messages):
    from_z = send_z(sh, z_messages)

    corners = sh.x_links * sh.y_links

    def packer(*refs):
        take = Taker(refs)
        field_ref, z_refs = take.one(), take(sh.z_links)
        x_refs, y_refs, corner_refs, scratch = take(sh.x_links), take(sh.y_links), take(corners), take.one()
        merge_z(sh, ex, field_ref, z_refs, scratch, 0)
        pack_xy(sh, ex, scratch, x_refs, y_refs, corner_refs)

    plane = (sh.rows, LANES)
    messages = call(
        packer,
        name,
        [plane] * sh.x_links
        + [folded_shape(sh, ex.fields * ex.layers)] * sh.y_links
        + [folded_shape(sh, ex.layers)] * corners,
        [field] + from_z,
        [(ex.fields,) + plane],
    )
    take = Taker(messages)
    x_messages, y_messages = take(sh.x_links), take(sh.y_links)
    from_y, straight = send_faces(sh, x_messages, y_messages)
    from_x = []
    for link in range(sh.x_links):
        from_x.append(straight[link])
        from_x.extend(send(sh, take.one(), {0: link, 1: other}) for other in range(sh.y_links))
    return from_z, from_y, from_x


class Taker:
    def __init__(self, refs):
        self.refs, self.at = refs, 0

    def __call__(self, count):
        self.at += count
        return self.refs[self.at - count : self.at]

    def one(self):
        return self(1)[0]


def merge_all(sh, ex, take, scratch, rim, guard):
    field = take.one()
    from_z, from_y = take(sh.z_links), take(sh.y_links)
    from_x = take(sh.x_links * (1 + sh.y_links))
    merge_z(sh, ex, field, from_z, scratch, guard)
    merge_xy(sh, ex, scratch, rim, guard, from_y, from_x)


def body(right_side, phase_labels, phase_moduli, coarse_nodes, coarse_inverse):
    sizes = tuple(lax.axis_size(axis) for axis in AXES)
    _, size_x, size_y, size_z = right_side.shape
    sh = Shape(size_x, size_y, size_z, phase_moduli.shape[0], sizes)
    unknowns = coarse_inverse.shape[0]
    node_count = unknowns // 6
    sum_rows = -(-unknowns // 8) * 8 + 8
    share_rows = coarse_inverse.shape[1] // LANES
    own = slice(EDGE, EDGE + sh.z)
    plane = (sh.rows, LANES)
    fields = (3,) + plane
    tall = (3, sh.tall, LANES)
    slots = (sh.devices, LANES)
    z_shape = lambda ex: [(8 * ex.fields, LANES)] * sh.z_links
    natural = right_side.reshape(3, sh.cells, sh.z)
    nodes_natural = coarse_nodes.reshape(sh.cells, sh.z)
    label_x, label_y, label_z = phase_labels.shape

    def block_places():
        lane, along, across = sh.lane_grid(label_x * label_y)
        inside = (along >= 0) & (along < sh.x) & (across >= 0) & (across < sh.y)
        block = lax.broadcasted_iota(jnp.int32, along.shape, 0)
        return (inside & (block == (along >> 1) * label_y + (across >> 1))).astype(f32)

    def end_layers(values, places):
        length = values.shape[1]
        row = lax.broadcasted_iota(jnp.int32, (8, length), 0)
        at = lax.broadcasted_iota(jnp.int32, (8, length), 1)
        ends = ((row == 0) & (at == length - 1)) | ((row == 1) & (at == 0))
        return jnp.dot(to_cells(values, ends.astype(f32)), places, precision=highest, preferred_element_type=f32)

    def begin(natural_in, labels_in, moduli_in, nodes_in, stiff, slots_ref, *rest):
        x_refs, y_refs = rest[: sh.x_links], rest[sh.x_links : sh.x_links + sh.y_links]
        natural_ref, labels_ref, moduli_ref, nodes_ref, sems, sums, lines = rest[sh.x_links + sh.y_links :]
        pairs = ((natural_in, natural_ref.at[0:3, 0 : sh.cells, :]), (labels_in, labels_ref.at[0:label_x]), (moduli_in, moduli_ref), (nodes_in, nodes_ref))
        copies = [pltpu.make_async_copy(a, b, sems.at[i]) for i, (a, b) in enumerate(pairs)]
        for copy in copies:
            copy.start()
        sums[...] = jnp.zeros(sums.shape, f32)
        lines[...] = jnp.zeros(lines.shape, f32)
        for copy in copies:
            copy.wait()
        for i in range(label_x):
            labels = labels_ref[i]
            moduli = jnp.zeros(labels.shape, f32)
            for phase in range(sh.phases):
                moduli = jnp.where(labels == phase, moduli_ref[phase], moduli)
            stiff[i * label_y : (i + 1) * label_y, :] = moduli * (1.0 / SCALE)
        natural_ref[3, 0 : sh.cells, :] = nodes_ref[...].astype(f32) + 1.0
        cells = [natural_ref[m, 0 : sh.cells, :] for m in range(4)]
        coarse_sums(nodes_ref[...], cells[:3], cell_coords(sh), node_count, sums)
        line = sums_line(sh, sums, unknowns)
        for i, (cell, block) in enumerate(
            (
                (0, 0),
                (sh.y - 1, label_y - 1),
                ((sh.x - 1) * sh.y, (label_x - 1) * label_y),
                (sh.cells - 1, label_x * label_y - 1),
            )
        ):
            for m in range(3):
                lines[8 * i + m : 8 * i + m + 1, :] = natural_ref[m, cell : cell + 1, :]
            lines[8 * i + 3 : 8 * i + 4, 0:label_z] = stiff[block : block + 1, :]
            lines[8 * i + 5 : 8 * i + 6, :] = natural_ref[3, cell : cell + 1, :]
        select = selection(sh)
        layers = [end_layers(cells[m], select) for m in range(4)] + [end_layers(stiff[0 : label_x * label_y, :], block_places())]
        for i in range(2):
            for layer, row in zip(layers, (0, 1, 2, 5, 3)):
                lines[8 * (4 + i) + row : 8 * (4 + i) + row + 1, :] = layer[i : i + 1]
        for i in range(6):
            lines[8 * i + 4 : 8 * i + 5, :] = line
        send_lines(sh, lines, slots_ref)
        pack_faces(sh, natural_ref, stiff, label_x, label_y, x_refs, y_refs)

    block_rows = (8 * -(-(label_x + 8) * label_y // 8), label_z)
    stiff_blocks, lines, *messages = call(
        begin,
        "begin",
        [block_rows, (8 * sh.devices, LANES)]
        + [face_shape(sh, label_x, label_y)] * (sh.x_links + sh.y_links),
        [natural, phase_labels, phase_moduli, nodes_natural],
        [
            (4, sh.cells + 8, sh.z),
            pltpu.VMEM((label_x + 2, label_y, label_z), jnp.int32),
            pltpu.SMEM(phase_moduli.shape, f32),
            pltpu.VMEM(nodes_natural.shape, jnp.int32),
            pltpu.SemaphoreType.DMA((4,)),
            (LANES, LANES),
            (56, LANES),
        ],
        remote_ins=True,
    )

    def spread(natural_ref, nodes_ref, stiff, inverse_in, field_ref, lanes_ref, inverse_ref):
        inverse_ref[...] = inverse_in[...]
        select = selection(sh)
        field_ref[...] = jnp.zeros(field_ref.shape, f32)
        for m in range(3):
            field_ref[m, own, :] = to_lanes(natural_ref[m], select)
        by_z = lax.dot_general(
            repeat_twice(label_z),
            stiff[0 : label_x * label_y, :],
            (((1,), (1,)), ((), ())),
            precision=highest,
            preferred_element_type=f32,
        )
        field_ref[3, own, :] = jnp.dot(by_z, block_places(), precision=highest, preferred_element_type=f32)
        lanes_ref[...] = to_lanes(nodes_ref[...].astype(f32) + 1.0, select, small) - 1.0

    start_field, nodes, inverse = call(
        spread,
        "spread",
        [(4,) + plane, (sh.z, LANES), coarse_inverse.shape],
        [natural, nodes_natural, stiff_blocks, coarse_inverse],
    )
    from_y, from_x = send_faces(sh, messages[: sh.x_links], messages[sh.x_links :])
    lines = to_all(lines)

    short = (3, 6 * EDGE, LANES)
    short_fields = (3, 4 * EDGE, LANES)
    tall_columns = (len(COLUMNS), sh.tall, LANES)
    solve_scratch = [tall] * 4 + [fields, tall_columns]
    short_scratch = [short] * 4 + [short_fields, (len(COLUMNS), 6 * EDGE, LANES)]

    def end_rows(ref):
        def rows(f, start, count):
            place = start + EDGE if start < 2 * EDGE else start - sh.rows + 5 * EDGE
            return ref[f, place : place + count, :]

        return rows

    def first_ends(*refs):
        take = Taker(refs)
        field_ref = take.one()
        y_refs, x_refs = take(sh.y_links), take(sh.x_links)
        nodes_ref, lines_ref, inverse_ref = take(3)
        residual, wide_nodes, stiffness_ref, values = take(4)
        z_refs = take(sh.z_links)
        stiff, stiff_rim, cells, labels, short_stiff, some_residual, springs = take(7)
        v0, v1, kv0, kv1, factor, columns = take(6)
        clear_guards(sh, (stiff, stiff_rim, short_stiff, v0, v1, kv0, kv1, columns))
        residual[...] = field_ref[0:3]
        put(stiff, 0, field_ref[3])
        put(stiff_rim, 0, jnp.zeros(plane, f32))
        sizes = phase_labels.shape
        wide_nodes[...] = jnp.zeros(plane, f32)
        wide_nodes[own, :] = nodes_ref[...] + 1.0
        merge_start(sh, (residual, wide_nodes, stiff, stiff_rim), x_refs, y_refs, lines_ref, sizes, cells, labels)
        wide_nodes[...] = wide_nodes[...] - 1.0
        stiffness_ref[0] = inner(stiff, 0)
        stiffness_ref[1] = inner(stiff_rim, 0)
        coarse_solution(lines_ref[pl.ds(4, sh.devices, stride=8), :], inverse_ref, values)
        lane, _, _ = sh.lane_grid(1)
        put(short_stiff, 0, ends(stiffness_ref[0]))
        put_columns(sh, ends(stiffness_ref[0]), ends(stiffness_ref[1]), columns)
        for f, entry in enumerate(own_block(short_stiff, columns)):
            springs[f] = entry
        springs[6] = inner(short_stiff, 0)
        for m in range(3):
            some_residual[m] = ends(residual[m])
        index = local_solve(sh, ends_level(sh), some_residual, springs, columns, (v0, v1), (kv0, kv1), factor)
        solution = (v0, v1)[index]
        z = lax.broadcasted_iota(jnp.int32, (2 * EDGE, LANES), 0)
        z = jnp.where(z < EDGE, z, z + sh.z - 2 * EDGE)
        some_nodes = jnp.concatenate([nodes_ref[0:EDGE, :], nodes_ref[sh.z - EDGE : sh.z, :]], axis=0)
        added = coarse_cells(some_nodes, coords(sh, z), values, node_count)
        for m in range(3):
            solution[m, 2 * EDGE : 4 * EDGE, :] += pick(some_nodes >= 0.0, added[m])
        pack_z(sh, DEEP, end_rows(solution), z_refs)

    residual, wide_nodes, stiffness, values, *z_messages = call(
        first_ends,
        "first_ends",
        [fields, plane, (2,) + plane, (sum_rows, LANES)] + z_shape(DEEP),
        [start_field, *from_y, *from_x, nodes, lines, inverse],
        [(1, sh.tall, LANES)] * 2
        + [
            (4, 8 * -(-(2 * sh.x + 2 * sh.y + 4) // 8) + 8, LANES),
            (8 * -(-(2 * label_x + 2 * label_y + 4) // 8) + 8, label_z),
        ]
        + [(1, 6 * EDGE, LANES)]
        + [short_fields, (7, 4 * EDGE, LANES)]
        + short_scratch,
    )

    def first_solve(residual_ref, stiffness_ref, values, nodes_ref, solution_ref, springs_ref, *rest):
        stiff, v0, v1, kv0, kv1, factor, columns = rest
        clear_guards(sh, (stiff, v0, v1, kv0, kv1, columns))
        put(stiff, 0, stiffness_ref[0])
        put_columns(sh, stiffness_ref[0], stiffness_ref[1], columns)
        springs_ref[6] = stiffness_ref[0]
        springs_ref[7] = stiffness_ref[1]
        lane, _, _ = sh.lane_grid(1)
        for f, entry in enumerate(own_block(stiff, columns)):
            springs_ref[f] = entry
        index = local_solve(sh, level(sh), residual_ref, springs_ref, columns, (v0, v1), (kv0, kv1), factor)
        for m in range(3):
            solution_ref[m] = inner((v0, v1)[index], m)
        added = coarse_cells(nodes_ref[...], coords(sh, own_level(sh)), values, node_count)
        for m in range(3):
            solution_ref[m, own, :] += pick(nodes_ref[...] >= 0.0, added[m])

    solved, springs = call(
        first_solve,
        "first_solve",
        [fields, (8,) + plane],
        [residual, stiffness, values, nodes],
        [(1, sh.tall, LANES)] + solve_scratch,
    )
    from_z, from_y, from_x = exchange(sh, DEEP, "deep", solved, z_messages)

    def first_image(*refs):
        take = Taker(refs)
        merging = take(1 + sh.z_links + sh.y_links + sh.x_links * (1 + sh.y_links))
        nodes_ref, springs_ref, inverse_ref = take(3)
        search_ref, image_ref, slots_out = take(3)
        z_refs = take(sh.z_links)
        v, rim, kv, k_rim, sums, shares, slots_ref, sem = take(8)
        some_residual, some_springs, v0, v1, kv0, kv1, factor, some_columns, columns = take(9)
        clear_guards(sh, (v0, v1, kv0, kv1))
        clear_guards(sh, (v, rim, kv, k_rim))
        merge_all(sh, DEEP, Taker(merging), v, rim, EDGE)
        lane, _, _ = sh.lane_grid(1)

        in_grid, in_rim = grid_masks(sh)
        for m in range(3):
            value = pick(in_grid, inner(v, m))
            put(v, m, value)
            search_ref[m] = value
            put(kv, m, springs_ref[6] * value)
            value = pick(in_rim, inner(rim, m))
            put(rim, m, value)
            put(k_rim, m, springs_ref[7] * value)
        put_columns(sh, springs_ref[6], None, columns)
        image = image_of(sh, lane, v, kv, (rim, k_rim), springs_ref, columns)
        keep = in_grid & extended_mask(sh, level(sh))
        for m in range(3):
            image_ref[m] = pick(keep, image[m])
        sums[...] = jnp.zeros(sums.shape, f32)
        field = [image_ref[m, own, :] for m in range(3)]
        coarse_sums(nodes_ref[...], field, coords(sh, own_level(sh)), node_count, sums)
        coarse_shares(sums, inverse_ref, shares)
        for device in range(sh.devices):
            slots_ref[device * share_rows : (device + 1) * share_rows, :] = shares[0:share_rows, :]
        copy = pltpu.make_async_copy(slots_ref.at[0 : slots_out.shape[0], :], slots_out, sem)
        copy.start()
        for m in range(3):
            some_residual[m] = ends(image_ref[m])
        for f in range(7):
            some_springs[f] = ends(springs_ref[f])
        put_columns(sh, some_springs[6], None, some_columns)
        index = local_solve(sh, ends_level(sh), some_residual, some_springs, some_columns, (v0, v1), (kv0, kv1), factor)
        pack_z(sh, NEAR, end_rows((v0, v1)[index]), z_refs)
        copy.wait()

    all_slots = (sh.devices * share_rows, LANES)
    search, image, shares, *z_messages = call(
        first_image,
        "first_image",
        [fields, fields, all_slots] + z_shape(NEAR),
        [solved, *from_z, *from_y, *from_x, nodes, springs, inverse],
        [tall] * 4
        + [(LANES, LANES), (8 * -(-share_rows // 8) + 8, LANES)]
        + [(8 * -(-all_slots[0] // 8) + 8, LANES), pltpu.SemaphoreType.DMA]
        + [short_fields, (7, 4 * EDGE, LANES)]
        + short_scratch
        + [tall_columns],
        remote_outs=(2,),
    )
    shares = to_all(shares.reshape(sh.devices, 1, share_rows * LANES)).reshape(shares.shape)

    def second_solve(image_ref, springs_ref, local_ref, v0, v1, kv0, kv1, factor, columns):
        clear_guards(sh, (v0, v1, kv0, kv1))
        put_columns(sh, springs_ref[6], None, columns)
        index = local_solve(sh, level(sh), image_ref, springs_ref, columns, (v0, v1), (kv0, kv1), factor)
        for m in range(3):
            local_ref[m] = inner((v0, v1)[index], m)

    (solved,) = call(second_solve, "second_solve", [fields], [image, springs], solve_scratch)
    from_z, from_y, from_x = exchange(sh, NEAR, "near", solved, z_messages)

    def between(shares_ref, wide_nodes, nodes_ref, start_ref, search_ref, first_ref, coarse_ref, sums, *scratch):
        flat, table, values = scratch
        coarse_ref[...] = jnp.zeros(coarse_ref.shape, f32)
        coarse_table(sh, shares_ref, unknowns, flat, table)
        last = lax.broadcasted_iota(jnp.int32, (1, LANES), 0) + sh.z - 1
        for dz, first, z in ((0, EDGE, own_level(sh)), (-1, EDGE - 1, last), (1, EDGE + sh.z, last - sh.z + 1)):
            values[...] = region_values(sh, table, dz)
            rows = slice(first, first + z.shape[0])
            added = coarse_cells(wide_nodes[rows, :], coords(sh, z), values, node_count)
            for m in range(3):
                coarse_ref[m, rows, :] = added[m]
        valid = nodes_ref[...] >= 0.0
        row = lax.broadcasted_iota(jnp.int32, sums.shape, 0)
        total = jnp.zeros(sums.shape, f32)
        for i, other in enumerate((start_ref, first_ref)):
            product = sum(search_ref[m, own, :] * other[m, own, :] for m in range(3))
            total = jnp.where(row == i, fold_rows(pick(valid, product)), total)
        sums[...] = total

    coarse_field, sums = call(
        between,
        "between",
        [fields, (8, LANES)],
        [shares, wide_nodes, nodes, start_field, search, image],
        [(8 * -(-share_rows // 8) + 8, LANES), (8 * -(-sh.devices // 8) + 8, LANES), (LANES, LANES)],
    )

    def second_image(*refs):
        take = Taker(refs)
        merging = take(1 + sh.z_links + sh.y_links + sh.x_links * (1 + sh.y_links))
        nodes_ref, springs_ref, first_ref, coarse_ref, early_ref = take(5)
        second_ref, image_ref, slots_ref = take(3)
        v, kv, sums, columns = take(4)
        clear_guards(sh, (v, kv))
        put_columns(sh, springs_ref[6], None, columns)
        merge_all(sh, NEAR, Taker(merging), v, None, EDGE)
        lane, _, _ = sh.lane_grid(1)
        in_grid, _ = grid_masks(sh)
        for m in range(3):
            value = pick(in_grid, inner(v, m)) + coarse_ref[m]
            put(v, m, value)
            second_ref[m] = value
            put(kv, m, springs_ref[6] * value)
        image = image_of(sh, lane, v, kv, None, springs_ref, columns)
        for m in range(3):
            image_ref[m] = image[m]
        valid = nodes_ref[...] >= 0.0
        sums[...] = jnp.zeros(sums.shape, f32)
        sums[0:8, :] = early_ref[...]
        for i, other in ((2, first_ref), (3, image_ref)):
            product = sum(second_ref[m, own, :] * other[m, own, :] for m in range(3))
            sums[i : i + 1, :] = fold_rows(pick(valid, product))
        slots_ref[...] = jnp.broadcast_to(lane_sums(sums)[0:1], slots_ref.shape)

    second, second_image_field, sums = call(
        second_image,
        "second_image",
        [fields, fields, slots],
        [solved, *from_z, *from_y, *from_x, nodes, springs, image, coarse_field, sums],
        [tall] * 2 + [(LANES, LANES), tall_columns],
    )
    totals = to_all(sums)

    def turn(search_ref, first_ref, second_ref, image_ref, out_ref):
        select = selection(sh)
        for i, ref in enumerate((search_ref, first_ref, second_ref, image_ref)):
            for m in range(3):
                out_ref[i, m] = to_cells(ref[m, own, :], select)

    (turned,) = call(turn, "turn", [(4,) + natural.shape], [search, image, second, second_image_field])

    def finish(totals_ref, natural_ref, turned_ref, field_ref, residual_ref):
        total = jnp.sum(totals_ref[...], axis=0, keepdims=True)
        rz, zw, wq, qv = [total[:, i : i + 1] for i in range(4)]
        step0 = rz / zw
        rho = step0 * step0 * wq - step0 * zw
        grow = 1.0 + rho / rz
        curvature = grow * grow * zw - 2.0 * grow * step0 * wq + step0 * step0 * qv
        step1 = rho / curvature
        first = step0 + step1 * grow
        second = step0 * step1
        for m in range(3):
            field_ref[m] = first * turned_ref[0, m] - second * turned_ref[2, m]
            residual_ref[m] = natural_ref[m] - (first * turned_ref[1, m] - second * turned_ref[3, m])

    solution_field, residual = call(
        finish, "finish", [natural.shape, natural.shape], [totals, natural, turned]
    )
    return solution_field.reshape(right_side.shape), residual.reshape(right_side.shape)


def solution(mesh):
    in_specs = (
        P(None, "gx", "gy", "gz"),
        P("gx", "gy", "gz"),
        P(),
        P("gx", "gy", "gz"),
        P(("gx", "gy", "gz"), None),
    )
    out_specs = (P(None, "gx", "gy", "gz"), P(None, "gx", "gy", "gz"))
    return jax.shard_map(body, mesh=mesh, in_specs=in_specs, out_specs=out_specs, check_vma=False)
```

```python
import jax
import jax.numpy as jnp
from jax import lax
from jax.experimental import pallas as pl
from jax.experimental.pallas import tpu as pltpu
from jax.sharding import PartitionSpec as P

AXES = ("gx", "gy", "gz")
SWEEPS = 4
relax = 0.6
highest = lax.Precision.HIGHEST
small = lax.Precision.DEFAULT
f32 = jnp.float32
LANES = 128
EDGE = 8

SCALE = 36.0
ALONG1, ACROSS1 = 27.0, 18.0
ALONG2, ACROSS2, MIXED2 = 11.25, 9.0, 2.25
SAME3 = 7.0
TOTAL = 2 * ALONG1 + 4 * ACROSS1 + 8 * ALONG2 + 4 * ACROSS2 + 8 * SAME3


class Exchange:
    def __init__(self, fields, layers, up, down):
        self.fields, self.layers, self.up, self.down = fields, layers, up, down


DEEP = Exchange(3, 3, -2, -1)
NEAR = Exchange(3, 2, -1, -1)


class Shape:
    def __init__(self, size_x, size_y, size_z, phases, mesh_sizes):
        self.x, self.y, self.z = size_x, size_y, size_z
        self.pitch = size_y + 4
        self.used = (size_x + 2) * self.pitch
        assert self.used <= LANES
        self.rows = size_z + 2 * EDGE
        self.tall = self.rows + 2 * EDGE
        self.phases = phases
        self.sizes = mesh_sizes
        self.devices = mesh_sizes[0] * mesh_sizes[1] * mesh_sizes[2]
        self.cells = size_x * size_y
        self.links = [1 if n <= 2 else 2 for n in mesh_sizes]
        self.x_links, self.y_links, self.z_links = self.links

    def lane_grid(self, rows):
        lane = lax.broadcasted_iota(jnp.int32, (rows, LANES), 1)
        column = jnp.zeros_like(lane)
        for j in range(1, self.x + 2):
            column = column + (lane >= j * self.pitch).astype(jnp.int32)
        offset = lane - column * self.pitch
        return lane, column - 1, offset - 2

    def here(self, axis):
        return lax.axis_index(AXES[axis])


def shift(value, amount):
    amount = amount % LANES
    return value if amount == 0 else pltpu.roll(value, amount, 1)


def shift_either(flag, value, first, second):
    return pltpu.roll(value, jnp.where(flag, first % LANES, second % LANES), 1)


def pick(mask, value):
    return jnp.where(mask, value, 0.0)


def scale(flag, value):
    return value * flag.astype(f32)


def pair(links, even, upward, downward):
    first = jnp.where(even, upward, downward)
    return (first,) if links == 1 else (first, jnp.where(even, downward, upward))


def sides(sh, axis, received):
    index, size = sh.here(axis), sh.sizes[axis]
    even = index % 2 == 0
    first = received[0]
    second = received[1] if len(received) > 1 else jnp.zeros_like(first)
    below = jnp.where(even, second, first)
    above = jnp.where(even, first, second)
    return scale(index > 0, below), scale(index < size - 1, above)


def lane_range(lane, start, count):
    return (lane >= start) & (lane < start + count)


def pack_z(sh, ex, source, out_refs):
    even = sh.here(2) % 2 == 0
    for ref in out_refs:
        ref[...] = jnp.zeros(ref.shape, f32)
    for f in range(ex.fields):
        upward = source(f, EDGE + sh.z + ex.up, ex.layers)
        downward = source(f, EDGE + ex.down, ex.layers)
        for ref, message in zip(out_refs, pair(sh.z_links, even, upward, downward)):
            ref[8 * f : 8 * f + ex.layers, :] = message


def merge_z(sh, ex, field_ref, received_refs, scratch, guard):
    below, above = sides(sh, 2, [ref[...] for ref in received_refs])
    for f in range(ex.fields):
        scratch[f, guard : guard + sh.rows, :] = field_ref[f]
        low = guard + EDGE + ex.up
        high = guard + EDGE + sh.z + ex.down
        scratch[f, low : low + ex.layers, :] += below[8 * f : 8 * f + ex.layers]
        scratch[f, high : high + ex.layers, :] += above[8 * f : 8 * f + ex.layers]


def fold(sh, value, layers, start=None):
    folds = sh.pitch // layers
    height = -(-sh.rows // (8 * folds)) * 8
    lane, _, across = sh.lane_grid(1)
    total = jnp.zeros((height, LANES), f32)
    for i, first in enumerate(range(0, sh.rows, height)):
        part = value[first : first + height]
        if start is not None:
            part = pick((lane < sh.used) & lane_range(across, start, layers), part)
        part = shift(part, i * layers - (0 if start is None else start + 2))
        if part.shape[0] < height:
            part = jnp.concatenate([part, jnp.zeros((height - part.shape[0], LANES), f32)], axis=0)
        total = total + part
    return total


def folded_shape(sh, layers):
    return (-(-sh.rows // (8 * (sh.pitch // layers))) * 8, LANES)


def unfold(sh, message, layers, start):
    height = message.shape[0]
    lane, _, across = sh.lane_grid(1)
    mask = (lane < sh.used) & lane_range(across, start, layers)
    parts = []
    for i, first in enumerate(range(0, sh.rows, height)):
        part = message[0 : min(height, sh.rows - first)]
        parts.append(pick(mask, shift(part, start + 2 - i * layers)))
    return jnp.concatenate(parts, axis=0) if len(parts) > 1 else parts[0]


def pack_xy(sh, ex, scratch, x_refs, y_refs, corner_refs):
    rows = sh.rows
    lane, _, across = sh.lane_grid(1)
    even_x, even_y = sh.here(0) % 2 == 0, sh.here(1) % 2 == 0
    span = ex.layers * sh.pitch
    x_up = x_down = y_up = y_down = jnp.zeros((rows, LANES), f32)
    inside = lane < sh.used
    y_above, y_below = sh.y + ex.up, ex.down
    for f in range(ex.fields):
        value = scratch[f]
        high, low = (sh.x + ex.up + 1) * sh.pitch, (ex.down + 1) * sh.pitch
        if sh.x_links == 1:
            part = pick(lane_range(lane, jnp.where(even_x, high, low), span), value)
            x_up = x_down = x_up + shift_either(even_x, part, f * span - high, f * span - low)
        else:
            x_up = x_up + shift(pick(lane_range(lane, high, span), value), f * span - high)
            x_down = x_down + shift(pick(lane_range(lane, low, span), value), f * span - low)
        mask = inside & lane_range(across, y_above, ex.layers)
        y_up = y_up + shift(pick(mask, value), f * ex.layers - y_above - 2)
        mask = inside & lane_range(across, y_below, ex.layers)
        y_down = y_down + shift(pick(mask, value), f * ex.layers - y_below - 2)
    packed = ex.fields * ex.layers
    y_up, y_down = fold(sh, y_up, packed), fold(sh, y_down, packed)
    for ref, message in zip(y_refs, pair(sh.y_links, even_y, y_up, y_down)):
        ref[...] = message
    for i, message in enumerate([x_up] if sh.x_links == 1 else pair(sh.x_links, even_x, x_up, x_down)):
        x_refs[i][...] = message
        upward, downward = fold(sh, message, ex.layers, y_above), fold(sh, message, ex.layers, y_below)
        for j, corner in enumerate(pair(sh.y_links, even_y, upward, downward)):
            corner_refs[i * sh.y_links + j][...] = corner


def merge_xy(sh, ex, scratch, rim, guard, y_refs, x_refs):
    lane, _, across = sh.lane_grid(1)
    inside = lane < sh.used
    low_mask = inside & lane_range(across, ex.up, ex.layers)
    high_mask = inside & lane_range(across, sh.y + ex.down, ex.layers)
    span = ex.layers * sh.pitch
    packed = ex.fields * ex.layers
    whole = lambda value: value if value.shape[0] == sh.rows else unfold(sh, value, packed, -2)
    below_y, above_y = [whole(value) for value in sides(sh, 1, [ref[...] for ref in y_refs])]
    per_link = 1 + sh.y_links
    sums = []
    for link in range(sh.x_links):
        straight, diagonal = x_refs[link * per_link], x_refs[link * per_link + 1 : (link + 1) * per_link]
        total = straight[...]
        below, above = sides(sh, 1, [ref[...] for ref in diagonal])
        total = total + unfold(sh, below, ex.layers, ex.up)
        sums.append(total + unfold(sh, above, ex.layers, sh.y + ex.down))
    single = sh.x_links == 1
    even = sh.here(0) % 2 == 0
    if single:
        message = scale(jnp.where(even, sh.here(0) < sh.sizes[0] - 1, sh.here(0) > 0), sums[0])
    else:
        below_x, above_x = sides(sh, 0, sums)
    first = 1 if ex.up == -2 else 0
    last = ex.layers - 1 if ex.down + ex.layers == 2 else ex.layers
    low, low_count = (ex.up + first + 1) * sh.pitch, (ex.layers - first) * sh.pitch
    high, high_count = (sh.x + ex.down + 1) * sh.pitch, last * sh.pitch
    edge = (sh.x + 1) * sh.pitch
    for f in range(ex.fields):
        addend = pick(low_mask, shift(below_y, ex.up + 2 - ex.layers * f))
        addend = addend + pick(high_mask, shift(above_y, sh.y + ex.down + 2 - ex.layers * f))
        from_low, from_high = low - f * span - first * sh.pitch, high - f * span
        if single:
            mask = lane_range(lane, jnp.where(even, high, low), jnp.where(even, high_count, low_count))
            addend = addend + pick(mask, shift_either(even, message, from_high, from_low))
        else:
            addend = addend + pick(lane_range(lane, low, low_count), shift(below_x, from_low))
            addend = addend + pick(lane_range(lane, high, high_count), shift(above_x, from_high))
        scratch[f, guard : guard + sh.rows, :] += addend
        if rim is not None:
            from_high = edge - f * span - last * sh.pitch
            if single:
                mask = lane_range(lane, jnp.where(even, edge, 0), sh.pitch)
                both = pick(mask, shift_either(even, message, from_high, -f * span))
            else:
                both = pick(lane_range(lane, 0, sh.pitch), shift(below_x, -f * span))
                both = both + pick(lane_range(lane, edge, sh.pitch), shift(above_x, from_high))
            rim[f, guard : guard + sh.rows, :] = both


def clear_guards(sh, refs):
    for ref in refs:
        for f in range(ref.shape[0]):
            ref[f, :EDGE, :] = jnp.zeros((EDGE, LANES), f32)
            ref[f, ref.shape[1] - EDGE :, :] = jnp.zeros((EDGE, LANES), f32)


def inner(ref, f):
    return ref[f, EDGE : ref.shape[1] - EDGE, :]


def z_stage(ref, f):
    end = ref.shape[1] - EDGE
    after = ref[f, EDGE + 1 : end + 1, :]
    before = ref[f, EDGE - 1 : end - 1, :]
    return inner(ref, f), before + after, after - before


COLUMNS = [(dx, dy) for dx in (-1, 0, 1) for dy in (-1, 0, 1) if dx or dy]


def column_parts(ref, sign=None):
    a, a_sum, a_dif = z_stage(ref, 0)
    b, b_sum, b_dif = z_stage(ref, 1)
    c, c_sum, c_dif = z_stage(ref, 2)
    mixed_x, mixed_y = MIXED2 * b + b_sum, MIXED2 * a + a_sum
    x_c_dif = c_dif
    if sign is not None:
        mixed_x, mixed_y, x_c_dif, a_dif = sign * mixed_x, sign * mixed_y, sign * c_dif, sign * a_dif
    both_z = ACROSS1 * c + ALONG2 * c_sum
    along_x, across_x = ALONG1 * a + ALONG2 * a_sum, ACROSS1 * a + ACROSS2 * a_sum
    along_y, across_y = ALONG1 * b + ALONG2 * b_sum, ACROSS1 * b + ACROSS2 * b_sum
    tilt_a, tilt_b, tilt_c, tilt_x = MIXED2 * a_dif, MIXED2 * b_dif, MIXED2 * c_dif, MIXED2 * x_c_dif
    same_x, same_y = ALONG2 * a + SAME3 * a_sum, ALONG2 * b + SAME3 * b_sum
    same_z = ACROSS2 * c + SAME3 * c_sum
    plus_x, plus_y, plus_z = same_x + mixed_x, same_y + mixed_y, same_z + a_dif
    minus_x, minus_y, minus_z = same_x - mixed_x, same_y - mixed_y, same_z - a_dif
    return {
        (0, 0): (ACROSS1 * a_sum, ACROSS1 * b_sum, ALONG1 * c_sum),
        (1, 0): (along_x + tilt_x, across_y, both_z + tilt_a),
        (-1, 0): (along_x - tilt_x, across_y, both_z - tilt_a),
        (0, 1): (across_x, along_y + tilt_c, both_z + tilt_b),
        (0, -1): (across_x, along_y - tilt_c, both_z - tilt_b),
        (1, 1): (plus_x + x_c_dif, plus_y + c_dif, plus_z + b_dif),
        (1, -1): (minus_x + x_c_dif, minus_y - c_dif, plus_z - b_dif),
        (-1, 1): (minus_x - x_c_dif, minus_y + c_dif, minus_z + b_dif),
        (-1, -1): (plus_x - x_c_dif, plus_y - c_dif, minus_z - b_dif),
    }


def put_columns(sh, k, rim, columns):
    lane, _, _ = sh.lane_grid(1)
    for i, (dx, dy) in enumerate(COLUMNS):
        value = shift(k, dx * sh.pitch + dy)
        if dx and rim is not None:
            edge = lane < sh.pitch if dx > 0 else lane >= (sh.x + 1) * sh.pitch
            value = jnp.where(edge, shift(rim, dy), value)
        put(columns, i, value)


def own_block(stiff, columns):
    k, k_sum, _ = z_stage(stiff, 0)
    at = {(-dx, -dy): z_stage(columns, i) for i, (dx, dy) in enumerate(COLUMNS)}
    total = lambda j, *places: sum(at[place][j] for place in places)
    in_x, in_y = ((1, 0), (-1, 0)), ((0, 1), (0, -1))
    same, other = ((1, 1), (-1, -1)), ((1, -1), (-1, 1))
    x, x_sum, y, y_sum = total(0, *in_x), total(1, *in_x), total(0, *in_y), total(1, *in_y)
    same_0, same_1, other_0, other_1 = total(0, *same), total(1, *same), total(0, *other), total(1, *other)
    corner, corner_sum = same_0 + other_0, SAME3 * (same_1 + other_1)
    shared = ALONG2 * corner + corner_sum + ACROSS1 * k_sum + TOTAL * k
    turn_x = at[1, 1][2] - at[-1, -1][2]
    turn_y = at[1, -1][2] - at[-1, 1][2]
    return (
        ALONG1 * x + ALONG2 * x_sum + ACROSS1 * y + ACROSS2 * y_sum + shared,
        ALONG1 * y + ALONG2 * y_sum + ACROSS1 * x + ACROSS2 * x_sum + shared,
        ACROSS1 * (x + y) + ALONG2 * (x_sum + y_sum) + ACROSS2 * corner + corner_sum + ALONG1 * k_sum + TOTAL * k,
        MIXED2 * (same_0 - other_0) + (same_1 - other_1),
        MIXED2 * (at[1, 0][2] - at[-1, 0][2]) + (turn_x + turn_y),
        MIXED2 * (at[0, 1][2] - at[0, -1][2]) + (turn_x - turn_y),
    )


def apply_block(d, v):
    return (
        d[0] * v[0] + d[3] * v[1] + d[4] * v[2],
        d[3] * v[0] + d[1] * v[1] + d[5] * v[2],
        d[4] * v[0] + d[5] * v[1] + d[2] * v[2],
    )


def image_of(sh, lane, v, kv, rims, springs_ref, columns):
    k = springs_ref[6]
    last = (sh.x + 1) * sh.pitch
    own = apply_block([springs_ref[f] for f in range(6)], [inner(v, m) for m in range(3)])
    plain, scaled = column_parts(v), column_parts(kv)
    total = [k * plain[0, 0][m] + scaled[0, 0][m] for m in range(3)]
    for dx in (0, -1, 1):
        for m in range(3):
            side = None
            for i, column in enumerate(COLUMNS):
                if column[0] == dx:
                    moved = inner(columns, i) * plain[column][m] + scaled[column][m]
                    moved = shift(moved, -(dx * sh.pitch + column[1]))
                    side = moved if side is None else side + moved
            if dx:
                side = pick(lane < last if dx > 0 else lane >= sh.pitch, side)
            total[m] = total[m] + side
    if rims is not None:
        sign = jnp.where(lane < sh.pitch, -1.0, 1.0)
        plain, scaled = column_parts(rims[0], sign), column_parts(rims[1], sign)
        at_rim = (lane < sh.pitch) | (lane >= last)
        for m in range(3):
            side = None
            for dy in (-1, 0, 1):
                moved = shift(k, dy) * plain[1, dy][m] + scaled[1, dy][m]
                moved = shift(moved, -dy)
                side = moved if side is None else side + moved
            total[m] = total[m] + pick(at_rim, side)
    return [own[m] - total[m] for m in range(3)]


def level(sh):
    return lax.broadcasted_iota(jnp.int32, (sh.rows, LANES), 0) - EDGE


def ends_level(sh):
    row = lax.broadcasted_iota(jnp.int32, (4 * EDGE, LANES), 0)
    return jnp.where(row < 2 * EDGE, row, row + sh.rows - 4 * EDGE) - EDGE


def ends(value):
    return jnp.concatenate([value[: 2 * EDGE], value[value.shape[0] - 2 * EDGE :]], axis=0)


def extended_mask(sh, z):
    lane, _, across = sh.lane_grid(1)
    return ((lane < sh.used) & (across >= -1) & (across <= sh.y)) & ((z >= -1) & (z <= sh.z))


def within(sh, axis, place, size):
    index = sh.here(axis)
    low = jnp.where(index > 0, -EDGE, 0)
    high = jnp.where(index < sh.sizes[axis] - 1, size + EDGE, size)
    return (place >= low) & (place < high)


def grid_masks(sh):
    lane, along, across = sh.lane_grid(1)
    lanes = (lane < sh.used) & within(sh, 1, across, sh.y)
    rows = within(sh, 2, level(sh), sh.z)
    return (lanes & within(sh, 0, along, sh.x)) & rows, lanes & rows


def put(ref, f, value):
    ref[f, EDGE : ref.shape[1] - EDGE, :] = value


def local_solve(sh, z, residual_ref, springs_ref, columns, v, kv, factor):
    lane, _, _ = sh.lane_grid(1)
    mask = extended_mask(sh, z)
    for m in range(3):
        factor[m] = pick(mask, relax / jnp.where(mask, springs_ref[m], 1.0))
        value = residual_ref[m] * factor[m]
        put(v[0], m, value)
        put(kv[0], m, springs_ref[6] * value)
    for sweep in range(SWEEPS - 1):
        old, new = sweep % 2, (sweep + 1) % 2
        image = image_of(sh, lane, v[old], kv[old], None, springs_ref, columns)
        for m in range(3):
            value = inner(v[old], m) + factor[m] * (residual_ref[m] - image[m])
            put(v[new], m, value)
            put(kv[new], m, springs_ref[6] * value)
    return (SWEEPS - 1) % 2


def own_level(sh):
    return lax.broadcasted_iota(jnp.int32, (sh.z, LANES), 0)


def coords(sh, z):
    _, along, across = sh.lane_grid(z.shape[0])
    along = jnp.where(along < 0, along + sh.x, jnp.where(along < sh.x, along, along - sh.x))
    across = jnp.where(across < 0, across + sh.y, jnp.where(across < sh.y, across, across - sh.y))
    place = lambda index, size: (2 * index + 1).astype(f32) / size - 1.0
    return place(along, sh.x), place(across, sh.y), place(z, sh.z)


def cell_coords(sh):
    cell = lax.broadcasted_iota(jnp.int32, (sh.cells, sh.z), 0)
    z = lax.broadcasted_iota(jnp.int32, (sh.cells, sh.z), 1)
    x = cell // sh.y
    place = lambda index, size: (2 * index + 1).astype(f32) / size - 1.0
    return place(x, sh.x), place(cell - x * sh.y, sh.y), place(z, sh.z)


def cross(a, b):
    return (a[1] * b[2] - a[2] * b[1], a[2] * b[0] - a[0] * b[2], a[0] * b[1] - a[1] * b[0])


def fold_rows(value):
    total = value[0:8]
    for i in range(8, value.shape[0], 8):
        total = total + value[i : i + 8]
    return jnp.sum(total, axis=0, keepdims=True)


def lane_sums(rows_ref):
    ones = jnp.ones((8, LANES), f32)
    return lax.dot_general(
        ones, rows_ref[...], (((1,), (1,)), ((), ())), precision=highest, preferred_element_type=f32
    )


def coarse_sums(nodes, field, places, count, sums):
    moments = tuple(field) + cross(places, field)
    for node in range(count):
        mask = nodes == node
        for m in range(6):
            sums[node * 6 + m : node * 6 + m + 1, :] = fold_rows(pick(mask, moments[m]))


def sums_line(sh, sums, unknowns):
    flat = (sh.here(0) * sh.sizes[1] + sh.here(1)) * sh.sizes[2] + sh.here(2)
    return pltpu.roll(lane_sums(sums), lax.rem(flat * unknowns, LANES), 1)[0:1]


def coarse_solution(received, inverse_ref, values):
    unknowns, total = inverse_ref.shape
    row = lax.broadcasted_iota(jnp.int32, received.shape, 0)
    part = jnp.zeros((unknowns, LANES), f32)
    for i in range(0, total, LANES):
        owner = (i + lax.broadcasted_iota(jnp.int32, (1, LANES), 1)) // unknowns
        vector = jnp.sum(pick(row == owner, received), axis=0, keepdims=True)
        part = part + inverse_ref[:, i : i + LANES] * vector
    values[0:unknowns, :] = jnp.dot(
        part, jnp.ones((LANES, LANES), f32), precision=highest, preferred_element_type=f32
    )


def coarse_shares(sums, inverse_ref, shares):
    unknowns, total = inverse_ref.shape
    column = jnp.dot(sums[...], jnp.ones((LANES, LANES), f32), precision=highest, preferred_element_type=f32)
    for i in range(0, total, LANES):
        share = inverse_ref[:, i : i + LANES] * column[0:unknowns]
        shares[i // LANES : i // LANES + 1, :] = jnp.sum(share, axis=0, keepdims=True)


def coarse_table(sh, shares_ref, unknowns, flat, table):
    rows = shares_ref.shape[0] // sh.devices
    lane = lax.broadcasted_iota(jnp.int32, (1, LANES), 1)
    for i in range(rows):
        flat[i : i + 1, :] = jnp.sum(shares_ref[pl.ds(i, sh.devices, stride=rows), :], axis=0, keepdims=True)
    for device in range(sh.devices):
        row, place = divmod(device * unknowns, LANES)
        part = shift(flat[row : row + 1, :], -place)
        if place + unknowns > LANES:
            part = jnp.where(lane < LANES - place, part, shift(flat[row + 1 : row + 2, :], -place))
        table[device : device + 1, :] = pick(lane < unknowns, part)


def region_values(sh, table, dz):
    lane, along, across = sh.lane_grid(1)
    x = sh.here(0) + jnp.where(along < 0, -1, jnp.where(along < sh.x, 0, 1))
    y = sh.here(1) + jnp.where(across < 0, -1, jnp.where(across < sh.y, 0, 1))
    z = sh.here(2) + dz
    exists = (lane < sh.used) & (x >= 0) & (x < sh.sizes[0]) & (y >= 0) & (y < sh.sizes[1])
    exists = exists & (z >= 0) & (z < sh.sizes[2])
    device = jnp.where(exists, (x * sh.sizes[1] + y) * sh.sizes[2] + z, -1)
    owner = lax.broadcasted_iota(jnp.int32, (sh.devices, LANES), 0) == device
    return lax.dot_general(
        table[0 : sh.devices, :], owner.astype(f32), (((0,), (0,)), ((), ())), precision=highest, preferred_element_type=f32
    )


def coarse_cells(nodes, places, values, count):
    cells = []
    for m in range(6):
        cell = jnp.zeros(nodes.shape, f32)
        for node in range(count):
            cell = jnp.where(nodes == float(node), values[node * 6 + m : node * 6 + m + 1, :], cell)
        cells.append(cell)
    turned = cross(cells[3:], places)
    return [cells[m] + turned[m] for m in range(3)]


def selection(sh):
    lane, along, across = sh.lane_grid(sh.cells)
    inside = (along >= 0) & (along < sh.x) & (across >= 0) & (across < sh.y)
    row = lax.broadcasted_iota(jnp.int32, (sh.cells, LANES), 0)
    return (inside & (row == along * sh.y + across)).astype(f32)


def to_lanes(value, select, precision=highest):
    return lax.dot_general(
        value, select, (((0,), (0,)), ((), ())), precision=precision, preferred_element_type=f32
    )


def to_cells(value, select):
    return lax.dot_general(
        select, value, (((1,), (1,)), ((), ())), precision=highest, preferred_element_type=f32
    )


def send_lines(sh, lines, slots_ref):
    here = [sh.here(axis) for axis in range(3)]
    corner = [lines[8 * i : 8 * i + 8, :] for i in range(4)]
    top, bottom = lines[32:40, :], lines[40:48, :]
    for x in range(sh.sizes[0]):
        low_high = [jnp.where(x > here[0], corner[2 + high], corner[high]) for high in range(2)]
        for y in range(sh.sizes[1]):
            column = jnp.where(y > here[1], low_high[1], low_high[0])
            for z in range(sh.sizes[2]):
                slot = jnp.where(z == here[2] + 1, top, jnp.where(z == here[2] - 1, bottom, column))
                place = 8 * ((x * sh.sizes[1] + y) * sh.sizes[2] + z)
                slots_ref[place : place + 8, :] = slot


def slot_from(sh, received_ref, step):
    place, exists = 0, None
    for axis in range(3):
        index = sh.here(axis) + step[axis]
        inside = (index >= 0) & (index < sh.sizes[axis])
        exists = inside if exists is None else exists & inside
        place = place * sh.sizes[axis] + jnp.clip(index, 0, sh.sizes[axis] - 1)
    return scale(exists, received_ref[pl.ds(pl.multiple_of(place * 8, 8), 8), :])


def repeat_twice(count):
    row = lax.broadcasted_iota(jnp.int32, (2 * count, count), 0)
    column = lax.broadcasted_iota(jnp.int32, (2 * count, count), 1)
    return ((row >= 2 * column) & (row < 2 * column + 2)).astype(f32)


def ring(size_x, size_y, rows):
    row = lax.broadcasted_iota(jnp.int32, (rows, LANES), 0)
    sides_x, both = 2 * size_y, 2 * size_y + 2 * size_x
    corner = row - both
    x = jnp.where(row < size_y, -1, size_x)
    x = jnp.where(row < sides_x, x, jnp.where(row < sides_x + size_x, row - sides_x, row - sides_x - size_x))
    x = jnp.where(row < both, x, jnp.where(corner < 2, -1, size_x))
    y = jnp.where(row < size_y, row, row - size_y)
    y = jnp.where(row < sides_x, y, jnp.where(row < sides_x + size_x, -1, size_y))
    y = jnp.where(row < both, y, jnp.where((corner == 0) | (corner == 2), -1, size_y))
    return x, y, (row < sides_x) | (row >= both), row < both + 4


def face_shape(sh, label_x, label_y):
    rows = max(4 * sh.x + label_x, 4 * sh.y + label_y)
    return (-(-rows // 8) * 8, LANES)


def pack_faces(sh, natural_ref, stiff, label_x, label_y, x_refs, y_refs):
    even_x, even_y = sh.here(0) % 2 == 0, sh.here(1) % 2 == 0

    def face(at, count, stride, label_at, label_count, label_stride):
        rows = [natural_ref[m, pl.ds(at, count, stride=stride), :] for m in range(4)]
        return rows, stiff[pl.ds(label_at, label_count, stride=label_stride), :]

    above = face(sh.cells - sh.y, sh.y, 1, (label_x - 1) * label_y, label_y, 1)
    below = face(0, sh.y, 1, 0, label_y, 1)
    for refs, links, even, above, below in (
        (x_refs, sh.x_links, even_x, above, below),
        (
            y_refs,
            sh.y_links,
            even_y,
            face(sh.y - 1, sh.x, sh.y, label_y - 1, label_x, label_y),
            face(0, sh.x, sh.y, 0, label_x, label_y),
        ),
    ):
        for i, ref in enumerate(refs):
            ref[...] = jnp.zeros(ref.shape, f32)
            count = above[0][0].shape[0]
            for m in range(4):
                ref[m * count : (m + 1) * count, :] = pair(links, even, above[0][m], below[0][m])[i]
            labels, length = above[1].shape
            ref[4 * count : 4 * count + labels, 0:length] = pair(links, even, above[1], below[1])[i]


def merge_start(sh, refs, x_refs, y_refs, received_ref, sizes, cells, labels):
    residual, nodes, stiff, stiff_rim = refs
    label_x, label_y, label_z = sizes
    lane, along, across = sh.lane_grid(1)
    inside = lane < sh.used
    last = (sh.x + 1) * sh.pitch
    x_mask = {-1: lane < sh.pitch, 0: (lane >= sh.pitch) & (lane < last), 1: (lane >= last) & inside}
    y_mask = {-1: across < 0, 0: (across >= 0) & (across < sh.y), 1: across >= sh.y}
    cells[...] = jnp.zeros(cells.shape, f32)
    labels[...] = jnp.zeros(labels.shape, f32)
    count, label_count = cells.shape[1], labels.shape[0]
    at = label_at = 0
    for axis, face_refs, size, label_size in ((0, x_refs, sh.y, label_y), (1, y_refs, sh.x, label_x)):
        for message in sides(sh, axis, [ref[...] for ref in face_refs]):
            for m in range(4):
                cells[m, at : at + size, :] = message[m * size : (m + 1) * size]
            labels[label_at : label_at + label_size, :] = message[4 * size : 4 * size + label_size, 0:label_z]
            at, label_at = at + size, label_at + label_size
    for dx, dy in ((-1, -1), (-1, 1), (1, -1), (1, 1)):
        slot = slot_from(sh, received_ref, (dx, dy, 0))
        for m, row in enumerate((0, 1, 2, 5)):
            cells[m, at : at + 1, :] = slot[row : row + 1]
        labels[label_at : label_at + 1, :] = slot[3:4, 0:label_z]
        at, label_at = at + 1, label_at + 1
    x, y, _, valid = ring(sh.x, sh.y, count)
    place = (valid & inside & (along == x) & (across == y)).astype(f32)
    own = slice(EDGE, EDGE + sh.z)
    tall_own = slice(2 * EDGE, 2 * EDGE + sh.z)
    for m in range(3):
        residual[m, own, :] += to_lanes(cells[m], place)
    nodes[own, :] += to_lanes(cells[3], place, small)
    by_z = lax.dot_general(
        repeat_twice(label_z), labels[...], (((1,), (1,)), ((), ())), precision=highest, preferred_element_type=f32
    )
    x, y, at_x, valid = ring(label_x, label_y, label_count)
    match = valid & inside & ((along >> 1) == x) & ((across >> 1) == y)
    columns = jnp.dot(by_z, (match & at_x).astype(f32), precision=highest, preferred_element_type=f32)
    stiff_rim[0, tall_own, :] = columns
    columns = columns + jnp.dot(by_z, (match & ~at_x).astype(f32), precision=highest, preferred_element_type=f32)
    stiff[0, tall_own, :] += columns
    for dz in (-1, 1):
        main = edge = jnp.zeros((8, LANES), f32)
        for dx in (-1, 0, 1):
            for dy in (-1, 0, 1):
                slot = slot_from(sh, received_ref, (dx, dy, dz))
                mask = x_mask[dx] & y_mask[dy]
                main = main + pick(mask, shift(slot, dx * sh.x * sh.pitch + dy * sh.y))
                if dx:
                    edge = edge + pick(mask, shift(slot, dx * (sh.x - 1) * sh.pitch + dy * sh.y))
        near = EDGE + sh.z if dz > 0 else EDGE - 1
        for m in range(3):
            residual[m, near : near + 1, :] = main[m : m + 1]
        nodes[near : near + 1, :] = main[5:6]
        for row in (EDGE + near, EDGE + near + dz):
            stiff[0, row : row + 1, :] = main[3:4]
            stiff_rim[0, row : row + 1, :] = edge[3:4]


def call(kernel, name, outs, ins, scratch=(), remote_ins=False, remote_outs=()):
    space = pltpu.HBM if remote_ins else pltpu.VMEM
    return pl.pallas_call(
        kernel,
        out_shape=[jax.ShapeDtypeStruct(shape, f32) for shape in outs],
        in_specs=[pl.BlockSpec(memory_space=space) for _ in ins],
        out_specs=[
            pl.BlockSpec(memory_space=pltpu.HBM if i in remote_outs else pltpu.VMEM) for i in range(len(outs))
        ],
        scratch_shapes=[pltpu.VMEM(shape, f32) if isinstance(shape, tuple) else shape for shape in scratch],
        compiler_params=pltpu.CompilerParams(vmem_limit_bytes=(56 if remote_ins else 48) * 1024 * 1024),
        name=name,
    )(*ins)


def permutation(sizes, moves):
    def partner(axis, link, index):
        size = sizes[axis]
        other = index ^ 1 if link == 0 else index + (1 if index % 2 else -1)
        if 0 <= other < size:
            return other
        return size - 1 - index if axis == 2 and size % 2 == 0 else index

    pairs = []
    for x in range(sizes[0]):
        for y in range(sizes[1]):
            for z in range(sizes[2]):
                place = [x, y, z]
                goal = [partner(a, moves[a], place[a]) if a in moves else place[a] for a in range(3)]
                if any(goal[a] == place[a] for a in moves) and sizes[2] % 2 == 0:
                    goal = [x, y, partner(2, 0, z)]
                flat = [(p[0] * sizes[1] + p[1]) * sizes[2] + p[2] for p in (place, goal)]
                pairs.append(tuple(flat))
    return pairs


def send(sh, value, moves):
    return lax.ppermute(value, AXES, permutation(sh.sizes, moves))


def send_z(sh, messages):
    return [send(sh, message, {2: link}) for link, message in enumerate(messages)]


def send_faces(sh, x_messages, y_messages):
    from_x = [send(sh, message, {0: link}) for link, message in enumerate(x_messages)]
    from_y = [send(sh, message, {1: link}) for link, message in enumerate(y_messages)]
    return from_y, from_x


def to_all(slots):
    return lax.all_to_all(slots, AXES, 0, 0, tiled=True)


def exchange(sh, ex, name, field, z_messages):
    from_z = send_z(sh, z_messages)

    corners = sh.x_links * sh.y_links

    def packer(*refs):
        take = Taker(refs)
        field_ref, z_refs = take.one(), take(sh.z_links)
        x_refs, y_refs, corner_refs, scratch = take(sh.x_links), take(sh.y_links), take(corners), take.one()
        merge_z(sh, ex, field_ref, z_refs, scratch, 0)
        pack_xy(sh, ex, scratch, x_refs, y_refs, corner_refs)

    plane = (sh.rows, LANES)
    messages = call(
        packer,
        name,
        [plane] * sh.x_links
        + [folded_shape(sh, ex.fields * ex.layers)] * sh.y_links
        + [folded_shape(sh, ex.layers)] * corners,
        [field] + from_z,
        [(ex.fields,) + plane],
    )
    take = Taker(messages)
    x_messages, y_messages = take(sh.x_links), take(sh.y_links)
    from_y, straight = send_faces(sh, x_messages, y_messages)
    from_x = []
    for link in range(sh.x_links):
        from_x.append(straight[link])
        from_x.extend(send(sh, take.one(), {0: link, 1: other}) for other in range(sh.y_links))
    return from_z, from_y, from_x


class Taker:
    def __init__(self, refs):
        self.refs, self.at = refs, 0

    def __call__(self, count):
        self.at += count
        return self.refs[self.at - count : self.at]

    def one(self):
        return self(1)[0]


def merge_all(sh, ex, take, scratch, rim, guard):
    field = take.one()
    from_z, from_y = take(sh.z_links), take(sh.y_links)
    from_x = take(sh.x_links * (1 + sh.y_links))
    merge_z(sh, ex, field, from_z, scratch, guard)
    merge_xy(sh, ex, scratch, rim, guard, from_y, from_x)


def body(right_side, phase_labels, phase_moduli, coarse_nodes, coarse_inverse):
    sizes = tuple(lax.axis_size(axis) for axis in AXES)
    _, size_x, size_y, size_z = right_side.shape
    sh = Shape(size_x, size_y, size_z, phase_moduli.shape[0], sizes)
    unknowns = coarse_inverse.shape[0]
    node_count = unknowns // 6
    sum_rows = -(-unknowns // 8) * 8 + 8
    share_rows = coarse_inverse.shape[1] // LANES
    own = slice(EDGE, EDGE + sh.z)
    plane = (sh.rows, LANES)
    fields = (3,) + plane
    tall = (3, sh.tall, LANES)
    slots = (sh.devices, LANES)
    z_shape = lambda ex: [(8 * ex.fields, LANES)] * sh.z_links
    natural = right_side.reshape(3, sh.cells, sh.z)
    nodes_natural = coarse_nodes.reshape(sh.cells, sh.z)
    label_x, label_y, label_z = phase_labels.shape

    def block_places():
        lane, along, across = sh.lane_grid(label_x * label_y)
        inside = (along >= 0) & (along < sh.x) & (across >= 0) & (across < sh.y)
        block = lax.broadcasted_iota(jnp.int32, along.shape, 0)
        return (inside & (block == (along >> 1) * label_y + (across >> 1))).astype(f32)

    def end_layers(values, places):
        length = values.shape[1]
        row = lax.broadcasted_iota(jnp.int32, (8, length), 0)
        at = lax.broadcasted_iota(jnp.int32, (8, length), 1)
        ends = ((row == 0) & (at == length - 1)) | ((row == 1) & (at == 0))
        return jnp.dot(to_cells(values, ends.astype(f32)), places, precision=highest, preferred_element_type=f32)

    def begin(natural_in, labels_in, moduli_in, nodes_in, stiff, slots_ref, *rest):
        x_refs, y_refs = rest[: sh.x_links], rest[sh.x_links : sh.x_links + sh.y_links]
        natural_ref, labels_ref, moduli_ref, nodes_ref, sems, sums, lines = rest[sh.x_links + sh.y_links :]
        pairs = ((natural_in, natural_ref.at[0:3, 0 : sh.cells, :]), (labels_in, labels_ref.at[0:label_x]), (moduli_in, moduli_ref), (nodes_in, nodes_ref))
        copies = [pltpu.make_async_copy(a, b, sems.at[i]) for i, (a, b) in enumerate(pairs)]
        for copy in copies:
            copy.start()
        sums[...] = jnp.zeros(sums.shape, f32)
        lines[...] = jnp.zeros(lines.shape, f32)
        for copy in copies:
            copy.wait()
        for i in range(label_x):
            labels = labels_ref[i]
            moduli = jnp.zeros(labels.shape, f32)
            for phase in range(sh.phases):
                moduli = jnp.where(labels == phase, moduli_ref[phase], moduli)
            stiff[i * label_y : (i + 1) * label_y, :] = moduli * (1.0 / SCALE)
        natural_ref[3, 0 : sh.cells, :] = nodes_ref[...].astype(f32) + 1.0
        cells = [natural_ref[m, 0 : sh.cells, :] for m in range(4)]
        coarse_sums(nodes_ref[...], cells[:3], cell_coords(sh), node_count, sums)
        line = sums_line(sh, sums, unknowns)
        for i, (cell, block) in enumerate(
            (
                (0, 0),
                (sh.y - 1, label_y - 1),
                ((sh.x - 1) * sh.y, (label_x - 1) * label_y),
                (sh.cells - 1, label_x * label_y - 1),
            )
        ):
            for m in range(3):
                lines[8 * i + m : 8 * i + m + 1, :] = natural_ref[m, cell : cell + 1, :]
            lines[8 * i + 3 : 8 * i + 4, 0:label_z] = stiff[block : block + 1, :]
            lines[8 * i + 5 : 8 * i + 6, :] = natural_ref[3, cell : cell + 1, :]
        select = selection(sh)
        layers = [end_layers(cells[m], select) for m in range(4)] + [end_layers(stiff[0 : label_x * label_y, :], block_places())]
        for i in range(2):
            for layer, row in zip(layers, (0, 1, 2, 5, 3)):
                lines[8 * (4 + i) + row : 8 * (4 + i) + row + 1, :] = layer[i : i + 1]
        for i in range(6):
            lines[8 * i + 4 : 8 * i + 5, :] = line
        send_lines(sh, lines, slots_ref)
        pack_faces(sh, natural_ref, stiff, label_x, label_y, x_refs, y_refs)

    block_rows = (8 * -(-(label_x + 8) * label_y // 8), label_z)
    stiff_blocks, lines, *messages = call(
        begin,
        "begin",
        [block_rows, (8 * sh.devices, LANES)]
        + [face_shape(sh, label_x, label_y)] * (sh.x_links + sh.y_links),
        [natural, phase_labels, phase_moduli, nodes_natural],
        [
            (4, sh.cells + 8, sh.z),
            pltpu.VMEM((label_x + 2, label_y, label_z), jnp.int32),
            pltpu.SMEM(phase_moduli.shape, f32),
            pltpu.VMEM(nodes_natural.shape, jnp.int32),
            pltpu.SemaphoreType.DMA((4,)),
            (LANES, LANES),
            (56, LANES),
        ],
        remote_ins=True,
    )

    def spread(natural_ref, nodes_ref, stiff, inverse_in, field_ref, lanes_ref, inverse_ref):
        inverse_ref[...] = inverse_in[...]
        select = selection(sh)
        field_ref[...] = jnp.zeros(field_ref.shape, f32)
        for m in range(3):
            field_ref[m, own, :] = to_lanes(natural_ref[m], select)
        by_z = lax.dot_general(
            repeat_twice(label_z),
            stiff[0 : label_x * label_y, :],
            (((1,), (1,)), ((), ())),
            precision=highest,
            preferred_element_type=f32,
        )
        field_ref[3, own, :] = jnp.dot(by_z, block_places(), precision=highest, preferred_element_type=f32)
        lanes_ref[...] = to_lanes(nodes_ref[...].astype(f32) + 1.0, select, small) - 1.0

    start_field, nodes, inverse = call(
        spread,
        "spread",
        [(4,) + plane, (sh.z, LANES), coarse_inverse.shape],
        [natural, nodes_natural, stiff_blocks, coarse_inverse],
    )
    from_y, from_x = send_faces(sh, messages[: sh.x_links], messages[sh.x_links :])
    lines = to_all(lines)

    short = (3, 6 * EDGE, LANES)
    short_fields = (3, 4 * EDGE, LANES)
    tall_columns = (len(COLUMNS), sh.tall, LANES)
    solve_scratch = [tall] * 4 + [fields, tall_columns]
    short_scratch = [short] * 4 + [short_fields, (len(COLUMNS), 6 * EDGE, LANES)]

    def end_rows(ref):
        def rows(f, start, count):
            place = start + EDGE if start < 2 * EDGE else start - sh.rows + 5 * EDGE
            return ref[f, place : place + count, :]

        return rows

    def first_ends(*refs):
        take = Taker(refs)
        field_ref = take.one()
        y_refs, x_refs = take(sh.y_links), take(sh.x_links)
        nodes_ref, lines_ref, inverse_ref = take(3)
        residual, wide_nodes, stiffness_ref, values = take(4)
        z_refs = take(sh.z_links)
        stiff, stiff_rim, cells, labels, short_stiff, some_residual, springs = take(7)
        v0, v1, kv0, kv1, factor, columns = take(6)
        clear_guards(sh, (stiff, stiff_rim, short_stiff, v0, v1, kv0, kv1, columns))
        residual[...] = field_ref[0:3]
        put(stiff, 0, field_ref[3])
        put(stiff_rim, 0, jnp.zeros(plane, f32))
        sizes = phase_labels.shape
        wide_nodes[...] = jnp.zeros(plane, f32)
        wide_nodes[own, :] = nodes_ref[...] + 1.0
        merge_start(sh, (residual, wide_nodes, stiff, stiff_rim), x_refs, y_refs, lines_ref, sizes, cells, labels)
        wide_nodes[...] = wide_nodes[...] - 1.0
        stiffness_ref[0] = inner(stiff, 0)
        stiffness_ref[1] = inner(stiff_rim, 0)
        coarse_solution(lines_ref[pl.ds(4, sh.devices, stride=8), :], inverse_ref, values)
        lane, _, _ = sh.lane_grid(1)
        put(short_stiff, 0, ends(stiffness_ref[0]))
        put_columns(sh, ends(stiffness_ref[0]), ends(stiffness_ref[1]), columns)
        for f, entry in enumerate(own_block(short_stiff, columns)):
            springs[f] = entry
        springs[6] = inner(short_stiff, 0)
        for m in range(3):
            some_residual[m] = ends(residual[m])
        index = local_solve(sh, ends_level(sh), some_residual, springs, columns, (v0, v1), (kv0, kv1), factor)
        solution = (v0, v1)[index]
        z = lax.broadcasted_iota(jnp.int32, (2 * EDGE, LANES), 0)
        z = jnp.where(z < EDGE, z, z + sh.z - 2 * EDGE)
        some_nodes = jnp.concatenate([nodes_ref[0:EDGE, :], nodes_ref[sh.z - EDGE : sh.z, :]], axis=0)
        added = coarse_cells(some_nodes, coords(sh, z), values, node_count)
        for m in range(3):
            solution[m, 2 * EDGE : 4 * EDGE, :] += added[m]
        pack_z(sh, DEEP, end_rows(solution), z_refs)

    residual, wide_nodes, stiffness, values, *z_messages = call(
        first_ends,
        "first_ends",
        [fields, plane, (2,) + plane, (sum_rows, LANES)] + z_shape(DEEP),
        [start_field, *from_y, *from_x, nodes, lines, inverse],
        [(1, sh.tall, LANES)] * 2
        + [
            (4, 8 * -(-(2 * sh.x + 2 * sh.y + 4) // 8) + 8, LANES),
            (8 * -(-(2 * label_x + 2 * label_y + 4) // 8) + 8, label_z),
        ]
        + [(1, 6 * EDGE, LANES)]
        + [short_fields, (7, 4 * EDGE, LANES)]
        + short_scratch,
    )

    def first_solve(residual_ref, stiffness_ref, values, nodes_ref, solution_ref, springs_ref, *rest):
        stiff, v0, v1, kv0, kv1, factor, columns = rest
        clear_guards(sh, (stiff, v0, v1, kv0, kv1, columns))
        put(stiff, 0, stiffness_ref[0])
        put_columns(sh, stiffness_ref[0], stiffness_ref[1], columns)
        springs_ref[6] = stiffness_ref[0]
        springs_ref[7] = stiffness_ref[1]
        lane, _, _ = sh.lane_grid(1)
        for f, entry in enumerate(own_block(stiff, columns)):
            springs_ref[f] = entry
        index = local_solve(sh, level(sh), residual_ref, springs_ref, columns, (v0, v1), (kv0, kv1), factor)
        for m in range(3):
            solution_ref[m] = inner((v0, v1)[index], m)
        added = coarse_cells(nodes_ref[...], coords(sh, own_level(sh)), values, node_count)
        for m in range(3):
            solution_ref[m, own, :] += added[m]

    solved, springs = call(
        first_solve,
        "first_solve",
        [fields, (8,) + plane],
        [residual, stiffness, values, nodes],
        [(1, sh.tall, LANES)] + solve_scratch,
    )
    from_z, from_y, from_x = exchange(sh, DEEP, "deep", solved, z_messages)

    def first_image(*refs):
        take = Taker(refs)
        merging = take(1 + sh.z_links + sh.y_links + sh.x_links * (1 + sh.y_links))
        nodes_ref, springs_ref, inverse_ref = take(3)
        search_ref, image_ref, slots_out = take(3)
        z_refs = take(sh.z_links)
        v, rim, kv, k_rim, sums, shares, slots_ref, sem = take(8)
        some_residual, some_springs, v0, v1, kv0, kv1, factor, some_columns, columns = take(9)
        clear_guards(sh, (v0, v1, kv0, kv1))
        clear_guards(sh, (v, rim, kv, k_rim))
        merge_all(sh, DEEP, Taker(merging), v, rim, EDGE)
        lane, _, _ = sh.lane_grid(1)

        in_grid, in_rim = grid_masks(sh)
        for m in range(3):
            value = pick(in_grid, inner(v, m))
            put(v, m, value)
            search_ref[m] = value
            put(kv, m, springs_ref[6] * value)
            value = pick(in_rim, inner(rim, m))
            put(rim, m, value)
            put(k_rim, m, springs_ref[7] * value)
        put_columns(sh, springs_ref[6], None, columns)
        image = image_of(sh, lane, v, kv, (rim, k_rim), springs_ref, columns)
        keep = in_grid & extended_mask(sh, level(sh))
        for m in range(3):
            image_ref[m] = pick(keep, image[m])
        sums[...] = jnp.zeros(sums.shape, f32)
        field = [image_ref[m, own, :] for m in range(3)]
        coarse_sums(nodes_ref[...], field, coords(sh, own_level(sh)), node_count, sums)
        coarse_shares(sums, inverse_ref, shares)
        for device in range(sh.devices):
            slots_ref[device * share_rows : (device + 1) * share_rows, :] = shares[0:share_rows, :]
        copy = pltpu.make_async_copy(slots_ref.at[0 : slots_out.shape[0], :], slots_out, sem)
        copy.start()
        for m in range(3):
            some_residual[m] = ends(image_ref[m])
        for f in range(7):
            some_springs[f] = ends(springs_ref[f])
        put_columns(sh, some_springs[6], None, some_columns)
        index = local_solve(sh, ends_level(sh), some_residual, some_springs, some_columns, (v0, v1), (kv0, kv1), factor)
        pack_z(sh, NEAR, end_rows((v0, v1)[index]), z_refs)
        copy.wait()

    all_slots = (sh.devices * share_rows, LANES)
    search, image, shares, *z_messages = call(
        first_image,
        "first_image",
        [fields, fields, all_slots] + z_shape(NEAR),
        [solved, *from_z, *from_y, *from_x, nodes, springs, inverse],
        [tall] * 4
        + [(LANES, LANES), (8 * -(-share_rows // 8) + 8, LANES)]
        + [(8 * -(-all_slots[0] // 8) + 8, LANES), pltpu.SemaphoreType.DMA]
        + [short_fields, (7, 4 * EDGE, LANES)]
        + short_scratch
        + [tall_columns],
        remote_outs=(2,),
    )
    shares = to_all(shares.reshape(sh.devices, 1, share_rows * LANES)).reshape(shares.shape)

    def second_solve(image_ref, springs_ref, local_ref, v0, v1, kv0, kv1, factor, columns):
        clear_guards(sh, (v0, v1, kv0, kv1))
        put_columns(sh, springs_ref[6], None, columns)
        index = local_solve(sh, level(sh), image_ref, springs_ref, columns, (v0, v1), (kv0, kv1), factor)
        for m in range(3):
            local_ref[m] = inner((v0, v1)[index], m)

    (solved,) = call(second_solve, "second_solve", [fields], [image, springs], solve_scratch)
    from_z, from_y, from_x = exchange(sh, NEAR, "near", solved, z_messages)

    def between(shares_ref, wide_nodes, nodes_ref, start_ref, search_ref, first_ref, coarse_ref, sums, *scratch):
        flat, table, values = scratch
        coarse_ref[...] = jnp.zeros(coarse_ref.shape, f32)
        coarse_table(sh, shares_ref, unknowns, flat, table)
        last = lax.broadcasted_iota(jnp.int32, (1, LANES), 0) + sh.z - 1
        for dz, first, z in ((0, EDGE, own_level(sh)), (-1, EDGE - 1, last), (1, EDGE + sh.z, last - sh.z + 1)):
            values[...] = region_values(sh, table, dz)
            rows = slice(first, first + z.shape[0])
            added = coarse_cells(wide_nodes[rows, :], coords(sh, z), values, node_count)
            for m in range(3):
                coarse_ref[m, rows, :] = added[m]
        valid = nodes_ref[...] >= 0.0
        row = lax.broadcasted_iota(jnp.int32, sums.shape, 0)
        total = jnp.zeros(sums.shape, f32)
        for i, other in enumerate((start_ref, first_ref)):
            product = sum(search_ref[m, own, :] * other[m, own, :] for m in range(3))
            total = jnp.where(row == i, fold_rows(pick(valid, product)), total)
        sums[...] = total

    coarse_field, sums = call(
        between,
        "between",
        [fields, (8, LANES)],
        [shares, wide_nodes, nodes, start_field, search, image],
        [(8 * -(-share_rows // 8) + 8, LANES), (8 * -(-sh.devices // 8) + 8, LANES), (LANES, LANES)],
    )

    def second_image(*refs):
        take = Taker(refs)
        merging = take(1 + sh.z_links + sh.y_links + sh.x_links * (1 + sh.y_links))
        nodes_ref, springs_ref, first_ref, coarse_ref, early_ref = take(5)
        second_ref, image_ref, slots_ref = take(3)
        v, kv, sums, columns = take(4)
        clear_guards(sh, (v, kv))
        put_columns(sh, springs_ref[6], None, columns)
        merge_all(sh, NEAR, Taker(merging), v, None, EDGE)
        lane, _, _ = sh.lane_grid(1)
        in_grid, _ = grid_masks(sh)
        for m in range(3):
            value = pick(in_grid, inner(v, m)) + coarse_ref[m]
            put(v, m, value)
            second_ref[m] = value
            put(kv, m, springs_ref[6] * value)
        image = image_of(sh, lane, v, kv, None, springs_ref, columns)
        for m in range(3):
            image_ref[m] = image[m]
        valid = nodes_ref[...] >= 0.0
        sums[...] = jnp.zeros(sums.shape, f32)
        sums[0:8, :] = early_ref[...]
        for i, other in ((2, first_ref), (3, image_ref)):
            product = sum(second_ref[m, own, :] * other[m, own, :] for m in range(3))
            sums[i : i + 1, :] = fold_rows(pick(valid, product))
        slots_ref[...] = jnp.broadcast_to(lane_sums(sums)[0:1], slots_ref.shape)

    second, second_image_field, sums = call(
        second_image,
        "second_image",
        [fields, fields, slots],
        [solved, *from_z, *from_y, *from_x, nodes, springs, image, coarse_field, sums],
        [tall] * 2 + [(LANES, LANES), tall_columns],
    )
    totals = to_all(sums)

    def turn(search_ref, first_ref, second_ref, image_ref, out_ref):
        select = selection(sh)
        for i, ref in enumerate((search_ref, first_ref, second_ref, image_ref)):
            for m in range(3):
                out_ref[i, m] = to_cells(ref[m, own, :], select)

    (turned,) = call(turn, "turn", [(4,) + natural.shape], [search, image, second, second_image_field])

    def finish(totals_ref, natural_ref, turned_ref, field_ref, residual_ref):
        total = jnp.sum(totals_ref[...], axis=0, keepdims=True)
        rz, zw, wq, qv = [total[:, i : i + 1] for i in range(4)]
        step0 = rz / zw
        rho = step0 * step0 * wq - step0 * zw
        grow = 1.0 + rho / rz
        curvature = grow * grow * zw - 2.0 * grow * step0 * wq + step0 * step0 * qv
        step1 = rho / curvature
        first = step0 + step1 * grow
        second = step0 * step1
        for m in range(3):
            field_ref[m] = first * turned_ref[0, m] - second * turned_ref[2, m]
            residual_ref[m] = natural_ref[m] - (first * turned_ref[1, m] - second * turned_ref[3, m])

    solution_field, residual = call(
        finish, "finish", [natural.shape, natural.shape], [totals, natural, turned]
    )
    return solution_field.reshape(right_side.shape), residual.reshape(right_side.shape)


def solution(mesh):
    in_specs = (
        P(None, "gx", "gy", "gz"),
        P("gx", "gy", "gz"),
        P(),
        P("gx", "gy", "gz"),
        P(("gx", "gy", "gz"), None),
    )
    out_specs = (P(None, "gx", "gy", "gz"), P(None, "gx", "gy", "gz"))
    return jax.shard_map(body, mesh=mesh, in_specs=in_specs, out_specs=out_specs, check_vma=False)
```
